32 devices in a mesh: ang: 8 (over z, y), pos: 4 (over x, core).
Axes of the slice: x: 2, y: 2, z: 4, core: 2. Of those that a mesh axis runs over, the one named last changes fastest.
Arguments:
- volume: bfloat16 [2, 256, 32768], P(None, 'ang', 'pos'), may hold values from -6 to 6
- radon_tiles: bfloat16 [32, 64, 256], replicated, may hold values from -0.375 to 0.375
- tile_blocks: int32 [32, 32, 4], replicated, may hold values from 0 to 511
- probe_field: bfloat16 [2, 256, 256], replicated, may hold values from -6 to 6
- amplitudes: bfloat16 [32, 16, 256, 256], P('ang', 'pos'), may hold values from 0.099609375 to 3
- offsets: int32 [32, 16], P('ang', 'pos'), may hold values from 0 to 2047, as said below
- counts: int32 [32, 4], P('ang', 'pos'), may hold values from 1 to 4, 12 in all within a row
Outputs:
- new_volume: float32 [2, 256, 32768], P(None, 'ang', 'pos')
- proj_grad: float32 [2, 256, 32, 2048], P(None, None, 'ang', 'pos')
The draws below stay inside these ranges and needn't reach their ends.
Inputs may be any that keep to these rules, and one draw needn't show every extreme that they name: Each position lies in the tile of the device that holds its slot: 512 * (q // 4) <= offsets[a, q] < 512 * (q // 4 + 1). Every row of counts has an entry equal to 4.
All inputs are finite; a program needn't handle non-finite values. No bound on the sum of `counts` on one device may be relied on, other than what follows from the above.
Results may differ from the reference program's by a relative error of at most 0.0062.
Values may be sent and summed in bfloat16 or wider, within the bound.
No kernel may reach another device: no remote copies, remote signals or barrier semaphores. Data moves between devices by JAX's collectives and lax.ppermute only.
A program may use at most 192 MiB of HBM per device.

```python
import math
import jax
import jax.numpy as jnp
import numpy as np
from jax import lax

PROBE = 256
U = 2048
BLOCK = 64
J = 4
POS_DEV = 4
ANG = 32
SLICES = 256
TILE_W = 512
UB = 32
KB = 512
KCOEF = 32768
POSITIONS = 16
N_POS = 4


def draw_offsets(key, part):
    slot_index = jnp.arange(POS_DEV * N_POS, dtype=jnp.int32)
    jitter = jax.random.randint(key, (ANG, POS_DEV * N_POS), 0, TILE_W, dtype=jnp.int32)
    jitter = jitter.at[0, 0].set(0)
    jitter = jitter.at[0, POS_DEV * N_POS - 1].set(TILE_W - 1)
    return (slot_index // POS_DEV * TILE_W)[None, :] + jitter


def with_ends(values, stream_key, low, high):
    extent = values.shape
    place = [jax.random.randint(jax.random.fold_in(stream_key, axis), (), 0, extent[axis]) for axis in range(len(extent))]
    values = values.at[tuple(place)].set(low)
    longest = extent.index(max(extent))
    place[longest] = (place[longest] + 1) % extent[longest]
    return values.at[tuple(place)].set(high)


def level_of(rng, dims, pieces, low, top_value):
    def one(dim, blocks):
        heights = jax.random.uniform(jax.random.fold_in(jax.random.fold_in(rng, 6), dim), (blocks,), jnp.float32, low / len(pieces), top_value / len(pieces))
        return jnp.repeat(jnp.exp(heights), dims[dim] // blocks).reshape((-1,) + (1,) * (len(dims) - dim - 1))

    loudness = one(*pieces[0])
    for cut in pieces[1:]:
        loudness = loudness * one(*cut)
    return loudness


def split_up(count, total, reach, lean):
    weights = [(1 << 20) // math.isqrt(grade ** lean) + 1 for grade in range(2, count + 1)]
    surplus, holding = total - reach - (count - 1), [1] * (count - 1)
    while surplus > 0:
        free = [i for i in range(count - 1) if holding[i] < reach]
        whole, remaining = sum([weights[i] for i in free]), surplus
        for i in free:
            extra = min(reach - holding[i], max(1, remaining * weights[i] // whole), surplus)
            holding[i] = holding[i] + extra
            surplus = surplus - extra
    return np.array([reach] + holding)


def uneven_parts(rng, count, total, reach, lean):
    if count == 2:
        one = jax.random.randint(rng, (), max(1, total - reach), min(reach, total - 1) + 1)
        return jnp.stack([one, total - one])
    sizes = jnp.asarray(split_up(count, total, reach, lean), jnp.int32)
    twos = (count - 1) // 2
    donor, taker = sizes[1:1 + 2 * twos:2], sizes[2:2 + 2 * twos:2]
    room = jnp.minimum(donor - 1, reach - taker)
    passed = jax.random.randint(jax.random.fold_in(rng, 1), (twos,), 0, 1 << 20) % (room + 1)
    sizes = sizes.at[1:1 + 2 * twos:2].set(donor - passed).at[2:2 + 2 * twos:2].set(taker + passed)
    return sizes[jax.random.permutation(jax.random.fold_in(rng, 2), count)]


def gaussian(rng, dims, deviation, bound, pieces=(), kind=jnp.bfloat16):
    drawn = deviation * jax.random.normal(rng, dims, jnp.float32)
    if pieces:
        drawn = drawn * level_of(rng, dims, pieces, -0.22, 0.18)
    return jnp.clip(drawn, -bound, bound).astype(kind)


def setup_inputs(seed: int = 0) -> dict:
    splits = jax.random.split(jax.random.key(seed), 8)
    return {
        "volume": gaussian(splits[0], (2, SLICES, KCOEF), 1.0, 6.0, ((1, 8), (2, 4))),
        "radon_tiles": gaussian(splits[1], (ANG, BLOCK, J * BLOCK), (J * BLOCK) ** -0.5, 0.375),
        "tile_blocks": with_ends(jax.random.randint(splits[2], (ANG, UB, J), 0, KB), jax.random.fold_in(splits[2], 1), 0, KB - 1).astype(jnp.int32),
        "probe_field": gaussian(splits[3], (2, PROBE, PROBE), 1.0, 6.0),
        "amplitudes": jnp.clip(jnp.exp(math.log(3.0) - 3.4051113 * jax.random.uniform(splits[4], (ANG, POSITIONS, PROBE, PROBE), jnp.float32) ** level_of(splits[4], (ANG, POSITIONS, PROBE, PROBE), ((0, 8), (1, 4)), -0.2, 0.2)), 0.099609375, 3.0).astype(jnp.bfloat16),
        "offsets": draw_offsets(jax.random.fold_in(splits[7], 71), 0),
        "counts": jax.vmap(lambda own: uneven_parts(own, N_POS, POS_DEV * N_POS * 3 // 4, POS_DEV, 2))(jax.random.split(splits[6], ANG)).reshape((ANG, N_POS)).astype(jnp.int32),
    }


step_size = 0.1

def rounded(value):
    return lax.optimization_barrier(value.astype(jnp.bfloat16))

def dft_tables(width):
    index = jnp.arange(width, dtype=jnp.int32)
    phase = index[:, None] * index[None, :] % width
    turn = 2.0 * math.pi / width * phase.astype(jnp.float32)
    cosine = (jnp.cos(turn) / math.sqrt(width)).astype(jnp.bfloat16)
    sine_neg = (-jnp.sin(turn) / math.sqrt(width)).astype(jnp.bfloat16)
    return (cosine, sine_neg)

def left_mul(table, field):
    return jnp.einsum('zy,qyu->qzu', table.astype(jnp.float32), field.astype(jnp.float32))

def right_mul(field, table):
    return jnp.einsum('qzy,yu->qzu', field.astype(jnp.float32), table.astype(jnp.float32))

def exit_gradient(patches, probe_field, amplitude_rows, live_mask):
    probe_re = probe_field[0].astype(jnp.float32)
    probe_im = probe_field[1].astype(jnp.float32)
    patch_re = patches[:, 0].astype(jnp.float32)
    patch_im = patches[:, 1].astype(jnp.float32)
    wave_re = rounded(probe_re * patch_re - probe_im * patch_im)
    wave_im = rounded(probe_re * patch_im + probe_im * patch_re)
    cosine, sine_neg = dft_tables(patches.shape[-1])
    half_re = rounded(left_mul(cosine, wave_re) - left_mul(sine_neg, wave_im))
    half_im = rounded(left_mul(cosine, wave_im) + left_mul(sine_neg, wave_re))
    far_re = right_mul(half_re, cosine) - right_mul(half_im, sine_neg)
    far_im = right_mul(half_re, sine_neg) + right_mul(half_im, cosine)
    modulus = jnp.sqrt(far_re * far_re + far_im * far_im)
    factor = amplitude_rows.astype(jnp.float32) / jnp.maximum(modulus, 1.0) - 1.0
    delta_re = rounded(far_re * factor)
    delta_im = rounded(far_im * factor)
    back_re = rounded(left_mul(cosine, delta_re) + left_mul(sine_neg, delta_im))
    back_im = rounded(left_mul(cosine, delta_im) - left_mul(sine_neg, delta_re))
    near_re = right_mul(back_re, cosine) + right_mul(back_im, sine_neg)
    near_im = right_mul(back_im, cosine) - right_mul(back_re, sine_neg)
    scale_mask = live_mask[:, None, None]
    grad_re = (probe_re * near_re + probe_im * near_im) * scale_mask
    grad_im = (probe_re * near_im - probe_im * near_re) * scale_mask
    return jnp.stack([grad_re, grad_im], axis=1)

def reference(volume, radon_tiles, tile_blocks, probe_field, amplitudes, offsets, counts):
    blocks = volume.reshape(2, SLICES, KB, BLOCK)

    def forward(pair):
        tile_angle, ids_angle = pair
        picked = jnp.take(blocks, ids_angle.reshape(-1), axis=2)
        picked = picked.reshape(2, SLICES, UB, J * BLOCK)
        products = jnp.einsum('csux,mx->csum', picked.astype(jnp.float32), tile_angle.astype(jnp.float32))
        return products.reshape(2, SLICES, U)
    projection = rounded(lax.map(forward, (radon_tiles, tile_blocks)))

    def angle_step(group):
        proj_angle, offset_row, amplitude_row, counts_row = group
        columns = (offset_row[:, None] + jnp.arange(PROBE, dtype=jnp.int32)[None, :]) % U
        patches = jnp.transpose(proj_angle[:, :, columns], (2, 0, 1, 3))
        slot_index = jnp.arange(POSITIONS, dtype=jnp.int32)
        live_mask = (slot_index % POS_DEV < counts_row[slot_index // POS_DEV]).astype(jnp.float32)
        patch_grads = exit_gradient(patches, probe_field, amplitude_row, live_mask)
        summed = jnp.zeros((2, SLICES, U), jnp.float32)
        return summed.at[:, :, columns].add(jnp.transpose(patch_grads, (1, 2, 0, 3)))
    grads = lax.map(angle_step, (projection, offsets, amplitudes, counts))
    proj_grad = jnp.transpose(grads, (1, 2, 0, 3))
    grad_rounded = rounded(grads)

    def backward(summed, group):
        grad_angle, tile_angle, ids_angle = group
        grad_blocks = grad_angle.reshape(2, SLICES, UB, BLOCK).astype(jnp.float32)
        contrib = jnp.einsum('csum,mx->csux', grad_blocks, tile_angle.astype(jnp.float32))
        contrib = contrib.reshape(2, SLICES, UB * J, BLOCK)
        return (summed.at[:, :, ids_angle.reshape(-1)].add(contrib), None)
    start_sum = jnp.zeros((2, SLICES, KB, BLOCK), jnp.float32)
    object_grad, unused_out = lax.scan(backward, start_sum, (grad_rounded, radon_tiles, tile_blocks))
    new_volume = volume.astype(jnp.float32) + step_size * object_grad.reshape(2, SLICES, KCOEF)
    return (new_volume, proj_grad)
```

```python
import functools
import math

import jax
import jax.numpy as jnp
import numpy as np
from jax import lax
from jax.experimental import pallas as pl
from jax.experimental.pallas import tpu as pltpu
from jax.sharding import PartitionSpec as P

step_size = 0.1
LANES = 128
ROWS = 16
GROUP = 8
VMEM_LIMIT = 50 * 1024 * 1024
everywhere = pl.BlockSpec(memory_space=pltpu.VMEM)
scalars = pl.BlockSpec(memory_space=pltpu.SMEM)


def dft_tables(width):
    index = np.arange(width)
    turn = 2.0 * math.pi / width * (index[:, None] * index[None, :] % width)
    cosine = jnp.asarray(np.cos(turn) / math.sqrt(width), jnp.bfloat16)
    sine_neg = jnp.asarray(-np.sin(turn) / math.sqrt(width), jnp.bfloat16)
    forward = jnp.block([[cosine, -sine_neg], [sine_neg, cosine]])
    inverse = jnp.block([[cosine, sine_neg], [-sine_neg, cosine]])
    return (forward, inverse)


def swap_pos(pieces):
    count = len(pieces)
    out = [pieces[0]]
    for k in range(1, count):
        out.append(lax.ppermute(pieces[k], "pos", [(i, i ^ k) for i in range(count)]))
    return out


def lower_half(shape):
    return lax.broadcasted_iota(jnp.int32, shape, len(shape) - 1) < LANES // 2


def swap_halves(tile):
    return pltpu.roll(tile, LANES // 2, 1)


def pair_tile(w_ref, tile):
    m, n = tile.shape
    w_ref[0:m, 0:n] = tile
    w_ref[m : 2 * m, n : 2 * n] = tile


def project_kernel(pieces, idx_ref, radon_ref, *refs):
    vol_refs = refs[:pieces]
    out_ref, vv_ref, lhs_ref, w_ref = refs[pieces:]
    angles = radon_ref.shape[0]
    per_piece = vol_refs[0].shape[1] // LANES
    tiles = per_piece * pieces
    pairs = out_ref.shape[2] // LANES
    feeds = idx_ref.shape[1] // (2 * pairs)
    span = radon_ref.shape[2]
    w_ref[...] = jnp.zeros_like(w_ref)
    for k in range(pieces):

        @pl.loop(0, per_piece, unroll=4)
        def _(t):
            tile = vol_refs[k][:, pl.ds(pl.multiple_of(t * LANES, LANES), LANES)]
            vv_ref[k * per_piece + t] = tile
            swapped = swap_halves(tile.astype(jnp.float32)).astype(jnp.bfloat16)
            vv_ref[tiles + k * per_piece + t] = swapped

    low = lower_half((ROWS, LANES))

    @pl.loop(0, angles // 2)
    def _(step):
        for n in range(2):
            a = step * 2 + n
            pair_tile(w_ref.at[n], radon_ref[a])
            for pair in range(pairs):
                for side in range(2):
                    for jp in range(feeds // 2):
                        at = (2 * pair + side) * feeds + 2 * jp
                        first = vv_ref[idx_ref[a, at]]
                        second = vv_ref[idx_ref[a, at + 1]]
                        lane = side * span + jp * LANES
                        lhs_ref[n, pair * ROWS : (pair + 1) * ROWS, lane : lane + LANES] = jnp.where(
                            low, first, second
                        )
        for n in range(2):
            a = step * 2 + n
            product = lax.dot_general(
                lhs_ref[n], w_ref[n], (((1,), (1,)), ((), ())), preferred_element_type=jnp.float32
            )
            for pair in range(pairs):
                out_ref[a, :, pair * LANES : (pair + 1) * LANES] = product[
                    pair * ROWS : (pair + 1) * ROWS
                ].astype(jnp.bfloat16)


def project(idx, radon_tiles, vol_pieces, columns):
    angles, block, span = radon_tiles.shape
    pieces = len(vol_pieces)
    tiles = pieces * vol_pieces[0].shape[1] // LANES
    pairs = columns // LANES
    return pl.pallas_call(
        functools.partial(project_kernel, pieces),
        out_shape=jax.ShapeDtypeStruct((angles, ROWS, columns), jnp.bfloat16),
        in_specs=[scalars, everywhere] + [everywhere] * pieces,
        out_specs=everywhere,
        scratch_shapes=[
            pltpu.VMEM((2 * tiles, ROWS, LANES), jnp.bfloat16),
            pltpu.VMEM((2, pairs * ROWS, 2 * span), jnp.bfloat16),
            pltpu.VMEM((2, 2 * block, 2 * span), jnp.bfloat16),
        ],
        compiler_params=pltpu.CompilerParams(vmem_limit_bytes=VMEM_LIMIT),
        name="project",
    )(idx, radon_tiles, *vol_pieces)


CHAINS = 4


def back_project_kernel(pieces, idx_ref, radon_ref, grad_ref, *refs):
    out_refs = refs[:pieces]
    acc_refs = refs[pieces : pieces + CHAINS]
    contrib_ref, w_ref = refs[pieces + CHAINS :]
    angles = radon_ref.shape[0]
    per_piece = out_refs[0].shape[1] // LANES
    tiles = per_piece * pieces
    pairs = grad_ref.shape[2] // LANES
    feeds = idx_ref.shape[1] // (2 * pairs)
    span = radon_ref.shape[2]
    w_ref[...] = jnp.zeros_like(w_ref)

    @pl.loop(0, 2 * tiles, unroll=8)
    def _(t):
        for acc_ref in acc_refs:
            acc_ref[t] = jnp.zeros((ROWS, LANES), jnp.float32)

    low = lower_half((ROWS, LANES))

    @pl.loop(0, angles // CHAINS)
    def _(step):
        for n in range(CHAINS):
            a = step * CHAINS + n
            pair_tile(w_ref.at[n], radon_ref[a])
            lhs = jnp.concatenate(
                [grad_ref[a, :, p * LANES : (p + 1) * LANES] for p in range(pairs)], axis=0
            )
            contrib_ref[n] = jnp.dot(lhs, w_ref[n], preferred_element_type=jnp.float32)
        for pair in range(pairs):
            for side in range(2):
                for jp in range(feeds // 2):
                    at = (2 * pair + side) * feeds + 2 * jp
                    lane = side * span + jp * LANES
                    for n in range(CHAINS):
                        a = step * CHAINS + n
                        tile = contrib_ref[n, pair * ROWS : (pair + 1) * ROWS, lane : lane + LANES]
                        first, second = idx_ref[a, at], idx_ref[a, at + 1]
                        acc_refs[n][first] += jnp.where(low, tile, 0.0)
                        acc_refs[n][second] += jnp.where(low, 0.0, tile)

    for k in range(pieces):

        @pl.loop(0, per_piece, unroll=4)
        def _(t):
            straight = acc_refs[0][k * per_piece + t]
            crossed = acc_refs[0][tiles + k * per_piece + t]
            for acc_ref in acc_refs[1:]:
                straight += acc_ref[k * per_piece + t]
                crossed += acc_ref[tiles + k * per_piece + t]
            total = straight + swap_halves(crossed)
            out_refs[k][:, pl.ds(pl.multiple_of(t * LANES, LANES), LANES)] = total.astype(jnp.bfloat16)


def back_project(idx, radon_tiles, grads, pieces, piece_width):
    angles, block, span = radon_tiles.shape
    tiles = pieces * piece_width // LANES
    pairs = grads.shape[2] // LANES
    return pl.pallas_call(
        functools.partial(back_project_kernel, pieces),
        out_shape=[jax.ShapeDtypeStruct((ROWS, piece_width), jnp.bfloat16)] * pieces,
        in_specs=[scalars, everywhere, everywhere],
        out_specs=[everywhere] * pieces,
        scratch_shapes=[pltpu.VMEM((2 * tiles, ROWS, LANES), jnp.float32)] * CHAINS
        + [
            pltpu.VMEM((CHAINS, pairs * ROWS, 2 * span), jnp.float32),
            pltpu.VMEM((CHAINS, 2 * block, 2 * span), jnp.bfloat16),
        ],
        compiler_params=pltpu.CompilerParams(vmem_limit_bytes=VMEM_LIMIT),
        name="back_project",
    )(idx, radon_tiles, grads)


def exit_kernel(pieces, meta_ref, probe_ref, forward_ref, inverse_ref, sino_ref, *refs):
    amp_refs = refs[:pieces]
    grad_ref, tile_ref, acc_ref, wave_ref, half_ref = refs[pieces:]
    pos = lax.axis_index("pos")
    groups = sino_ref.shape[0]
    width = probe_ref.shape[1]
    columns = sino_ref.shape[2]
    lane_tiles = columns // LANES
    slots = amp_refs[0].shape[0]
    chunk = 4
    crows = chunk * GROUP
    lane_id = lax.broadcasted_iota(jnp.int32, (crows, LANES), 1)
    wide = width // LANES

    @pl.loop(0, groups)
    def _(g):
        zero = jnp.zeros((GROUP, columns), jnp.float32)
        for c in range(2):
            acc_ref[c, pl.ds(pl.multiple_of(g * GROUP, GROUP), GROUP), :] = zero

    def product(left, right):
        return jnp.dot(left, right, preferred_element_type=jnp.float32)

    for k in range(pieces):
        owner = jnp.bitwise_xor(pos, k)

        def slot_step(q, carry):
            offset = meta_ref[owner, q]
            first_tile = offset // LANES
            shift = offset % LANES
            starts = [
                pl.multiple_of((first_tile + m) % lane_tiles * LANES, LANES) for m in range(wide + 1)
            ]
            keep = lane_id < LANES - shift
            back_shift = (LANES - shift) % LANES
            for ch in range(groups // chunk):
                rows = slice(ch * crows, (ch + 1) * crows)
                turned = []
                for start in starts:
                    both = sino_ref[ch * chunk : (ch + 1) * chunk, :, pl.ds(start, LANES)].astype(
                        jnp.float32
                    )
                    turned.append(
                        [
                            pltpu.roll(
                                both[:, c * GROUP : (c + 1) * GROUP].reshape(crows, LANES),
                                back_shift,
                                1,
                            )
                            for c in range(2)
                        ]
                    )
                for m in range(wide):
                    lanes = slice(m * LANES, (m + 1) * LANES)
                    patch_re = jnp.where(keep, turned[m][0], turned[m + 1][0])
                    patch_im = jnp.where(keep, turned[m][1], turned[m + 1][1])
                    probe_re = probe_ref[0, rows, lanes].astype(jnp.float32)
                    probe_im = probe_ref[1, rows, lanes].astype(jnp.float32)
                    wave_ref[rows, lanes] = (probe_re * patch_re - probe_im * patch_im).astype(
                        jnp.bfloat16
                    )
                    wave_ref[width + ch * crows : width + (ch + 1) * crows, lanes] = (
                        probe_re * patch_im + probe_im * patch_re
                    ).astype(jnp.bfloat16)
            half = product(forward_ref[...], wave_ref[...]).astype(jnp.bfloat16)
            half_ref[:, :width] = half[:width]
            half_ref[:, width:] = half[width:]
            far = product(half_ref[...], inverse_ref[...])
            for ch in range(groups // chunk):
                rows = slice(ch * crows, (ch + 1) * crows)
                far_re, far_im = far[rows, :width], far[rows, width:]
                power = far_re * far_re + far_im * far_im
                amps = amp_refs[k][q, rows, :].astype(jnp.float32)
                factor = amps * lax.rsqrt(jnp.maximum(power, 1.0)) - 1.0
                wave_ref[rows, :] = (far_re * factor).astype(jnp.bfloat16)
                wave_ref[width + ch * crows : width + (ch + 1) * crows, :] = (far_im * factor).astype(
                    jnp.bfloat16
                )
            back = product(inverse_ref[...], wave_ref[...]).astype(jnp.bfloat16)
            half_ref[:, :width] = back[:width]
            half_ref[:, width:] = back[width:]
            near = product(half_ref[...], forward_ref[...])
            past = lane_id >= shift
            for ch in range(groups // chunk):
                rows = slice(ch * crows, (ch + 1) * crows)
                turned = []
                for m in range(wide):
                    lanes = slice(m * LANES, (m + 1) * LANES)
                    probe_re = probe_ref[0, rows, lanes].astype(jnp.float32)
                    probe_im = probe_ref[1, rows, lanes].astype(jnp.float32)
                    near_re = near[rows, m * LANES : (m + 1) * LANES]
                    near_im = near[rows, width + m * LANES : width + (m + 1) * LANES]
                    turned.append(
                        [
                            pltpu.roll(probe_re * near_re + probe_im * near_im, shift, 1),
                            pltpu.roll(probe_re * near_im - probe_im * near_re, shift, 1),
                        ]
                    )
                for m in range(wide + 1):
                    for c in range(2):
                        behind = turned[m - 1][c] if m > 0 else 0.0
                        ahead = turned[m][c] if m < wide else 0.0
                        acc_ref[c, rows, pl.ds(starts[m], LANES)] += jnp.where(past, ahead, behind)
            return carry

        lax.fori_loop(0, meta_ref[owner, slots], slot_step, 0)

    @pl.loop(0, groups)
    def _(g):
        rows = pl.ds(pl.multiple_of(g * GROUP, GROUP), GROUP)
        both = jnp.concatenate([acc_ref[0, rows, :], acc_ref[1, rows, :]], axis=0)
        grad_ref[g] = both.astype(jnp.bfloat16)

    tile_width = tile_ref.shape[3]
    for k in range(pieces):
        start = pl.multiple_of(jnp.bitwise_xor(pos, k) * tile_width, tile_width)

        @pl.loop(0, groups // 2)
        def _(g):
            rows = pl.ds(pl.multiple_of(g * 2 * GROUP, 2 * GROUP), 2 * GROUP)
            for c in range(2):
                tile_ref[k, c, rows, :] = acc_ref[c, rows, pl.ds(start, tile_width)].astype(
                    jnp.bfloat16
                )


def exit_gradient(meta, probe_field, forward, inverse, sino, amp_pieces):
    groups, rows, columns = sino.shape
    width = probe_field.shape[1]
    pieces = len(amp_pieces)
    slices = groups * GROUP
    return pl.pallas_call(
        functools.partial(exit_kernel, pieces),
        out_shape=[
            jax.ShapeDtypeStruct(sino.shape, jnp.bfloat16),
            jax.ShapeDtypeStruct((pieces, 2, slices, columns // pieces), jnp.bfloat16),
        ],
        in_specs=[scalars] + [everywhere] * (4 + pieces),
        out_specs=[everywhere] * 2,
        scratch_shapes=[
            pltpu.VMEM((2, slices, columns), jnp.float32),
            pltpu.VMEM((2 * width, width), jnp.bfloat16),
            pltpu.VMEM((width, 2 * width), jnp.bfloat16),
        ],
        compiler_params=pltpu.CompilerParams(vmem_limit_bytes=VMEM_LIMIT),
        name="exit_gradient",
    )(meta, probe_field, forward, inverse, sino, *amp_pieces)


def by_owner(pieces, pos):
    count = len(pieces)
    bit = 1
    while bit < count:
        flip = (pos & bit) != 0
        pieces = [jnp.where(flip, pieces[k ^ bit], pieces[k]) for k in range(count)]
        bit *= 2
    return pieces


def to_groups(received, own_slices):
    if own_slices == GROUP:
        return received
    devices, rows, columns = received.shape
    merge = GROUP // own_slices
    split = received.reshape(devices // merge, merge, 2, own_slices, columns)
    return split.transpose(0, 2, 1, 3, 4).reshape(devices // merge, ROWS, columns)


def from_groups(grouped, own_slices):
    if own_slices == GROUP:
        return grouped
    groups, rows, columns = grouped.shape
    merge = GROUP // own_slices
    split = grouped.reshape(groups, 2, merge, own_slices, columns)
    return split.transpose(0, 2, 1, 3, 4).reshape(groups * merge, 2 * own_slices, columns)


def pad_rows(block):
    return jnp.pad(block, [(0, 0)] * (block.ndim - 2) + [(0, ROWS - block.shape[-2]), (0, 0)])


def on_device(volume, radon_tiles, tile_blocks, probe_field, amplitudes, offsets, counts):
    n_pos = lax.axis_size("pos")
    pos = lax.axis_index("pos")
    angles, det_blocks, feeds = tile_blocks.shape
    block_size = radon_tiles.shape[1]
    columns = det_blocks * block_size
    slab = volume.shape[1]
    width = volume.shape[2]
    own = slab // n_pos
    rows = 2 * own
    blocks_each = width // block_size

    def slices_of(k):
        start = jnp.bitwise_xor(pos, k) * own
        return lax.dynamic_slice_in_dim(volume, start, own, 1).reshape(rows, width)

    vol_pieces = swap_pos([slices_of(k) for k in range(n_pos)])
    meta = lax.all_gather(jnp.concatenate([offsets, counts], axis=1), "pos", axis=0)
    meta = lax.dynamic_index_in_dim(meta, pos, 1, keepdims=False)
    vol_pieces, amplitudes = lax.optimization_barrier((vol_pieces, amplitudes))
    amp_pieces = swap_pos(
        [
            lax.dynamic_index_in_dim(amplitudes, jnp.bitwise_xor(pos, k), 0, keepdims=False)
            for k in range(n_pos)
        ]
    )

    owner = tile_blocks // blocks_each
    within = tile_blocks % blocks_each
    crossed = (within + jnp.arange(feeds, dtype=jnp.int32)) % 2
    tiles_each = width // LANES
    idx = crossed * (n_pos * tiles_each) + (owner ^ pos) * tiles_each + within // 2
    idx = idx.reshape(angles, det_blocks * feeds)

    sino = project(idx, radon_tiles, [pad_rows(piece) for piece in vol_pieces], columns)[:, :rows]
    received = lax.all_to_all(sino, ("ang", "pos"), 0, 0, tiled=True)
    forward, inverse = dft_tables(probe_field.shape[1])
    grads, grad_tiles = exit_gradient(
        meta, probe_field, forward, inverse, to_groups(received, own), amp_pieces
    )
    tile_pieces = swap_pos([grad_tiles[k] for k in range(n_pos)])
    returned = lax.all_to_all(from_groups(grads, own), ("ang", "pos"), 0, 0, tiled=True)
    proj_grad = jnp.stack(by_owner(tile_pieces, pos), axis=2).astype(jnp.float32)
    obj_pieces = back_project(idx, radon_tiles, pad_rows(returned), n_pos, width)
    obj_pieces = swap_pos([piece[:rows] for piece in obj_pieces])
    obj_pieces = [piece.reshape(2, own, width) for piece in by_owner(obj_pieces, pos)]
    object_grad = jnp.concatenate(obj_pieces, axis=1).astype(jnp.float32)
    new_volume = volume.astype(jnp.float32) + step_size * object_grad
    return (new_volume, proj_grad)


def solution(mesh):
    in_specs = (
        P(None, "ang", "pos"),
        P(),
        P(),
        P(),
        P("ang", "pos", None, None),
        P("ang", "pos"),
        P("ang", "pos"),
    )
    out_specs = (P(None, "ang", "pos"), P(None, None, "ang", "pos"))
    return jax.shard_map(
        on_device, mesh=mesh, in_specs=in_specs, out_specs=out_specs, check_vma=False
    )
```

```python
import functools
import math

import jax
import jax.numpy as jnp
import numpy as np
from jax import lax
from jax.experimental import pallas as pl
from jax.experimental.pallas import tpu as pltpu
from jax.sharding import PartitionSpec as P

step_size = 0.1
LANES = 128
ROWS = 16
GROUP = 8
VMEM_LIMIT = 50 * 1024 * 1024
everywhere = pl.BlockSpec(memory_space=pltpu.VMEM)
scalars = pl.BlockSpec(memory_space=pltpu.SMEM)
CHAINS = 4


def dft_tables(width):
    index = np.arange(width)
    turn = 2.0 * math.pi / width * (index[:, None] * index[None, :] % width)
    cosine = jnp.asarray(np.cos(turn) / math.sqrt(width), jnp.bfloat16)
    sine_neg = jnp.asarray(-np.sin(turn) / math.sqrt(width), jnp.bfloat16)
    forward = jnp.block([[cosine, -sine_neg], [sine_neg, cosine]])
    inverse = jnp.block([[cosine, sine_neg], [-sine_neg, cosine]])
    return (forward, inverse)


def rotate_pos(pieces, sign):
    count = len(pieces)
    return [pieces[0]] + [
        lax.ppermute(pieces[j], "pos", [(i, (i + sign * j) % count) for i in range(count)])
        for j in range(1, count)
    ]


def in_order(pieces, first):
    count = len(pieces)
    bit = 1
    while bit < count:
        flip = (first & bit) != 0
        pieces = [jnp.where(flip, pieces[(k + bit) % count], pieces[k]) for k in range(count)]
        bit *= 2
    return pieces


def lower_half(shape):
    return lax.broadcasted_iota(jnp.int32, shape, len(shape) - 1) < LANES // 2


def swap_halves(tile):
    return pltpu.roll(tile, LANES // 2, 1)


def arrange_kernel(pieces, *refs):
    vol_refs, vv_ref = refs[:pieces], refs[pieces]
    per_piece = vol_refs[0].shape[1] // LANES
    tiles = per_piece * pieces
    for k in range(pieces):

        @pl.loop(0, per_piece, unroll=4)
        def _(t):
            tile = vol_refs[k][:, pl.ds(pl.multiple_of(t * LANES, LANES), LANES)]
            vv_ref[k * per_piece + t] = tile
            swapped = swap_halves(tile.astype(jnp.float32)).astype(jnp.bfloat16)
            vv_ref[tiles + k * per_piece + t] = swapped


def project_chunk(chunks, idx_ref, radon_ref, vv_ref, out_refs, lhs_ref):
    angles, block, span = radon_ref.shape
    blocks = out_refs[0].shape[2] // block
    feeds = span // block
    low = lower_half((ROWS, LANES))

    @pl.loop(0, angles // 2)
    def _(step):
        for n in range(2):
            a = step * 2 + n
            for i, chunk in enumerate(chunks):
                for b in range(blocks):
                    row = (i * blocks + b) * ROWS
                    for jp in range(feeds // 2):
                        at = (chunk * blocks + b) * feeds + 2 * jp
                        first = vv_ref[idx_ref[a, at]]
                        second = vv_ref[idx_ref[a, at + 1]]
                        lhs_ref[n, row : row + ROWS, jp * LANES : (jp + 1) * LANES] = jnp.where(
                            low, first, second
                        )
        for n in range(2):
            a = step * 2 + n
            product = lax.dot_general(
                lhs_ref[n], radon_ref[a], (((1,), (1,)), ((), ())), preferred_element_type=jnp.float32
            )
            for i in range(len(chunks)):
                for pair in range(blocks // 2):
                    row = (i * blocks + 2 * pair) * ROWS
                    tile = jnp.concatenate(
                        [product[row : row + ROWS], product[row + ROWS : row + 2 * ROWS]], axis=1
                    )
                    out_refs[i][a, :, pair * LANES : (pair + 1) * LANES] = tile.astype(jnp.bfloat16)


def project_first_kernel(pieces, idx_ref, radon_ref, *refs):
    vol_refs = refs[:pieces]
    out_ref, vv_ref, lhs_ref = refs[pieces:]
    arrange_kernel(pieces, *vol_refs, vv_ref)
    project_chunk([0], idx_ref, radon_ref, vv_ref, [out_ref], lhs_ref)


def project_rest_kernel(pieces, idx_ref, radon_ref, vv_ref, *refs):
    out_refs, lhs_ref = refs[: pieces - 1], refs[pieces - 1]
    project_chunk(list(range(1, pieces)), idx_ref, radon_ref, vv_ref, out_refs, lhs_ref)


def project(idx, radon_tiles, vol_pieces, tile_width):
    angles, block, span = radon_tiles.shape
    pieces = len(vol_pieces)
    tiles = pieces * vol_pieces[0].shape[1] // LANES
    rows = tile_width // block * ROWS
    chunk_shape = jax.ShapeDtypeStruct((angles, ROWS, tile_width), jnp.bfloat16)
    params = pltpu.CompilerParams(vmem_limit_bytes=VMEM_LIMIT)
    first, vv = pl.pallas_call(
        functools.partial(project_first_kernel, pieces),
        out_shape=[chunk_shape, jax.ShapeDtypeStruct((2 * tiles, ROWS, LANES), jnp.bfloat16)],
        in_specs=[scalars, everywhere] + [everywhere] * pieces,
        out_specs=[everywhere] * 2,
        scratch_shapes=[pltpu.VMEM((2, rows, span), jnp.bfloat16)],
        compiler_params=params,
        name="project_first",
    )(idx, radon_tiles, *vol_pieces)
    rest = pl.pallas_call(
        functools.partial(project_rest_kernel, pieces),
        out_shape=[chunk_shape] * (pieces - 1),
        in_specs=[scalars, everywhere, everywhere],
        out_specs=[everywhere] * (pieces - 1),
        scratch_shapes=[pltpu.VMEM((2, (pieces - 1) * rows, span), jnp.bfloat16)],
        compiler_params=params,
        name="project_rest",
    )(idx, radon_tiles, vv)
    return [first] + list(rest)


def back_project_kernel(chunks, pieces, has_start, idx_ref, radon_ref, *refs):
    grad_refs, refs = refs[: len(chunks)], refs[len(chunks) :]
    start_refs, refs = (refs[:pieces], refs[pieces:]) if has_start else (None, refs)
    out_refs, refs = refs[:pieces], refs[pieces:]
    acc_refs, contrib_ref = refs[:CHAINS], refs[CHAINS]
    angles, block, span = radon_ref.shape
    per_piece = out_refs[0].shape[1] // LANES
    tiles = per_piece * pieces
    blocks = grad_refs[0].shape[2] // block
    pairs = blocks // 2
    feeds = span // block

    @pl.loop(0, 2 * tiles, unroll=8)
    def _(t):
        for acc_ref in acc_refs:
            acc_ref[t] = jnp.zeros((ROWS, LANES), jnp.float32)

    low = lower_half((ROWS, LANES))

    @pl.loop(0, angles // CHAINS)
    def _(step):
        for n in range(CHAINS):
            a = step * CHAINS + n
            lhs = []
            for grad_ref in grad_refs:
                for pair in range(pairs):
                    tile = grad_ref[a, :, pair * LANES : (pair + 1) * LANES]
                    lhs += [tile[:, :block], tile[:, block:]]
            contrib_ref[n] = jnp.dot(
                jnp.concatenate(lhs, axis=0), radon_ref[a], preferred_element_type=jnp.float32
            )
        for i, chunk in enumerate(chunks):
            for b in range(blocks):
                row = (i * blocks + b) * ROWS
                for jp in range(feeds // 2):
                    at = (chunk * blocks + b) * feeds + 2 * jp
                    for n in range(CHAINS):
                        a = step * CHAINS + n
                        tile = contrib_ref[n, row : row + ROWS, jp * LANES : (jp + 1) * LANES]
                        first, second = idx_ref[a, at], idx_ref[a, at + 1]
                        acc_refs[n][first] += jnp.where(low, tile, 0.0)
                        acc_refs[n][second] += jnp.where(low, 0.0, tile)

    for k in range(pieces):

        @pl.loop(0, per_piece, unroll=4)
        def _(t):
            lanes = pl.ds(pl.multiple_of(t * LANES, LANES), LANES)
            straight = acc_refs[0][k * per_piece + t]
            crossed = acc_refs[0][tiles + k * per_piece + t]
            for acc_ref in acc_refs[1:]:
                straight += acc_ref[k * per_piece + t]
                crossed += acc_ref[tiles + k * per_piece + t]
            total = straight + swap_halves(crossed)
            if has_start:
                total += start_refs[k][:, lanes]
            out_refs[k][:, lanes] = total.astype(out_refs[k].dtype)


def back_project(idx, radon_tiles, grads, chunks, start, pieces, piece_width, out_type, name):
    angles, block, span = radon_tiles.shape
    tiles = pieces * piece_width // LANES
    rows = len(chunks) * grads[0].shape[2] // block * ROWS
    has_start = start is not None
    operands = [idx, radon_tiles] + list(grads) + (list(start) if has_start else [])
    return pl.pallas_call(
        functools.partial(back_project_kernel, chunks, pieces, has_start),
        out_shape=[jax.ShapeDtypeStruct((ROWS, piece_width), out_type)] * pieces,
        in_specs=[scalars] + [everywhere] * (len(operands) - 1),
        out_specs=[everywhere] * pieces,
        scratch_shapes=[pltpu.VMEM((2 * tiles, ROWS, LANES), jnp.float32)] * CHAINS
        + [pltpu.VMEM((CHAINS, rows, span), jnp.float32)],
        compiler_params=pltpu.CompilerParams(vmem_limit_bytes=VMEM_LIMIT),
        name=name,
    )(*operands)


def exit_kernel(
    step, last, meta_ref, probe_ref, forward_ref, inverse_ref, own_ref, next_ref, amp_ref, *refs
):
    spill_in_ref, refs = (refs[0], refs[1:]) if step > 0 else (None, refs)
    partial_ref, refs = (refs[0], refs[1:]) if step == last else (None, refs)
    out_ref, beyond_ref, ext_ref, acc_ref, wave_ref, half_ref = refs
    owner = lax.rem(lax.axis_index("pos") + step, last + 1)
    groups = own_ref.shape[0]
    width = probe_ref.shape[1]
    tile_width = own_ref.shape[2]
    reach = tile_width + width
    slots = amp_ref.shape[0]
    chunk = 4
    crows = chunk * GROUP
    lane_id = lax.broadcasted_iota(jnp.int32, (crows, LANES), 1)
    wide = width // LANES

    @pl.loop(0, groups)
    def _(g):
        ext_ref[g, :, :tile_width] = own_ref[g]
        ext_ref[g, :, tile_width:] = next_ref[g, :, :width]
        rows = pl.ds(pl.multiple_of(g * GROUP, GROUP), GROUP)
        for c in range(2):
            if step > 0:
                acc_ref[c, rows, :width] = spill_in_ref[c, rows, :]
                acc_ref[c, rows, width:] = jnp.zeros((GROUP, tile_width), jnp.float32)
            else:
                acc_ref[c, rows, :] = jnp.zeros((GROUP, reach), jnp.float32)

    def product(left, right):
        return jnp.dot(left, right, preferred_element_type=jnp.float32)

    def slot_step(q, carry):
        offset = meta_ref[owner, q] - owner * tile_width
        first_tile = offset // LANES
        shift = offset % LANES
        starts = [pl.multiple_of((first_tile + m) * LANES, LANES) for m in range(wide + 1)]
        keep = lane_id < LANES - shift
        back_shift = (LANES - shift) % LANES
        for ch in range(groups // chunk):
            rows = slice(ch * crows, (ch + 1) * crows)
            turned = []
            for start in starts:
                both = ext_ref[ch * chunk : (ch + 1) * chunk, :, pl.ds(start, LANES)].astype(
                    jnp.float32
                )
                turned.append(
                    [
                        pltpu.roll(
                            both[:, c * GROUP : (c + 1) * GROUP].reshape(crows, LANES), back_shift, 1
                        )
                        for c in range(2)
                    ]
                )
            for m in range(wide):
                lanes = slice(m * LANES, (m + 1) * LANES)
                patch_re = jnp.where(keep, turned[m][0], turned[m + 1][0])
                patch_im = jnp.where(keep, turned[m][1], turned[m + 1][1])
                probe_re = probe_ref[0, rows, lanes].astype(jnp.float32)
                probe_im = probe_ref[1, rows, lanes].astype(jnp.float32)
                wave_ref[rows, lanes] = (probe_re * patch_re - probe_im * patch_im).astype(
                    jnp.bfloat16
                )
                wave_ref[width + ch * crows : width + (ch + 1) * crows, lanes] = (
                    probe_re * patch_im + probe_im * patch_re
                ).astype(jnp.bfloat16)
        half = product(forward_ref[...], wave_ref[...]).astype(jnp.bfloat16)
        half_ref[:, :width] = half[:width]
        half_ref[:, width:] = half[width:]
        far = product(half_ref[...], inverse_ref[...])
        for ch in range(groups // chunk):
            rows = slice(ch * crows, (ch + 1) * crows)
            far_re, far_im = far[rows, :width], far[rows, width:]
            power = far_re * far_re + far_im * far_im
            amps = amp_ref[q, rows, :].astype(jnp.float32)
            factor = amps * lax.rsqrt(jnp.maximum(power, 1.0)) - 1.0
            wave_ref[rows, :] = (far_re * factor).astype(jnp.bfloat16)
            wave_ref[width + ch * crows : width + (ch + 1) * crows, :] = (far_im * factor).astype(
                jnp.bfloat16
            )
        back = product(inverse_ref[...], wave_ref[...]).astype(jnp.bfloat16)
        half_ref[:, :width] = back[:width]
        half_ref[:, width:] = back[width:]
        near = product(half_ref[...], forward_ref[...])
        past = lane_id >= shift
        for ch in range(groups // chunk):
            rows = slice(ch * crows, (ch + 1) * crows)
            turned = []
            for m in range(wide):
                lanes = slice(m * LANES, (m + 1) * LANES)
                probe_re = probe_ref[0, rows, lanes].astype(jnp.float32)
                probe_im = probe_ref[1, rows, lanes].astype(jnp.float32)
                near_re = near[rows, m * LANES : (m + 1) * LANES]
                near_im = near[rows, width + m * LANES : width + (m + 1) * LANES]
                turned.append(
                    [
                        pltpu.roll(probe_re * near_re + probe_im * near_im, shift, 1),
                        pltpu.roll(probe_re * near_im - probe_im * near_re, shift, 1),
                    ]
                )
            for m in range(wide + 1):
                for c in range(2):
                    behind = turned[m - 1][c] if m > 0 else 0.0
                    ahead = turned[m][c] if m < wide else 0.0
                    acc_ref[c, rows, pl.ds(starts[m], LANES)] += jnp.where(past, ahead, behind)
        return carry

    lax.fori_loop(0, meta_ref[owner, slots], slot_step, 0)

    @pl.loop(0, groups)
    def _(g):
        rows = pl.ds(pl.multiple_of(g * GROUP, GROUP), GROUP)
        if step == 0:
            for c in range(2):
                out_ref[c, rows, :] = acc_ref[c, rows, :tile_width]
        else:
            both = [acc_ref[c, rows, :tile_width] for c in range(2)]
            out_ref[g] = jnp.concatenate(both, axis=0).astype(jnp.bfloat16)
        if step == last:
            both = []
            for c in range(2):
                whole = partial_ref[c, rows, :]
                spilled = whole[:, :width] + acc_ref[c, rows, tile_width:]
                both.append(jnp.concatenate([spilled, whole[:, width:]], axis=1))
            beyond_ref[g] = jnp.concatenate(both, axis=0).astype(jnp.bfloat16)
        else:
            for c in range(2):
                beyond_ref[c, rows, :] = acc_ref[c, rows, tile_width:]


def exit_gradient(step, last, meta, probe_field, tables, own, ahead, amps, spill, partial):
    groups, rows, tile_width = own.shape
    width = probe_field.shape[1]
    slices = groups * GROUP
    grad_shape = jax.ShapeDtypeStruct(own.shape, jnp.bfloat16)
    partial_shape = jax.ShapeDtypeStruct((2, slices, tile_width), jnp.float32)
    spill_shape = jax.ShapeDtypeStruct((2, slices, width), jnp.float32)
    operands = [meta, probe_field, *tables, own, ahead, amps]
    if step > 0:
        operands.append(spill)
    if step == last:
        operands.append(partial)
    return pl.pallas_call(
        functools.partial(exit_kernel, step, last),
        out_shape=[
            partial_shape if step == 0 else grad_shape,
            grad_shape if step == last else spill_shape,
        ],
        in_specs=[scalars] + [everywhere] * (len(operands) - 1),
        out_specs=[everywhere] * 2,
        scratch_shapes=[
            pltpu.VMEM((groups, rows, tile_width + width), jnp.bfloat16),
            pltpu.VMEM((2, slices, tile_width + width), jnp.float32),
            pltpu.VMEM((2 * width, width), jnp.bfloat16),
            pltpu.VMEM((width, 2 * width), jnp.bfloat16),
        ],
        compiler_params=pltpu.CompilerParams(vmem_limit_bytes=VMEM_LIMIT),
        name="exit_gradient_" + str(step),
    )(*operands)


def to_groups(received, own_slices):
    if own_slices == GROUP:
        return received
    devices, rows, columns = received.shape
    merge = GROUP // own_slices
    split = received.reshape(devices // merge, merge, 2, own_slices, columns)
    return split.transpose(0, 2, 1, 3, 4).reshape(devices // merge, ROWS, columns)


def from_groups(grouped, own_slices):
    if own_slices == GROUP:
        return grouped
    groups, rows, columns = grouped.shape
    merge = GROUP // own_slices
    split = grouped.reshape(groups, 2, merge, own_slices, columns)
    return split.transpose(0, 2, 1, 3, 4).reshape(groups * merge, 2 * own_slices, columns)


def pad_rows(block):
    return jnp.pad(block, [(0, 0)] * (block.ndim - 2) + [(0, ROWS - block.shape[-2]), (0, 0)])


def everyone(chunk):
    return lax.all_to_all(chunk, ("ang", "pos"), 0, 0, tiled=True)


def on_device(volume, radon_tiles, tile_blocks, probe_field, amplitudes, offsets, counts):
    n_pos = lax.axis_size("pos")
    pos = lax.axis_index("pos")
    angles, det_blocks, feeds = tile_blocks.shape
    block_size = radon_tiles.shape[1]
    columns = det_blocks * block_size
    tile_width = columns // n_pos
    slab = volume.shape[1]
    width = volume.shape[2]
    own = slab // n_pos
    rows = 2 * own
    blocks_each = width // block_size
    last = n_pos - 1

    def slices_for(j):
        start = (pos + j) % n_pos * own
        return lax.dynamic_slice_in_dim(volume, start, own, 1).reshape(rows, width)

    vol_pieces = rotate_pos([slices_for(j) for j in range(n_pos)], 1)
    meta = lax.all_gather(jnp.concatenate([offsets, counts], axis=1), "pos", axis=0)
    meta = lax.dynamic_index_in_dim(meta, pos, 1, keepdims=False)
    vol_pieces, amplitudes = lax.optimization_barrier((vol_pieces, amplitudes))
    amp_pieces = rotate_pos(
        [
            lax.dynamic_index_in_dim(amplitudes, (pos - j) % n_pos, 0, keepdims=False)
            for j in range(n_pos)
        ],
        -1,
    )

    owner = tile_blocks // blocks_each
    within = tile_blocks % blocks_each
    crossed = (within + jnp.arange(feeds, dtype=jnp.int32)) % 2
    tiles_each = width // LANES
    idx = crossed * (n_pos * tiles_each) + (pos - owner) % n_pos * tiles_each + within // 2
    idx = idx.reshape(angles // n_pos, n_pos, n_pos, det_blocks // n_pos * feeds)
    idx = jnp.stack([jnp.roll(idx[:, p], -p, axis=1) for p in range(n_pos)], axis=1)
    idx = idx.reshape(angles, det_blocks * feeds)

    sino = project(idx, radon_tiles, [pad_rows(piece) for piece in vol_pieces], tile_width)
    received = [to_groups(everyone(chunk[:, :rows]), own) for chunk in sino]
    tables = dft_tables(probe_field.shape[1])
    grads = [None] * n_pos
    partial = spill = None
    for j in range(n_pos):
        ahead = received[(j + 1) % n_pos]
        one, other = exit_gradient(
            j, last, meta, probe_field, tables, received[j], ahead, amp_pieces[j], spill, partial
        )
        if j == 0:
            partial, spill = one, other
        elif j < last:
            grads[j], spill = one, other
        else:
            grads[j], grads[0] = one, other
    order = list(range(1, n_pos)) + [0]
    returned = {j: pad_rows(everyone(from_groups(grads[j], own))) for j in order}
    early = order[:-1]
    partial_grad = back_project(
        idx, radon_tiles, [returned[j] for j in early], early, None, n_pos, width, jnp.float32, "back_early"
    )
    tile_pieces = rotate_pos(grads, 1)
    obj_pieces = back_project(
        idx, radon_tiles, [returned[0]], [0], partial_grad, n_pos, width, jnp.bfloat16, "back_last"
    )
    groups = grads[0].shape[0]
    tile_pieces = [tile_pieces[-j % n_pos] for j in range(n_pos)]
    tile_pieces = [
        piece.reshape(groups, 2, GROUP, tile_width).transpose(1, 0, 2, 3).reshape(2, groups * GROUP, tile_width)
        for piece in tile_pieces
    ]
    proj_grad = jnp.stack(in_order(tile_pieces, -pos % n_pos), axis=2).astype(jnp.float32)
    obj_pieces = rotate_pos([piece[:rows] for piece in obj_pieces], -1)
    obj_pieces = [piece.reshape(2, own, width) for piece in in_order(obj_pieces, -pos % n_pos)]
    object_grad = jnp.concatenate(obj_pieces, axis=1).astype(jnp.float32)
    new_volume = volume.astype(jnp.float32) + step_size * object_grad
    return (new_volume, proj_grad)


def solution(mesh):
    in_specs = (
        P(None, "ang", "pos"),
        P(),
        P(),
        P(),
        P("ang", "pos", None, None),
        P("ang", "pos"),
        P("ang", "pos"),
    )
    out_specs = (P(None, "ang", "pos"), P(None, None, "ang", "pos"))
    return jax.shard_map(
        on_device, mesh=mesh, in_specs=in_specs, out_specs=out_specs, check_vma=False
    )
```

```python
import functools
import math

import jax
import jax.numpy as jnp
import numpy as np
from jax import lax
from jax.experimental import pallas as pl
from jax.experimental.pallas import tpu as pltpu
from jax.sharding import PartitionSpec as P

step_size = 0.1
LANES = 128
ROWS = 16
GROUP = 8
VMEM_LIMIT = 50 * 1024 * 1024
everywhere = pl.BlockSpec(memory_space=pltpu.VMEM)
scalars = pl.BlockSpec(memory_space=pltpu.SMEM)
CHAINS = 4


def dft_tables(width):
    index = np.arange(width)
    turn = 2.0 * math.pi / width * (index[:, None] * index[None, :] % width)
    cosine = jnp.asarray(np.cos(turn) / math.sqrt(width), jnp.bfloat16)
    sine_neg = jnp.asarray(-np.sin(turn) / math.sqrt(width), jnp.bfloat16)
    forward = jnp.block([[cosine, -sine_neg], [sine_neg, cosine]])
    inverse = jnp.block([[cosine, sine_neg], [-sine_neg, cosine]])
    return (forward, inverse)


def rotate_pos(pieces, sign):
    count = len(pieces)
    return [pieces[0]] + [
        lax.ppermute(pieces[j], "pos", [(i, (i + sign * j) % count) for i in range(count)])
        for j in range(1, count)
    ]


def in_order(pieces, first):
    count = len(pieces)
    bit = 1
    while bit < count:
        flip = (first & bit) != 0
        pieces = [jnp.where(flip, pieces[(k + bit) % count], pieces[k]) for k in range(count)]
        bit *= 2
    return pieces


def lower_half(shape):
    return lax.broadcasted_iota(jnp.int32, shape, len(shape) - 1) < LANES // 2


def swap_halves(tile):
    return pltpu.roll(tile, LANES // 2, 1)


def arrange_kernel(pieces, *refs):
    vol_refs, vv_ref = refs[:pieces], refs[pieces]
    per_piece = vol_refs[0].shape[1] // LANES
    tiles = per_piece * pieces
    for k in range(pieces):

        @pl.loop(0, per_piece, unroll=16)
        def _(t):
            tile = vol_refs[k][:, pl.ds(pl.multiple_of(t * LANES, LANES), LANES)]
            vv_ref[k * per_piece + t] = tile
            swapped = swap_halves(tile.astype(jnp.float32)).astype(jnp.bfloat16)
            vv_ref[tiles + k * per_piece + t] = swapped


def project_chunk(chunks, idx_ref, radon_ref, vv_ref, out_ref, lhs_refs):
    angles, block, span = radon_ref.shape
    blocks = out_ref.shape[2] // block // len(chunks)
    feeds = span // block
    low = lower_half((ROWS, LANES))
    batch = lhs_refs[0].shape[0]

    def gather(start, lhs_ref):
        for n in range(batch):
            a = start + n
            for i, chunk in enumerate(chunks):
                for b in range(blocks):
                    row = (i * blocks + b) * ROWS
                    for jp in range(feeds // 2):
                        at = (chunk * blocks + b) * feeds + 2 * jp
                        first = vv_ref[idx_ref[a, at]]
                        second = vv_ref[idx_ref[a, at + 1]]
                        lhs_ref[n, row : row + ROWS, jp * LANES : (jp + 1) * LANES] = jnp.where(
                            low, first, second
                        )

    def multiply(start, lhs_ref):
        for n in range(batch):
            a = start + n
            product = lax.dot_general(
                lhs_ref[n], radon_ref[a], (((1,), (1,)), ((), ())), preferred_element_type=jnp.float32
            )
            for pair in range(len(chunks) * blocks // 2):
                row = 2 * pair * ROWS
                tile = jnp.concatenate(
                    [product[row : row + ROWS], product[row + ROWS : row + 2 * ROWS]], axis=1
                )
                out_ref[a, :, pair * LANES : (pair + 1) * LANES] = tile.astype(jnp.bfloat16)

    gather(0, lhs_refs[0])

    @pl.loop(0, angles // (2 * batch))
    def _(step):
        start = step * 2 * batch
        multiply(start, lhs_refs[0])
        gather(start + batch, lhs_refs[1])
        multiply(start + batch, lhs_refs[1])
        gather(jnp.minimum(start + 2 * batch, angles - batch), lhs_refs[0])


def project_first_kernel(chunks, pieces, idx_ref, radon_ref, *refs):
    vol_refs = refs[:pieces]
    out_ref, vv_ref, *lhs_refs = refs[pieces:]
    arrange_kernel(pieces, *vol_refs, vv_ref)
    project_chunk(chunks, idx_ref, radon_ref, vv_ref, out_ref, lhs_refs)


def project_rest_kernel(chunks, idx_ref, radon_ref, vv_ref, out_ref, *lhs_refs):
    project_chunk(chunks, idx_ref, radon_ref, vv_ref, out_ref, lhs_refs)


def guess(microseconds):
    return pl.CostEstimate(
        flops=int(microseconds * 1.15e9), bytes_accessed=int(microseconds * 1e5), transcendentals=0
    )


def project_first(idx, radon_tiles, vol_pieces, tile_width, chunks):
    angles, block, span = radon_tiles.shape
    pieces = len(vol_pieces)
    tiles = pieces * vol_pieces[0].shape[1] // LANES
    rows = len(chunks) * tile_width // block * ROWS
    return pl.pallas_call(
        functools.partial(project_first_kernel, chunks, pieces),
        out_shape=[
            jax.ShapeDtypeStruct((angles, ROWS, len(chunks) * tile_width), jnp.bfloat16),
            jax.ShapeDtypeStruct((2 * tiles, ROWS, LANES), jnp.bfloat16),
        ],
        in_specs=[scalars, everywhere] + [everywhere] * pieces,
        out_specs=[everywhere] * 2,
        scratch_shapes=[pltpu.VMEM((2, rows, span), jnp.bfloat16)] * 2,
        compiler_params=pltpu.CompilerParams(vmem_limit_bytes=VMEM_LIMIT),
        cost_estimate=guess(8),
        name="project_first",
    )(idx, radon_tiles, *vol_pieces)


def project_rest(idx, radon_tiles, vv, tile_width, chunks):
    angles, block, span = radon_tiles.shape
    rows = len(chunks) * tile_width // block * ROWS
    return pl.pallas_call(
        functools.partial(project_rest_kernel, chunks),
        out_shape=jax.ShapeDtypeStruct((angles, ROWS, len(chunks) * tile_width), jnp.bfloat16),
        in_specs=[scalars, everywhere, everywhere],
        out_specs=everywhere,
        scratch_shapes=[pltpu.VMEM((2, rows, span), jnp.bfloat16)] * 2,
        compiler_params=pltpu.CompilerParams(vmem_limit_bytes=VMEM_LIMIT),
        cost_estimate=guess(5),
        name="project_rest",
    )(idx, radon_tiles, vv)


def back_project_kernel(chunks, pieces, has_start, idx_ref, radon_ref, grad_ref, *refs):
    start_refs, refs = (refs[:pieces], refs[pieces:]) if has_start else (None, refs)
    out_refs, refs = refs[:pieces], refs[pieces:]
    acc_refs, contrib_refs = refs[:CHAINS], refs[CHAINS:]
    angles, block, span = radon_ref.shape
    per_piece = out_refs[0].shape[1] // LANES
    tiles = per_piece * pieces
    blocks = grad_ref.shape[2] // block // len(chunks)
    pairs = len(chunks) * blocks // 2
    feeds = span // block

    @pl.loop(0, 2 * tiles, unroll=16)
    def _(t):
        for acc_ref in acc_refs:
            acc_ref[t] = jnp.zeros((ROWS, LANES), jnp.float32)

    low = lower_half((ROWS, LANES))

    def multiply(start, contrib_ref):
        for n in range(CHAINS):
            a = start + n
            lhs = []
            for pair in range(pairs):
                tile = grad_ref[a, :, pair * LANES : (pair + 1) * LANES]
                lhs += [tile[:, :block], tile[:, block:]]
            contrib_ref[n] = jnp.dot(
                jnp.concatenate(lhs, axis=0), radon_ref[a], preferred_element_type=jnp.float32
            )

    def scatter(start, contrib_ref):
        for i, chunk in enumerate(chunks):
            for b in range(blocks):
                row = (i * blocks + b) * ROWS
                for jp in range(feeds // 2):
                    at = (chunk * blocks + b) * feeds + 2 * jp
                    for n in range(CHAINS):
                        a = start + n
                        tile = contrib_ref[n, row : row + ROWS, jp * LANES : (jp + 1) * LANES]
                        first, second = idx_ref[a, at], idx_ref[a, at + 1]
                        acc_refs[n][first] += jnp.where(low, tile, 0.0)
                        acc_refs[n][second] += jnp.where(low, 0.0, tile)

    multiply(0, contrib_refs[0])

    @pl.loop(0, angles // (2 * CHAINS))
    def _(step):
        start = step * 2 * CHAINS
        multiply(start + CHAINS, contrib_refs[1])
        scatter(start, contrib_refs[0])
        multiply(jnp.minimum(start + 2 * CHAINS, angles - CHAINS), contrib_refs[0])
        scatter(start + CHAINS, contrib_refs[1])

    for k in range(pieces):

        @pl.loop(0, per_piece, unroll=16)
        def _(t):
            lanes = pl.ds(pl.multiple_of(t * LANES, LANES), LANES)
            straight = acc_refs[0][k * per_piece + t]
            crossed = acc_refs[0][tiles + k * per_piece + t]
            for acc_ref in acc_refs[1:]:
                straight += acc_ref[k * per_piece + t]
                crossed += acc_ref[tiles + k * per_piece + t]
            total = straight + swap_halves(crossed)
            if has_start:
                total += start_refs[k][:, lanes]
            out_refs[k][:, lanes] = total.astype(out_refs[k].dtype)


def back_project(idx, radon_tiles, grads, chunks, start, pieces, piece_width, out_type, name):
    angles, block, span = radon_tiles.shape
    tiles = pieces * piece_width // LANES
    rows = grads.shape[2] // block * ROWS
    has_start = start is not None
    operands = [idx, radon_tiles, grads] + (list(start) if has_start else [])
    return pl.pallas_call(
        functools.partial(back_project_kernel, chunks, pieces, has_start),
        out_shape=[jax.ShapeDtypeStruct((ROWS, piece_width), out_type)] * pieces,
        in_specs=[scalars] + [everywhere] * (len(operands) - 1),
        out_specs=[everywhere] * pieces,
        scratch_shapes=[pltpu.VMEM((2 * tiles, ROWS, LANES), jnp.float32)] * CHAINS
        + [pltpu.VMEM((CHAINS, rows, span), jnp.float32)] * 2,
        compiler_params=pltpu.CompilerParams(vmem_limit_bytes=VMEM_LIMIT),
        cost_estimate=guess(3 + 2 * len(chunks)),
        name=name,
    )(*operands)


def exit_kernel(
    step, last, meta_ref, probe_ref, forward_ref, inverse_ref, own_ref, next_ref, amp_ref, *refs
):
    spill_in_ref, refs = (refs[0], refs[1:]) if step > 0 else (None, refs)
    (partial_ref, before_ref), refs = (refs[:2], refs[2:]) if step == last else ((None, None), refs)
    out_ref, refs = refs[0], refs[1:]
    beyond_ref, refs = (None, refs) if step == last else (refs[0], refs[1:])
    ext_ref, acc_ref, wave_ref, half_ref = refs
    owner = lax.rem(lax.axis_index("pos") + step, last + 1)
    groups = own_ref.shape[0]
    width = probe_ref.shape[1]
    tile_width = own_ref.shape[2]
    reach = tile_width + width
    slots = amp_ref.shape[0]
    chunk = 4
    crows = chunk * GROUP
    lane_id = lax.broadcasted_iota(jnp.int32, (crows, LANES), 1)
    wide = width // LANES

    @pl.loop(0, groups)
    def _(g):
        ext_ref[g, :, :tile_width] = own_ref[g]
        ext_ref[g, :, tile_width:] = next_ref[g]
        rows = pl.ds(pl.multiple_of(g * GROUP, GROUP), GROUP)
        for c in range(2):
            if step > 0:
                acc_ref[c, rows, :width] = spill_in_ref[c, rows, :]
                acc_ref[c, rows, width:] = jnp.zeros((GROUP, tile_width), jnp.float32)
            else:
                acc_ref[c, rows, :] = jnp.zeros((GROUP, reach), jnp.float32)

    def product(left, right):
        return jnp.dot(left, right, preferred_element_type=jnp.float32)

    def slot_step(q, carry):
        offset = meta_ref[step, q] - owner * tile_width
        first_tile = offset // LANES
        shift = offset % LANES
        starts = [pl.multiple_of((first_tile + m) * LANES, LANES) for m in range(wide + 1)]
        keep = lane_id < LANES - shift
        back_shift = (LANES - shift) % LANES
        for ch in range(groups // chunk):
            rows = slice(ch * crows, (ch + 1) * crows)
            turned = []
            for start in starts:
                both = ext_ref[ch * chunk : (ch + 1) * chunk, :, pl.ds(start, LANES)].astype(
                    jnp.float32
                )
                turned.append(
                    [
                        pltpu.roll(
                            both[:, c * GROUP : (c + 1) * GROUP].reshape(crows, LANES), back_shift, 1
                        )
                        for c in range(2)
                    ]
                )
            for m in range(wide):
                lanes = slice(m * LANES, (m + 1) * LANES)
                patch_re = jnp.where(keep, turned[m][0], turned[m + 1][0])
                patch_im = jnp.where(keep, turned[m][1], turned[m + 1][1])
                probe_re = probe_ref[0, rows, lanes].astype(jnp.float32)
                probe_im = probe_ref[1, rows, lanes].astype(jnp.float32)
                wave_ref[rows, lanes] = (probe_re * patch_re - probe_im * patch_im).astype(
                    jnp.bfloat16
                )
                wave_ref[width + ch * crows : width + (ch + 1) * crows, lanes] = (
                    probe_re * patch_im + probe_im * patch_re
                ).astype(jnp.bfloat16)
        half = product(forward_ref[...], wave_ref[...]).astype(jnp.bfloat16)
        half_ref[:, :width] = half[:width]
        half_ref[:, width:] = half[width:]
        far = product(half_ref[...], inverse_ref[...])
        for ch in range(groups // chunk):
            rows = slice(ch * crows, (ch + 1) * crows)
            far_re, far_im = far[rows, :width], far[rows, width:]
            power = far_re * far_re + far_im * far_im
            amps = amp_ref[q, rows, :].astype(jnp.float32)
            factor = amps * lax.rsqrt(jnp.maximum(power, 1.0)) - 1.0
            wave_ref[rows, :] = (far_re * factor).astype(jnp.bfloat16)
            wave_ref[width + ch * crows : width + (ch + 1) * crows, :] = (far_im * factor).astype(
                jnp.bfloat16
            )
        back = product(inverse_ref[...], wave_ref[...]).astype(jnp.bfloat16)
        half_ref[:, :width] = back[:width]
        half_ref[:, width:] = back[width:]
        near = product(half_ref[...], forward_ref[...])
        past = lane_id >= shift
        for ch in range(groups // chunk):
            rows = slice(ch * crows, (ch + 1) * crows)
            turned = []
            for m in range(wide):
                lanes = slice(m * LANES, (m + 1) * LANES)
                probe_re = probe_ref[0, rows, lanes].astype(jnp.float32)
                probe_im = probe_ref[1, rows, lanes].astype(jnp.float32)
                near_re = near[rows, m * LANES : (m + 1) * LANES]
                near_im = near[rows, width + m * LANES : width + (m + 1) * LANES]
                turned.append(
                    [
                        pltpu.roll(probe_re * near_re + probe_im * near_im, shift, 1),
                        pltpu.roll(probe_re * near_im - probe_im * near_re, shift, 1),
                    ]
                )
            for m in range(wide + 1):
                for c in range(2):
                    behind = turned[m - 1][c] if m > 0 else 0.0
                    ahead = turned[m][c] if m < wide else 0.0
                    acc_ref[c, rows, pl.ds(starts[m], LANES)] += jnp.where(past, ahead, behind)
        return carry

    lax.fori_loop(0, meta_ref[step, slots], slot_step, 0)

    @pl.loop(0, groups)
    def _(g):
        rows = pl.ds(pl.multiple_of(g * GROUP, GROUP), GROUP)
        if step == 0:
            for c in range(2):
                out_ref[c, rows, :] = acc_ref[c, rows, :tile_width]
        else:
            both = [acc_ref[c, rows, :tile_width] for c in range(2)]
            here = jnp.concatenate(both, axis=0).astype(jnp.bfloat16)
        if step == last:
            both = []
            for c in range(2):
                whole = partial_ref[c, rows, :]
                spilled = whole[:, :width] + acc_ref[c, rows, tile_width:]
                both.append(jnp.concatenate([spilled, whole[:, width:]], axis=1))
            waiting = before_ref.shape[2]
            out_ref[g, :, :waiting] = before_ref[g]
            out_ref[g, :, waiting : waiting + tile_width] = here
            out_ref[g, :, waiting + tile_width :] = jnp.concatenate(both, axis=0).astype(jnp.bfloat16)
        else:
            if step > 0:
                out_ref[g] = here
            for c in range(2):
                beyond_ref[c, rows, :] = acc_ref[c, rows, tile_width:]


def lanes_of(source, width):
    array, at = source
    return pl.BlockSpec(array.shape[:2] + (width,), lambda i: (0, 0, at))


def exit_gradient(step, last, meta, probe_field, tables, own, ahead, amps, spill, partial, before):
    groups, rows = own[0].shape[:2]
    width = probe_field.shape[1]
    tile_width = own[2]
    slices = groups * GROUP
    grad_shape = jax.ShapeDtypeStruct((groups, rows, tile_width), jnp.bfloat16)
    partial_shape = jax.ShapeDtypeStruct((2, slices, tile_width), jnp.float32)
    spill_shape = jax.ShapeDtypeStruct((2, slices, width), jnp.float32)
    operands = [meta, probe_field, *tables, own[0], ahead[0], amps]
    specs = [scalars] + [everywhere] * 3
    specs += [lanes_of(own[:2], tile_width), lanes_of(ahead[:2], width), everywhere]
    if step > 0:
        operands.append(spill)
    if step == last:
        operands += [partial, before]
        joined = (groups, rows, before.shape[2] + 2 * tile_width)
        out_shape = [jax.ShapeDtypeStruct(joined, jnp.bfloat16)]
    else:
        out_shape = [partial_shape if step == 0 else grad_shape, spill_shape]
    specs += [everywhere] * (len(operands) - len(specs))
    return pl.pallas_call(
        functools.partial(exit_kernel, step, last),
        grid=(1,),
        out_shape=out_shape,
        in_specs=specs,
        out_specs=[everywhere] * len(out_shape),
        scratch_shapes=[
            pltpu.VMEM((groups, rows, tile_width + width), jnp.bfloat16),
            pltpu.VMEM((2, slices, tile_width + width), jnp.float32),
            pltpu.VMEM((2 * width, width), jnp.bfloat16),
            pltpu.VMEM((width, 2 * width), jnp.bfloat16),
        ],
        compiler_params=pltpu.CompilerParams(vmem_limit_bytes=VMEM_LIMIT),
        cost_estimate=guess(7),
        name="exit_gradient_" + str(step),
    )(*operands)


def to_groups(received, own_slices):
    if own_slices == GROUP:
        return received
    devices, rows, columns = received.shape
    merge = GROUP // own_slices
    split = received.reshape(devices // merge, merge, 2, own_slices, columns)
    return split.transpose(0, 2, 1, 3, 4).reshape(devices // merge, ROWS, columns)


def from_groups(grouped, own_slices):
    if own_slices == GROUP:
        return grouped
    groups, rows, columns = grouped.shape
    merge = GROUP // own_slices
    split = grouped.reshape(groups, 2, merge, own_slices, columns)
    return split.transpose(0, 2, 1, 3, 4).reshape(groups * merge, 2 * own_slices, columns)


def pad_rows(block):
    return jnp.pad(block, [(0, 0)] * (block.ndim - 2) + [(0, ROWS - block.shape[-2]), (0, 0)])


def everyone(chunk):
    return lax.all_to_all(chunk, ("ang", "pos"), 0, 0, tiled=True)


def on_device(volume, radon_tiles, tile_blocks, probe_field, amplitudes, offsets, counts):
    n_pos = lax.axis_size("pos")
    pos = lax.axis_index("pos")
    angles, det_blocks, feeds = tile_blocks.shape
    block_size = radon_tiles.shape[1]
    columns = det_blocks * block_size
    tile_width = columns // n_pos
    slab = volume.shape[1]
    width = volume.shape[2]
    own = slab // n_pos
    rows = 2 * own
    blocks_each = width // block_size
    last = n_pos - 1

    def slices_for(j):
        start = (pos + j) % n_pos * own
        return lax.dynamic_slice_in_dim(volume, start, own, 1).reshape(rows, width)

    vol_pieces = rotate_pos([slices_for(j) for j in range(n_pos)], 1)
    meta = jnp.concatenate([offsets, counts], axis=1)
    meta = rotate_pos(
        [lax.dynamic_slice_in_dim(meta, (pos - j) % n_pos, 1, 0) for j in range(n_pos)], -1
    )
    meta = jnp.concatenate(meta, axis=0)
    vol_pieces, amplitudes = lax.optimization_barrier((vol_pieces, amplitudes))
    amp_pieces = rotate_pos(
        [
            lax.dynamic_index_in_dim(amplitudes, (pos - j) % n_pos, 0, keepdims=False)
            for j in range(n_pos)
        ],
        -1,
    )

    owner = tile_blocks // blocks_each
    within = tile_blocks % blocks_each
    crossed = (within + jnp.arange(feeds, dtype=jnp.int32)) % 2
    tiles_each = width // LANES
    idx = crossed * (n_pos * tiles_each) + (pos - owner) % n_pos * tiles_each + within // 2
    idx = idx.reshape(angles // n_pos, n_pos, n_pos, det_blocks // n_pos * feeds)
    idx = jnp.stack([jnp.roll(idx[:, p], -p, axis=1) for p in range(n_pos)], axis=1)
    idx = idx.reshape(angles, det_blocks * feeds)

    padded = [pad_rows(piece) for piece in vol_pieces]
    most = list(range(last))
    sino_most, vv = project_first(idx, radon_tiles, padded, tile_width, most)
    sino_last = project_rest(idx, radon_tiles, vv, tile_width, [last])
    got_most = everyone(sino_most[:, :rows])
    got_most, sino_last = lax.optimization_barrier((got_most, sino_last))
    got_last = everyone(sino_last[:, :rows])
    got_most, got_last = to_groups(got_most, own), to_groups(got_last, own)
    probe_width = probe_field.shape[1]
    tables = dft_tables(probe_width)

    def tile_from(j):
        return (got_most, j, tile_width) if j < last else (got_last, 0, tile_width)

    def edge_from(j):
        per_tile = tile_width // probe_width
        return (got_most, j % n_pos * per_tile) if j % n_pos < last else (got_last, 0)

    grads = [None] * last
    partial = spill = before = None
    for j in range(n_pos):
        out = exit_gradient(
            j, last, meta, probe_field, tables, tile_from(j), edge_from(j + 1), amp_pieces[j],
            spill, partial, before,
        )
        if j == 0:
            partial, spill = out
        elif j < last:
            grads[j], spill = out
            if j == 1:
                first_grad, got_last = lax.optimization_barrier((grads[1], got_last))
            else:
                before = grads[j] if before is None else jnp.concatenate([before, grads[j]], axis=2)
        else:
            joined = out[0]
    back_first = everyone(from_groups(first_grad, own))
    back_first, joined_sent = lax.optimization_barrier((back_first, joined))
    back_rest = everyone(from_groups(joined_sent, own))
    partial_grad = back_project(
        idx, radon_tiles, pad_rows(back_first), [1], None, n_pos, width, jnp.float32, "back_first"
    )
    order = list(range(2, n_pos)) + [0]
    joined_tiles = {j: joined[:, :, i * tile_width : (i + 1) * tile_width] for i, j in enumerate(order)}
    joined_tiles[1] = grads[1]
    tile_pieces = rotate_pos([joined_tiles[j] for j in range(n_pos)], 1)
    obj_pieces = back_project(
        idx, radon_tiles, pad_rows(back_rest), order, partial_grad, n_pos, width, jnp.bfloat16, "back_rest"
    )
    groups = joined.shape[0]
    tile_pieces = [tile_pieces[-j % n_pos] for j in range(n_pos)]
    tile_pieces = [
        piece.reshape(groups, 2, GROUP, tile_width).transpose(1, 0, 2, 3).reshape(2, groups * GROUP, tile_width)
        for piece in tile_pieces
    ]
    proj_grad = jnp.stack(in_order(tile_pieces, -pos % n_pos), axis=2).astype(jnp.float32)
    obj_pieces = rotate_pos([piece[:rows] for piece in obj_pieces], -1)
    obj_pieces = [piece.reshape(2, own, width) for piece in in_order(obj_pieces, -pos % n_pos)]
    object_grad = jnp.concatenate(obj_pieces, axis=1).astype(jnp.float32)
    new_volume = volume.astype(jnp.float32) + step_size * object_grad
    return (new_volume, proj_grad)


def solution(mesh):
    in_specs = (
        P(None, "ang", "pos"),
        P(),
        P(),
        P(),
        P("ang", "pos", None, None),
        P("ang", "pos"),
        P("ang", "pos"),
    )
    out_specs = (P(None, "ang", "pos"), P(None, None, "ang", "pos"))
    return jax.shard_map(
        on_device, mesh=mesh, in_specs=in_specs, out_specs=out_specs, check_vma=False
    )
```

```python
import functools
import math

import jax
import jax.numpy as jnp
import numpy as np
from jax import lax
from jax.experimental import pallas as pl
from jax.experimental.pallas import tpu as pltpu
from jax.sharding import PartitionSpec as P

step_size = 0.1
LANES = 128
ROWS = 16
GROUP = 8
VMEM_LIMIT = 50 * 1024 * 1024
everywhere = pl.BlockSpec(memory_space=pltpu.VMEM)
scalars = pl.BlockSpec(memory_space=pltpu.SMEM)
CHAINS = 4


def dft_tables(width):
    index = np.arange(width)
    turn = 2.0 * math.pi / width * (index[:, None] * index[None, :] % width)
    cosine = jnp.asarray(np.cos(turn) / math.sqrt(width), jnp.bfloat16)
    sine_neg = jnp.asarray(-np.sin(turn) / math.sqrt(width), jnp.bfloat16)
    forward = jnp.block([[cosine, -sine_neg], [sine_neg, cosine]])
    inverse = jnp.block([[cosine, sine_neg], [-sine_neg, cosine]])
    return (forward, inverse)


def rotate_pos(pieces, sign):
    count = len(pieces)
    return [pieces[0]] + [
        lax.ppermute(pieces[j], "pos", [(i, (i + sign * j) % count) for i in range(count)])
        for j in range(1, count)
    ]


def in_order(pieces, first):
    count = len(pieces)
    bit = 1
    while bit < count:
        flip = (first & bit) != 0
        pieces = [jnp.where(flip, pieces[(k + bit) % count], pieces[k]) for k in range(count)]
        bit *= 2
    return pieces


def lower_half(shape):
    return lax.broadcasted_iota(jnp.int32, shape, len(shape) - 1) < LANES // 2


def swap_halves(tile):
    return pltpu.roll(tile, LANES // 2, 1)


def arrange_kernel(pieces, *refs):
    vol_refs, vv_ref = refs[:pieces], refs[pieces]
    per_piece = vol_refs[0].shape[1] // LANES
    tiles = per_piece * pieces
    for k in range(pieces):

        @pl.loop(0, per_piece, unroll=16)
        def _(t):
            tile = vol_refs[k][:, pl.ds(pl.multiple_of(t * LANES, LANES), LANES)]
            vv_ref[k * per_piece + t] = tile
            swapped = swap_halves(tile.astype(jnp.float32)).astype(jnp.bfloat16)
            vv_ref[tiles + k * per_piece + t] = swapped


def project_chunk(chunks, idx_ref, radon_ref, vv_ref, out_ref, lhs_refs):
    angles, block, span = radon_ref.shape
    blocks = out_ref.shape[2] // block // len(chunks)
    feeds = span // block
    low = lower_half((ROWS, LANES))
    batch = lhs_refs[0].shape[0]

    def gather(start, lhs_ref):
        for n in range(batch):
            a = start + n
            for i, chunk in enumerate(chunks):
                for b in range(blocks):
                    row = (i * blocks + b) * ROWS
                    for jp in range(feeds // 2):
                        at = (chunk * blocks + b) * feeds + 2 * jp
                        first = vv_ref[idx_ref[a, at]]
                        second = vv_ref[idx_ref[a, at + 1]]
                        lhs_ref[n, row : row + ROWS, jp * LANES : (jp + 1) * LANES] = jnp.where(
                            low, first, second
                        )

    def multiply(start, lhs_ref):
        for n in range(batch):
            a = start + n
            product = lax.dot_general(
                lhs_ref[n], radon_ref[a], (((1,), (1,)), ((), ())), preferred_element_type=jnp.float32
            )
            for pair in range(len(chunks) * blocks // 2):
                row = 2 * pair * ROWS
                tile = jnp.concatenate(
                    [product[row : row + ROWS], product[row + ROWS : row + 2 * ROWS]], axis=1
                )
                out_ref[a, :, pair * LANES : (pair + 1) * LANES] = tile.astype(jnp.bfloat16)

    gather(0, lhs_refs[0])

    @pl.loop(0, angles // (2 * batch))
    def _(step):
        start = step * 2 * batch
        multiply(start, lhs_refs[0])
        gather(start + batch, lhs_refs[1])
        multiply(start + batch, lhs_refs[1])
        gather(jnp.minimum(start + 2 * batch, angles - batch), lhs_refs[0])


def project_first_kernel(chunks, pieces, idx_ref, radon_ref, *refs):
    vol_refs = refs[:pieces]
    out_ref, vv_ref, *lhs_refs = refs[pieces:]
    arrange_kernel(pieces, *vol_refs, vv_ref)
    project_chunk(chunks, idx_ref, radon_ref, vv_ref, out_ref, lhs_refs)


def project_rest_kernel(chunks, idx_ref, radon_ref, vv_ref, out_ref, *lhs_refs):
    project_chunk(chunks, idx_ref, radon_ref, vv_ref, out_ref, lhs_refs)


def guess(microseconds):
    return pl.CostEstimate(
        flops=int(microseconds * 1.15e9), bytes_accessed=int(microseconds * 1e5), transcendentals=0
    )


def project_first(idx, radon_tiles, vol_pieces, tile_width, chunks):
    angles, block, span = radon_tiles.shape
    pieces = len(vol_pieces)
    tiles = pieces * vol_pieces[0].shape[1] // LANES
    rows = len(chunks) * tile_width // block * ROWS
    return pl.pallas_call(
        functools.partial(project_first_kernel, chunks, pieces),
        out_shape=[
            jax.ShapeDtypeStruct((angles, ROWS, len(chunks) * tile_width), jnp.bfloat16),
            jax.ShapeDtypeStruct((2 * tiles, ROWS, LANES), jnp.bfloat16),
        ],
        in_specs=[scalars, everywhere] + [everywhere] * pieces,
        out_specs=[everywhere] * 2,
        scratch_shapes=[pltpu.VMEM((2, rows, span), jnp.bfloat16)] * 2,
        compiler_params=pltpu.CompilerParams(vmem_limit_bytes=VMEM_LIMIT),
        cost_estimate=guess(8),
        name="project_first",
    )(idx, radon_tiles, *vol_pieces)


def project_rest(idx, radon_tiles, vv, tile_width, chunks):
    angles, block, span = radon_tiles.shape
    rows = len(chunks) * tile_width // block * ROWS
    return pl.pallas_call(
        functools.partial(project_rest_kernel, chunks),
        out_shape=jax.ShapeDtypeStruct((angles, ROWS, len(chunks) * tile_width), jnp.bfloat16),
        in_specs=[scalars, everywhere, everywhere],
        out_specs=everywhere,
        scratch_shapes=[pltpu.VMEM((2, rows, span), jnp.bfloat16)] * 2,
        compiler_params=pltpu.CompilerParams(vmem_limit_bytes=VMEM_LIMIT),
        cost_estimate=guess(5),
        name="project_rest",
    )(idx, radon_tiles, vv)


def back_project_kernel(chunks, pieces, has_start, idx_ref, radon_ref, grad_ref, *refs):
    start_refs, refs = (refs[:pieces], refs[pieces:]) if has_start else (None, refs)
    out_refs, refs = refs[:pieces], refs[pieces:]
    acc_refs, contrib_refs = refs[:CHAINS], refs[CHAINS:]
    angles, block, span = radon_ref.shape
    per_piece = out_refs[0].shape[1] // LANES
    tiles = per_piece * pieces
    blocks = grad_ref.shape[2] // block // len(chunks)
    pairs = len(chunks) * blocks // 2
    feeds = span // block

    @pl.loop(0, 2 * tiles, unroll=16)
    def _(t):
        for acc_ref in acc_refs:
            acc_ref[t] = jnp.zeros((ROWS, LANES), jnp.float32)

    low = lower_half((ROWS, LANES))

    def multiply(start, contrib_ref):
        for n in range(CHAINS):
            a = start + n
            lhs = []
            for pair in range(pairs):
                tile = grad_ref[a, :, pair * LANES : (pair + 1) * LANES]
                lhs += [tile[:, :block], tile[:, block:]]
            contrib_ref[n] = jnp.dot(
                jnp.concatenate(lhs, axis=0), radon_ref[a], preferred_element_type=jnp.float32
            )

    def scatter(start, contrib_ref):
        for i, chunk in enumerate(chunks):
            for b in range(blocks):
                row = (i * blocks + b) * ROWS
                for jp in range(feeds // 2):
                    at = (chunk * blocks + b) * feeds + 2 * jp
                    for n in range(CHAINS):
                        a = start + n
                        tile = contrib_ref[n, row : row + ROWS, jp * LANES : (jp + 1) * LANES]
                        first, second = idx_ref[a, at], idx_ref[a, at + 1]
                        acc_refs[n][first] += jnp.where(low, tile, 0.0)
                        acc_refs[n][second] += jnp.where(low, 0.0, tile)

    multiply(0, contrib_refs[0])

    @pl.loop(0, angles // (2 * CHAINS))
    def _(step):
        start = step * 2 * CHAINS
        multiply(start + CHAINS, contrib_refs[1])
        scatter(start, contrib_refs[0])
        multiply(jnp.minimum(start + 2 * CHAINS, angles - CHAINS), contrib_refs[0])
        scatter(start + CHAINS, contrib_refs[1])

    for k in range(pieces):

        @pl.loop(0, per_piece, unroll=16)
        def _(t):
            lanes = pl.ds(pl.multiple_of(t * LANES, LANES), LANES)
            straight = acc_refs[0][k * per_piece + t]
            crossed = acc_refs[0][tiles + k * per_piece + t]
            for acc_ref in acc_refs[1:]:
                straight += acc_ref[k * per_piece + t]
                crossed += acc_ref[tiles + k * per_piece + t]
            total = straight + swap_halves(crossed)
            if has_start:
                total += start_refs[k][:, lanes]
            out_refs[k][:, lanes] = total.astype(out_refs[k].dtype)


def back_project(idx, radon_tiles, grads, chunks, start, pieces, piece_width, out_type, name):
    angles, block, span = radon_tiles.shape
    tiles = pieces * piece_width // LANES
    rows = grads.shape[2] // block * ROWS
    has_start = start is not None
    operands = [idx, radon_tiles, grads] + (list(start) if has_start else [])
    return pl.pallas_call(
        functools.partial(back_project_kernel, chunks, pieces, has_start),
        out_shape=[jax.ShapeDtypeStruct((ROWS, piece_width), out_type)] * pieces,
        in_specs=[scalars] + [everywhere] * (len(operands) - 1),
        out_specs=[everywhere] * pieces,
        scratch_shapes=[pltpu.VMEM((2 * tiles, ROWS, LANES), jnp.float32)] * CHAINS
        + [pltpu.VMEM((CHAINS, rows, span), jnp.float32)] * 2,
        compiler_params=pltpu.CompilerParams(vmem_limit_bytes=VMEM_LIMIT),
        cost_estimate=guess(3 + 2 * len(chunks)),
        name=name,
    )(*operands)


def add_slots(meta_ref, probe_ref, forward_ref, inverse_ref, ext_ref, acc_ref, amp_refs, scratch, first):
    wave_ref, half_ref, delta_ref, back_ref = scratch
    n_pos = lax.axis_size("pos")
    groups = ext_ref.shape[0]
    width = probe_ref.shape[1]
    slots = amp_refs[0].shape[0]
    tile_width = (acc_ref.shape[2] - width) // len(amp_refs)
    chunk = 4
    crows = chunk * GROUP
    chunks = groups // chunk
    wide = width // LANES
    lane_id = lax.broadcasted_iota(jnp.int32, (crows, LANES), 1)

    def product(left, right):
        return jnp.dot(left, right, preferred_element_type=jnp.float32)

    for tile, amp_ref in enumerate(amp_refs):
        order = first + tile
        tile_start = lax.rem(lax.axis_index("pos") + order, n_pos) * tile_width - tile * tile_width
        count = meta_ref[order, slots]

        @pl.loop(0, (count + 1) // 2)
        def _(step):
            shifts, starts, lives = [], [], []
            for n in range(2):
                offset = meta_ref[order, step * 2 + n] - tile_start
                shifts.append(offset % LANES)
                lane_tile = offset // LANES
                starts.append(
                    [pl.multiple_of((lane_tile + m) * LANES, LANES) for m in range(wide + 1)]
                )
                lives.append((step * 2 + n < count).astype(jnp.float32))
            for n in range(2):
                keep = lane_id < LANES - shifts[n]
                back_shift = (LANES - shifts[n]) % LANES
                for ch in range(chunks):
                    rows = slice(ch * crows, (ch + 1) * crows)
                    low_rows = slice(width + ch * crows, width + (ch + 1) * crows)
                    turned = []
                    for start in starts[n]:
                        both = ext_ref[ch * chunk : (ch + 1) * chunk, :, pl.ds(start, LANES)]
                        both = both.astype(jnp.float32)
                        turned.append(
                            [
                                pltpu.roll(
                                    both[:, c * GROUP : (c + 1) * GROUP].reshape(crows, LANES),
                                    back_shift,
                                    1,
                                )
                                for c in range(2)
                            ]
                        )
                    for m in range(wide):
                        lanes = slice(m * LANES, (m + 1) * LANES)
                        put = slice(n * width + m * LANES, n * width + (m + 1) * LANES)
                        patch_re = jnp.where(keep, turned[m][0], turned[m + 1][0])
                        patch_im = jnp.where(keep, turned[m][1], turned[m + 1][1])
                        probe_re = probe_ref[0, rows, lanes].astype(jnp.float32)
                        probe_im = probe_ref[1, rows, lanes].astype(jnp.float32)
                        wave_re = probe_re * patch_re - probe_im * patch_im
                        wave_im = probe_re * patch_im + probe_im * patch_re
                        wave_ref[rows, put] = wave_re.astype(jnp.bfloat16)
                        wave_ref[low_rows, put] = wave_im.astype(jnp.bfloat16)
                mine = slice(n * width, (n + 1) * width)
                half = product(forward_ref[...], wave_ref[:, mine]).astype(jnp.bfloat16)
                half_ref[mine, :width] = half[:width]
                half_ref[mine, width:] = half[width:]
            for n in range(2):
                mine = slice(n * width, (n + 1) * width)
                far = product(half_ref[mine, :], inverse_ref[...])
                for ch in range(chunks):
                    rows = slice(ch * crows, (ch + 1) * crows)
                    low_rows = slice(width + ch * crows, width + (ch + 1) * crows)
                    far_re, far_im = far[rows, :width], far[rows, width:]
                    power = far_re * far_re + far_im * far_im
                    amps = amp_ref[step * 2 + n, rows, :].astype(jnp.float32)
                    factor = amps * lax.rsqrt(jnp.maximum(power, 1.0)) - 1.0
                    delta_ref[rows, mine] = (far_re * factor).astype(jnp.bfloat16)
                    delta_ref[low_rows, mine] = (far_im * factor).astype(jnp.bfloat16)
                back = product(inverse_ref[...], delta_ref[:, mine]).astype(jnp.bfloat16)
                back_ref[mine, :width] = back[:width]
                back_ref[mine, width:] = back[width:]
            for n in range(2):
                mine = slice(n * width, (n + 1) * width)
                near = product(back_ref[mine, :], forward_ref[...])
                past = lane_id >= shifts[n]
                for ch in range(chunks):
                    rows = slice(ch * crows, (ch + 1) * crows)
                    turned = []
                    for m in range(wide):
                        lanes = slice(m * LANES, (m + 1) * LANES)
                        probe_re = probe_ref[0, rows, lanes].astype(jnp.float32) * lives[n]
                        probe_im = probe_ref[1, rows, lanes].astype(jnp.float32) * lives[n]
                        near_re = near[rows, m * LANES : (m + 1) * LANES]
                        near_im = near[rows, width + m * LANES : width + (m + 1) * LANES]
                        turned.append(
                            [
                                pltpu.roll(probe_re * near_re + probe_im * near_im, shifts[n], 1),
                                pltpu.roll(probe_re * near_im - probe_im * near_re, shifts[n], 1),
                            ]
                        )
                    for m in range(wide + 1):
                        for c in range(2):
                            behind = turned[m - 1][c] if m > 0 else 0.0
                            ahead = turned[m][c] if m < wide else 0.0
                            here = (c, rows, pl.ds(starts[n][m], LANES))
                            acc_ref[here] += jnp.where(past, ahead, behind)


def exit_first_kernel(
    tiles, meta_ref, probe_ref, forward_ref, inverse_ref, most_ref, *refs
):
    amp_refs, refs = refs[:tiles], refs[tiles:]
    partial_ref, grad_ref, spill_ref, acc_ref, *scratch = refs
    groups = most_ref.shape[0]
    tile_width = partial_ref.shape[2]
    done = tiles * tile_width

    @pl.loop(0, groups)
    def _(g):
        rows = pl.ds(pl.multiple_of(g * GROUP, GROUP), GROUP)
        for c in range(2):
            acc_ref[c, rows, :] = jnp.zeros((GROUP, acc_ref.shape[2]), jnp.float32)

    add_slots(
        meta_ref, probe_ref, forward_ref, inverse_ref, most_ref, acc_ref, amp_refs, scratch, 0
    )

    @pl.loop(0, groups)
    def _(g):
        rows = pl.ds(pl.multiple_of(g * GROUP, GROUP), GROUP)
        whole = [acc_ref[c, rows, tile_width:done] for c in range(2)]
        grad_ref[g] = jnp.concatenate(whole, axis=0).astype(jnp.bfloat16)
        for c in range(2):
            partial_ref[c, rows, :] = acc_ref[c, rows, :tile_width]
            spill_ref[c, rows, :] = acc_ref[c, rows, done:]


def exit_rest_kernel(
    tiles, meta_ref, probe_ref, forward_ref, inverse_ref, most_ref, last_ref, partial_ref, spill_ref, *refs
):
    amp_refs, refs = refs[:tiles], refs[tiles:]
    out_ref, ext_ref, acc_ref, *scratch = refs
    groups = most_ref.shape[0]
    width = probe_ref.shape[1]
    tile_width = partial_ref.shape[2]
    done = tiles * tile_width
    kept = done - tile_width

    @pl.loop(0, groups)
    def _(g):
        ext_ref[g, :, :kept] = most_ref[g, :, most_ref.shape[2] - kept :]
        ext_ref[g, :, kept:done] = last_ref[g]
        ext_ref[g, :, done:] = most_ref[g, :, :width]
        rows = pl.ds(pl.multiple_of(g * GROUP, GROUP), GROUP)
        for c in range(2):
            acc_ref[c, rows, :width] = spill_ref[c, rows, :]
            acc_ref[c, rows, width:] = jnp.zeros((GROUP, done), jnp.float32)

    add_slots(
        meta_ref, probe_ref, forward_ref, inverse_ref, ext_ref, acc_ref, amp_refs, scratch,
        lax.axis_size("pos") - tiles,
    )

    @pl.loop(0, groups)
    def _(g):
        rows = pl.ds(pl.multiple_of(g * GROUP, GROUP), GROUP)
        here, wrapped = [], []
        for c in range(2):
            here.append(acc_ref[c, rows, :done])
            whole = partial_ref[c, rows, :]
            spilled = whole[:, :width] + acc_ref[c, rows, done:]
            wrapped.append(jnp.concatenate([spilled, whole[:, width:]], axis=1))
        out_ref[g, :, :done] = jnp.concatenate(here, axis=0).astype(jnp.bfloat16)
        out_ref[g, :, done:] = jnp.concatenate(wrapped, axis=0).astype(jnp.bfloat16)


def exit_scratch(groups, width, reach):
    return [pltpu.VMEM((2, groups * GROUP, reach), jnp.float32)] + [
        pltpu.VMEM((2 * width, 2 * width), jnp.bfloat16)
    ] * 4


def exit_first(meta, probe_field, tables, most, amps, tile_width):
    groups, rows = most.shape[:2]
    width = probe_field.shape[1]
    tiles = len(amps)
    slices = groups * GROUP
    return pl.pallas_call(
        functools.partial(exit_first_kernel, tiles),
        out_shape=[
            jax.ShapeDtypeStruct((2, slices, tile_width), jnp.float32),
            jax.ShapeDtypeStruct((groups, rows, (tiles - 1) * tile_width), jnp.bfloat16),
            jax.ShapeDtypeStruct((2, slices, width), jnp.float32),
        ],
        in_specs=[scalars] + [everywhere] * (4 + tiles),
        out_specs=[everywhere] * 3,
        scratch_shapes=exit_scratch(groups, width, tiles * tile_width + width),
        compiler_params=pltpu.CompilerParams(vmem_limit_bytes=VMEM_LIMIT),
        cost_estimate=guess(10),
        name="exit_first",
    )(meta, probe_field, *tables, most, *amps)


def exit_rest(meta, probe_field, tables, most, final, partial, spill, amps):
    groups, rows, tile_width = final.shape
    width = probe_field.shape[1]
    tiles = len(amps)
    reach = tiles * tile_width + width
    return pl.pallas_call(
        functools.partial(exit_rest_kernel, tiles),
        out_shape=jax.ShapeDtypeStruct((groups, rows, (tiles + 1) * tile_width), jnp.bfloat16),
        in_specs=[scalars] + [everywhere] * (7 + tiles),
        out_specs=everywhere,
        scratch_shapes=[pltpu.VMEM((groups, rows, reach), jnp.bfloat16)]
        + exit_scratch(groups, width, reach),
        compiler_params=pltpu.CompilerParams(vmem_limit_bytes=VMEM_LIMIT),
        cost_estimate=guess(10),
        name="exit_rest",
    )(meta, probe_field, *tables, most, final, partial, spill, *amps)


def to_groups(received, own_slices):
    if own_slices == GROUP:
        return received
    devices, rows, columns = received.shape
    merge = GROUP // own_slices
    split = received.reshape(devices // merge, merge, 2, own_slices, columns)
    return split.transpose(0, 2, 1, 3, 4).reshape(devices // merge, ROWS, columns)


def from_groups(grouped, own_slices):
    if own_slices == GROUP:
        return grouped
    groups, rows, columns = grouped.shape
    merge = GROUP // own_slices
    split = grouped.reshape(groups, 2, merge, own_slices, columns)
    return split.transpose(0, 2, 1, 3, 4).reshape(groups * merge, 2 * own_slices, columns)


def pad_rows(block):
    return jnp.pad(block, [(0, 0)] * (block.ndim - 2) + [(0, ROWS - block.shape[-2]), (0, 0)])


def everyone(chunk):
    return lax.all_to_all(chunk, ("ang", "pos"), 0, 0, tiled=True)


def on_device(volume, radon_tiles, tile_blocks, probe_field, amplitudes, offsets, counts):
    n_pos = lax.axis_size("pos")
    pos = lax.axis_index("pos")
    angles, det_blocks, feeds = tile_blocks.shape
    block_size = radon_tiles.shape[1]
    columns = det_blocks * block_size
    tile_width = columns // n_pos
    slab = volume.shape[1]
    width = volume.shape[2]
    own = slab // n_pos
    rows = 2 * own
    blocks_each = width // block_size
    last = n_pos - 1

    def slices_for(j):
        start = (pos + j) % n_pos * own
        return lax.dynamic_slice_in_dim(volume, start, own, 1).reshape(rows, width)

    vol_pieces = rotate_pos([slices_for(j) for j in range(n_pos)], 1)
    meta = jnp.concatenate([offsets, counts], axis=1)
    meta = rotate_pos(
        [lax.dynamic_slice_in_dim(meta, (pos - j) % n_pos, 1, 0) for j in range(n_pos)], -1
    )
    meta = jnp.concatenate(meta, axis=0)
    vol_pieces, amplitudes = lax.optimization_barrier((vol_pieces, amplitudes))
    amp_pieces = rotate_pos(
        [
            lax.dynamic_index_in_dim(amplitudes, (pos - j) % n_pos, 0, keepdims=False)
            for j in range(n_pos)
        ],
        -1,
    )

    owner = tile_blocks // blocks_each
    within = tile_blocks % blocks_each
    crossed = (within + jnp.arange(feeds, dtype=jnp.int32)) % 2
    tiles_each = width // LANES
    idx = crossed * (n_pos * tiles_each) + (pos - owner) % n_pos * tiles_each + within // 2
    idx = idx.reshape(angles // n_pos, n_pos, n_pos, det_blocks // n_pos * feeds)
    idx = jnp.stack([jnp.roll(idx[:, p], -p, axis=1) for p in range(n_pos)], axis=1)
    idx = idx.reshape(angles, det_blocks * feeds)

    padded = [pad_rows(piece) for piece in vol_pieces]
    most = list(range(last))
    sino_most, vv = project_first(idx, radon_tiles, padded, tile_width, most)
    sino_last = project_rest(idx, radon_tiles, vv, tile_width, [last])
    got_most = everyone(sino_most[:, :rows])
    got_most, sino_last = lax.optimization_barrier((got_most, sino_last))
    got_last = everyone(sino_last[:, :rows])
    got_most, got_last = to_groups(got_most, own), to_groups(got_last, own)
    tables = dft_tables(probe_field.shape[1])
    partial, first_grad, spill = exit_first(
        meta, probe_field, tables, got_most, amp_pieces[:2], tile_width
    )
    own_grad = first_grad
    first_grad, got_last = lax.optimization_barrier((first_grad, got_last))
    joined = exit_rest(
        meta, probe_field, tables, got_most, got_last, partial, spill, amp_pieces[2:]
    )
    back_first = everyone(from_groups(first_grad, own))
    back_first, joined_sent = lax.optimization_barrier((back_first, joined))
    back_rest = everyone(from_groups(joined_sent, own))
    partial_grad = back_project(
        idx, radon_tiles, pad_rows(back_first), [1], None, n_pos, width, jnp.float32, "back_first"
    )
    order = list(range(2, n_pos)) + [0]
    joined_tiles = {j: joined[:, :, i * tile_width : (i + 1) * tile_width] for i, j in enumerate(order)}
    joined_tiles[1] = own_grad
    tile_pieces = rotate_pos([joined_tiles[j] for j in range(n_pos)], 1)
    obj_pieces = back_project(
        idx, radon_tiles, pad_rows(back_rest), order, partial_grad, n_pos, width, jnp.bfloat16, "back_rest"
    )
    groups = joined.shape[0]
    tile_pieces = [tile_pieces[-j % n_pos] for j in range(n_pos)]
    tile_pieces = [
        piece.reshape(groups, 2, GROUP, tile_width).transpose(1, 0, 2, 3).reshape(2, groups * GROUP, tile_width)
        for piece in tile_pieces
    ]
    proj_grad = jnp.stack(in_order(tile_pieces, -pos % n_pos), axis=2).astype(jnp.float32)
    obj_pieces = rotate_pos([piece[:rows] for piece in obj_pieces], -1)
    obj_pieces = [piece.reshape(2, own, width) for piece in in_order(obj_pieces, -pos % n_pos)]
    object_grad = jnp.concatenate(obj_pieces, axis=1).astype(jnp.float32)
    new_volume = volume.astype(jnp.float32) + step_size * object_grad
    return (new_volume, proj_grad)


def solution(mesh):
    in_specs = (
        P(None, "ang", "pos"),
        P(),
        P(),
        P(),
        P("ang", "pos", None, None),
        P("ang", "pos"),
        P("ang", "pos"),
    )
    out_specs = (P(None, "ang", "pos"), P(None, None, "ang", "pos"))
    return jax.shard_map(
        on_device, mesh=mesh, in_specs=in_specs, out_specs=out_specs, check_vma=False
    )
```

```python
import functools
import math

import jax
import jax.numpy as jnp
import numpy as np
from jax import lax
from jax.experimental import pallas as pl
from jax.experimental.pallas import tpu as pltpu
from jax.sharding import PartitionSpec as P

step_size = 0.1
LANES = 128
ROWS = 16
GROUP = 8
VMEM_LIMIT = 50 * 1024 * 1024
everywhere = pl.BlockSpec(memory_space=pltpu.VMEM)
scalars = pl.BlockSpec(memory_space=pltpu.SMEM)
CHAINS = 4
BATCH = 4


def dft_tables(width):
    index = np.arange(width)
    turn = 2.0 * math.pi / width * (index[:, None] * index[None, :] % width)
    cosine = jnp.asarray(np.cos(turn) / math.sqrt(width), jnp.bfloat16)
    sine_neg = jnp.asarray(-np.sin(turn) / math.sqrt(width), jnp.bfloat16)
    forward = jnp.block([[cosine, -sine_neg], [sine_neg, cosine]])
    inverse = jnp.block([[cosine, sine_neg], [-sine_neg, cosine]])
    return (forward, inverse)


def rotate_pos(pieces, sign):
    count = len(pieces)
    return [pieces[0]] + [
        lax.ppermute(pieces[j], "pos", [(i, (i + sign * j) % count) for i in range(count)])
        for j in range(1, count)
    ]


def in_order(pieces, first):
    count = len(pieces)
    bit = 1
    while bit < count:
        flip = (first & bit) != 0
        pieces = [jnp.where(flip, pieces[(k + bit) % count], pieces[k]) for k in range(count)]
        bit *= 2
    return pieces


def lower_half(shape):
    return lax.broadcasted_iota(jnp.int32, shape, len(shape) - 1) < LANES // 2


def swap_halves(tile):
    return pltpu.roll(tile, LANES // 2, 1)


def arrange(vol_refs, vv_ref):
    per_piece = vol_refs[0].shape[1] // LANES
    tiles = per_piece * len(vol_refs)
    batch = 16
    source = lax.broadcasted_iota(jnp.int32, (LANES, LANES), 0)
    target = lax.broadcasted_iota(jnp.int32, (LANES, LANES), 1)
    swap = ((source + LANES // 2) % LANES == target).astype(jnp.bfloat16)
    for k, vol_ref in enumerate(vol_refs):

        @pl.loop(0, per_piece // batch, unroll=2)
        def _(step):
            stack = []
            for i in range(batch):
                t = step * batch + i
                tile = vol_ref[:, pl.ds(pl.multiple_of(t * LANES, LANES), LANES)]
                vv_ref[k * per_piece + t] = tile
                stack.append(tile)
            swapped = jnp.dot(
                jnp.concatenate(stack, axis=0), swap, preferred_element_type=jnp.float32
            ).astype(jnp.bfloat16)
            for i in range(batch):
                t = step * batch + i
                vv_ref[tiles + k * per_piece + t] = swapped[i * ROWS : (i + 1) * ROWS]


def project_chunk(chunks, idx_ref, radon_ref, vv_ref, out_ref, lhs_refs):
    angles, block, span = radon_ref.shape
    blocks = out_ref.shape[2] // block // len(chunks)
    feeds = span // block
    low = lower_half((ROWS, LANES))
    batch = lhs_refs[0].shape[0]

    def gather(start, lhs_ref):
        for n in range(batch):
            a = start + n
            for i, chunk in enumerate(chunks):
                for b in range(blocks):
                    row = (i * blocks + b) * ROWS
                    for jp in range(feeds // 2):
                        at = (chunk * blocks + b) * feeds + 2 * jp
                        first = vv_ref[idx_ref[a, at]]
                        second = vv_ref[idx_ref[a, at + 1]]
                        lhs_ref[n, row : row + ROWS, jp * LANES : (jp + 1) * LANES] = jnp.where(
                            low, first, second
                        )

    def multiply(start, lhs_ref):
        for n in range(batch):
            a = start + n
            product = lax.dot_general(
                lhs_ref[n], radon_ref[a], (((1,), (1,)), ((), ())), preferred_element_type=jnp.float32
            )
            for pair in range(len(chunks) * blocks // 2):
                row = 2 * pair * ROWS
                tile = jnp.concatenate(
                    [product[row : row + ROWS], product[row + ROWS : row + 2 * ROWS]], axis=1
                )
                out_ref[a, :, pair * LANES : (pair + 1) * LANES] = tile.astype(jnp.bfloat16)

    gather(0, lhs_refs[0])

    @pl.loop(0, angles // (2 * batch))
    def _(step):
        start = step * 2 * batch
        multiply(start, lhs_refs[0])
        gather(start + batch, lhs_refs[1])
        multiply(start + batch, lhs_refs[1])
        gather(jnp.minimum(start + 2 * batch, angles - batch), lhs_refs[0])


def project_kernel(chunks, pieces, idx_ref, radon_ref, *refs):
    vol_refs = refs[:pieces]
    out_ref, vv_ref, *lhs_refs = refs[pieces:]
    arrange(vol_refs, vv_ref)
    project_chunk(chunks, idx_ref, radon_ref, vv_ref, out_ref, lhs_refs)


def guess(microseconds):
    return pl.CostEstimate(
        flops=int(microseconds * 1.15e9), bytes_accessed=int(microseconds * 1e5), transcendentals=0
    )


def project(idx, radon_tiles, vol_pieces, tile_width, chunks, name):
    angles, block, span = radon_tiles.shape
    pieces = len(vol_pieces)
    tiles = pieces * vol_pieces[0].shape[1] // LANES
    rows = len(chunks) * tile_width // block * ROWS
    return pl.pallas_call(
        functools.partial(project_kernel, chunks, pieces),
        out_shape=jax.ShapeDtypeStruct((angles, ROWS, len(chunks) * tile_width), jnp.bfloat16),
        in_specs=[scalars, everywhere] + [everywhere] * pieces,
        out_specs=everywhere,
        scratch_shapes=[pltpu.VMEM((2 * tiles, ROWS, LANES), jnp.bfloat16)]
        + [pltpu.VMEM((BATCH, rows, span), jnp.bfloat16)] * 2,
        compiler_params=pltpu.CompilerParams(vmem_limit_bytes=VMEM_LIMIT),
        cost_estimate=guess(4 + 2 * len(chunks)),
        name=name,
    )(idx, radon_tiles, *vol_pieces)


def back_project_kernel(chunks, pieces, has_start, idx_ref, radon_ref, grad_ref, *refs):
    start_refs, refs = (refs[:pieces], refs[pieces:]) if has_start else (None, refs)
    out_refs, refs = refs[:pieces], refs[pieces:]
    acc_refs, (w_ref, *contrib_refs) = refs[:CHAINS], refs[CHAINS:]
    angles, block, span = radon_ref.shape
    per_piece = out_refs[0].shape[1] // LANES
    blocks = grad_ref.shape[2] // block // len(chunks)
    pairs = len(chunks) * blocks // 2
    feeds = span // block

    @pl.loop(0, acc_refs[0].shape[0], unroll=16)
    def _(t):
        for acc_ref in acc_refs:
            acc_ref[t] = jnp.zeros((GROUP, LANES), jnp.float32)

    low = lower_half((GROUP, LANES))
    low_rows = lower_half((block, LANES))
    w_ref[...] = jnp.zeros_like(w_ref)

    def widen(slot, a):
        for jp in range(feeds // 2):
            tile = radon_ref[a, :, jp * LANES : (jp + 1) * LANES].astype(jnp.float32)
            turned = swap_halves(tile)
            for side, (first, second) in enumerate(((tile, turned), (turned, tile))):
                lanes = slice((2 * jp + side) * LANES, (2 * jp + side + 1) * LANES)
                w_ref[slot, :block, lanes] = jnp.where(low_rows, first, 0.0).astype(jnp.bfloat16)
                w_ref[slot, block:, lanes] = jnp.where(low_rows, 0.0, second).astype(jnp.bfloat16)

    def multiply(start, half, contrib_ref):
        for n in range(CHAINS):
            a = start + n
            widen(half * CHAINS + n, a)
            lhs = []
            for pair in range(pairs):
                tile = grad_ref[a, :, pair * LANES : (pair + 1) * LANES].astype(jnp.float32)
                real, imag = tile[:GROUP], tile[GROUP:]
                even = jnp.where(low, real, swap_halves(imag))
                odd = jnp.where(low, swap_halves(real), imag)
                lhs.append(jnp.concatenate([even, odd], axis=0).astype(jnp.bfloat16))
            contrib_ref[n] = jnp.dot(
                jnp.concatenate(lhs, axis=0),
                w_ref[half * CHAINS + n],
                preferred_element_type=jnp.float32,
            )

    def scatter(start, contrib_ref):
        for i, chunk in enumerate(chunks):
            for b in range(blocks):
                row = (i * blocks + b) * GROUP
                for j in range(feeds):
                    at = (chunk * blocks + b) * feeds + j
                    for n in range(CHAINS):
                        tile = contrib_ref[n, row : row + GROUP, j * LANES : (j + 1) * LANES]
                        acc_refs[n][idx_ref[start + n, at]] += tile

    multiply(0, 0, contrib_refs[0])

    @pl.loop(0, angles // (2 * CHAINS))
    def _(step):
        start = step * 2 * CHAINS
        multiply(start + CHAINS, 1, contrib_refs[1])
        scatter(start, contrib_refs[0])
        multiply(jnp.minimum(start + 2 * CHAINS, angles - CHAINS), 0, contrib_refs[0])
        scatter(start + CHAINS, contrib_refs[1])

    for k in range(pieces):

        @pl.loop(0, per_piece, unroll=16)
        def _(t):
            lanes = pl.ds(pl.multiple_of(t * LANES, LANES), LANES)
            at = 2 * (k * per_piece + t)
            even, odd = acc_refs[0][at], acc_refs[0][at + 1]
            for acc_ref in acc_refs[1:]:
                even += acc_ref[at]
                odd += acc_ref[at + 1]
            real = jnp.where(low, even, swap_halves(odd))
            imag = jnp.where(low, swap_halves(even), odd)
            total = jnp.concatenate([real, imag], axis=0)
            if has_start:
                total += start_refs[k][:, lanes]
            out_refs[k][:, lanes] = total.astype(out_refs[k].dtype)


def back_project(idx, radon_tiles, grads, chunks, start, pieces, piece_width, out_type, name):
    angles, block, span = radon_tiles.shape
    coef_blocks = pieces * piece_width // block
    rows = grads.shape[2] // block * GROUP
    has_start = start is not None
    operands = [idx, radon_tiles, grads] + (list(start) if has_start else [])
    return pl.pallas_call(
        functools.partial(back_project_kernel, chunks, pieces, has_start),
        out_shape=[jax.ShapeDtypeStruct((ROWS, piece_width), out_type)] * pieces,
        in_specs=[scalars] + [everywhere] * (len(operands) - 1),
        out_specs=[everywhere] * pieces,
        scratch_shapes=[pltpu.VMEM((coef_blocks, GROUP, LANES), jnp.float32)] * CHAINS
        + [pltpu.VMEM((2 * CHAINS, 2 * block, 2 * span), jnp.bfloat16)]
        + [pltpu.VMEM((CHAINS, rows, 2 * span), jnp.float32)] * 2,
        compiler_params=pltpu.CompilerParams(vmem_limit_bytes=VMEM_LIMIT),
        cost_estimate=guess(3 + 2 * len(chunks)),
        name=name,
    )(*operands)


def add_slots(meta_ref, probe_ref, forward_ref, inverse_ref, ext_ref, acc_ref, amp_refs, scratch, first):
    wave_ref, half_ref, delta_ref, back_ref = scratch
    n_pos = lax.axis_size("pos")
    groups = ext_ref.shape[0]
    width = probe_ref.shape[1]
    slots = amp_refs[0].shape[0]
    tile_width = (acc_ref.shape[2] - width) // len(amp_refs)
    chunk = 4
    crows = chunk * GROUP
    chunks = groups // chunk
    wide = width // LANES
    lane_id = lax.broadcasted_iota(jnp.int32, (crows, LANES), 1)

    def product(left, right):
        return jnp.dot(left, right, preferred_element_type=jnp.float32)

    for tile, amp_ref in enumerate(amp_refs):
        order = first + tile
        tile_start = lax.rem(lax.axis_index("pos") + order, n_pos) * tile_width - tile * tile_width
        count = meta_ref[order, slots]

        @pl.loop(0, (count + 1) // 2)
        def _(step):
            shifts, starts, lives = [], [], []
            for n in range(2):
                offset = meta_ref[order, step * 2 + n] - tile_start
                shifts.append(offset % LANES)
                lane_tile = offset // LANES
                starts.append(
                    [pl.multiple_of((lane_tile + m) * LANES, LANES) for m in range(wide + 1)]
                )
                lives.append((step * 2 + n < count).astype(jnp.float32))
            for n in range(2):
                keep = lane_id < LANES - shifts[n]
                back_shift = (LANES - shifts[n]) % LANES
                for ch in range(chunks):
                    rows = slice(ch * crows, (ch + 1) * crows)
                    low_rows = slice(width + ch * crows, width + (ch + 1) * crows)
                    turned = []
                    for start in starts[n]:
                        both = ext_ref[ch * chunk : (ch + 1) * chunk, :, pl.ds(start, LANES)]
                        both = both.astype(jnp.float32)
                        turned.append(
                            [
                                pltpu.roll(
                                    both[:, c * GROUP : (c + 1) * GROUP].reshape(crows, LANES),
                                    back_shift,
                                    1,
                                )
                                for c in range(2)
                            ]
                        )
                    for m in range(wide):
                        lanes = slice(m * LANES, (m + 1) * LANES)
                        put = slice(n * width + m * LANES, n * width + (m + 1) * LANES)
                        patch_re = jnp.where(keep, turned[m][0], turned[m + 1][0])
                        patch_im = jnp.where(keep, turned[m][1], turned[m + 1][1])
                        probe_re = probe_ref[0, rows, lanes].astype(jnp.float32)
                        probe_im = probe_ref[1, rows, lanes].astype(jnp.float32)
                        wave_re = probe_re * patch_re - probe_im * patch_im
                        wave_im = probe_re * patch_im + probe_im * patch_re
                        wave_ref[rows, put] = wave_re.astype(jnp.bfloat16)
                        wave_ref[low_rows, put] = wave_im.astype(jnp.bfloat16)
                mine = slice(n * width, (n + 1) * width)
                half = product(forward_ref[...], wave_ref[:, mine]).astype(jnp.bfloat16)
                half_ref[mine, :width] = half[:width]
                half_ref[mine, width:] = half[width:]
            for n in range(2):
                mine = slice(n * width, (n + 1) * width)
                far = product(half_ref[mine, :], inverse_ref[...])
                for ch in range(chunks):
                    rows = slice(ch * crows, (ch + 1) * crows)
                    low_rows = slice(width + ch * crows, width + (ch + 1) * crows)
                    far_re, far_im = far[rows, :width], far[rows, width:]
                    power = far_re * far_re + far_im * far_im
                    amps = amp_ref[step * 2 + n, rows, :].astype(jnp.float32)
                    factor = amps * lax.rsqrt(jnp.maximum(power, 1.0)) - 1.0
                    delta_ref[rows, mine] = (far_re * factor).astype(jnp.bfloat16)
                    delta_ref[low_rows, mine] = (far_im * factor).astype(jnp.bfloat16)
                back = product(inverse_ref[...], delta_ref[:, mine]).astype(jnp.bfloat16)
                back_ref[mine, :width] = back[:width]
                back_ref[mine, width:] = back[width:]
            for n in range(2):
                mine = slice(n * width, (n + 1) * width)
                near = product(back_ref[mine, :], forward_ref[...])
                past = lane_id >= shifts[n]
                for ch in range(chunks):
                    rows = slice(ch * crows, (ch + 1) * crows)
                    turned = []
                    for m in range(wide):
                        lanes = slice(m * LANES, (m + 1) * LANES)
                        probe_re = probe_ref[0, rows, lanes].astype(jnp.float32) * lives[n]
                        probe_im = probe_ref[1, rows, lanes].astype(jnp.float32) * lives[n]
                        near_re = near[rows, m * LANES : (m + 1) * LANES]
                        near_im = near[rows, width + m * LANES : width + (m + 1) * LANES]
                        turned.append(
                            [
                                pltpu.roll(probe_re * near_re + probe_im * near_im, shifts[n], 1),
                                pltpu.roll(probe_re * near_im - probe_im * near_re, shifts[n], 1),
                            ]
                        )
                    for m in range(wide + 1):
                        for c in range(2):
                            behind = turned[m - 1][c] if m > 0 else 0.0
                            ahead = turned[m][c] if m < wide else 0.0
                            here = (c, rows, pl.ds(starts[n][m], LANES))
                            acc_ref[here] += jnp.where(past, ahead, behind)


def exit_first_kernel(
    tiles, meta_ref, probe_ref, forward_ref, inverse_ref, most_ref, *refs
):
    amp_refs, refs = refs[:tiles], refs[tiles:]
    partial_ref, grad_ref, spill_ref, acc_ref, *scratch = refs
    groups = most_ref.shape[0]
    tile_width = partial_ref.shape[2]
    done = tiles * tile_width

    @pl.loop(0, groups)
    def _(g):
        rows = pl.ds(pl.multiple_of(g * GROUP, GROUP), GROUP)
        for c in range(2):
            acc_ref[c, rows, :] = jnp.zeros((GROUP, acc_ref.shape[2]), jnp.float32)

    add_slots(
        meta_ref, probe_ref, forward_ref, inverse_ref, most_ref, acc_ref, amp_refs, scratch, 0
    )

    @pl.loop(0, groups)
    def _(g):
        rows = pl.ds(pl.multiple_of(g * GROUP, GROUP), GROUP)
        whole = [acc_ref[c, rows, tile_width:done] for c in range(2)]
        grad_ref[g] = jnp.concatenate(whole, axis=0).astype(jnp.bfloat16)
        for c in range(2):
            partial_ref[c, rows, :] = acc_ref[c, rows, :tile_width]
            spill_ref[c, rows, :] = acc_ref[c, rows, done:]


def exit_rest_kernel(
    tiles, meta_ref, probe_ref, forward_ref, inverse_ref, most_ref, last_ref, partial_ref, spill_ref, *refs
):
    amp_refs, refs = refs[:tiles], refs[tiles:]
    out_ref, ext_ref, acc_ref, *scratch = refs
    groups = most_ref.shape[0]
    width = probe_ref.shape[1]
    tile_width = partial_ref.shape[2]
    done = tiles * tile_width
    kept = done - tile_width

    @pl.loop(0, groups)
    def _(g):
        ext_ref[g, :, :kept] = most_ref[g, :, most_ref.shape[2] - kept :]
        ext_ref[g, :, kept:done] = last_ref[g]
        ext_ref[g, :, done:] = most_ref[g, :, :width]
        rows = pl.ds(pl.multiple_of(g * GROUP, GROUP), GROUP)
        for c in range(2):
            acc_ref[c, rows, :width] = spill_ref[c, rows, :]
            acc_ref[c, rows, width:] = jnp.zeros((GROUP, done), jnp.float32)

    add_slots(
        meta_ref, probe_ref, forward_ref, inverse_ref, ext_ref, acc_ref, amp_refs, scratch,
        lax.axis_size("pos") - tiles,
    )

    @pl.loop(0, groups)
    def _(g):
        rows = pl.ds(pl.multiple_of(g * GROUP, GROUP), GROUP)
        here, wrapped = [], []
        for c in range(2):
            here.append(acc_ref[c, rows, :done])
            whole = partial_ref[c, rows, :]
            spilled = whole[:, :width] + acc_ref[c, rows, done:]
            wrapped.append(jnp.concatenate([spilled, whole[:, width:]], axis=1))
        out_ref[g, :, :done] = jnp.concatenate(here, axis=0).astype(jnp.bfloat16)
        out_ref[g, :, done:] = jnp.concatenate(wrapped, axis=0).astype(jnp.bfloat16)


def exit_scratch(groups, width, reach):
    return [pltpu.VMEM((2, groups * GROUP, reach), jnp.float32)] + [
        pltpu.VMEM((2 * width, 2 * width), jnp.bfloat16)
    ] * 4


def exit_first(meta, probe_field, tables, most, amps, tile_width):
    groups, rows = most.shape[:2]
    width = probe_field.shape[1]
    tiles = len(amps)
    slices = groups * GROUP
    return pl.pallas_call(
        functools.partial(exit_first_kernel, tiles),
        out_shape=[
            jax.ShapeDtypeStruct((2, slices, tile_width), jnp.float32),
            jax.ShapeDtypeStruct((groups, rows, (tiles - 1) * tile_width), jnp.bfloat16),
            jax.ShapeDtypeStruct((2, slices, width), jnp.float32),
        ],
        in_specs=[scalars] + [everywhere] * (4 + tiles),
        out_specs=[everywhere] * 3,
        scratch_shapes=exit_scratch(groups, width, tiles * tile_width + width),
        compiler_params=pltpu.CompilerParams(vmem_limit_bytes=VMEM_LIMIT),
        cost_estimate=guess(10),
        name="exit_first",
    )(meta, probe_field, *tables, most, *amps)


def exit_rest(meta, probe_field, tables, most, final, partial, spill, amps):
    groups, rows, tile_width = final.shape
    width = probe_field.shape[1]
    tiles = len(amps)
    reach = tiles * tile_width + width
    return pl.pallas_call(
        functools.partial(exit_rest_kernel, tiles),
        out_shape=jax.ShapeDtypeStruct((groups, rows, (tiles + 1) * tile_width), jnp.bfloat16),
        in_specs=[scalars] + [everywhere] * (7 + tiles),
        out_specs=everywhere,
        scratch_shapes=[pltpu.VMEM((groups, rows, reach), jnp.bfloat16)]
        + exit_scratch(groups, width, reach),
        compiler_params=pltpu.CompilerParams(vmem_limit_bytes=VMEM_LIMIT),
        cost_estimate=guess(10),
        name="exit_rest",
    )(meta, probe_field, *tables, most, final, partial, spill, *amps)


def to_groups(received, own_slices):
    if own_slices == GROUP:
        return received
    devices, rows, columns = received.shape
    merge = GROUP // own_slices
    split = received.reshape(devices // merge, merge, 2, own_slices, columns)
    return split.transpose(0, 2, 1, 3, 4).reshape(devices // merge, ROWS, columns)


def from_groups(grouped, own_slices):
    if own_slices == GROUP:
        return grouped
    groups, rows, columns = grouped.shape
    merge = GROUP // own_slices
    split = grouped.reshape(groups, 2, merge, own_slices, columns)
    return split.transpose(0, 2, 1, 3, 4).reshape(groups * merge, 2 * own_slices, columns)


def pad_rows(block, own_slices):
    if own_slices == GROUP:
        return block
    lead, columns = block.shape[:-2], block.shape[-1]
    split = block.reshape(lead + (2, own_slices, columns))
    more = [(0, 0)] * (split.ndim - 2) + [(0, GROUP - own_slices), (0, 0)]
    return jnp.pad(split, more).reshape(lead + (ROWS, columns))


def cut_rows(block, own_slices):
    if own_slices == GROUP:
        return block
    lead, columns = block.shape[:-2], block.shape[-1]
    split = block.reshape(lead + (2, GROUP, columns))[..., :own_slices, :]
    return split.reshape(lead + (2 * own_slices, columns))


def everyone(chunk):
    return lax.all_to_all(chunk, ("ang", "pos"), 0, 0, tiled=True)


def on_device(volume, radon_tiles, tile_blocks, probe_field, amplitudes, offsets, counts):
    n_pos = lax.axis_size("pos")
    pos = lax.axis_index("pos")
    angles, det_blocks, feeds = tile_blocks.shape
    block_size = radon_tiles.shape[1]
    columns = det_blocks * block_size
    tile_width = columns // n_pos
    slab = volume.shape[1]
    width = volume.shape[2]
    own = slab // n_pos
    rows = 2 * own
    blocks_each = width // block_size
    last = n_pos - 1

    def slices_for(j):
        start = (pos + j) % n_pos * own
        return lax.dynamic_slice_in_dim(volume, start, own, 1).reshape(rows, width)

    vol_pieces = rotate_pos([slices_for(j) for j in range(n_pos)], 1)
    meta = jnp.concatenate([offsets, counts], axis=1)
    meta = rotate_pos(
        [lax.dynamic_slice_in_dim(meta, (pos - j) % n_pos, 1, 0) for j in range(n_pos)], -1
    )
    meta = jnp.concatenate(meta, axis=0)
    vol_pieces, amplitudes = lax.optimization_barrier((vol_pieces, amplitudes))
    amp_pieces = rotate_pos(
        [
            lax.dynamic_index_in_dim(amplitudes, (pos - j) % n_pos, 0, keepdims=False)
            for j in range(n_pos)
        ],
        -1,
    )

    owner = tile_blocks // blocks_each
    within = tile_blocks % blocks_each
    piece = (pos - owner) % n_pos
    crossed = (within + jnp.arange(feeds, dtype=jnp.int32)) % 2
    tiles_each = width // LANES

    def by_chunk(idx):
        idx = idx.reshape(angles // n_pos, n_pos, n_pos, det_blocks // n_pos * feeds)
        idx = jnp.stack([jnp.roll(idx[:, p], -p, axis=1) for p in range(n_pos)], axis=1)
        return idx.reshape(angles, det_blocks * feeds)

    tile_idx = by_chunk(crossed * (n_pos * tiles_each) + piece * tiles_each + within // 2)
    block_idx = by_chunk(piece * blocks_each + within)
    padded = [pad_rows(piece, own) for piece in vol_pieces]
    most = list(range(last))
    sino_most = project(tile_idx, radon_tiles, padded, tile_width, most, "project_most")
    sino_most, padded = lax.optimization_barrier((sino_most, padded))
    sino_last = project(tile_idx, radon_tiles, padded, tile_width, [last], "project_last")
    got_most = everyone(cut_rows(sino_most, own))
    got_most, sino_last = lax.optimization_barrier((got_most, sino_last))
    got_last = everyone(cut_rows(sino_last, own))
    got_most, got_last = to_groups(got_most, own), to_groups(got_last, own)
    tables = dft_tables(probe_field.shape[1])
    partial, first_grad, spill = exit_first(
        meta, probe_field, tables, got_most, amp_pieces[:2], tile_width
    )
    own_grad = first_grad
    first_grad, got_last = lax.optimization_barrier((first_grad, got_last))
    joined = exit_rest(
        meta, probe_field, tables, got_most, got_last, partial, spill, amp_pieces[2:]
    )
    back_first = everyone(from_groups(first_grad, own))
    back_first, joined_sent = lax.optimization_barrier((back_first, joined))
    back_rest = everyone(from_groups(joined_sent, own))
    partial_grad = back_project(
        block_idx, radon_tiles, pad_rows(back_first, own), [1], None, n_pos, width, jnp.float32, "back_first"
    )
    order = list(range(2, n_pos)) + [0]
    joined_tiles = {j: joined[:, :, i * tile_width : (i + 1) * tile_width] for i, j in enumerate(order)}
    joined_tiles[1] = own_grad
    tile_pieces = rotate_pos([joined_tiles[j] for j in range(n_pos)], 1)
    obj_pieces = back_project(
        block_idx, radon_tiles, pad_rows(back_rest, own), order, partial_grad, n_pos, width, jnp.bfloat16, "back_rest"
    )
    groups = joined.shape[0]
    tile_pieces = [tile_pieces[-j % n_pos] for j in range(n_pos)]
    tile_pieces = [
        piece.reshape(groups, 2, GROUP, tile_width).transpose(1, 0, 2, 3).reshape(2, groups * GROUP, tile_width)
        for piece in tile_pieces
    ]
    proj_grad = jnp.stack(in_order(tile_pieces, -pos % n_pos), axis=2).astype(jnp.float32)
    obj_pieces = rotate_pos([cut_rows(piece, own) for piece in obj_pieces], -1)
    obj_pieces = [piece.reshape(2, own, width) for piece in in_order(obj_pieces, -pos % n_pos)]
    object_grad = jnp.concatenate(obj_pieces, axis=1).astype(jnp.float32)
    new_volume = volume.astype(jnp.float32) + step_size * object_grad
    return (new_volume, proj_grad)


def solution(mesh):
    in_specs = (
        P(None, "ang", "pos"),
        P(),
        P(),
        P(),
        P("ang", "pos", None, None),
        P("ang", "pos"),
        P("ang", "pos"),
    )
    out_specs = (P(None, "ang", "pos"), P(None, None, "ang", "pos"))
    return jax.shard_map(
        on_device, mesh=mesh, in_specs=in_specs, out_specs=out_specs, check_vma=False
    )
```

```python
import functools
import math

import jax
import jax.numpy as jnp
import numpy as np
from jax import lax
from jax.experimental import pallas as pl
from jax.experimental.pallas import tpu as pltpu
from jax.sharding import PartitionSpec as P

step_size = 0.1
LANES = 128
ROWS = 16
GROUP = 8
MEBI = 1024 * 1024
everywhere = pl.BlockSpec(memory_space=pltpu.VMEM)
scalars = pl.BlockSpec(memory_space=pltpu.SMEM)
CHAINS = 8
BATCH = 4


def dft_tables(width):
    index = np.arange(width)
    turn = 2.0 * math.pi / width * (index[:, None] * index[None, :] % width)
    cosine = jnp.asarray(np.cos(turn) / math.sqrt(width), jnp.bfloat16)
    sine_neg = jnp.asarray(-np.sin(turn) / math.sqrt(width), jnp.bfloat16)
    forward = jnp.block([[cosine, -sine_neg], [sine_neg, cosine]])
    inverse = jnp.block([[cosine, sine_neg], [-sine_neg, cosine]])
    return (forward, inverse)


def rotate_pos(pieces, sign):
    count = len(pieces)
    return [pieces[0]] + [
        lax.ppermute(pieces[j], "pos", [(i, (i + sign * j) % count) for i in range(count)])
        for j in range(1, count)
    ]


def in_order(pieces, first):
    count = len(pieces)
    bit = 1
    while bit < count:
        flip = (first & bit) != 0
        pieces = [jnp.where(flip, pieces[(k + bit) % count], pieces[k]) for k in range(count)]
        bit *= 2
    return pieces


def lower_half(shape):
    return lax.broadcasted_iota(jnp.int32, shape, len(shape) - 1) < LANES // 2


def swap_halves(tile):
    return pltpu.roll(tile, LANES // 2, 1)


def arrange(vol_refs, vv_ref):
    per_piece = vol_refs[0].shape[1] // LANES
    tiles = per_piece * len(vol_refs)
    batch = 16
    source = lax.broadcasted_iota(jnp.int32, (LANES, LANES), 0)
    target = lax.broadcasted_iota(jnp.int32, (LANES, LANES), 1)
    swap = ((source + LANES // 2) % LANES == target).astype(jnp.bfloat16)
    for k, vol_ref in enumerate(vol_refs):

        @pl.loop(0, per_piece // batch, unroll=2)
        def _(step):
            stack = []
            for i in range(batch):
                t = step * batch + i
                tile = vol_ref[:, pl.ds(pl.multiple_of(t * LANES, LANES), LANES)]
                vv_ref[k * per_piece + t] = tile
                stack.append(tile)
            swapped = jnp.dot(
                jnp.concatenate(stack, axis=0), swap, preferred_element_type=jnp.float32
            ).astype(jnp.bfloat16)
            for i in range(batch):
                t = step * batch + i
                vv_ref[tiles + k * per_piece + t] = swapped[i * ROWS : (i + 1) * ROWS]


def project_blocks(blocks, idx_ref, radon_ref, vv_ref, out_ref, lhs_refs):
    angles, block, span = radon_ref.shape
    feeds = span // block
    low = lower_half((ROWS, LANES))
    batch = lhs_refs[0].shape[0]

    def gather(start, lhs_ref):
        for n in range(batch):
            a = start + n
            for i, b in enumerate(blocks):
                row = i * ROWS
                for jp in range(feeds // 2):
                    at = b * feeds + 2 * jp
                    first = vv_ref[idx_ref[a, at]]
                    second = vv_ref[idx_ref[a, at + 1]]
                    lhs_ref[n, row : row + ROWS, jp * LANES : (jp + 1) * LANES] = jnp.where(
                        low, first, second
                    )

    def multiply(start, lhs_ref):
        for n in range(batch):
            a = start + n
            product = lax.dot_general(
                lhs_ref[n], radon_ref[a], (((1,), (1,)), ((), ())), preferred_element_type=jnp.float32
            )
            for pair in range(len(blocks) // 2):
                row = 2 * pair * ROWS
                tile = jnp.concatenate(
                    [product[row : row + ROWS], product[row + ROWS : row + 2 * ROWS]], axis=1
                )
                out_ref[a, :, pair * LANES : (pair + 1) * LANES] = tile.astype(jnp.bfloat16)

    gather(0, lhs_refs[0])

    @pl.loop(0, angles // (2 * batch))
    def _(step):
        start = step * 2 * batch
        multiply(start, lhs_refs[0])
        gather(start + batch, lhs_refs[1])
        multiply(start + batch, lhs_refs[1])
        gather(jnp.minimum(start + 2 * batch, angles - batch), lhs_refs[0])


def project_kernel(blocks, pieces, idx_ref, radon_ref, *refs):
    vol_refs = refs[:pieces]
    out_ref, vv_ref, *lhs_refs = refs[pieces:]
    arrange(vol_refs, vv_ref)
    project_blocks(blocks, idx_ref, radon_ref, vv_ref, out_ref, lhs_refs)


def guess(microseconds):
    return pl.CostEstimate(
        flops=int(microseconds * 1.15e9), bytes_accessed=int(microseconds * 1e5), transcendentals=0
    )


def project(idx, radon_tiles, vol_pieces, blocks, name):
    angles, block, span = radon_tiles.shape
    pieces = len(vol_pieces)
    tiles = pieces * vol_pieces[0].shape[1] // LANES
    out_shape = (angles, ROWS, len(blocks) * block)
    return pl.pallas_call(
        functools.partial(project_kernel, blocks, pieces),
        out_shape=jax.ShapeDtypeStruct(out_shape, jnp.bfloat16),
        in_specs=[scalars, everywhere] + [everywhere] * pieces,
        out_specs=everywhere,
        scratch_shapes=[pltpu.VMEM((2 * tiles, ROWS, LANES), jnp.bfloat16)]
        + [pltpu.VMEM((BATCH, len(blocks) * ROWS, span), jnp.bfloat16)] * 2,
        compiler_params=pltpu.CompilerParams(
            vmem_limit_bytes=14 * MEBI + 2 * radon_tiles.size + 2 * math.prod(out_shape)
        ),
        cost_estimate=guess(4 + len(blocks) // 4),
        name=name,
    )(idx, radon_tiles, *vol_pieces)


def back_project_kernel(blocks, has_start, outs, idx_ref, radon_ref, grad_ref, *refs):
    start_ref, refs = (refs[0], refs[1:]) if has_start else (None, refs)
    out_refs, refs = refs[:outs], refs[outs:]
    acc_refs, (w_ref, *contrib_refs) = refs[:CHAINS], refs[CHAINS:]
    angles, block, span = radon_ref.shape
    pairs = len(blocks) // 2
    feeds = span // block
    coef_blocks = acc_refs[0].shape[0]

    @pl.loop(0, coef_blocks, unroll=16)
    def _(t):
        for n, acc_ref in enumerate(acc_refs):
            if n == 0 and has_start:
                acc_ref[t] = start_ref[t]
            else:
                acc_ref[t] = jnp.zeros((GROUP, LANES), jnp.float32)

    low = lower_half((GROUP, LANES))
    low_rows = lower_half((block, LANES))
    w_ref[...] = jnp.zeros_like(w_ref)

    def widen(slot, a):
        for jp in range(feeds // 2):
            tile = radon_ref[a, :, jp * LANES : (jp + 1) * LANES].astype(jnp.float32)
            turned = swap_halves(tile)
            for side, (first, second) in enumerate(((tile, turned), (turned, tile))):
                lanes = slice((2 * jp + side) * LANES, (2 * jp + side + 1) * LANES)
                w_ref[slot, :block, lanes] = jnp.where(low_rows, first, 0.0).astype(jnp.bfloat16)
                w_ref[slot, block:, lanes] = jnp.where(low_rows, 0.0, second).astype(jnp.bfloat16)

    def multiply(start, half, contrib_ref):
        for n in range(CHAINS):
            a = start + n
            widen(half * CHAINS + n, a)
            lhs = []
            for pair in range(pairs):
                tile = grad_ref[a, :, pair * LANES : (pair + 1) * LANES].astype(jnp.float32)
                real, imag = tile[:GROUP], tile[GROUP:]
                even = jnp.where(low, real, swap_halves(imag))
                odd = jnp.where(low, swap_halves(real), imag)
                lhs.append(jnp.concatenate([even, odd], axis=0).astype(jnp.bfloat16))
            contrib_ref[n] = jnp.dot(
                jnp.concatenate(lhs, axis=0),
                w_ref[half * CHAINS + n],
                preferred_element_type=jnp.float32,
            )

    def scatter(start, contrib_ref):
        for i, b in enumerate(blocks):
            row = i * GROUP
            for j in range(feeds):
                for n in range(CHAINS):
                    tile = contrib_ref[n, row : row + GROUP, j * LANES : (j + 1) * LANES]
                    acc_refs[n][idx_ref[start + n, b * feeds + j]] += tile

    multiply(0, 0, contrib_refs[0])

    @pl.loop(0, angles // (2 * CHAINS))
    def _(step):
        start = step * 2 * CHAINS
        multiply(start + CHAINS, 1, contrib_refs[1])
        scatter(start, contrib_refs[0])
        multiply(jnp.minimum(start + 2 * CHAINS, angles - CHAINS), 0, contrib_refs[0])
        scatter(start + CHAINS, contrib_refs[1])

    def total(t):
        sums = [acc_ref[t] for acc_ref in acc_refs]
        while len(sums) > 1:
            sums = [sums[i] + sums[i + 1] for i in range(0, len(sums), 2)]
        return sums[0]

    if outs == 1:

        @pl.loop(0, coef_blocks, unroll=16)
        def _(t):
            out_refs[0][t] = total(t)

    else:
        per_piece = out_refs[0].shape[1] // LANES
        for k, out_ref in enumerate(out_refs):

            @pl.loop(0, per_piece, unroll=16)
            def _(t):
                lanes = pl.ds(pl.multiple_of(t * LANES, LANES), LANES)
                even = total(2 * (k * per_piece + t))
                odd = total(2 * (k * per_piece + t) + 1)
                real = jnp.where(low, even, swap_halves(odd))
                imag = jnp.where(low, swap_halves(even), odd)
                out_ref[:, lanes] = jnp.concatenate([real, imag], axis=0).astype(out_ref.dtype)


def back_project(idx, radon_tiles, grads, blocks, start, pieces, piece_width, name):
    angles, block, span = radon_tiles.shape
    coef_blocks = pieces * piece_width // block
    rows = len(blocks) * GROUP
    has_start = start is not None
    if has_start:
        out_shape = [jax.ShapeDtypeStruct((ROWS, piece_width), jnp.bfloat16)] * pieces
    else:
        out_shape = [jax.ShapeDtypeStruct((coef_blocks, GROUP, LANES), jnp.float32)]
    operands = [idx, radon_tiles, grads] + ([start] if has_start else [])
    return pl.pallas_call(
        functools.partial(back_project_kernel, blocks, has_start, len(out_shape)),
        out_shape=out_shape,
        in_specs=[scalars] + [everywhere] * (len(operands) - 1),
        out_specs=[everywhere] * len(out_shape),
        scratch_shapes=[pltpu.VMEM((coef_blocks, GROUP, LANES), jnp.float32)] * CHAINS
        + [pltpu.VMEM((2 * CHAINS, 2 * block, 2 * span), jnp.bfloat16)]
        + [pltpu.VMEM((CHAINS, rows, 2 * span), jnp.float32)] * 2,
        compiler_params=pltpu.CompilerParams(
            vmem_limit_bytes=34 * MEBI + 2 * radon_tiles.size + 2 * grads.size
        ),
        cost_estimate=guess(4 + len(blocks) // 4),
        name=name,
    )(*operands)


def add_slots(meta_ref, probe_ref, forward_ref, inverse_ref, ext_ref, acc_ref, amp_refs, scratch, first):
    wave_ref, half_ref, delta_ref, back_ref = scratch
    n_pos = lax.axis_size("pos")
    groups = ext_ref.shape[0]
    width = probe_ref.shape[1]
    slots = amp_refs[0].shape[0]
    tile_width = (acc_ref.shape[2] - width) // len(amp_refs)
    chunk = 4
    crows = chunk * GROUP
    chunks = groups // chunk
    wide = width // LANES
    lane_id = lax.broadcasted_iota(jnp.int32, (crows, LANES), 1)

    def product(left, right):
        return jnp.dot(left, right, preferred_element_type=jnp.float32)

    for tile, amp_ref in enumerate(amp_refs):
        order = first + tile
        tile_start = lax.rem(lax.axis_index("pos") + order, n_pos) * tile_width - tile * tile_width
        count = meta_ref[order, slots]

        @pl.loop(0, (count + 1) // 2)
        def _(step):
            shifts, starts, lives = [], [], []
            for n in range(2):
                offset = meta_ref[order, step * 2 + n] - tile_start
                shifts.append(offset % LANES)
                lane_tile = offset // LANES
                starts.append(
                    [pl.multiple_of((lane_tile + m) * LANES, LANES) for m in range(wide + 1)]
                )
                lives.append((step * 2 + n < count).astype(jnp.float32))
            for n in range(2):
                keep = lane_id < LANES - shifts[n]
                back_shift = (LANES - shifts[n]) % LANES
                for ch in range(chunks):
                    rows = slice(ch * crows, (ch + 1) * crows)
                    low_rows = slice(width + ch * crows, width + (ch + 1) * crows)
                    turned = []
                    for start in starts[n]:
                        both = ext_ref[ch * chunk : (ch + 1) * chunk, :, pl.ds(start, LANES)]
                        both = both.astype(jnp.float32)
                        turned.append(
                            [
                                pltpu.roll(
                                    both[:, c * GROUP : (c + 1) * GROUP].reshape(crows, LANES),
                                    back_shift,
                                    1,
                                )
                                for c in range(2)
                            ]
                        )
                    for m in range(wide):
                        lanes = slice(m * LANES, (m + 1) * LANES)
                        put = slice(n * width + m * LANES, n * width + (m + 1) * LANES)
                        patch_re = jnp.where(keep, turned[m][0], turned[m + 1][0])
                        patch_im = jnp.where(keep, turned[m][1], turned[m + 1][1])
                        probe_re = probe_ref[0, rows, lanes].astype(jnp.float32)
                        probe_im = probe_ref[1, rows, lanes].astype(jnp.float32)
                        wave_re = probe_re * patch_re - probe_im * patch_im
                        wave_im = probe_re * patch_im + probe_im * patch_re
                        wave_ref[rows, put] = wave_re.astype(jnp.bfloat16)
                        wave_ref[low_rows, put] = wave_im.astype(jnp.bfloat16)
                mine = slice(n * width, (n + 1) * width)
                half = product(forward_ref[...], wave_ref[:, mine]).astype(jnp.bfloat16)
                half_ref[mine, :width] = half[:width]
                half_ref[mine, width:] = half[width:]
            for n in range(2):
                mine = slice(n * width, (n + 1) * width)
                far = product(half_ref[mine, :], inverse_ref[...])
                for ch in range(chunks):
                    rows = slice(ch * crows, (ch + 1) * crows)
                    low_rows = slice(width + ch * crows, width + (ch + 1) * crows)
                    far_re, far_im = far[rows, :width], far[rows, width:]
                    power = far_re * far_re + far_im * far_im
                    amps = amp_ref[step * 2 + n, rows, :].astype(jnp.float32)
                    factor = amps * lax.rsqrt(jnp.maximum(power, 1.0)) - 1.0
                    delta_ref[rows, mine] = (far_re * factor).astype(jnp.bfloat16)
                    delta_ref[low_rows, mine] = (far_im * factor).astype(jnp.bfloat16)
                back = product(inverse_ref[...], delta_ref[:, mine]).astype(jnp.bfloat16)
                back_ref[mine, :width] = back[:width]
                back_ref[mine, width:] = back[width:]
            for n in range(2):
                mine = slice(n * width, (n + 1) * width)
                near = product(back_ref[mine, :], forward_ref[...])
                past = lane_id >= shifts[n]
                for ch in range(chunks):
                    rows = slice(ch * crows, (ch + 1) * crows)
                    turned = []
                    for m in range(wide):
                        lanes = slice(m * LANES, (m + 1) * LANES)
                        probe_re = probe_ref[0, rows, lanes].astype(jnp.float32) * lives[n]
                        probe_im = probe_ref[1, rows, lanes].astype(jnp.float32) * lives[n]
                        near_re = near[rows, m * LANES : (m + 1) * LANES]
                        near_im = near[rows, width + m * LANES : width + (m + 1) * LANES]
                        turned.append(
                            [
                                pltpu.roll(probe_re * near_re + probe_im * near_im, shifts[n], 1),
                                pltpu.roll(probe_re * near_im - probe_im * near_re, shifts[n], 1),
                            ]
                        )
                    for m in range(wide + 1):
                        for c in range(2):
                            behind = turned[m - 1][c] if m > 0 else 0.0
                            ahead = turned[m][c] if m < wide else 0.0
                            here = (c, rows, pl.ds(starts[n][m], LANES))
                            acc_ref[here] += jnp.where(past, ahead, behind)


def exit_first_kernel(tiles, meta_ref, probe_ref, forward_ref, inverse_ref, sino_ref, *refs):
    amp_refs, refs = refs[:tiles], refs[tiles:]
    partial_ref, grad_ref, spill_ref, acc_ref, *scratch = refs
    groups = sino_ref.shape[0]
    width = probe_ref.shape[1]
    done = sino_ref.shape[2] - width

    @pl.loop(0, groups)
    def _(g):
        rows = pl.ds(pl.multiple_of(g * GROUP, GROUP), GROUP)
        for c in range(2):
            acc_ref[c, rows, :] = jnp.zeros((GROUP, acc_ref.shape[2]), jnp.float32)

    add_slots(
        meta_ref, probe_ref, forward_ref, inverse_ref, sino_ref, acc_ref, amp_refs, scratch, 0
    )

    @pl.loop(0, groups)
    def _(g):
        rows = pl.ds(pl.multiple_of(g * GROUP, GROUP), GROUP)
        whole = [acc_ref[c, rows, width:done] for c in range(2)]
        grad_ref[g] = jnp.concatenate(whole, axis=0).astype(jnp.bfloat16)
        for c in range(2):
            partial_ref[c, rows, :] = acc_ref[c, rows, :width]
            spill_ref[c, rows, :] = acc_ref[c, rows, done:]


def exit_rest_kernel(
    tiles, meta_ref, probe_ref, forward_ref, inverse_ref, early_ref, late_ref, partial_ref, spill_ref, *refs
):
    amp_refs, refs = refs[:tiles], refs[tiles:]
    out_ref, ext_ref, acc_ref, *scratch = refs
    groups = early_ref.shape[0]
    width = probe_ref.shape[1]
    done = width + late_ref.shape[2]

    @pl.loop(0, groups)
    def _(g):
        ext_ref[g, :, :width] = early_ref[g, :, early_ref.shape[2] - width :]
        ext_ref[g, :, width:done] = late_ref[g]
        ext_ref[g, :, done:] = early_ref[g, :, :width]
        rows = pl.ds(pl.multiple_of(g * GROUP, GROUP), GROUP)
        for c in range(2):
            acc_ref[c, rows, :width] = spill_ref[c, rows, :]
            acc_ref[c, rows, width:] = jnp.zeros((GROUP, done), jnp.float32)

    add_slots(
        meta_ref, probe_ref, forward_ref, inverse_ref, ext_ref, acc_ref, amp_refs, scratch,
        lax.axis_size("pos") - tiles,
    )

    @pl.loop(0, groups)
    def _(g):
        rows = pl.ds(pl.multiple_of(g * GROUP, GROUP), GROUP)
        here = [acc_ref[c, rows, :done] for c in range(2)]
        wrapped = [acc_ref[c, rows, done:] + partial_ref[c, rows, :] for c in range(2)]
        out_ref[g, :, :done] = jnp.concatenate(here, axis=0).astype(jnp.bfloat16)
        out_ref[g, :, done:] = jnp.concatenate(wrapped, axis=0).astype(jnp.bfloat16)


def exit_scratch(groups, width, reach):
    return [pltpu.VMEM((2, groups * GROUP, reach), jnp.float32)] + [
        pltpu.VMEM((2 * width, 2 * width), jnp.bfloat16)
    ] * 4


def exit_first(meta, probe_field, tables, sino, amps):
    groups, rows, reach = sino.shape
    width = probe_field.shape[1]
    slices = groups * GROUP
    edge = jax.ShapeDtypeStruct((2, slices, width), jnp.float32)
    grad = jax.ShapeDtypeStruct((groups, rows, reach - 2 * width), jnp.bfloat16)
    return pl.pallas_call(
        functools.partial(exit_first_kernel, len(amps)),
        out_shape=[edge, grad, edge],
        in_specs=[scalars] + [everywhere] * (4 + len(amps)),
        out_specs=[everywhere] * 3,
        scratch_shapes=exit_scratch(groups, width, reach),
        compiler_params=pltpu.CompilerParams(vmem_limit_bytes=28 * MEBI),
        cost_estimate=guess(10),
        name="exit_first",
    )(meta, probe_field, *tables, sino, *amps)


def exit_rest(meta, probe_field, tables, early, late, partial, spill, amps):
    groups, rows = late.shape[:2]
    width = probe_field.shape[1]
    reach = late.shape[2] + 2 * width
    return pl.pallas_call(
        functools.partial(exit_rest_kernel, len(amps)),
        out_shape=jax.ShapeDtypeStruct((groups, rows, reach), jnp.bfloat16),
        in_specs=[scalars] + [everywhere] * (7 + len(amps)),
        out_specs=everywhere,
        scratch_shapes=[pltpu.VMEM((groups, rows, reach), jnp.bfloat16)]
        + exit_scratch(groups, width, reach),
        compiler_params=pltpu.CompilerParams(vmem_limit_bytes=30 * MEBI),
        cost_estimate=guess(10),
        name="exit_rest",
    )(meta, probe_field, *tables, early, late, partial, spill, *amps)


def to_groups(received, own_slices):
    if own_slices == GROUP:
        return received
    devices, rows, columns = received.shape
    merge = GROUP // own_slices
    split = received.reshape(devices // merge, merge, 2, own_slices, columns)
    return split.transpose(0, 2, 1, 3, 4).reshape(devices // merge, ROWS, columns)


def from_groups(grouped, own_slices):
    if own_slices == GROUP:
        return grouped
    groups, rows, columns = grouped.shape
    merge = GROUP // own_slices
    split = grouped.reshape(groups, 2, merge, own_slices, columns)
    return split.transpose(0, 2, 1, 3, 4).reshape(groups * merge, 2 * own_slices, columns)


def pad_rows(block, own_slices):
    if own_slices == GROUP:
        return block
    lead, columns = block.shape[:-2], block.shape[-1]
    split = block.reshape(lead + (2, own_slices, columns))
    more = [(0, 0)] * (split.ndim - 2) + [(0, GROUP - own_slices), (0, 0)]
    return jnp.pad(split, more).reshape(lead + (ROWS, columns))


def cut_rows(block, own_slices):
    if own_slices == GROUP:
        return block
    lead, columns = block.shape[:-2], block.shape[-1]
    split = block.reshape(lead + (2, GROUP, columns))[..., :own_slices, :]
    return split.reshape(lead + (2 * own_slices, columns))


def everyone(chunk):
    return lax.all_to_all(chunk, ("ang", "pos"), 0, 0, tiled=True)


def on_device(volume, radon_tiles, tile_blocks, probe_field, amplitudes, offsets, counts):
    n_pos = lax.axis_size("pos")
    pos = lax.axis_index("pos")
    angles, det_blocks, feeds = tile_blocks.shape
    block_size = radon_tiles.shape[1]
    columns = det_blocks * block_size
    tile_width = columns // n_pos
    slab = volume.shape[1]
    width = volume.shape[2]
    own = slab // n_pos
    rows = 2 * own
    blocks_each = width // block_size

    def slices_for(j):
        start = (pos + j) % n_pos * own
        return lax.dynamic_slice_in_dim(volume, start, own, 1).reshape(rows, width)

    vol_pieces = rotate_pos([slices_for(j) for j in range(n_pos)], 1)
    meta = jnp.concatenate([offsets, counts], axis=1)
    meta = rotate_pos(
        [lax.dynamic_slice_in_dim(meta, (pos - j) % n_pos, 1, 0) for j in range(n_pos)], -1
    )
    meta = jnp.concatenate(meta, axis=0)
    vol_pieces, amplitudes = lax.optimization_barrier((vol_pieces, amplitudes))
    amp_pieces = rotate_pos(
        [
            lax.dynamic_index_in_dim(amplitudes, (pos - j) % n_pos, 0, keepdims=False)
            for j in range(n_pos)
        ],
        -1,
    )

    owner = tile_blocks // blocks_each
    within = tile_blocks % blocks_each
    piece = (pos - owner) % n_pos
    crossed = (within + jnp.arange(feeds, dtype=jnp.int32)) % 2
    tiles_each = width // LANES

    def by_chunk(idx):
        idx = idx.reshape(angles // n_pos, n_pos, n_pos, det_blocks // n_pos * feeds)
        idx = jnp.stack([jnp.roll(idx[:, p], -p, axis=1) for p in range(n_pos)], axis=1)
        return idx.reshape(angles, det_blocks * feeds)

    tile_idx = by_chunk(crossed * (n_pos * tiles_each) + piece * tiles_each + within // 2)
    block_idx = by_chunk(piece * blocks_each + within)
    padded = [pad_rows(piece, own) for piece in vol_pieces]
    probe_width = probe_field.shape[1]
    tables = dft_tables(probe_width)
    half = n_pos // 2
    reach = (half * tile_width + probe_width) // block_size
    edge = probe_width // block_size
    early_blocks = list(range(reach))
    late_blocks = list(range(reach, det_blocks))
    first_blocks = list(range(edge, half * tile_width // block_size))
    rest_blocks = list(range(half * tile_width // block_size, det_blocks)) + list(range(edge))

    sino_early = project(tile_idx, radon_tiles, padded, early_blocks, "project_early")
    sino_early, padded = lax.optimization_barrier((sino_early, padded))
    sino_late = project(tile_idx, radon_tiles, padded, late_blocks, "project_late")
    got_early = everyone(cut_rows(sino_early, own))
    got_early, sino_late = lax.optimization_barrier((got_early, sino_late))
    got_late = everyone(cut_rows(sino_late, own))
    got_early, got_late = to_groups(got_early, own), to_groups(got_late, own)
    partial, first_grad, spill = exit_first(meta, probe_field, tables, got_early, amp_pieces[:half])
    first_sent, got_late = lax.optimization_barrier((first_grad, got_late))
    rest_grad = exit_rest(
        meta, probe_field, tables, got_early, got_late, partial, spill, amp_pieces[half:]
    )
    back_first = everyone(from_groups(first_sent, own))
    back_first, rest_sent = lax.optimization_barrier((back_first, rest_grad))
    back_rest = everyone(from_groups(rest_sent, own))
    first_sum = back_project(
        block_idx, radon_tiles, pad_rows(back_first, own), first_blocks, None, n_pos, width, "back_first"
    )[0]
    wrapped = rest_grad.shape[2] - probe_width
    tile_pieces = [jnp.concatenate([rest_grad[:, :, wrapped:], first_grad[:, :, : tile_width - probe_width]], axis=2)]
    for j in range(1, n_pos):
        source, begin = (first_grad, j * tile_width - probe_width) if j < half else (rest_grad, (j - half) * tile_width)
        tile_pieces.append(source[:, :, begin : begin + tile_width])
    tile_pieces = rotate_pos(tile_pieces, 1)
    obj_pieces = back_project(
        block_idx, radon_tiles, pad_rows(back_rest, own), rest_blocks, first_sum, n_pos, width, "back_rest"
    )
    groups = rest_grad.shape[0]
    tile_pieces = [tile_pieces[-j % n_pos] for j in range(n_pos)]
    tile_pieces = [
        piece.reshape(groups, 2, GROUP, tile_width).transpose(1, 0, 2, 3).reshape(2, groups * GROUP, tile_width)
        for piece in tile_pieces
    ]
    proj_grad = jnp.stack(in_order(tile_pieces, -pos % n_pos), axis=2).astype(jnp.float32)
    obj_pieces = rotate_pos([cut_rows(piece, own) for piece in obj_pieces], -1)
    obj_pieces = [piece.reshape(2, own, width) for piece in in_order(obj_pieces, -pos % n_pos)]
    object_grad = jnp.concatenate(obj_pieces, axis=1).astype(jnp.float32)
    new_volume = volume.astype(jnp.float32) + step_size * object_grad
    return (new_volume, proj_grad)


def solution(mesh):
    in_specs = (
        P(None, "ang", "pos"),
        P(),
        P(),
        P(),
        P("ang", "pos", None, None),
        P("ang", "pos"),
        P("ang", "pos"),
    )
    out_specs = (P(None, "ang", "pos"), P(None, None, "ang", "pos"))
    return jax.shard_map(
        on_device, mesh=mesh, in_specs=in_specs, out_specs=out_specs, check_vma=False
    )
```

```python
import functools
import math

import jax
import jax.numpy as jnp
import numpy as np
from jax import lax
from jax.experimental import pallas as pl
from jax.experimental.pallas import tpu as pltpu
from jax.sharding import PartitionSpec as P

step_size = 0.1
LANES = 128
ROWS = 16
GROUP = 8
MEBI = 1024 * 1024
everywhere = pl.BlockSpec(memory_space=pltpu.VMEM)
scalars = pl.BlockSpec(memory_space=pltpu.SMEM)
CHAINS = 4
BATCH = 4


def dft_tables(width):
    index = np.arange(width)
    turn = 2.0 * math.pi / width * (index[:, None] * index[None, :] % width)
    cosine = jnp.asarray(np.cos(turn) / math.sqrt(width), jnp.bfloat16)
    sine_neg = jnp.asarray(-np.sin(turn) / math.sqrt(width), jnp.bfloat16)
    forward = jnp.block([[cosine, -sine_neg], [sine_neg, cosine]])
    inverse = jnp.block([[cosine, sine_neg], [-sine_neg, cosine]])
    return (forward, inverse)


def rotate_pos(pieces, sign):
    count = len(pieces)
    return [pieces[0]] + [
        lax.ppermute(pieces[j], "pos", [(i, (i + sign * j) % count) for i in range(count)])
        for j in range(1, count)
    ]


def in_order(pieces, first):
    count = len(pieces)
    bit = 1
    while bit < count:
        flip = (first & bit) != 0
        pieces = [jnp.where(flip, pieces[(k + bit) % count], pieces[k]) for k in range(count)]
        bit *= 2
    return pieces


def lower_half(shape):
    return lax.broadcasted_iota(jnp.int32, shape, len(shape) - 1) < LANES // 2


def swap_halves(tile):
    return pltpu.roll(tile, LANES // 2, 1)


def arrange(vol_refs, vv_ref):
    per_piece = vol_refs[0].shape[1] // LANES
    tiles = per_piece * len(vol_refs)
    batch = 16
    source = lax.broadcasted_iota(jnp.int32, (LANES, LANES), 0)
    target = lax.broadcasted_iota(jnp.int32, (LANES, LANES), 1)
    swap = ((source + LANES // 2) % LANES == target).astype(jnp.bfloat16)
    for k, vol_ref in enumerate(vol_refs):

        @pl.loop(0, per_piece // batch, unroll=2)
        def _(step):
            stack = []
            for i in range(batch):
                t = step * batch + i
                tile = vol_ref[:, pl.ds(pl.multiple_of(t * LANES, LANES), LANES)]
                vv_ref[k * per_piece + t] = tile
                stack.append(tile)
            swapped = jnp.dot(
                jnp.concatenate(stack, axis=0), swap, preferred_element_type=jnp.float32
            ).astype(jnp.bfloat16)
            for i in range(batch):
                t = step * batch + i
                vv_ref[tiles + k * per_piece + t] = swapped[i * ROWS : (i + 1) * ROWS]


def project_blocks(blocks, idx_ref, radon_ref, vv_ref, out_ref, lhs_refs):
    angles, block, span = radon_ref.shape
    feeds = span // block
    low = lower_half((ROWS, LANES))
    batch = lhs_refs[0].shape[0]

    def gather(start, lhs_ref):
        for n in range(batch):
            a = start + n
            for i, b in enumerate(blocks):
                row = i * ROWS
                for jp in range(feeds // 2):
                    at = b * feeds + 2 * jp
                    first = vv_ref[idx_ref[a, at]]
                    second = vv_ref[idx_ref[a, at + 1]]
                    lhs_ref[n, row : row + ROWS, jp * LANES : (jp + 1) * LANES] = jnp.where(
                        low, first, second
                    )

    def multiply(start, lhs_ref):
        for n in range(batch):
            a = start + n
            product = lax.dot_general(
                lhs_ref[n], radon_ref[a], (((1,), (1,)), ((), ())), preferred_element_type=jnp.float32
            )
            for pair in range(len(blocks) // 2):
                row = 2 * pair * ROWS
                tile = jnp.concatenate(
                    [product[row : row + ROWS], product[row + ROWS : row + 2 * ROWS]], axis=1
                )
                out_ref[a, :, pair * LANES : (pair + 1) * LANES] = tile.astype(jnp.bfloat16)

    gather(0, lhs_refs[0])

    @pl.loop(0, angles // (2 * batch))
    def _(step):
        start = step * 2 * batch
        multiply(start, lhs_refs[0])
        gather(start + batch, lhs_refs[1])
        multiply(start + batch, lhs_refs[1])
        gather(jnp.minimum(start + 2 * batch, angles - batch), lhs_refs[0])


def project_kernel(blocks, pieces, idx_ref, radon_ref, *refs):
    vol_refs = refs[:pieces]
    out_ref, vv_ref, *lhs_refs = refs[pieces:]
    arrange(vol_refs, vv_ref)
    project_blocks(blocks, idx_ref, radon_ref, vv_ref, out_ref, lhs_refs)


def guess(microseconds):
    return pl.CostEstimate(
        flops=int(microseconds * 1.15e9), bytes_accessed=int(microseconds * 1e5), transcendentals=0
    )


def project(idx, radon_tiles, vol_pieces, blocks, name):
    angles, block, span = radon_tiles.shape
    pieces = len(vol_pieces)
    tiles = pieces * vol_pieces[0].shape[1] // LANES
    out_shape = (angles, ROWS, len(blocks) * block)
    return pl.pallas_call(
        functools.partial(project_kernel, blocks, pieces),
        out_shape=jax.ShapeDtypeStruct(out_shape, jnp.bfloat16),
        in_specs=[scalars, everywhere] + [everywhere] * pieces,
        out_specs=everywhere,
        scratch_shapes=[pltpu.VMEM((2 * tiles, ROWS, LANES), jnp.bfloat16)]
        + [pltpu.VMEM((BATCH, len(blocks) * ROWS, span), jnp.bfloat16)] * 2,
        compiler_params=pltpu.CompilerParams(
            vmem_limit_bytes=14 * MEBI + 2 * radon_tiles.size + 2 * math.prod(out_shape)
        ),
        cost_estimate=guess(4 + len(blocks) // 4),
        name=name,
    )(idx, radon_tiles, *vol_pieces)


def back_project_kernel(blocks, has_start, outs, idx_ref, radon_ref, grad_ref, *refs):
    start_ref, refs = (refs[0], refs[1:]) if has_start else (None, refs)
    out_refs, refs = refs[:outs], refs[outs:]
    acc_refs, (w_ref, *contrib_refs) = refs[:CHAINS], refs[CHAINS:]
    if has_start:
        contrib_refs, start_sem = contrib_refs[:-1], contrib_refs[-1]
        start_copy = pltpu.make_async_copy(start_ref, acc_refs[0], start_sem)
        start_copy.start()
    angles, block, span = radon_ref.shape
    pairs = len(blocks) // 2
    feeds = span // block
    coef_blocks = acc_refs[0].shape[0]

    @pl.loop(0, coef_blocks, unroll=16)
    def _(t):
        for acc_ref in acc_refs[1:] if has_start else acc_refs:
            acc_ref[t] = jnp.zeros((GROUP, LANES), jnp.float32)

    low = lower_half((GROUP, LANES))
    low_rows = lower_half((block, LANES))
    w_ref[...] = jnp.zeros_like(w_ref)

    def widen(slot, a):
        for jp in range(feeds // 2):
            tile = radon_ref[a, :, jp * LANES : (jp + 1) * LANES].astype(jnp.float32)
            turned = swap_halves(tile)
            for side, (first, second) in enumerate(((tile, turned), (turned, tile))):
                lanes = slice((2 * jp + side) * LANES, (2 * jp + side + 1) * LANES)
                w_ref[slot, :block, lanes] = jnp.where(low_rows, first, 0.0).astype(jnp.bfloat16)
                w_ref[slot, block:, lanes] = jnp.where(low_rows, 0.0, second).astype(jnp.bfloat16)

    def multiply(start, half, contrib_ref):
        for n in range(CHAINS):
            a = start + n
            widen(half * CHAINS + n, a)
            lhs = []
            for pair in range(pairs):
                tile = grad_ref[a, :, pair * LANES : (pair + 1) * LANES].astype(jnp.float32)
                real, imag = tile[:GROUP], tile[GROUP:]
                even = jnp.where(low, real, swap_halves(imag))
                odd = jnp.where(low, swap_halves(real), imag)
                lhs.append(jnp.concatenate([even, odd], axis=0).astype(jnp.bfloat16))
            contrib_ref[n] = jnp.dot(
                jnp.concatenate(lhs, axis=0),
                w_ref[half * CHAINS + n],
                preferred_element_type=jnp.float32,
            )

    def scatter(start, contrib_ref):
        for i, b in enumerate(blocks):
            row = i * GROUP
            for j in range(feeds):
                for n in range(CHAINS):
                    tile = contrib_ref[n, row : row + GROUP, j * LANES : (j + 1) * LANES]
                    acc_refs[n][idx_ref[start + n, b * feeds + j]] += tile

    multiply(0, 0, contrib_refs[0])
    if has_start:
        start_copy.wait()

    @pl.loop(0, angles // (2 * CHAINS))
    def _(step):
        start = step * 2 * CHAINS
        multiply(start + CHAINS, 1, contrib_refs[1])
        scatter(start, contrib_refs[0])
        multiply(jnp.minimum(start + 2 * CHAINS, angles - CHAINS), 0, contrib_refs[0])
        scatter(start + CHAINS, contrib_refs[1])

    def total(t):
        sums = [acc_ref[t] for acc_ref in acc_refs]
        while len(sums) > 1:
            sums = [sums[i] + sums[i + 1] for i in range(0, len(sums), 2)]
        return sums[0]

    if outs == 1:

        @pl.loop(0, coef_blocks, unroll=16)
        def _(t):
            out_refs[0][t] = total(t)

    else:
        per_piece = out_refs[0].shape[1] // LANES
        for k, out_ref in enumerate(out_refs):

            @pl.loop(0, per_piece, unroll=16)
            def _(t):
                lanes = pl.ds(pl.multiple_of(t * LANES, LANES), LANES)
                even = total(2 * (k * per_piece + t))
                odd = total(2 * (k * per_piece + t) + 1)
                real = jnp.where(low, even, swap_halves(odd))
                imag = jnp.where(low, swap_halves(even), odd)
                out_ref[:, lanes] = jnp.concatenate([real, imag], axis=0).astype(out_ref.dtype)


def back_project(idx, radon_tiles, grads, blocks, start, pieces, piece_width, name):
    angles, block, span = radon_tiles.shape
    coef_blocks = pieces * piece_width // block
    rows = len(blocks) * GROUP
    has_start = start is not None
    if has_start:
        out_shape = [jax.ShapeDtypeStruct((ROWS, piece_width), jnp.bfloat16)] * pieces
    else:
        out_shape = [jax.ShapeDtypeStruct((coef_blocks, GROUP, LANES), jnp.float32)]
    operands = [idx, radon_tiles, grads] + ([start] if has_start else [])
    return pl.pallas_call(
        functools.partial(back_project_kernel, blocks, has_start, len(out_shape)),
        out_shape=out_shape,
        in_specs=[scalars] + [everywhere] * 2 + [pl.BlockSpec(memory_space=pl.ANY)] * has_start,
        out_specs=[everywhere] * len(out_shape),
        scratch_shapes=[pltpu.VMEM((coef_blocks, GROUP, LANES), jnp.float32)] * CHAINS
        + [pltpu.VMEM((2 * CHAINS, 2 * block, 2 * span), jnp.bfloat16)]
        + [pltpu.VMEM((CHAINS, rows, 2 * span), jnp.float32)] * 2
        + [pltpu.SemaphoreType.DMA] * has_start,
        compiler_params=pltpu.CompilerParams(vmem_limit_bytes=60 * MEBI),
        cost_estimate=guess(4 + len(blocks) // 4),
        name=name,
    )(*operands)


def add_slots(meta_ref, probe_ref, forward_ref, inverse_ref, ext_ref, acc_ref, amp_refs, scratch, first):
    wave_ref, half_ref, delta_ref, back_ref = scratch
    n_pos = lax.axis_size("pos")
    groups = ext_ref.shape[0]
    width = probe_ref.shape[1]
    slots = amp_refs[0].shape[0]
    tile_width = (acc_ref.shape[2] - width) // len(amp_refs)
    chunk = 4
    crows = chunk * GROUP
    chunks = groups // chunk
    wide = width // LANES
    lane_id = lax.broadcasted_iota(jnp.int32, (crows, LANES), 1)

    def product(left, right):
        return jnp.dot(left, right, preferred_element_type=jnp.float32)

    for tile, amp_ref in enumerate(amp_refs):
        order = first + tile
        tile_start = lax.rem(lax.axis_index("pos") + order, n_pos) * tile_width - tile * tile_width
        count = meta_ref[order, slots]

        @pl.loop(0, (count + 1) // 2)
        def _(step):
            shifts, starts, lives = [], [], []
            for n in range(2):
                offset = meta_ref[order, step * 2 + n] - tile_start
                shifts.append(offset % LANES)
                lane_tile = offset // LANES
                starts.append(
                    [pl.multiple_of((lane_tile + m) * LANES, LANES) for m in range(wide + 1)]
                )
                lives.append((step * 2 + n < count).astype(jnp.float32))
            for n in range(2):
                keep = lane_id < LANES - shifts[n]
                back_shift = (LANES - shifts[n]) % LANES
                for ch in range(chunks):
                    rows = slice(ch * crows, (ch + 1) * crows)
                    low_rows = slice(width + ch * crows, width + (ch + 1) * crows)
                    turned = []
                    for start in starts[n]:
                        both = ext_ref[ch * chunk : (ch + 1) * chunk, :, pl.ds(start, LANES)]
                        both = both.astype(jnp.float32)
                        turned.append(
                            [
                                pltpu.roll(
                                    both[:, c * GROUP : (c + 1) * GROUP].reshape(crows, LANES),
                                    back_shift,
                                    1,
                                )
                                for c in range(2)
                            ]
                        )
                    for m in range(wide):
                        lanes = slice(m * LANES, (m + 1) * LANES)
                        put = slice(n * width + m * LANES, n * width + (m + 1) * LANES)
                        patch_re = jnp.where(keep, turned[m][0], turned[m + 1][0])
                        patch_im = jnp.where(keep, turned[m][1], turned[m + 1][1])
                        probe_re = probe_ref[0, rows, lanes].astype(jnp.float32)
                        probe_im = probe_ref[1, rows, lanes].astype(jnp.float32)
                        wave_re = probe_re * patch_re - probe_im * patch_im
                        wave_im = probe_re * patch_im + probe_im * patch_re
                        wave_ref[rows, put] = wave_re.astype(jnp.bfloat16)
                        wave_ref[low_rows, put] = wave_im.astype(jnp.bfloat16)
                mine = slice(n * width, (n + 1) * width)
                half = product(forward_ref[...], wave_ref[:, mine]).astype(jnp.bfloat16)
                half_ref[mine, :width] = half[:width]
                half_ref[mine, width:] = half[width:]
            for n in range(2):
                mine = slice(n * width, (n + 1) * width)
                far = product(half_ref[mine, :], inverse_ref[...])
                for ch in range(chunks):
                    rows = slice(ch * crows, (ch + 1) * crows)
                    low_rows = slice(width + ch * crows, width + (ch + 1) * crows)
                    far_re, far_im = far[rows, :width], far[rows, width:]
                    power = far_re * far_re + far_im * far_im
                    amps = amp_ref[step * 2 + n, rows, :].astype(jnp.float32)
                    factor = amps * lax.rsqrt(jnp.maximum(power, 1.0)) - 1.0
                    delta_ref[rows, mine] = (far_re * factor).astype(jnp.bfloat16)
                    delta_ref[low_rows, mine] = (far_im * factor).astype(jnp.bfloat16)
                back = product(inverse_ref[...], delta_ref[:, mine]).astype(jnp.bfloat16)
                back_ref[mine, :width] = back[:width]
                back_ref[mine, width:] = back[width:]
            for n in range(2):
                mine = slice(n * width, (n + 1) * width)
                near = product(back_ref[mine, :], forward_ref[...])
                past = lane_id >= shifts[n]
                for ch in range(chunks):
                    rows = slice(ch * crows, (ch + 1) * crows)
                    turned = []
                    for m in range(wide):
                        lanes = slice(m * LANES, (m + 1) * LANES)
                        probe_re = probe_ref[0, rows, lanes].astype(jnp.float32) * lives[n]
                        probe_im = probe_ref[1, rows, lanes].astype(jnp.float32) * lives[n]
                        near_re = near[rows, m * LANES : (m + 1) * LANES]
                        near_im = near[rows, width + m * LANES : width + (m + 1) * LANES]
                        turned.append(
                            [
                                pltpu.roll(probe_re * near_re + probe_im * near_im, shifts[n], 1),
                                pltpu.roll(probe_re * near_im - probe_im * near_re, shifts[n], 1),
                            ]
                        )
                    for m in range(wide + 1):
                        for c in range(2):
                            behind = turned[m - 1][c] if m > 0 else 0.0
                            ahead = turned[m][c] if m < wide else 0.0
                            here = (c, rows, pl.ds(starts[n][m], LANES))
                            acc_ref[here] += jnp.where(past, ahead, behind)


def exit_first_kernel(tiles, meta_ref, probe_ref, forward_ref, inverse_ref, sino_ref, *refs):
    amp_refs, refs = refs[:tiles], refs[tiles:]
    partial_ref, grad_ref, spill_ref, acc_ref, *scratch = refs
    groups = sino_ref.shape[0]
    width = probe_ref.shape[1]
    done = sino_ref.shape[2] - width

    @pl.loop(0, groups)
    def _(g):
        rows = pl.ds(pl.multiple_of(g * GROUP, GROUP), GROUP)
        for c in range(2):
            acc_ref[c, rows, :] = jnp.zeros((GROUP, acc_ref.shape[2]), jnp.float32)

    add_slots(
        meta_ref, probe_ref, forward_ref, inverse_ref, sino_ref, acc_ref, amp_refs, scratch, 0
    )

    @pl.loop(0, groups)
    def _(g):
        rows = pl.ds(pl.multiple_of(g * GROUP, GROUP), GROUP)
        whole = [acc_ref[c, rows, width:done] for c in range(2)]
        grad_ref[g] = jnp.concatenate(whole, axis=0).astype(jnp.bfloat16)
        for c in range(2):
            partial_ref[c, rows, :] = acc_ref[c, rows, :width]
            spill_ref[c, rows, :] = acc_ref[c, rows, done:]


def exit_rest_kernel(
    tiles, meta_ref, probe_ref, forward_ref, inverse_ref, early_ref, late_ref, partial_ref, spill_ref, *refs
):
    amp_refs, refs = refs[:tiles], refs[tiles:]
    out_ref, ext_ref, acc_ref, *scratch = refs
    groups = early_ref.shape[0]
    width = probe_ref.shape[1]
    done = width + late_ref.shape[2]

    @pl.loop(0, groups)
    def _(g):
        ext_ref[g, :, :width] = early_ref[g, :, early_ref.shape[2] - width :]
        ext_ref[g, :, width:done] = late_ref[g]
        ext_ref[g, :, done:] = early_ref[g, :, :width]
        rows = pl.ds(pl.multiple_of(g * GROUP, GROUP), GROUP)
        for c in range(2):
            acc_ref[c, rows, :width] = spill_ref[c, rows, :]
            acc_ref[c, rows, width:] = jnp.zeros((GROUP, done), jnp.float32)

    add_slots(
        meta_ref, probe_ref, forward_ref, inverse_ref, ext_ref, acc_ref, amp_refs, scratch,
        lax.axis_size("pos") - tiles,
    )

    @pl.loop(0, groups)
    def _(g):
        rows = pl.ds(pl.multiple_of(g * GROUP, GROUP), GROUP)
        here = [acc_ref[c, rows, :done] for c in range(2)]
        wrapped = [acc_ref[c, rows, done:] + partial_ref[c, rows, :] for c in range(2)]
        out_ref[g, :, :done] = jnp.concatenate(here, axis=0).astype(jnp.bfloat16)
        out_ref[g, :, done:] = jnp.concatenate(wrapped, axis=0).astype(jnp.bfloat16)


def exit_scratch(groups, width, reach):
    return [pltpu.VMEM((2, groups * GROUP, reach), jnp.float32)] + [
        pltpu.VMEM((2 * width, 2 * width), jnp.bfloat16)
    ] * 4


def exit_first(meta, probe_field, tables, sino, amps):
    groups, rows, reach = sino.shape
    width = probe_field.shape[1]
    slices = groups * GROUP
    edge = jax.ShapeDtypeStruct((2, slices, width), jnp.float32)
    grad = jax.ShapeDtypeStruct((groups, rows, reach - 2 * width), jnp.bfloat16)
    return pl.pallas_call(
        functools.partial(exit_first_kernel, len(amps)),
        out_shape=[edge, grad, edge],
        in_specs=[scalars] + [everywhere] * (4 + len(amps)),
        out_specs=[everywhere] * 3,
        scratch_shapes=exit_scratch(groups, width, reach),
        compiler_params=pltpu.CompilerParams(vmem_limit_bytes=60 * MEBI),
        cost_estimate=guess(10),
        name="exit_first",
    )(meta, probe_field, *tables, sino, *amps)


def exit_rest(meta, probe_field, tables, early, late, partial, spill, amps):
    groups, rows = late.shape[:2]
    width = probe_field.shape[1]
    reach = late.shape[2] + 2 * width
    return pl.pallas_call(
        functools.partial(exit_rest_kernel, len(amps)),
        out_shape=jax.ShapeDtypeStruct((groups, rows, reach), jnp.bfloat16),
        in_specs=[scalars] + [everywhere] * (7 + len(amps)),
        out_specs=everywhere,
        scratch_shapes=[pltpu.VMEM((groups, rows, reach), jnp.bfloat16)]
        + exit_scratch(groups, width, reach),
        compiler_params=pltpu.CompilerParams(vmem_limit_bytes=60 * MEBI),
        cost_estimate=guess(10),
        name="exit_rest",
    )(meta, probe_field, *tables, early, late, partial, spill, *amps)


def to_groups(received, own_slices):
    if own_slices == GROUP:
        return received
    devices, rows, columns = received.shape
    merge = GROUP // own_slices
    split = received.reshape(devices // merge, merge, 2, own_slices, columns)
    return split.transpose(0, 2, 1, 3, 4).reshape(devices // merge, ROWS, columns)


def from_groups(grouped, own_slices):
    if own_slices == GROUP:
        return grouped
    groups, rows, columns = grouped.shape
    merge = GROUP // own_slices
    split = grouped.reshape(groups, 2, merge, own_slices, columns)
    return split.transpose(0, 2, 1, 3, 4).reshape(groups * merge, 2 * own_slices, columns)


def pad_rows(block, own_slices):
    if own_slices == GROUP:
        return block
    lead, columns = block.shape[:-2], block.shape[-1]
    split = block.reshape(lead + (2, own_slices, columns))
    more = [(0, 0)] * (split.ndim - 2) + [(0, GROUP - own_slices), (0, 0)]
    return jnp.pad(split, more).reshape(lead + (ROWS, columns))


def cut_rows(block, own_slices):
    if own_slices == GROUP:
        return block
    lead, columns = block.shape[:-2], block.shape[-1]
    split = block.reshape(lead + (2, GROUP, columns))[..., :own_slices, :]
    return split.reshape(lead + (2 * own_slices, columns))


def everyone(chunk):
    return lax.all_to_all(chunk, ("ang", "pos"), 0, 0, tiled=True)


def on_device(volume, radon_tiles, tile_blocks, probe_field, amplitudes, offsets, counts):
    n_pos = lax.axis_size("pos")
    pos = lax.axis_index("pos")
    angles, det_blocks, feeds = tile_blocks.shape
    block_size = radon_tiles.shape[1]
    columns = det_blocks * block_size
    tile_width = columns // n_pos
    slab = volume.shape[1]
    width = volume.shape[2]
    own = slab // n_pos
    rows = 2 * own
    blocks_each = width // block_size

    def slices_for(j):
        start = (pos + j) % n_pos * own
        return lax.dynamic_slice_in_dim(volume, start, own, 1).reshape(rows, width)

    vol_pieces = rotate_pos([slices_for(j) for j in range(n_pos)], 1)
    vol_pieces, amplitudes = lax.optimization_barrier((vol_pieces, amplitudes))
    amp_pieces = rotate_pos(
        [
            lax.dynamic_index_in_dim(amplitudes, (pos - j) % n_pos, 0, keepdims=False)
            for j in range(n_pos)
        ],
        -1,
    )

    owner = tile_blocks // blocks_each
    within = tile_blocks % blocks_each
    piece = (pos - owner) % n_pos
    crossed = (within + jnp.arange(feeds, dtype=jnp.int32)) % 2
    tiles_each = width // LANES

    def by_chunk(idx):
        idx = idx.reshape(angles // n_pos, n_pos, n_pos, det_blocks // n_pos * feeds)
        idx = jnp.stack([jnp.roll(idx[:, p], -p, axis=1) for p in range(n_pos)], axis=1)
        return idx.reshape(angles, det_blocks * feeds)

    tile_idx = by_chunk(crossed * (n_pos * tiles_each) + piece * tiles_each + within // 2)
    block_idx = by_chunk(piece * blocks_each + within)
    padded = [pad_rows(piece, own) for piece in vol_pieces]
    probe_width = probe_field.shape[1]
    tables = dft_tables(probe_width)
    half = n_pos // 2
    reach = (half * tile_width + probe_width) // block_size
    edge = probe_width // block_size
    early_blocks = list(range(reach))
    late_blocks = list(range(reach, det_blocks))
    first_blocks = list(range(edge, half * tile_width // block_size))
    rest_blocks = list(range(half * tile_width // block_size, det_blocks)) + list(range(edge))

    sino_early = project(tile_idx, radon_tiles, padded, early_blocks, "project_early")
    sino_early, padded, offsets, counts = lax.optimization_barrier(
        (sino_early, padded, offsets, counts)
    )
    meta = jnp.concatenate([offsets, counts], axis=1)
    meta = rotate_pos(
        [lax.dynamic_slice_in_dim(meta, (pos - j) % n_pos, 1, 0) for j in range(n_pos)], -1
    )
    meta = jnp.concatenate(meta, axis=0)
    padded, meta = lax.optimization_barrier((padded, meta))
    sino_late = project(tile_idx, radon_tiles, padded, late_blocks, "project_late")
    got_early = everyone(cut_rows(sino_early, own))
    got_early, sino_late = lax.optimization_barrier((got_early, sino_late))
    got_late = everyone(cut_rows(sino_late, own))
    got_early, got_late = to_groups(got_early, own), to_groups(got_late, own)
    got_early, amp_pieces = lax.optimization_barrier((got_early, amp_pieces))
    partial, first_grad, spill = exit_first(meta, probe_field, tables, got_early, amp_pieces[:half])
    first_sent, got_late = lax.optimization_barrier((first_grad, got_late))
    rest_grad = exit_rest(
        meta, probe_field, tables, got_early, got_late, partial, spill, amp_pieces[half:]
    )
    back_first = everyone(from_groups(first_sent, own))
    back_first, rest_sent = lax.optimization_barrier((back_first, rest_grad))
    back_rest = everyone(from_groups(rest_sent, own))
    first_sum = back_project(
        block_idx, radon_tiles, pad_rows(back_first, own), first_blocks, None, n_pos, width, "back_first"
    )[0]
    wrapped = rest_grad.shape[2] - probe_width
    tile_pieces = [jnp.concatenate([rest_grad[:, :, wrapped:], first_grad[:, :, : tile_width - probe_width]], axis=2)]
    for j in range(1, n_pos):
        source, begin = (first_grad, j * tile_width - probe_width) if j < half else (rest_grad, (j - half) * tile_width)
        tile_pieces.append(source[:, :, begin : begin + tile_width])
    tile_pieces = rotate_pos(tile_pieces, 1)
    obj_pieces = back_project(
        block_idx, radon_tiles, pad_rows(back_rest, own), rest_blocks, first_sum, n_pos, width, "back_rest"
    )
    groups = rest_grad.shape[0]
    tile_pieces = [tile_pieces[-j % n_pos] for j in range(n_pos)]
    tile_pieces = [
        piece.reshape(groups, 2, GROUP, tile_width).transpose(1, 0, 2, 3).reshape(2, groups * GROUP, tile_width)
        for piece in tile_pieces
    ]
    proj_grad = jnp.stack(in_order(tile_pieces, -pos % n_pos), axis=2).astype(jnp.float32)
    obj_pieces = rotate_pos([cut_rows(piece, own) for piece in obj_pieces], -1)
    obj_pieces = [piece.reshape(2, own, width) for piece in in_order(obj_pieces, -pos % n_pos)]
    object_grad = jnp.concatenate(obj_pieces, axis=1).astype(jnp.float32)
    new_volume = volume.astype(jnp.float32) + step_size * object_grad
    return (new_volume, proj_grad)


def solution(mesh):
    in_specs = (
        P(None, "ang", "pos"),
        P(),
        P(),
        P(),
        P("ang", "pos", None, None),
        P("ang", "pos"),
        P("ang", "pos"),
    )
    out_specs = (P(None, "ang", "pos"), P(None, None, "ang", "pos"))
    return jax.shard_map(
        on_device, mesh=mesh, in_specs=in_specs, out_specs=out_specs, check_vma=False
    )
```

```python
import functools
import math

import jax
import jax.numpy as jnp
import numpy as np
from jax import lax
from jax.experimental import pallas as pl
from jax.experimental.pallas import tpu as pltpu
from jax.sharding import PartitionSpec as P

step_size = 0.1
LANES = 128
ROWS = 16
GROUP = 8
MEBI = 1024 * 1024
everywhere = pl.BlockSpec(memory_space=pltpu.VMEM)
scalars = pl.BlockSpec(memory_space=pltpu.SMEM)
CHAINS = 4
BATCH = 4
AHEAD = 16


def dft_tables(width):
    index = np.arange(width)
    turn = 2.0 * math.pi / width * (index[:, None] * index[None, :] % width)
    cosine = jnp.asarray(np.cos(turn) / math.sqrt(width), jnp.bfloat16)
    sine_neg = jnp.asarray(-np.sin(turn) / math.sqrt(width), jnp.bfloat16)
    forward = jnp.block([[cosine, -sine_neg], [sine_neg, cosine]])
    inverse = jnp.block([[cosine, sine_neg], [-sine_neg, cosine]])
    return (forward, inverse)


def rotate_pos(pieces, sign):
    count = len(pieces)
    return [pieces[0]] + [
        lax.ppermute(pieces[j], "pos", [(i, (i + sign * j) % count) for i in range(count)])
        for j in range(1, count)
    ]


def in_order(pieces, first):
    count = len(pieces)
    bit = 1
    while bit < count:
        flip = (first & bit) != 0
        pieces = [jnp.where(flip, pieces[(k + bit) % count], pieces[k]) for k in range(count)]
        bit *= 2
    return pieces


def lower_half(shape):
    return lax.broadcasted_iota(jnp.int32, shape, len(shape) - 1) < LANES // 2


def swap_halves(tile):
    return pltpu.roll(tile, LANES // 2, 1)


def arrange(vol_refs, vv_ref):
    per_piece = vol_refs[0].shape[1] // LANES
    tiles = per_piece * len(vol_refs)
    batch = 16
    source = lax.broadcasted_iota(jnp.int32, (LANES, LANES), 0)
    target = lax.broadcasted_iota(jnp.int32, (LANES, LANES), 1)
    swap = ((source + LANES // 2) % LANES == target).astype(jnp.bfloat16)
    for k, vol_ref in enumerate(vol_refs):

        @pl.loop(0, per_piece // batch, unroll=2)
        def _(step):
            stack = []
            for i in range(batch):
                t = step * batch + i
                tile = vol_ref[:, pl.ds(pl.multiple_of(t * LANES, LANES), LANES)]
                vv_ref[k * per_piece + t] = tile
                stack.append(tile)
            swapped = jnp.dot(
                jnp.concatenate(stack, axis=0), swap, preferred_element_type=jnp.float32
            ).astype(jnp.bfloat16)
            for i in range(batch):
                t = step * batch + i
                vv_ref[tiles + k * per_piece + t] = swapped[i * ROWS : (i + 1) * ROWS]


def project_blocks(blocks, idx_ref, radon_ref, vv_ref, out_ref, lhs_refs):
    angles, block, span = radon_ref.shape
    feeds = span // block
    low = lower_half((ROWS, LANES))
    batch = lhs_refs[0].shape[0]

    def gather(start, lhs_ref):
        for n in range(batch):
            a = start + n
            places = [(i, b, jp) for i, b in enumerate(blocks) for jp in range(feeds // 2)]
            for group in range(0, len(places), AHEAD):
                tiles = []
                for i, b, jp in places[group : group + AHEAD]:
                    at = b * feeds + 2 * jp
                    tiles.append((vv_ref[idx_ref[a, at]], vv_ref[idx_ref[a, at + 1]]))
                for (i, b, jp), (first, second) in zip(places[group : group + AHEAD], tiles):
                    rows = slice(i * ROWS, (i + 1) * ROWS)
                    lhs_ref[n, rows, jp * LANES : (jp + 1) * LANES] = jnp.where(low, first, second)

    def multiply(start, lhs_ref):
        for n in range(batch):
            a = start + n
            product = lax.dot_general(
                lhs_ref[n], radon_ref[a], (((1,), (1,)), ((), ())), preferred_element_type=jnp.float32
            )
            for pair in range(len(blocks) // 2):
                row = 2 * pair * ROWS
                tile = jnp.concatenate(
                    [product[row : row + ROWS], product[row + ROWS : row + 2 * ROWS]], axis=1
                )
                out_ref[a, :, pair * LANES : (pair + 1) * LANES] = tile.astype(jnp.bfloat16)

    gather(0, lhs_refs[0])

    @pl.loop(0, angles // (2 * batch))
    def _(step):
        start = step * 2 * batch
        multiply(start, lhs_refs[0])
        gather(start + batch, lhs_refs[1])
        multiply(start + batch, lhs_refs[1])
        gather(jnp.minimum(start + 2 * batch, angles - batch), lhs_refs[0])


def project_kernel(blocks, pieces, idx_ref, radon_ref, *refs):
    vol_refs = refs[:pieces]
    out_ref, vv_ref, *lhs_refs = refs[pieces:]
    arrange(vol_refs, vv_ref)
    project_blocks(blocks, idx_ref, radon_ref, vv_ref, out_ref, lhs_refs)


def guess(microseconds):
    return pl.CostEstimate(
        flops=int(microseconds * 1.15e9), bytes_accessed=int(microseconds * 1e5), transcendentals=0
    )


def project(idx, radon_tiles, vol_pieces, blocks, name):
    angles, block, span = radon_tiles.shape
    pieces = len(vol_pieces)
    tiles = pieces * vol_pieces[0].shape[1] // LANES
    out_shape = (angles, ROWS, len(blocks) * block)
    return pl.pallas_call(
        functools.partial(project_kernel, blocks, pieces),
        out_shape=jax.ShapeDtypeStruct(out_shape, jnp.bfloat16),
        in_specs=[scalars, everywhere] + [everywhere] * pieces,
        out_specs=everywhere,
        scratch_shapes=[pltpu.VMEM((2 * tiles, ROWS, LANES), jnp.bfloat16)]
        + [pltpu.VMEM((BATCH, len(blocks) * ROWS, span), jnp.bfloat16)] * 2,
        compiler_params=pltpu.CompilerParams(
            vmem_limit_bytes=14 * MEBI + 2 * radon_tiles.size + 2 * math.prod(out_shape)
        ),
        cost_estimate=guess(4 + len(blocks) // 4),
        name=name,
    )(idx, radon_tiles, *vol_pieces)


def back_project_kernel(blocks, has_start, outs, idx_ref, radon_ref, grad_ref, *refs):
    start_ref, refs = (refs[0], refs[1:]) if has_start else (None, refs)
    out_refs, refs = refs[:outs], refs[outs:]
    acc_refs, (w_ref, *contrib_refs) = refs[:CHAINS], refs[CHAINS:]
    if has_start:
        contrib_refs, start_sem = contrib_refs[:-1], contrib_refs[-1]
        start_copy = pltpu.make_async_copy(start_ref, acc_refs[0], start_sem)
        start_copy.start()
    angles, block, span = radon_ref.shape
    pairs = len(blocks) // 2
    feeds = span // block
    coef_blocks = acc_refs[0].shape[0]

    @pl.loop(0, coef_blocks, unroll=16)
    def _(t):
        for acc_ref in acc_refs[1:] if has_start else acc_refs:
            acc_ref[t] = jnp.zeros((GROUP, LANES), jnp.float32)

    low = lower_half((GROUP, LANES))
    low_rows = lower_half((block, LANES))
    w_ref[...] = jnp.zeros_like(w_ref)

    def widen(slot, a):
        for jp in range(feeds // 2):
            tile = radon_ref[a, :, jp * LANES : (jp + 1) * LANES].astype(jnp.float32)
            turned = swap_halves(tile)
            for side, (first, second) in enumerate(((tile, turned), (turned, tile))):
                lanes = slice((2 * jp + side) * LANES, (2 * jp + side + 1) * LANES)
                w_ref[slot, :block, lanes] = jnp.where(low_rows, first, 0.0).astype(jnp.bfloat16)
                w_ref[slot, block:, lanes] = jnp.where(low_rows, 0.0, second).astype(jnp.bfloat16)

    def multiply(start, half, contrib_ref):
        for n in range(CHAINS):
            a = start + n
            widen(half * CHAINS + n, a)
            lhs = []
            for pair in range(pairs):
                tile = grad_ref[a, :, pair * LANES : (pair + 1) * LANES].astype(jnp.float32)
                real, imag = tile[:GROUP], tile[GROUP:]
                even = jnp.where(low, real, swap_halves(imag))
                odd = jnp.where(low, swap_halves(real), imag)
                lhs.append(jnp.concatenate([even, odd], axis=0).astype(jnp.bfloat16))
            contrib_ref[n] = jnp.dot(
                jnp.concatenate(lhs, axis=0),
                w_ref[half * CHAINS + n],
                preferred_element_type=jnp.float32,
            )

    def scatter(start, contrib_ref):
        for i, b in enumerate(blocks):
            row = i * GROUP
            for j in range(0, feeds, 2):
                sums = []
                for n in range(CHAINS):
                    here, there = (idx_ref[start + n, b * feeds + j + i] for i in range(2))
                    one, two = (
                        contrib_ref[n, row : row + GROUP, (j + i) * LANES : (j + i + 1) * LANES]
                        for i in range(2)
                    )
                    first = acc_refs[n][here] + one
                    second = jnp.where(here == there, first, acc_refs[n][there]) + two
                    sums.append((here, first, there, second))
                for n, (here, first, there, second) in enumerate(sums):
                    acc_refs[n][here] = first
                    acc_refs[n][there] = second

    multiply(0, 0, contrib_refs[0])
    if has_start:
        start_copy.wait()

    @pl.loop(0, angles // (2 * CHAINS))
    def _(step):
        start = step * 2 * CHAINS
        multiply(start + CHAINS, 1, contrib_refs[1])
        scatter(start, contrib_refs[0])
        multiply(jnp.minimum(start + 2 * CHAINS, angles - CHAINS), 0, contrib_refs[0])
        scatter(start + CHAINS, contrib_refs[1])

    def total(t):
        sums = [acc_ref[t] for acc_ref in acc_refs]
        while len(sums) > 1:
            sums = [sums[i] + sums[i + 1] for i in range(0, len(sums), 2)]
        return sums[0]

    if outs == 1:

        @pl.loop(0, coef_blocks, unroll=16)
        def _(t):
            out_refs[0][t] = total(t)

    else:
        per_piece = out_refs[0].shape[1] // LANES
        for k, out_ref in enumerate(out_refs):

            @pl.loop(0, per_piece, unroll=16)
            def _(t):
                lanes = pl.ds(pl.multiple_of(t * LANES, LANES), LANES)
                even = total(2 * (k * per_piece + t))
                odd = total(2 * (k * per_piece + t) + 1)
                real = jnp.where(low, even, swap_halves(odd))
                imag = jnp.where(low, swap_halves(even), odd)
                out_ref[:, lanes] = jnp.concatenate([real, imag], axis=0).astype(out_ref.dtype)


def back_project(idx, radon_tiles, grads, blocks, start, pieces, piece_width, name):
    angles, block, span = radon_tiles.shape
    coef_blocks = pieces * piece_width // block
    rows = len(blocks) * GROUP
    has_start = start is not None
    if has_start:
        out_shape = [jax.ShapeDtypeStruct((ROWS, piece_width), jnp.bfloat16)] * pieces
    else:
        out_shape = [jax.ShapeDtypeStruct((coef_blocks, GROUP, LANES), jnp.float32)]
    operands = [idx, radon_tiles, grads] + ([start] if has_start else [])
    return pl.pallas_call(
        functools.partial(back_project_kernel, blocks, has_start, len(out_shape)),
        out_shape=out_shape,
        in_specs=[scalars] + [everywhere] * 2 + [pl.BlockSpec(memory_space=pl.ANY)] * has_start,
        out_specs=[everywhere] * len(out_shape),
        scratch_shapes=[pltpu.VMEM((coef_blocks, GROUP, LANES), jnp.float32)] * CHAINS
        + [pltpu.VMEM((2 * CHAINS, 2 * block, 2 * span), jnp.bfloat16)]
        + [pltpu.VMEM((CHAINS, rows, 2 * span), jnp.float32)] * 2
        + [pltpu.SemaphoreType.DMA] * has_start,
        compiler_params=pltpu.CompilerParams(vmem_limit_bytes=60 * MEBI),
        cost_estimate=guess(4 + len(blocks) // 4),
        name=name,
    )(*operands)


def add_slots(meta_ref, probe_ref, forward_ref, inverse_ref, ext_ref, acc_ref, amp_refs, scratch, first):
    wave_ref, half_ref, delta_ref, back_ref = scratch
    n_pos = lax.axis_size("pos")
    groups = ext_ref.shape[0]
    width = probe_ref.shape[1]
    slots = amp_refs[0].shape[0]
    tile_width = (acc_ref.shape[2] - width) // len(amp_refs)
    chunk = 4
    crows = chunk * GROUP
    chunks = groups // chunk
    wide = width // LANES
    lane_id = lax.broadcasted_iota(jnp.int32, (crows, LANES), 1)

    def product(left, right):
        return jnp.dot(left, right, preferred_element_type=jnp.float32)

    for tile, amp_ref in enumerate(amp_refs):
        order = first + tile
        tile_start = lax.rem(lax.axis_index("pos") + order, n_pos) * tile_width - tile * tile_width
        count = meta_ref[order, slots]

        @pl.loop(0, (count + 1) // 2)
        def _(step):
            shifts, starts, lives = [], [], []
            for n in range(2):
                offset = meta_ref[order, step * 2 + n] - tile_start
                shifts.append(offset % LANES)
                lane_tile = offset // LANES
                starts.append(
                    [pl.multiple_of((lane_tile + m) * LANES, LANES) for m in range(wide + 1)]
                )
                lives.append((step * 2 + n < count).astype(jnp.float32))
            for n in range(2):
                keep = lane_id < LANES - shifts[n]
                back_shift = (LANES - shifts[n]) % LANES
                for ch in range(chunks):
                    rows = slice(ch * crows, (ch + 1) * crows)
                    low_rows = slice(width + ch * crows, width + (ch + 1) * crows)
                    turned = []
                    for start in starts[n]:
                        both = ext_ref[ch * chunk : (ch + 1) * chunk, :, pl.ds(start, LANES)]
                        both = both.astype(jnp.float32)
                        turned.append(
                            [
                                pltpu.roll(
                                    both[:, c * GROUP : (c + 1) * GROUP].reshape(crows, LANES),
                                    back_shift,
                                    1,
                                )
                                for c in range(2)
                            ]
                        )
                    for m in range(wide):
                        lanes = slice(m * LANES, (m + 1) * LANES)
                        put = slice(n * width + m * LANES, n * width + (m + 1) * LANES)
                        patch_re = jnp.where(keep, turned[m][0], turned[m + 1][0])
                        patch_im = jnp.where(keep, turned[m][1], turned[m + 1][1])
                        probe_re = probe_ref[0, rows, lanes].astype(jnp.float32)
                        probe_im = probe_ref[1, rows, lanes].astype(jnp.float32)
                        wave_re = probe_re * patch_re - probe_im * patch_im
                        wave_im = probe_re * patch_im + probe_im * patch_re
                        wave_ref[rows, put] = wave_re.astype(jnp.bfloat16)
                        wave_ref[low_rows, put] = wave_im.astype(jnp.bfloat16)
                mine = slice(n * width, (n + 1) * width)
                half = product(forward_ref[...], wave_ref[:, mine]).astype(jnp.bfloat16)
                half_ref[mine, :width] = half[:width]
                half_ref[mine, width:] = half[width:]
            for n in range(2):
                mine = slice(n * width, (n + 1) * width)
                far = product(half_ref[mine, :], inverse_ref[...])
                for ch in range(chunks):
                    rows = slice(ch * crows, (ch + 1) * crows)
                    low_rows = slice(width + ch * crows, width + (ch + 1) * crows)
                    far_re, far_im = far[rows, :width], far[rows, width:]
                    power = far_re * far_re + far_im * far_im
                    amps = amp_ref[step * 2 + n, rows, :].astype(jnp.float32)
                    factor = amps * lax.rsqrt(jnp.maximum(power, 1.0)) - 1.0
                    delta_ref[rows, mine] = (far_re * factor).astype(jnp.bfloat16)
                    delta_ref[low_rows, mine] = (far_im * factor).astype(jnp.bfloat16)
                back = product(inverse_ref[...], delta_ref[:, mine]).astype(jnp.bfloat16)
                back_ref[mine, :width] = back[:width]
                back_ref[mine, width:] = back[width:]
            for n in range(2):
                mine = slice(n * width, (n + 1) * width)
                near = product(back_ref[mine, :], forward_ref[...])
                past = lane_id >= shifts[n]
                for ch in range(chunks):
                    rows = slice(ch * crows, (ch + 1) * crows)
                    turned = []
                    for m in range(wide):
                        lanes = slice(m * LANES, (m + 1) * LANES)
                        probe_re = probe_ref[0, rows, lanes].astype(jnp.float32) * lives[n]
                        probe_im = probe_ref[1, rows, lanes].astype(jnp.float32) * lives[n]
                        near_re = near[rows, m * LANES : (m + 1) * LANES]
                        near_im = near[rows, width + m * LANES : width + (m + 1) * LANES]
                        turned.append(
                            [
                                pltpu.roll(probe_re * near_re + probe_im * near_im, shifts[n], 1),
                                pltpu.roll(probe_re * near_im - probe_im * near_re, shifts[n], 1),
                            ]
                        )
                    for m in range(wide + 1):
                        for c in range(2):
                            behind = turned[m - 1][c] if m > 0 else 0.0
                            ahead = turned[m][c] if m < wide else 0.0
                            here = (c, rows, pl.ds(starts[n][m], LANES))
                            acc_ref[here] += jnp.where(past, ahead, behind)


def exit_first_kernel(tiles, meta_ref, probe_ref, forward_ref, inverse_ref, sino_ref, *refs):
    amp_refs, refs = refs[:tiles], refs[tiles:]
    partial_ref, grad_ref, spill_ref, acc_ref, *scratch = refs
    groups = sino_ref.shape[0]
    width = probe_ref.shape[1]
    done = sino_ref.shape[2] - width

    @pl.loop(0, groups)
    def _(g):
        rows = pl.ds(pl.multiple_of(g * GROUP, GROUP), GROUP)
        for c in range(2):
            acc_ref[c, rows, :] = jnp.zeros((GROUP, acc_ref.shape[2]), jnp.float32)

    add_slots(
        meta_ref, probe_ref, forward_ref, inverse_ref, sino_ref, acc_ref, amp_refs, scratch, 0
    )

    @pl.loop(0, groups)
    def _(g):
        rows = pl.ds(pl.multiple_of(g * GROUP, GROUP), GROUP)
        whole = [acc_ref[c, rows, width:done] for c in range(2)]
        grad_ref[g] = jnp.concatenate(whole, axis=0).astype(jnp.bfloat16)
        for c in range(2):
            partial_ref[c, rows, :] = acc_ref[c, rows, :width]
            spill_ref[c, rows, :] = acc_ref[c, rows, done:]


def exit_rest_kernel(
    tiles, meta_ref, probe_ref, forward_ref, inverse_ref, early_ref, late_ref, partial_ref, spill_ref, *refs
):
    amp_refs, refs = refs[:tiles], refs[tiles:]
    out_ref, ext_ref, acc_ref, *scratch = refs
    groups = early_ref.shape[0]
    width = probe_ref.shape[1]
    done = width + late_ref.shape[2]

    @pl.loop(0, groups)
    def _(g):
        ext_ref[g, :, :width] = early_ref[g, :, early_ref.shape[2] - width :]
        ext_ref[g, :, width:done] = late_ref[g]
        ext_ref[g, :, done:] = early_ref[g, :, :width]
        rows = pl.ds(pl.multiple_of(g * GROUP, GROUP), GROUP)
        for c in range(2):
            acc_ref[c, rows, :width] = spill_ref[c, rows, :]
            acc_ref[c, rows, width:] = jnp.zeros((GROUP, done), jnp.float32)

    add_slots(
        meta_ref, probe_ref, forward_ref, inverse_ref, ext_ref, acc_ref, amp_refs, scratch,
        lax.axis_size("pos") - tiles,
    )

    @pl.loop(0, groups)
    def _(g):
        rows = pl.ds(pl.multiple_of(g * GROUP, GROUP), GROUP)
        here = [acc_ref[c, rows, :done] for c in range(2)]
        wrapped = [acc_ref[c, rows, done:] + partial_ref[c, rows, :] for c in range(2)]
        out_ref[g, :, :done] = jnp.concatenate(here, axis=0).astype(jnp.bfloat16)
        out_ref[g, :, done:] = jnp.concatenate(wrapped, axis=0).astype(jnp.bfloat16)


def exit_scratch(groups, width, reach):
    return [pltpu.VMEM((2, groups * GROUP, reach), jnp.float32)] + [
        pltpu.VMEM((2 * width, 2 * width), jnp.bfloat16)
    ] * 4


def exit_first(meta, probe_field, tables, sino, amps):
    groups, rows, reach = sino.shape
    width = probe_field.shape[1]
    slices = groups * GROUP
    edge = jax.ShapeDtypeStruct((2, slices, width), jnp.float32)
    grad = jax.ShapeDtypeStruct((groups, rows, reach - 2 * width), jnp.bfloat16)
    return pl.pallas_call(
        functools.partial(exit_first_kernel, len(amps)),
        out_shape=[edge, grad, edge],
        in_specs=[scalars] + [everywhere] * (4 + len(amps)),
        out_specs=[everywhere] * 3,
        scratch_shapes=exit_scratch(groups, width, reach),
        compiler_params=pltpu.CompilerParams(vmem_limit_bytes=60 * MEBI),
        cost_estimate=guess(10),
        name="exit_first",
    )(meta, probe_field, *tables, sino, *amps)


def exit_rest(meta, probe_field, tables, early, late, partial, spill, amps):
    groups, rows = late.shape[:2]
    width = probe_field.shape[1]
    reach = late.shape[2] + 2 * width
    return pl.pallas_call(
        functools.partial(exit_rest_kernel, len(amps)),
        out_shape=jax.ShapeDtypeStruct((groups, rows, reach), jnp.bfloat16),
        in_specs=[scalars] + [everywhere] * (7 + len(amps)),
        out_specs=everywhere,
        scratch_shapes=[pltpu.VMEM((groups, rows, reach), jnp.bfloat16)]
        + exit_scratch(groups, width, reach),
        compiler_params=pltpu.CompilerParams(vmem_limit_bytes=60 * MEBI),
        cost_estimate=guess(10),
        name="exit_rest",
    )(meta, probe_field, *tables, early, late, partial, spill, *amps)


def to_groups(received, own_slices):
    if own_slices == GROUP:
        return received
    devices, rows, columns = received.shape
    merge = GROUP // own_slices
    split = received.reshape(devices // merge, merge, 2, own_slices, columns)
    return split.transpose(0, 2, 1, 3, 4).reshape(devices // merge, ROWS, columns)


def from_groups(grouped, own_slices):
    if own_slices == GROUP:
        return grouped
    groups, rows, columns = grouped.shape
    merge = GROUP // own_slices
    split = grouped.reshape(groups, 2, merge, own_slices, columns)
    return split.transpose(0, 2, 1, 3, 4).reshape(groups * merge, 2 * own_slices, columns)


def pad_rows(block, own_slices):
    if own_slices == GROUP:
        return block
    lead, columns = block.shape[:-2], block.shape[-1]
    split = block.reshape(lead + (2, own_slices, columns))
    more = [(0, 0)] * (split.ndim - 2) + [(0, GROUP - own_slices), (0, 0)]
    return jnp.pad(split, more).reshape(lead + (ROWS, columns))


def cut_rows(block, own_slices):
    if own_slices == GROUP:
        return block
    lead, columns = block.shape[:-2], block.shape[-1]
    split = block.reshape(lead + (2, GROUP, columns))[..., :own_slices, :]
    return split.reshape(lead + (2 * own_slices, columns))


def everyone(chunk):
    return lax.all_to_all(chunk, ("ang", "pos"), 0, 0, tiled=True)


def on_device(volume, radon_tiles, tile_blocks, probe_field, amplitudes, offsets, counts):
    n_pos = lax.axis_size("pos")
    pos = lax.axis_index("pos")
    angles, det_blocks, feeds = tile_blocks.shape
    block_size = radon_tiles.shape[1]
    columns = det_blocks * block_size
    tile_width = columns // n_pos
    slab = volume.shape[1]
    width = volume.shape[2]
    own = slab // n_pos
    rows = 2 * own
    blocks_each = width // block_size

    def slices_for(j):
        start = (pos + j) % n_pos * own
        return lax.dynamic_slice_in_dim(volume, start, own, 1).reshape(rows, width)

    vol_pieces = rotate_pos([slices_for(j) for j in range(n_pos)], 1)
    vol_pieces, amplitudes = lax.optimization_barrier((vol_pieces, amplitudes))
    amp_pieces = rotate_pos(
        [
            lax.dynamic_index_in_dim(amplitudes, (pos - j) % n_pos, 0, keepdims=False)
            for j in range(n_pos)
        ],
        -1,
    )

    owner = tile_blocks // blocks_each
    within = tile_blocks % blocks_each
    piece = (pos - owner) % n_pos
    crossed = (within + jnp.arange(feeds, dtype=jnp.int32)) % 2
    tiles_each = width // LANES

    def by_chunk(idx):
        idx = idx.reshape(angles // n_pos, n_pos, n_pos, det_blocks // n_pos * feeds)
        idx = jnp.stack([jnp.roll(idx[:, p], -p, axis=1) for p in range(n_pos)], axis=1)
        return idx.reshape(angles, det_blocks * feeds)

    tile_idx = by_chunk(crossed * (n_pos * tiles_each) + piece * tiles_each + within // 2)
    block_idx = by_chunk(piece * blocks_each + within)
    padded = [pad_rows(piece, own) for piece in vol_pieces]
    probe_width = probe_field.shape[1]
    tables = dft_tables(probe_width)
    half = n_pos // 2
    reach = (half * tile_width + probe_width) // block_size
    edge = probe_width // block_size
    early_blocks = list(range(reach))
    late_blocks = list(range(reach, det_blocks))
    first_blocks = list(range(edge, half * tile_width // block_size))
    rest_blocks = list(range(half * tile_width // block_size, det_blocks)) + list(range(edge))

    sino_early = project(tile_idx, radon_tiles, padded, early_blocks, "project_early")
    sino_early, padded, offsets, counts = lax.optimization_barrier(
        (sino_early, padded, offsets, counts)
    )
    meta = jnp.concatenate([offsets, counts], axis=1)
    meta = rotate_pos(
        [lax.dynamic_slice_in_dim(meta, (pos - j) % n_pos, 1, 0) for j in range(n_pos)], -1
    )
    meta = jnp.concatenate(meta, axis=0)
    padded, meta = lax.optimization_barrier((padded, meta))
    sino_late = project(tile_idx, radon_tiles, padded, late_blocks, "project_late")
    got_early = everyone(cut_rows(sino_early, own))
    got_early, sino_late = lax.optimization_barrier((got_early, sino_late))
    got_late = everyone(cut_rows(sino_late, own))
    got_early, got_late = to_groups(got_early, own), to_groups(got_late, own)
    got_early, amp_pieces = lax.optimization_barrier((got_early, amp_pieces))
    partial, first_grad, spill = exit_first(meta, probe_field, tables, got_early, amp_pieces[:half])
    first_sent, got_late = lax.optimization_barrier((first_grad, got_late))
    rest_grad = exit_rest(
        meta, probe_field, tables, got_early, got_late, partial, spill, amp_pieces[half:]
    )
    back_first = everyone(from_groups(first_sent, own))
    back_first, rest_sent = lax.optimization_barrier((back_first, rest_grad))
    back_rest = everyone(from_groups(rest_sent, own))
    first_sum = back_project(
        block_idx, radon_tiles, pad_rows(back_first, own), first_blocks, None, n_pos, width, "back_first"
    )[0]
    wrapped = rest_grad.shape[2] - probe_width
    tile_pieces = [jnp.concatenate([rest_grad[:, :, wrapped:], first_grad[:, :, : tile_width - probe_width]], axis=2)]
    for j in range(1, n_pos):
        source, begin = (first_grad, j * tile_width - probe_width) if j < half else (rest_grad, (j - half) * tile_width)
        tile_pieces.append(source[:, :, begin : begin + tile_width])
    tile_pieces = rotate_pos(tile_pieces, 1)
    obj_pieces = back_project(
        block_idx, radon_tiles, pad_rows(back_rest, own), rest_blocks, first_sum, n_pos, width, "back_rest"
    )
    groups = rest_grad.shape[0]
    tile_pieces = [tile_pieces[-j % n_pos] for j in range(n_pos)]
    tile_pieces = [
        piece.reshape(groups, 2, GROUP, tile_width).transpose(1, 0, 2, 3).reshape(2, groups * GROUP, tile_width)
        for piece in tile_pieces
    ]
    proj_grad = jnp.stack(in_order(tile_pieces, -pos % n_pos), axis=2).astype(jnp.float32)
    obj_pieces = rotate_pos([cut_rows(piece, own) for piece in obj_pieces], -1)
    obj_pieces = [piece.reshape(2, own, width) for piece in in_order(obj_pieces, -pos % n_pos)]
    object_grad = jnp.concatenate(obj_pieces, axis=1).astype(jnp.float32)
    new_volume = volume.astype(jnp.float32) + step_size * object_grad
    return (new_volume, proj_grad)


def solution(mesh):
    in_specs = (
        P(None, "ang", "pos"),
        P(),
        P(),
        P(),
        P("ang", "pos", None, None),
        P("ang", "pos"),
        P("ang", "pos"),
    )
    out_specs = (P(None, "ang", "pos"), P(None, None, "ang", "pos"))
    return jax.shard_map(
        on_device, mesh=mesh, in_specs=in_specs, out_specs=out_specs, check_vma=False
    )
```

```python
import functools
import math

import jax
import jax.numpy as jnp
import numpy as np
from jax import lax
from jax.experimental import pallas as pl
from jax.experimental.pallas import tpu as pltpu
from jax.sharding import PartitionSpec as P

step_size = 0.1
LANES = 128
ROWS = 16
GROUP = 8
MEBI = 1024 * 1024
everywhere = pl.BlockSpec(memory_space=pltpu.VMEM)
scalars = pl.BlockSpec(memory_space=pltpu.SMEM)
CHAINS = 4
BATCH = 4


def dft_tables(width):
    index = np.arange(width)
    turn = 2.0 * math.pi / width * (index[:, None] * index[None, :] % width)
    cosine = jnp.asarray(np.cos(turn) / math.sqrt(width), jnp.bfloat16)
    sine_neg = jnp.asarray(-np.sin(turn) / math.sqrt(width), jnp.bfloat16)
    forward = jnp.block([[cosine, -sine_neg], [sine_neg, cosine]])
    inverse = jnp.block([[cosine, sine_neg], [-sine_neg, cosine]])
    return (forward, inverse)


def rotate_pos(pieces, sign):
    count = len(pieces)
    return [pieces[0]] + [
        lax.ppermute(pieces[j], "pos", [(i, (i + sign * j) % count) for i in range(count)])
        for j in range(1, count)
    ]


def in_order(pieces, first):
    count = len(pieces)
    bit = 1
    while bit < count:
        flip = (first & bit) != 0
        pieces = [jnp.where(flip, pieces[(k + bit) % count], pieces[k]) for k in range(count)]
        bit *= 2
    return pieces


def lower_half(shape):
    return lax.broadcasted_iota(jnp.int32, shape, len(shape) - 1) < LANES // 2


def swap_halves(tile):
    return pltpu.roll(tile, LANES // 2, 1)


def arrange(vol_refs, vv_ref):
    per_piece = vol_refs[0].shape[1] // LANES
    tiles = per_piece * len(vol_refs)
    batch = 16
    source = lax.broadcasted_iota(jnp.int32, (LANES, LANES), 0)
    target = lax.broadcasted_iota(jnp.int32, (LANES, LANES), 1)
    swap = ((source + LANES // 2) % LANES == target).astype(jnp.bfloat16)
    for k, vol_ref in enumerate(vol_refs):

        @pl.loop(0, per_piece // batch, unroll=2)
        def _(step):
            stack = []
            for i in range(batch):
                t = step * batch + i
                tile = vol_ref[:, pl.ds(pl.multiple_of(t * LANES, LANES), LANES)]
                vv_ref[k * per_piece + t] = tile
                stack.append(tile)
            swapped = jnp.dot(
                jnp.concatenate(stack, axis=0), swap, preferred_element_type=jnp.float32
            ).astype(jnp.bfloat16)
            for i in range(batch):
                t = step * batch + i
                vv_ref[tiles + k * per_piece + t] = swapped[i * ROWS : (i + 1) * ROWS]


def project_blocks(blocks, idx_ref, radon_ref, vv_ref, out_ref, lhs_refs):
    angles, block, span = radon_ref.shape
    feeds = span // block
    low = lower_half((ROWS, LANES))
    batch = lhs_refs[0].shape[0]

    def gather(start, lhs_ref):
        for n in range(batch):
            a = start + n
            for i, b in enumerate(blocks):
                row = i * ROWS
                for jp in range(feeds // 2):
                    at = b * feeds + 2 * jp
                    first = vv_ref[idx_ref[a, at]]
                    second = vv_ref[idx_ref[a, at + 1]]
                    lhs_ref[n, row : row + ROWS, jp * LANES : (jp + 1) * LANES] = jnp.where(
                        low, first, second
                    )

    def multiply(start, lhs_ref):
        for n in range(batch):
            a = start + n
            product = lax.dot_general(
                lhs_ref[n], radon_ref[a], (((1,), (1,)), ((), ())), preferred_element_type=jnp.float32
            )
            for pair in range(len(blocks) // 2):
                row = 2 * pair * ROWS
                tile = jnp.concatenate(
                    [product[row : row + ROWS], product[row + ROWS : row + 2 * ROWS]], axis=1
                )
                out_ref[a, :, pair * LANES : (pair + 1) * LANES] = tile.astype(jnp.bfloat16)

    gather(0, lhs_refs[0])

    @pl.loop(0, angles // (2 * batch))
    def _(step):
        start = step * 2 * batch
        multiply(start, lhs_refs[0])
        gather(start + batch, lhs_refs[1])
        multiply(start + batch, lhs_refs[1])
        gather(jnp.minimum(start + 2 * batch, angles - batch), lhs_refs[0])


def project_kernel(blocks, pieces, idx_ref, radon_ref, *refs):
    vol_refs = refs[:pieces]
    out_ref, vv_ref, *lhs_refs = refs[pieces:]
    arrange(vol_refs, vv_ref)
    project_blocks(blocks, idx_ref, radon_ref, vv_ref, out_ref, lhs_refs)


def guess(microseconds):
    return pl.CostEstimate(
        flops=int(microseconds * 1.15e9), bytes_accessed=int(microseconds * 1e5), transcendentals=0
    )


def project(idx, radon_tiles, vol_pieces, blocks, name):
    angles, block, span = radon_tiles.shape
    pieces = len(vol_pieces)
    tiles = pieces * vol_pieces[0].shape[1] // LANES
    out_shape = (angles, ROWS, len(blocks) * block)
    return pl.pallas_call(
        functools.partial(project_kernel, blocks, pieces),
        out_shape=jax.ShapeDtypeStruct(out_shape, jnp.bfloat16),
        in_specs=[scalars, everywhere] + [everywhere] * pieces,
        out_specs=everywhere,
        scratch_shapes=[pltpu.VMEM((2 * tiles, ROWS, LANES), jnp.bfloat16)]
        + [pltpu.VMEM((BATCH, len(blocks) * ROWS, span), jnp.bfloat16)] * 2,
        compiler_params=pltpu.CompilerParams(
            vmem_limit_bytes=14 * MEBI + 2 * radon_tiles.size + 2 * math.prod(out_shape)
        ),
        cost_estimate=guess(4 + len(blocks) // 4),
        name=name,
    )(idx, radon_tiles, *vol_pieces)


def back_project_kernel(blocks, has_start, outs, idx_ref, radon_ref, grad_ref, *refs):
    start_ref, refs = (refs[0], refs[1:]) if has_start else (None, refs)
    out_refs, refs = refs[:outs], refs[outs:]
    acc_refs, (w_ref, *contrib_refs) = refs[:CHAINS], refs[CHAINS:]
    if has_start:
        contrib_refs, start_sem = contrib_refs[:-1], contrib_refs[-1]
        start_copy = pltpu.make_async_copy(start_ref, acc_refs[0], start_sem)
        start_copy.start()
    angles, block, span = radon_ref.shape
    pairs = len(blocks) // 2
    feeds = span // block
    coef_blocks = acc_refs[0].shape[0]

    @pl.loop(0, coef_blocks, unroll=16)
    def _(t):
        for acc_ref in acc_refs[1:] if has_start else acc_refs:
            acc_ref[t] = jnp.zeros((GROUP, LANES), jnp.float32)

    low = lower_half((GROUP, LANES))
    low_rows = lower_half((block, LANES))
    w_ref[...] = jnp.zeros_like(w_ref)

    def widen(slot, a):
        for jp in range(feeds // 2):
            tile = radon_ref[a, :, jp * LANES : (jp + 1) * LANES].astype(jnp.float32)
            turned = swap_halves(tile)
            for side, (first, second) in enumerate(((tile, turned), (turned, tile))):
                lanes = slice((2 * jp + side) * LANES, (2 * jp + side + 1) * LANES)
                w_ref[slot, :block, lanes] = jnp.where(low_rows, first, 0.0).astype(jnp.bfloat16)
                w_ref[slot, block:, lanes] = jnp.where(low_rows, 0.0, second).astype(jnp.bfloat16)

    def multiply(start, half, contrib_ref):
        for n in range(CHAINS):
            a = start + n
            widen(half * CHAINS + n, a)
            lhs = []
            for pair in range(pairs):
                tile = grad_ref[a, :, pair * LANES : (pair + 1) * LANES].astype(jnp.float32)
                real, imag = tile[:GROUP], tile[GROUP:]
                even = jnp.where(low, real, swap_halves(imag))
                odd = jnp.where(low, swap_halves(real), imag)
                lhs.append(jnp.concatenate([even, odd], axis=0).astype(jnp.bfloat16))
            contrib_ref[n] = jnp.dot(
                jnp.concatenate(lhs, axis=0),
                w_ref[half * CHAINS + n],
                preferred_element_type=jnp.float32,
            )

    def scatter(start, contrib_ref):
        for i, b in enumerate(blocks):
            row = i * GROUP
            for j in range(feeds):
                for n in range(CHAINS):
                    tile = contrib_ref[n, row : row + GROUP, j * LANES : (j + 1) * LANES]
                    acc_refs[n][idx_ref[start + n, b * feeds + j]] += tile

    multiply(0, 0, contrib_refs[0])
    if has_start:
        start_copy.wait()

    @pl.loop(0, angles // (2 * CHAINS))
    def _(step):
        start = step * 2 * CHAINS
        multiply(start + CHAINS, 1, contrib_refs[1])
        scatter(start, contrib_refs[0])
        multiply(jnp.minimum(start + 2 * CHAINS, angles - CHAINS), 0, contrib_refs[0])
        scatter(start + CHAINS, contrib_refs[1])

    def total(t):
        sums = [acc_ref[t] for acc_ref in acc_refs]
        while len(sums) > 1:
            sums = [sums[i] + sums[i + 1] for i in range(0, len(sums), 2)]
        return sums[0]

    if outs == 1:

        @pl.loop(0, coef_blocks, unroll=16)
        def _(t):
            out_refs[0][t] = total(t)

    else:
        per_piece = out_refs[0].shape[1] // LANES
        for k, out_ref in enumerate(out_refs):

            @pl.loop(0, per_piece, unroll=16)
            def _(t):
                lanes = pl.ds(pl.multiple_of(t * LANES, LANES), LANES)
                even = total(2 * (k * per_piece + t))
                odd = total(2 * (k * per_piece + t) + 1)
                real = jnp.where(low, even, swap_halves(odd))
                imag = jnp.where(low, swap_halves(even), odd)
                out_ref[:, lanes] = jnp.concatenate([real, imag], axis=0).astype(out_ref.dtype)


def back_project(idx, radon_tiles, grads, blocks, start, pieces, piece_width, name):
    angles, block, span = radon_tiles.shape
    coef_blocks = pieces * piece_width // block
    rows = len(blocks) * GROUP
    has_start = start is not None
    if has_start:
        out_shape = [jax.ShapeDtypeStruct((ROWS, piece_width), jnp.bfloat16)] * pieces
    else:
        out_shape = [jax.ShapeDtypeStruct((coef_blocks, GROUP, LANES), jnp.float32)]
    operands = [idx, radon_tiles, grads] + ([start] if has_start else [])
    return pl.pallas_call(
        functools.partial(back_project_kernel, blocks, has_start, len(out_shape)),
        out_shape=out_shape,
        in_specs=[scalars] + [everywhere] * 2 + [pl.BlockSpec(memory_space=pl.ANY)] * has_start,
        out_specs=[everywhere] * len(out_shape),
        scratch_shapes=[pltpu.VMEM((coef_blocks, GROUP, LANES), jnp.float32)] * CHAINS
        + [pltpu.VMEM((2 * CHAINS, 2 * block, 2 * span), jnp.bfloat16)]
        + [pltpu.VMEM((CHAINS, rows, 2 * span), jnp.float32)] * 2
        + [pltpu.SemaphoreType.DMA] * has_start,
        compiler_params=pltpu.CompilerParams(vmem_limit_bytes=60 * MEBI),
        cost_estimate=guess(4 + len(blocks) // 4),
        name=name,
    )(*operands)


def add_slots(meta_ref, probe_ref, forward_ref, inverse_ref, ext_ref, acc_ref, amp_refs, scratch, first):
    wave_ref, half_ref, delta_ref, back_ref = scratch
    n_pos = lax.axis_size("pos")
    groups = ext_ref.shape[0]
    width = probe_ref.shape[1]
    slots = amp_refs[0].shape[0]
    tile_width = (acc_ref.shape[2] - width) // len(amp_refs)
    chunk = 4
    crows = chunk * GROUP
    chunks = groups // chunk
    wide = width // LANES
    lane_id = lax.broadcasted_iota(jnp.int32, (crows, LANES), 1)

    def product(left, right):
        return jnp.dot(left, right, preferred_element_type=jnp.float32)

    for tile, amp_ref in enumerate(amp_refs):
        order = first + tile
        tile_start = lax.rem(lax.axis_index("pos") + order, n_pos) * tile_width - tile * tile_width
        count = meta_ref[order, slots]

        @pl.loop(0, (count + 1) // 2)
        def _(step):
            shifts, starts, lives = [], [], []
            for n in range(2):
                offset = meta_ref[order, step * 2 + n] - tile_start
                shifts.append(offset % LANES)
                lane_tile = offset // LANES
                starts.append(
                    [pl.multiple_of((lane_tile + m) * LANES, LANES) for m in range(wide + 1)]
                )
                lives.append((step * 2 + n < count).astype(jnp.float32))
            for n in range(2):
                keep = lane_id < LANES - shifts[n]
                back_shift = (LANES - shifts[n]) % LANES
                for ch in range(chunks):
                    rows = slice(ch * crows, (ch + 1) * crows)
                    low_rows = slice(width + ch * crows, width + (ch + 1) * crows)
                    turned = []
                    for start in starts[n]:
                        both = ext_ref[ch * chunk : (ch + 1) * chunk, :, pl.ds(start, LANES)]
                        both = both.astype(jnp.float32)
                        turned.append(
                            [
                                pltpu.roll(
                                    both[:, c * GROUP : (c + 1) * GROUP].reshape(crows, LANES),
                                    back_shift,
                                    1,
                                )
                                for c in range(2)
                            ]
                        )
                    for m in range(wide):
                        lanes = slice(m * LANES, (m + 1) * LANES)
                        put = slice(n * width + m * LANES, n * width + (m + 1) * LANES)
                        patch_re = jnp.where(keep, turned[m][0], turned[m + 1][0])
                        patch_im = jnp.where(keep, turned[m][1], turned[m + 1][1])
                        probe_re = probe_ref[0, rows, lanes].astype(jnp.float32)
                        probe_im = probe_ref[1, rows, lanes].astype(jnp.float32)
                        wave_re = probe_re * patch_re - probe_im * patch_im
                        wave_im = probe_re * patch_im + probe_im * patch_re
                        wave_ref[rows, put] = wave_re.astype(jnp.bfloat16)
                        wave_ref[low_rows, put] = wave_im.astype(jnp.bfloat16)
                mine = slice(n * width, (n + 1) * width)
                half = product(forward_ref[...], wave_ref[:, mine]).astype(jnp.bfloat16)
                half_ref[mine, :width] = half[:width]
                half_ref[mine, width:] = half[width:]
            for n in range(2):
                mine = slice(n * width, (n + 1) * width)
                far = product(half_ref[mine, :], inverse_ref[...])
                for ch in range(chunks):
                    rows = slice(ch * crows, (ch + 1) * crows)
                    low_rows = slice(width + ch * crows, width + (ch + 1) * crows)
                    far_re, far_im = far[rows, :width], far[rows, width:]
                    power = far_re * far_re + far_im * far_im
                    amps = amp_ref[step * 2 + n, rows, :].astype(jnp.float32)
                    factor = amps * lax.rsqrt(jnp.maximum(power, 1.0)) - 1.0
                    delta_ref[rows, mine] = (far_re * factor).astype(jnp.bfloat16)
                    delta_ref[low_rows, mine] = (far_im * factor).astype(jnp.bfloat16)
                back = product(inverse_ref[...], delta_ref[:, mine]).astype(jnp.bfloat16)
                back_ref[mine, :width] = back[:width]
                back_ref[mine, width:] = back[width:]
            for n in range(2):
                mine = slice(n * width, (n + 1) * width)
                near = product(back_ref[mine, :], forward_ref[...])
                past = lane_id >= shifts[n]
                for ch in range(chunks):
                    rows = slice(ch * crows, (ch + 1) * crows)
                    turned = []
                    for m in range(wide):
                        lanes = slice(m * LANES, (m + 1) * LANES)
                        probe_re = probe_ref[0, rows, lanes].astype(jnp.float32) * lives[n]
                        probe_im = probe_ref[1, rows, lanes].astype(jnp.float32) * lives[n]
                        near_re = near[rows, m * LANES : (m + 1) * LANES]
                        near_im = near[rows, width + m * LANES : width + (m + 1) * LANES]
                        turned.append(
                            [
                                pltpu.roll(probe_re * near_re + probe_im * near_im, shifts[n], 1),
                                pltpu.roll(probe_re * near_im - probe_im * near_re, shifts[n], 1),
                            ]
                        )
                    for m in range(wide + 1):
                        for c in range(2):
                            behind = turned[m - 1][c] if m > 0 else 0.0
                            ahead = turned[m][c] if m < wide else 0.0
                            here = (c, rows, pl.ds(starts[n][m], LANES))
                            acc_ref[here] += jnp.where(past, ahead, behind)


def exit_first_kernel(tiles, meta_ref, probe_ref, forward_ref, inverse_ref, sino_ref, *refs):
    amp_refs, refs = refs[:tiles], refs[tiles:]
    partial_ref, grad_ref, spill_ref, acc_ref, *scratch = refs
    groups = sino_ref.shape[0]
    width = probe_ref.shape[1]
    done = sino_ref.shape[2] - width

    @pl.loop(0, groups)
    def _(g):
        rows = pl.ds(pl.multiple_of(g * GROUP, GROUP), GROUP)
        for c in range(2):
            acc_ref[c, rows, :] = jnp.zeros((GROUP, acc_ref.shape[2]), jnp.float32)

    add_slots(
        meta_ref, probe_ref, forward_ref, inverse_ref, sino_ref, acc_ref, amp_refs, scratch, 0
    )

    @pl.loop(0, groups)
    def _(g):
        rows = pl.ds(pl.multiple_of(g * GROUP, GROUP), GROUP)
        whole = [acc_ref[c, rows, width:done] for c in range(2)]
        grad_ref[g] = jnp.concatenate(whole, axis=0).astype(jnp.bfloat16)
        for c in range(2):
            partial_ref[c, rows, :] = acc_ref[c, rows, :width]
            spill_ref[c, rows, :] = acc_ref[c, rows, done:]


def exit_rest_kernel(
    tiles, meta_ref, probe_ref, forward_ref, inverse_ref, early_ref, late_ref, partial_ref, spill_ref, *refs
):
    amp_refs, refs = refs[:tiles], refs[tiles:]
    out_ref, ext_ref, acc_ref, *scratch = refs
    groups = early_ref.shape[0]
    width = probe_ref.shape[1]
    done = width + late_ref.shape[2]

    @pl.loop(0, groups)
    def _(g):
        ext_ref[g, :, :width] = early_ref[g, :, early_ref.shape[2] - width :]
        ext_ref[g, :, width:done] = late_ref[g]
        ext_ref[g, :, done:] = early_ref[g, :, :width]
        rows = pl.ds(pl.multiple_of(g * GROUP, GROUP), GROUP)
        for c in range(2):
            acc_ref[c, rows, :width] = spill_ref[c, rows, :]
            acc_ref[c, rows, width:] = jnp.zeros((GROUP, done), jnp.float32)

    add_slots(
        meta_ref, probe_ref, forward_ref, inverse_ref, ext_ref, acc_ref, amp_refs, scratch,
        lax.axis_size("pos") - tiles,
    )

    @pl.loop(0, groups)
    def _(g):
        rows = pl.ds(pl.multiple_of(g * GROUP, GROUP), GROUP)
        here = [acc_ref[c, rows, :done] for c in range(2)]
        wrapped = [acc_ref[c, rows, done:] + partial_ref[c, rows, :] for c in range(2)]
        out_ref[g, :, :done] = jnp.concatenate(here, axis=0).astype(jnp.bfloat16)
        out_ref[g, :, done:] = jnp.concatenate(wrapped, axis=0).astype(jnp.bfloat16)


def exit_scratch(groups, width, reach):
    return [pltpu.VMEM((2, groups * GROUP, reach), jnp.float32)] + [
        pltpu.VMEM((2 * width, 2 * width), jnp.bfloat16)
    ] * 4


def exit_first(meta, probe_field, tables, sino, amps):
    groups, rows, reach = sino.shape
    width = probe_field.shape[1]
    slices = groups * GROUP
    edge = jax.ShapeDtypeStruct((2, slices, width), jnp.float32)
    grad = jax.ShapeDtypeStruct((groups, rows, reach - 2 * width), jnp.bfloat16)
    return pl.pallas_call(
        functools.partial(exit_first_kernel, len(amps)),
        out_shape=[edge, grad, edge],
        in_specs=[scalars] + [everywhere] * (4 + len(amps)),
        out_specs=[everywhere] * 3,
        scratch_shapes=exit_scratch(groups, width, reach),
        compiler_params=pltpu.CompilerParams(vmem_limit_bytes=60 * MEBI),
        cost_estimate=guess(10),
        name="exit_first",
    )(meta, probe_field, *tables, sino, *amps)


def exit_rest(meta, probe_field, tables, early, late, partial, spill, amps):
    groups, rows = late.shape[:2]
    width = probe_field.shape[1]
    reach = late.shape[2] + 2 * width
    return pl.pallas_call(
        functools.partial(exit_rest_kernel, len(amps)),
        out_shape=jax.ShapeDtypeStruct((groups, rows, reach), jnp.bfloat16),
        in_specs=[scalars] + [everywhere] * (7 + len(amps)),
        out_specs=everywhere,
        scratch_shapes=[pltpu.VMEM((groups, rows, reach), jnp.bfloat16)]
        + exit_scratch(groups, width, reach),
        compiler_params=pltpu.CompilerParams(vmem_limit_bytes=60 * MEBI),
        cost_estimate=guess(10),
        name="exit_rest",
    )(meta, probe_field, *tables, early, late, partial, spill, *amps)


def to_groups(received, own_slices):
    if own_slices == GROUP:
        return received
    devices, rows, columns = received.shape
    merge = GROUP // own_slices
    split = received.reshape(devices // merge, merge, 2, own_slices, columns)
    return split.transpose(0, 2, 1, 3, 4).reshape(devices // merge, ROWS, columns)


def from_groups(grouped, own_slices):
    if own_slices == GROUP:
        return grouped
    groups, rows, columns = grouped.shape
    merge = GROUP // own_slices
    split = grouped.reshape(groups, 2, merge, own_slices, columns)
    return split.transpose(0, 2, 1, 3, 4).reshape(groups * merge, 2 * own_slices, columns)


def pad_rows(block, own_slices):
    if own_slices == GROUP:
        return block
    lead, columns = block.shape[:-2], block.shape[-1]
    split = block.reshape(lead + (2, own_slices, columns))
    more = [(0, 0)] * (split.ndim - 2) + [(0, GROUP - own_slices), (0, 0)]
    return jnp.pad(split, more).reshape(lead + (ROWS, columns))


def cut_rows(block, own_slices):
    if own_slices == GROUP:
        return block
    lead, columns = block.shape[:-2], block.shape[-1]
    split = block.reshape(lead + (2, GROUP, columns))[..., :own_slices, :]
    return split.reshape(lead + (2 * own_slices, columns))


def everyone(chunk):
    return lax.all_to_all(chunk, ("ang", "pos"), 0, 0, tiled=True)


def on_device(volume, radon_tiles, tile_blocks, probe_field, amplitudes, offsets, counts):
    n_pos = lax.axis_size("pos")
    pos = lax.axis_index("pos")
    angles, det_blocks, feeds = tile_blocks.shape
    block_size = radon_tiles.shape[1]
    columns = det_blocks * block_size
    tile_width = columns // n_pos
    slab = volume.shape[1]
    width = volume.shape[2]
    own = slab // n_pos
    rows = 2 * own
    blocks_each = width // block_size

    def slices_for(j):
        start = (pos + j) % n_pos * own
        return lax.dynamic_slice_in_dim(volume, start, own, 1).reshape(rows, width)

    vol_pieces = rotate_pos([slices_for(j) for j in range(n_pos)], 1)
    vol_pieces, amplitudes = lax.optimization_barrier((vol_pieces, amplitudes))
    amp_pieces = rotate_pos(
        [
            lax.dynamic_index_in_dim(amplitudes, (pos - j) % n_pos, 0, keepdims=False)
            for j in range(n_pos)
        ],
        -1,
    )

    owner = tile_blocks // blocks_each
    within = tile_blocks % blocks_each
    piece = (pos - owner) % n_pos
    crossed = (within + jnp.arange(feeds, dtype=jnp.int32)) % 2
    tiles_each = width // LANES

    def by_chunk(idx):
        idx = idx.reshape(angles // n_pos, n_pos, n_pos, det_blocks // n_pos * feeds)
        idx = jnp.stack([jnp.roll(idx[:, p], -p, axis=1) for p in range(n_pos)], axis=1)
        return idx.reshape(angles, det_blocks * feeds)

    tile_idx = by_chunk(crossed * (n_pos * tiles_each) + piece * tiles_each + within // 2)
    block_idx = by_chunk(piece * blocks_each + within)
    padded = [pad_rows(piece, own) for piece in vol_pieces]
    probe_width = probe_field.shape[1]
    tables = dft_tables(probe_width)
    half = n_pos // 2
    reach = (half * tile_width + probe_width) // block_size
    edge = probe_width // block_size
    early_blocks = list(range(reach))
    late_blocks = list(range(reach, det_blocks))
    first_blocks = list(range(edge, half * tile_width // block_size))
    rest_blocks = list(range(half * tile_width // block_size, det_blocks)) + list(range(edge))

    sino_early = project(tile_idx, radon_tiles, padded, early_blocks, "project_early")
    sino_early, padded, offsets, counts = lax.optimization_barrier(
        (sino_early, padded, offsets, counts)
    )
    meta = jnp.concatenate([offsets, counts], axis=1)
    meta = rotate_pos(
        [lax.dynamic_slice_in_dim(meta, (pos - j) % n_pos, 1, 0) for j in range(n_pos)], -1
    )
    meta = jnp.concatenate(meta, axis=0)
    padded, meta = lax.optimization_barrier((padded, meta))
    sino_late = project(tile_idx, radon_tiles, padded, late_blocks, "project_late")
    got_early = everyone(cut_rows(sino_early, own))
    got_late = everyone(cut_rows(sino_late, own))
    got_early, got_late = to_groups(got_early, own), to_groups(got_late, own)
    got_early, amp_pieces = lax.optimization_barrier((got_early, amp_pieces))
    partial, first_grad, spill = exit_first(meta, probe_field, tables, got_early, amp_pieces[:half])
    first_sent = first_grad
    rest_grad = exit_rest(
        meta, probe_field, tables, got_early, got_late, partial, spill, amp_pieces[half:]
    )
    back_first = everyone(from_groups(first_sent, own))
    rest_sent = rest_grad
    back_rest = everyone(from_groups(rest_sent, own))
    first_sum = back_project(
        block_idx, radon_tiles, pad_rows(back_first, own), first_blocks, None, n_pos, width, "back_first"
    )[0]
    wrapped = rest_grad.shape[2] - probe_width
    tile_pieces = [jnp.concatenate([rest_grad[:, :, wrapped:], first_grad[:, :, : tile_width - probe_width]], axis=2)]
    for j in range(1, n_pos):
        source, begin = (first_grad, j * tile_width - probe_width) if j < half else (rest_grad, (j - half) * tile_width)
        tile_pieces.append(source[:, :, begin : begin + tile_width])
    tile_pieces = rotate_pos(tile_pieces, 1)
    obj_pieces = back_project(
        block_idx, radon_tiles, pad_rows(back_rest, own), rest_blocks, first_sum, n_pos, width, "back_rest"
    )
    groups = rest_grad.shape[0]
    tile_pieces = [tile_pieces[-j % n_pos] for j in range(n_pos)]
    tile_pieces = [
        piece.reshape(groups, 2, GROUP, tile_width).transpose(1, 0, 2, 3).reshape(2, groups * GROUP, tile_width)
        for piece in tile_pieces
    ]
    proj_grad = jnp.stack(in_order(tile_pieces, -pos % n_pos), axis=2).astype(jnp.float32)
    obj_pieces = rotate_pos([cut_rows(piece, own) for piece in obj_pieces], -1)
    obj_pieces = [piece.reshape(2, own, width) for piece in in_order(obj_pieces, -pos % n_pos)]
    object_grad = jnp.concatenate(obj_pieces, axis=1).astype(jnp.float32)
    new_volume = volume.astype(jnp.float32) + step_size * object_grad
    return (new_volume, proj_grad)


def solution(mesh):
    in_specs = (
        P(None, "ang", "pos"),
        P(),
        P(),
        P(),
        P("ang", "pos", None, None),
        P("ang", "pos"),
        P("ang", "pos"),
    )
    out_specs = (P(None, "ang", "pos"), P(None, None, "ang", "pos"))
    return jax.shard_map(
        on_device, mesh=mesh, in_specs=in_specs, out_specs=out_specs, check_vma=False
    )
```

```python
import functools
import math

import jax
import jax.numpy as jnp
import numpy as np
from jax import lax
from jax.experimental import pallas as pl
from jax.experimental.pallas import tpu as pltpu
from jax.sharding import PartitionSpec as P

step_size = 0.1
LANES = 128
ROWS = 16
GROUP = 8
MEBI = 1024 * 1024
everywhere = pl.BlockSpec(memory_space=pltpu.VMEM)
scalars = pl.BlockSpec(memory_space=pltpu.SMEM)
CHAINS = 4
BATCH = 4


def dft_tables(width):
    index = np.arange(width)
    turn = 2.0 * math.pi / width * (index[:, None] * index[None, :] % width)
    cosine = jnp.asarray(np.cos(turn) / math.sqrt(width), jnp.bfloat16)
    sine_neg = jnp.asarray(-np.sin(turn) / math.sqrt(width), jnp.bfloat16)
    forward = jnp.block([[cosine, -sine_neg], [sine_neg, cosine]])
    inverse = jnp.block([[cosine, sine_neg], [-sine_neg, cosine]])
    return (forward, inverse)


def rotate_pos(pieces, sign):
    count = len(pieces)
    return [pieces[0]] + [
        lax.ppermute(pieces[j], "pos", [(i, (i + sign * j) % count) for i in range(count)])
        for j in range(1, count)
    ]


def in_order(pieces, first):
    count = len(pieces)
    bit = 1
    while bit < count:
        flip = (first & bit) != 0
        pieces = [jnp.where(flip, pieces[(k + bit) % count], pieces[k]) for k in range(count)]
        bit *= 2
    return pieces


def lower_half(shape):
    return lax.broadcasted_iota(jnp.int32, shape, len(shape) - 1) < LANES // 2


def swap_halves(tile):
    return pltpu.roll(tile, LANES // 2, 1)


def arrange(vol_refs, vv_ref):
    per_piece = vol_refs[0].shape[1] // LANES
    tiles = per_piece * len(vol_refs)
    batch = 16
    source = lax.broadcasted_iota(jnp.int32, (LANES, LANES), 0)
    target = lax.broadcasted_iota(jnp.int32, (LANES, LANES), 1)
    swap = ((source + LANES // 2) % LANES == target).astype(jnp.bfloat16)
    for k, vol_ref in enumerate(vol_refs):

        @pl.loop(0, per_piece // batch, unroll=2)
        def _(step):
            stack = []
            for i in range(batch):
                t = step * batch + i
                tile = vol_ref[:, pl.ds(pl.multiple_of(t * LANES, LANES), LANES)]
                vv_ref[k * per_piece + t] = tile
                stack.append(tile)
            swapped = jnp.dot(
                jnp.concatenate(stack, axis=0), swap, preferred_element_type=jnp.float32
            ).astype(jnp.bfloat16)
            for i in range(batch):
                t = step * batch + i
                vv_ref[tiles + k * per_piece + t] = swapped[i * ROWS : (i + 1) * ROWS]


def project_blocks(blocks, idx_ref, radon_ref, vv_ref, out_ref, lhs_refs):
    angles, span, twice = radon_ref.shape
    feeds = 2 * span // twice
    low = lower_half((ROWS, LANES))
    batch = lhs_refs[0].shape[0]

    def gather(start, lhs_ref):
        for n in range(batch):
            a = start + n
            for i, b in enumerate(blocks):
                row = i * ROWS
                for jp in range(feeds // 2):
                    at = b * feeds + 2 * jp
                    first = vv_ref[idx_ref[a, at]]
                    second = vv_ref[idx_ref[a, at + 1]]
                    lhs_ref[n, row : row + ROWS, jp * LANES : (jp + 1) * LANES] = jnp.where(
                        low, first, second
                    )

    def multiply(start, lhs_ref):
        for n in range(batch):
            a = start + n
            product = jnp.dot(lhs_ref[n], radon_ref[a], preferred_element_type=jnp.float32)
            for pair in range(len(blocks) // 2):
                row = 2 * pair * ROWS
                tile = jnp.where(
                    low, product[row : row + ROWS], product[row + ROWS : row + 2 * ROWS]
                )
                out_ref[a, :, pair * LANES : (pair + 1) * LANES] = tile.astype(jnp.bfloat16)

    gather(0, lhs_refs[0])

    @pl.loop(0, angles // (2 * batch))
    def _(step):
        start = step * 2 * batch
        multiply(start, lhs_refs[0])
        gather(start + batch, lhs_refs[1])
        multiply(start + batch, lhs_refs[1])
        gather(jnp.minimum(start + 2 * batch, angles - batch), lhs_refs[0])


def project_kernel(blocks, pieces, idx_ref, radon_ref, *refs):
    vol_refs = refs[:pieces]
    out_ref, vv_ref, *lhs_refs = refs[pieces:]
    arrange(vol_refs, vv_ref)
    project_blocks(blocks, idx_ref, radon_ref, vv_ref, out_ref, lhs_refs)


def guess(microseconds):
    return pl.CostEstimate(
        flops=int(microseconds * 1.15e9), bytes_accessed=int(microseconds * 1e5), transcendentals=0
    )


def project(idx, radon_twice, vol_pieces, blocks, name):
    angles, span, twice = radon_twice.shape
    block = twice // 2
    pieces = len(vol_pieces)
    tiles = pieces * vol_pieces[0].shape[1] // LANES
    out_shape = (angles, ROWS, len(blocks) * block)
    return pl.pallas_call(
        functools.partial(project_kernel, blocks, pieces),
        out_shape=jax.ShapeDtypeStruct(out_shape, jnp.bfloat16),
        in_specs=[scalars, everywhere] + [everywhere] * pieces,
        out_specs=everywhere,
        scratch_shapes=[pltpu.VMEM((2 * tiles, ROWS, LANES), jnp.bfloat16)]
        + [pltpu.VMEM((BATCH, len(blocks) * ROWS, span), jnp.bfloat16)] * 2,
        compiler_params=pltpu.CompilerParams(
            vmem_limit_bytes=14 * MEBI + 2 * radon_twice.size + 2 * math.prod(out_shape)
        ),
        cost_estimate=guess(4 + len(blocks) // 4),
        name=name,
    )(idx, radon_twice, *vol_pieces)


def back_project_kernel(blocks, has_start, outs, idx_ref, wide_hbm, grad_hbm, *refs):
    start_ref, refs = (refs[0], refs[1:]) if has_start else (None, refs)
    out_refs, refs = refs[:outs], refs[outs:]
    acc_refs, refs = refs[:CHAINS], refs[CHAINS:]
    wide_ref, grad_ref, wide_sems, grad_sems, *refs = refs
    contrib_refs = refs[:2]
    angles, both, span = wide_ref.shape
    pairs = len(blocks) // 2
    feeds = span // both
    coef_blocks = acc_refs[0].shape[0]
    low = lower_half((GROUP, LANES))

    def copies(step):
        here = pl.ds(step * CHAINS, CHAINS)
        return (
            pltpu.make_async_copy(wide_hbm.at[here], wide_ref.at[here], wide_sems.at[step]),
            pltpu.make_async_copy(grad_hbm.at[here], grad_ref.at[here], grad_sems.at[step]),
        )

    @pl.loop(0, angles // CHAINS)
    def _(step):
        for copy in copies(step):
            copy.start()

    if has_start:
        start_copy = pltpu.make_async_copy(start_ref, acc_refs[0], refs[2])
        start_copy.start()

    @pl.loop(0, coef_blocks, unroll=16)
    def _(t):
        for acc_ref in acc_refs[1:] if has_start else acc_refs:
            acc_ref[t] = jnp.zeros((GROUP, LANES), jnp.float32)

    def multiply(step, contrib_ref):
        for n in range(CHAINS):
            a = step * CHAINS + n
            lhs = []
            for pair in range(pairs):
                tile = grad_ref[a, :, pair * LANES : (pair + 1) * LANES].astype(jnp.float32)
                real, imag = tile[:GROUP], tile[GROUP:]
                even = jnp.where(low, real, swap_halves(imag))
                odd = jnp.where(low, swap_halves(real), imag)
                lhs.append(jnp.concatenate([even, odd], axis=0).astype(jnp.bfloat16))
            contrib_ref[n] = jnp.dot(
                jnp.concatenate(lhs, axis=0), wide_ref[a], preferred_element_type=jnp.float32
            )

    def arrived(step):
        for copy in copies(step):
            copy.wait()

    def scatter(start, contrib_ref):
        for i, b in enumerate(blocks):
            row = i * GROUP
            for j in range(feeds):
                for n in range(CHAINS):
                    tile = contrib_ref[n, row : row + GROUP, j * LANES : (j + 1) * LANES]
                    acc_refs[n][idx_ref[start + n, b * feeds + j]] += tile

    arrived(0)
    multiply(0, contrib_refs[0])
    if has_start:
        start_copy.wait()

    steps = angles // CHAINS

    @pl.loop(0, steps // 2)
    def _(half):
        step = 2 * half
        arrived(step + 1)
        multiply(step + 1, contrib_refs[1])
        scatter(step * CHAINS, contrib_refs[0])

        @pl.when(step + 2 < steps)
        def _():
            arrived(step + 2)

        multiply(jnp.minimum(step + 2, steps - 1), contrib_refs[0])
        scatter((step + 1) * CHAINS, contrib_refs[1])

    def total(t):
        sums = [acc_ref[t] for acc_ref in acc_refs]
        while len(sums) > 1:
            sums = [sums[i] + sums[i + 1] for i in range(0, len(sums), 2)]
        return sums[0]

    if outs == 1:

        @pl.loop(0, coef_blocks, unroll=16)
        def _(t):
            out_refs[0][t] = total(t)

    else:
        per_piece = out_refs[0].shape[1] // LANES
        for k, out_ref in enumerate(out_refs):

            @pl.loop(0, per_piece, unroll=16)
            def _(t):
                lanes = pl.ds(pl.multiple_of(t * LANES, LANES), LANES)
                even = total(2 * (k * per_piece + t))
                odd = total(2 * (k * per_piece + t) + 1)
                real = jnp.where(low, even, swap_halves(odd))
                imag = jnp.where(low, swap_halves(even), odd)
                out_ref[:, lanes] = jnp.concatenate([real, imag], axis=0).astype(out_ref.dtype)


def back_project(idx, radon_wide, grads, blocks, start, pieces, piece_width, name):
    angles, both, span = radon_wide.shape
    coef_blocks = pieces * piece_width // (both // 2)
    contrib = (CHAINS, len(blocks) * GROUP, span)
    has_start = start is not None
    if has_start:
        out_shape = [jax.ShapeDtypeStruct((ROWS, piece_width), jnp.bfloat16)] * pieces
    else:
        out_shape = [jax.ShapeDtypeStruct((coef_blocks, GROUP, LANES), jnp.float32)]
    operands = [idx, radon_wide, grads] + ([start] if has_start else [])
    return pl.pallas_call(
        functools.partial(back_project_kernel, blocks, has_start, len(out_shape)),
        out_shape=out_shape,
        in_specs=[scalars] + [pl.BlockSpec(memory_space=pl.ANY)] * (len(operands) - 1),
        out_specs=[everywhere] * len(out_shape),
        scratch_shapes=[pltpu.VMEM((coef_blocks, GROUP, LANES), jnp.float32)] * CHAINS
        + [pltpu.VMEM(radon_wide.shape, jnp.bfloat16), pltpu.VMEM(grads.shape, jnp.bfloat16)]
        + [pltpu.SemaphoreType.DMA((angles // CHAINS,))] * 2
        + [pltpu.VMEM(contrib, jnp.float32)] * 2
        + [pltpu.SemaphoreType.DMA] * has_start,
        compiler_params=pltpu.CompilerParams(vmem_limit_bytes=60 * MEBI),
        cost_estimate=guess(4 + len(blocks) // 4),
        name=name,
    )(*operands)


def add_slots(meta_ref, probe_ref, forward_ref, inverse_ref, ext_ref, acc_ref, amp_refs, scratch, first):
    wave_ref, half_ref, delta_ref, back_ref = scratch
    n_pos = lax.axis_size("pos")
    groups = ext_ref.shape[0]
    width = probe_ref.shape[1]
    slots = amp_refs[0].shape[0]
    tile_width = (acc_ref.shape[2] - width) // len(amp_refs)
    chunk = 4
    crows = chunk * GROUP
    chunks = groups // chunk
    wide = width // LANES
    lane_id = lax.broadcasted_iota(jnp.int32, (crows, LANES), 1)

    def product(left, right):
        return jnp.dot(left, right, preferred_element_type=jnp.float32)

    for tile, amp_ref in enumerate(amp_refs):
        order = first + tile
        tile_start = lax.rem(lax.axis_index("pos") + order, n_pos) * tile_width - tile * tile_width
        count = meta_ref[order, slots]

        @pl.loop(0, (count + 1) // 2)
        def _(step):
            shifts, starts, lives = [], [], []
            for n in range(2):
                offset = meta_ref[order, step * 2 + n] - tile_start
                shifts.append(offset % LANES)
                lane_tile = offset // LANES
                starts.append(
                    [pl.multiple_of((lane_tile + m) * LANES, LANES) for m in range(wide + 1)]
                )
                lives.append((step * 2 + n < count).astype(jnp.float32))
            for n in range(2):
                keep = lane_id < LANES - shifts[n]
                back_shift = (LANES - shifts[n]) % LANES
                for ch in range(chunks):
                    rows = slice(ch * crows, (ch + 1) * crows)
                    low_rows = slice(width + ch * crows, width + (ch + 1) * crows)
                    turned = []
                    for start in starts[n]:
                        both = ext_ref[ch * chunk : (ch + 1) * chunk, :, pl.ds(start, LANES)]
                        both = both.astype(jnp.float32)
                        turned.append(
                            [
                                pltpu.roll(
                                    both[:, c * GROUP : (c + 1) * GROUP].reshape(crows, LANES),
                                    back_shift,
                                    1,
                                )
                                for c in range(2)
                            ]
                        )
                    for m in range(wide):
                        lanes = slice(m * LANES, (m + 1) * LANES)
                        put = slice(n * width + m * LANES, n * width + (m + 1) * LANES)
                        patch_re = jnp.where(keep, turned[m][0], turned[m + 1][0])
                        patch_im = jnp.where(keep, turned[m][1], turned[m + 1][1])
                        probe_re = probe_ref[0, rows, lanes].astype(jnp.float32)
                        probe_im = probe_ref[1, rows, lanes].astype(jnp.float32)
                        wave_re = probe_re * patch_re - probe_im * patch_im
                        wave_im = probe_re * patch_im + probe_im * patch_re
                        wave_ref[rows, put] = wave_re.astype(jnp.bfloat16)
                        wave_ref[low_rows, put] = wave_im.astype(jnp.bfloat16)
                mine = slice(n * width, (n + 1) * width)
                half = product(forward_ref[...], wave_ref[:, mine]).astype(jnp.bfloat16)
                half_ref[mine, :width] = half[:width]
                half_ref[mine, width:] = half[width:]
            for n in range(2):
                mine = slice(n * width, (n + 1) * width)
                far = product(half_ref[mine, :], inverse_ref[...])
                for ch in range(chunks):
                    rows = slice(ch * crows, (ch + 1) * crows)
                    low_rows = slice(width + ch * crows, width + (ch + 1) * crows)
                    far_re, far_im = far[rows, :width], far[rows, width:]
                    power = far_re * far_re + far_im * far_im
                    amps = amp_ref[step * 2 + n, rows, :].astype(jnp.float32)
                    factor = amps * lax.rsqrt(jnp.maximum(power, 1.0)) - 1.0
                    delta_ref[rows, mine] = (far_re * factor).astype(jnp.bfloat16)
                    delta_ref[low_rows, mine] = (far_im * factor).astype(jnp.bfloat16)
                back = product(inverse_ref[...], delta_ref[:, mine]).astype(jnp.bfloat16)
                back_ref[mine, :width] = back[:width]
                back_ref[mine, width:] = back[width:]
            for n in range(2):
                mine = slice(n * width, (n + 1) * width)
                near = product(back_ref[mine, :], forward_ref[...])
                past = lane_id >= shifts[n]
                for ch in range(chunks):
                    rows = slice(ch * crows, (ch + 1) * crows)
                    turned = []
                    for m in range(wide):
                        lanes = slice(m * LANES, (m + 1) * LANES)
                        probe_re = probe_ref[0, rows, lanes].astype(jnp.float32) * lives[n]
                        probe_im = probe_ref[1, rows, lanes].astype(jnp.float32) * lives[n]
                        near_re = near[rows, m * LANES : (m + 1) * LANES]
                        near_im = near[rows, width + m * LANES : width + (m + 1) * LANES]
                        turned.append(
                            [
                                pltpu.roll(probe_re * near_re + probe_im * near_im, shifts[n], 1),
                                pltpu.roll(probe_re * near_im - probe_im * near_re, shifts[n], 1),
                            ]
                        )
                    for m in range(wide + 1):
                        for c in range(2):
                            behind = turned[m - 1][c] if m > 0 else 0.0
                            ahead = turned[m][c] if m < wide else 0.0
                            here = (c, rows, pl.ds(starts[n][m], LANES))
                            acc_ref[here] += jnp.where(past, ahead, behind)


def exit_first_kernel(tiles, meta_ref, probe_ref, forward_ref, inverse_ref, sino_ref, *refs):
    amp_refs, refs = refs[:tiles], refs[tiles:]
    partial_ref, grad_ref, spill_ref, acc_ref, *scratch = refs
    groups = sino_ref.shape[0]
    width = probe_ref.shape[1]
    done = sino_ref.shape[2] - width

    @pl.loop(0, groups)
    def _(g):
        rows = pl.ds(pl.multiple_of(g * GROUP, GROUP), GROUP)
        for c in range(2):
            acc_ref[c, rows, :] = jnp.zeros((GROUP, acc_ref.shape[2]), jnp.float32)

    add_slots(
        meta_ref, probe_ref, forward_ref, inverse_ref, sino_ref, acc_ref, amp_refs, scratch, 0
    )

    @pl.loop(0, groups)
    def _(g):
        rows = pl.ds(pl.multiple_of(g * GROUP, GROUP), GROUP)
        whole = [acc_ref[c, rows, width:done] for c in range(2)]
        grad_ref[g] = jnp.concatenate(whole, axis=0).astype(jnp.bfloat16)
        for c in range(2):
            partial_ref[c, rows, :] = acc_ref[c, rows, :width]
            spill_ref[c, rows, :] = acc_ref[c, rows, done:]


def exit_rest_kernel(
    tiles, meta_ref, probe_ref, forward_ref, inverse_ref, early_ref, late_ref, partial_ref, spill_ref, *refs
):
    amp_refs, refs = refs[:tiles], refs[tiles:]
    out_ref, ext_ref, acc_ref, *scratch = refs
    groups = early_ref.shape[0]
    width = probe_ref.shape[1]
    done = width + late_ref.shape[2]

    @pl.loop(0, groups)
    def _(g):
        ext_ref[g, :, :width] = early_ref[g, :, early_ref.shape[2] - width :]
        ext_ref[g, :, width:done] = late_ref[g]
        ext_ref[g, :, done:] = early_ref[g, :, :width]
        rows = pl.ds(pl.multiple_of(g * GROUP, GROUP), GROUP)
        for c in range(2):
            acc_ref[c, rows, :width] = spill_ref[c, rows, :]
            acc_ref[c, rows, width:] = jnp.zeros((GROUP, done), jnp.float32)

    add_slots(
        meta_ref, probe_ref, forward_ref, inverse_ref, ext_ref, acc_ref, amp_refs, scratch,
        lax.axis_size("pos") - tiles,
    )

    @pl.loop(0, groups)
    def _(g):
        rows = pl.ds(pl.multiple_of(g * GROUP, GROUP), GROUP)
        here = [acc_ref[c, rows, :done] for c in range(2)]
        wrapped = [acc_ref[c, rows, done:] + partial_ref[c, rows, :] for c in range(2)]
        out_ref[g, :, :done] = jnp.concatenate(here, axis=0).astype(jnp.bfloat16)
        out_ref[g, :, done:] = jnp.concatenate(wrapped, axis=0).astype(jnp.bfloat16)


def exit_scratch(groups, width, reach):
    return [pltpu.VMEM((2, groups * GROUP, reach), jnp.float32)] + [
        pltpu.VMEM((2 * width, 2 * width), jnp.bfloat16)
    ] * 4


def exit_first(meta, probe_field, tables, sino, amps):
    groups, rows, reach = sino.shape
    width = probe_field.shape[1]
    slices = groups * GROUP
    edge = jax.ShapeDtypeStruct((2, slices, width), jnp.float32)
    grad = jax.ShapeDtypeStruct((groups, rows, reach - 2 * width), jnp.bfloat16)
    return pl.pallas_call(
        functools.partial(exit_first_kernel, len(amps)),
        out_shape=[edge, grad, edge],
        in_specs=[scalars] + [everywhere] * (4 + len(amps)),
        out_specs=[everywhere] * 3,
        scratch_shapes=exit_scratch(groups, width, reach),
        compiler_params=pltpu.CompilerParams(vmem_limit_bytes=60 * MEBI),
        cost_estimate=guess(10),
        name="exit_first",
    )(meta, probe_field, *tables, sino, *amps)


def exit_rest(meta, probe_field, tables, early, late, partial, spill, amps):
    groups, rows = late.shape[:2]
    width = probe_field.shape[1]
    reach = late.shape[2] + 2 * width
    return pl.pallas_call(
        functools.partial(exit_rest_kernel, len(amps)),
        out_shape=jax.ShapeDtypeStruct((groups, rows, reach), jnp.bfloat16),
        in_specs=[scalars] + [everywhere] * (7 + len(amps)),
        out_specs=everywhere,
        scratch_shapes=[pltpu.VMEM((groups, rows, reach), jnp.bfloat16)]
        + exit_scratch(groups, width, reach),
        compiler_params=pltpu.CompilerParams(vmem_limit_bytes=60 * MEBI),
        cost_estimate=guess(10),
        name="exit_rest",
    )(meta, probe_field, *tables, early, late, partial, spill, *amps)


def to_groups(received, own_slices):
    if own_slices == GROUP:
        return received
    devices, rows, columns = received.shape
    merge = GROUP // own_slices
    split = received.reshape(devices // merge, merge, 2, own_slices, columns)
    return split.transpose(0, 2, 1, 3, 4).reshape(devices // merge, ROWS, columns)


def from_groups(grouped, own_slices):
    if own_slices == GROUP:
        return grouped
    groups, rows, columns = grouped.shape
    merge = GROUP // own_slices
    split = grouped.reshape(groups, 2, merge, own_slices, columns)
    return split.transpose(0, 2, 1, 3, 4).reshape(groups * merge, 2 * own_slices, columns)


def pad_rows(block, own_slices):
    if own_slices == GROUP:
        return block
    lead, columns = block.shape[:-2], block.shape[-1]
    split = block.reshape(lead + (2, own_slices, columns))
    more = [(0, 0)] * (split.ndim - 2) + [(0, GROUP - own_slices), (0, 0)]
    return jnp.pad(split, more).reshape(lead + (ROWS, columns))


def cut_rows(block, own_slices):
    if own_slices == GROUP:
        return block
    lead, columns = block.shape[:-2], block.shape[-1]
    split = block.reshape(lead + (2, GROUP, columns))[..., :own_slices, :]
    return split.reshape(lead + (2 * own_slices, columns))


def everyone(chunk):
    return lax.all_to_all(chunk, ("ang", "pos"), 0, 0, tiled=True)


def on_device(volume, radon_tiles, tile_blocks, probe_field, amplitudes, offsets, counts):
    n_pos = lax.axis_size("pos")
    pos = lax.axis_index("pos")
    angles, det_blocks, feeds = tile_blocks.shape
    block_size = radon_tiles.shape[1]
    columns = det_blocks * block_size
    tile_width = columns // n_pos
    slab = volume.shape[1]
    width = volume.shape[2]
    own = slab // n_pos
    rows = 2 * own
    blocks_each = width // block_size

    def slices_for(j):
        start = (pos + j) % n_pos * own
        return lax.dynamic_slice_in_dim(volume, start, own, 1).reshape(rows, width)

    vol_pieces = rotate_pos([slices_for(j) for j in range(n_pos)], 1)
    vol_pieces, amplitudes = lax.optimization_barrier((vol_pieces, amplitudes))
    amp_pieces = rotate_pos(
        [
            lax.dynamic_index_in_dim(amplitudes, (pos - j) % n_pos, 0, keepdims=False)
            for j in range(n_pos)
        ],
        -1,
    )

    owner = tile_blocks // blocks_each
    within = tile_blocks % blocks_each
    piece = (pos - owner) % n_pos
    crossed = (within + jnp.arange(feeds, dtype=jnp.int32)) % 2
    tiles_each = width // LANES

    def by_chunk(idx):
        idx = idx.reshape(angles // n_pos, n_pos, n_pos, det_blocks // n_pos * feeds)
        idx = jnp.stack([jnp.roll(idx[:, p], -p, axis=1) for p in range(n_pos)], axis=1)
        return idx.reshape(angles, det_blocks * feeds)

    tile_idx = by_chunk(crossed * (n_pos * tiles_each) + piece * tiles_each + within // 2)
    block_idx = by_chunk(piece * blocks_each + within)
    padded = [pad_rows(piece, own) for piece in vol_pieces]
    turned = jnp.transpose(radon_tiles, (0, 2, 1))
    radon_twice = jnp.concatenate([turned, turned], axis=2)
    probe_width = probe_field.shape[1]
    tables = dft_tables(probe_width)
    half = n_pos // 2
    reach = (half * tile_width + probe_width) // block_size
    edge = probe_width // block_size
    early_blocks = list(range(reach))
    late_blocks = list(range(reach, det_blocks))
    first_blocks = list(range(edge, half * tile_width // block_size))
    rest_blocks = list(range(half * tile_width // block_size, det_blocks)) + list(range(edge))

    sino_early = project(tile_idx, radon_twice, padded, early_blocks, "project_early")
    sino_early, padded, offsets, counts = lax.optimization_barrier(
        (sino_early, padded, offsets, counts)
    )
    meta = jnp.concatenate([offsets, counts], axis=1)
    meta = rotate_pos(
        [lax.dynamic_slice_in_dim(meta, (pos - j) % n_pos, 1, 0) for j in range(n_pos)], -1
    )
    meta = jnp.concatenate(meta, axis=0)
    padded, meta = lax.optimization_barrier((padded, meta))
    sino_late = project(tile_idx, radon_twice, padded, late_blocks, "project_late")
    got_early = everyone(cut_rows(sino_early, own))
    sino_late, radon_tiles = lax.optimization_barrier((sino_late, radon_tiles))
    split = radon_tiles.reshape(angles, 1, block_size, feeds, 1, block_size)
    same = jnp.eye(2, dtype=jnp.bfloat16).reshape(1, 2, 1, 1, 2, 1)
    radon_wide = (split * same).reshape(angles, 2 * block_size, 2 * feeds * block_size)
    got_early, sino_late = lax.optimization_barrier((got_early, sino_late))
    got_late = everyone(cut_rows(sino_late, own))
    got_early, got_late = to_groups(got_early, own), to_groups(got_late, own)
    got_early, amp_pieces = lax.optimization_barrier((got_early, amp_pieces))
    partial, first_grad, spill = exit_first(meta, probe_field, tables, got_early, amp_pieces[:half])
    first_sent, got_late = lax.optimization_barrier((first_grad, got_late))
    rest_grad = exit_rest(
        meta, probe_field, tables, got_early, got_late, partial, spill, amp_pieces[half:]
    )
    back_first = everyone(from_groups(first_sent, own))
    back_first, rest_sent = lax.optimization_barrier((back_first, rest_grad))
    back_rest = everyone(from_groups(rest_sent, own))
    first_sum = back_project(
        block_idx, radon_wide, pad_rows(back_first, own), first_blocks, None, n_pos, width, "back_first"
    )[0]
    wrapped = rest_grad.shape[2] - probe_width
    tile_pieces = [jnp.concatenate([rest_grad[:, :, wrapped:], first_grad[:, :, : tile_width - probe_width]], axis=2)]
    for j in range(1, n_pos):
        source, begin = (first_grad, j * tile_width - probe_width) if j < half else (rest_grad, (j - half) * tile_width)
        tile_pieces.append(source[:, :, begin : begin + tile_width])
    tile_pieces = rotate_pos(tile_pieces, 1)
    obj_pieces = back_project(
        block_idx, radon_wide, pad_rows(back_rest, own), rest_blocks, first_sum, n_pos, width, "back_rest"
    )
    groups = rest_grad.shape[0]
    tile_pieces = [tile_pieces[-j % n_pos] for j in range(n_pos)]
    tile_pieces = [
        piece.reshape(groups, 2, GROUP, tile_width).transpose(1, 0, 2, 3).reshape(2, groups * GROUP, tile_width)
        for piece in tile_pieces
    ]
    proj_grad = jnp.stack(in_order(tile_pieces, -pos % n_pos), axis=2).astype(jnp.float32)
    obj_pieces = rotate_pos([cut_rows(piece, own) for piece in obj_pieces], -1)
    obj_pieces = [piece.reshape(2, own, width) for piece in in_order(obj_pieces, -pos % n_pos)]
    object_grad = jnp.concatenate(obj_pieces, axis=1).astype(jnp.float32)
    new_volume = volume.astype(jnp.float32) + step_size * object_grad
    return (new_volume, proj_grad)


def solution(mesh):
    in_specs = (
        P(None, "ang", "pos"),
        P(),
        P(),
        P(),
        P("ang", "pos", None, None),
        P("ang", "pos"),
        P("ang", "pos"),
    )
    out_specs = (P(None, "ang", "pos"), P(None, None, "ang", "pos"))
    return jax.shard_map(
        on_device, mesh=mesh, in_specs=in_specs, out_specs=out_specs, check_vma=False
    )
```

```python
import functools
import math

import jax
import jax.numpy as jnp
import numpy as np
from jax import lax
from jax.experimental import pallas as pl
from jax.experimental.pallas import tpu as pltpu
from jax.sharding import PartitionSpec as P

step_size = 0.1
LANES = 128
ROWS = 16
GROUP = 8
MEBI = 1024 * 1024
everywhere = pl.BlockSpec(memory_space=pltpu.VMEM)
anywhere = pl.BlockSpec(memory_space=pl.ANY)
scalars = pl.BlockSpec(memory_space=pltpu.SMEM)
CHAINS = 4
BATCH = 4


def dft_tables(width):
    index = np.arange(width)
    turn = 2.0 * math.pi / width * (index[:, None] * index[None, :] % width)
    cosine = jnp.asarray(np.cos(turn) / math.sqrt(width), jnp.bfloat16)
    sine_neg = jnp.asarray(-np.sin(turn) / math.sqrt(width), jnp.bfloat16)
    forward = jnp.block([[cosine, -sine_neg], [sine_neg, cosine]])
    inverse = jnp.block([[cosine, sine_neg], [-sine_neg, cosine]])
    return (forward, inverse)


def rotate_pos(pieces, sign):
    count = len(pieces)
    return [pieces[0]] + [
        lax.ppermute(pieces[j], "pos", [(i, (i + sign * j) % count) for i in range(count)])
        for j in range(1, count)
    ]


def in_order(pieces, first):
    count = len(pieces)
    bit = 1
    while bit < count:
        flip = (first & bit) != 0
        pieces = [jnp.where(flip, pieces[(k + bit) % count], pieces[k]) for k in range(count)]
        bit *= 2
    return pieces


def lower_half(shape):
    return lax.broadcasted_iota(jnp.int32, shape, len(shape) - 1) < LANES // 2


def swap_halves(tile):
    return pltpu.roll(tile, LANES // 2, 1)


def arrange(vol_refs, vv_ref):
    per_piece = vol_refs[0].shape[1] // LANES
    tiles = per_piece * len(vol_refs)
    batch = 16
    source = lax.broadcasted_iota(jnp.int32, (LANES, LANES), 0)
    target = lax.broadcasted_iota(jnp.int32, (LANES, LANES), 1)
    swap = ((source + LANES // 2) % LANES == target).astype(jnp.bfloat16)
    for k, vol_ref in enumerate(vol_refs):

        @pl.loop(0, per_piece // batch, unroll=2)
        def _(step):
            stack = []
            for i in range(batch):
                t = step * batch + i
                tile = vol_ref[:, pl.ds(pl.multiple_of(t * LANES, LANES), LANES)]
                vv_ref[k * per_piece + t] = tile
                stack.append(tile)
            swapped = jnp.dot(
                jnp.concatenate(stack, axis=0), swap, preferred_element_type=jnp.float32
            ).astype(jnp.bfloat16)
            for i in range(batch):
                t = step * batch + i
                vv_ref[tiles + k * per_piece + t] = swapped[i * ROWS : (i + 1) * ROWS]


def project_blocks(blocks, idx_ref, radon_ref, vv_ref, out_hbm, out_ref, out_sems, lhs_refs):
    angles, block, span = radon_ref.shape
    feeds = span // block
    low = lower_half((ROWS, LANES))
    batch = lhs_refs[0].shape[0]

    def gather(start, lhs_ref):
        for n in range(batch):
            a = start + n
            for i, b in enumerate(blocks):
                row = i * ROWS
                for jp in range(feeds // 2):
                    at = b * feeds + 2 * jp
                    first = vv_ref[idx_ref[a, at]]
                    second = vv_ref[idx_ref[a, at + 1]]
                    lhs_ref[n, row : row + ROWS, jp * LANES : (jp + 1) * LANES] = jnp.where(
                        low, first, second
                    )

    def multiply(start, lhs_ref):
        for n in range(batch):
            a = start + n
            product = lax.dot_general(
                lhs_ref[n], radon_ref[a], (((1,), (1,)), ((), ())), preferred_element_type=jnp.float32
            )
            for pair in range(len(blocks) // 2):
                row = 2 * pair * ROWS
                tile = jnp.concatenate(
                    [product[row : row + ROWS], product[row + ROWS : row + 2 * ROWS]], axis=1
                )
                out_ref[a, :, pair * LANES : (pair + 1) * LANES] = tile.astype(jnp.bfloat16)

    def leave(step):
        here = pl.ds(step * 2 * batch, 2 * batch)
        return pltpu.make_async_copy(out_ref.at[here], out_hbm.at[here], out_sems.at[step])

    gather(0, lhs_refs[0])

    @pl.loop(0, angles // (2 * batch))
    def _(step):
        start = step * 2 * batch
        multiply(start, lhs_refs[0])
        gather(start + batch, lhs_refs[1])
        multiply(start + batch, lhs_refs[1])
        leave(step).start()
        gather(jnp.minimum(start + 2 * batch, angles - batch), lhs_refs[0])

    @pl.loop(0, angles // (2 * batch))
    def _(step):
        leave(step).wait()


def project_kernel(blocks, pieces, idx_ref, radon_ref, *refs):
    vol_refs = refs[:pieces]
    out_hbm, vv_ref, out_ref, out_sems, *lhs_refs = refs[pieces:]
    arrange(vol_refs, vv_ref)
    project_blocks(blocks, idx_ref, radon_ref, vv_ref, out_hbm, out_ref, out_sems, lhs_refs)


def guess(microseconds):
    return pl.CostEstimate(
        flops=int(microseconds * 1.15e9), bytes_accessed=int(microseconds * 1e5), transcendentals=0
    )


def project(idx, radon_tiles, vol_pieces, blocks, name):
    angles, block, span = radon_tiles.shape
    pieces = len(vol_pieces)
    tiles = pieces * vol_pieces[0].shape[1] // LANES
    out_shape = (angles, ROWS, len(blocks) * block)
    return pl.pallas_call(
        functools.partial(project_kernel, blocks, pieces),
        out_shape=jax.ShapeDtypeStruct(out_shape, jnp.bfloat16),
        in_specs=[scalars, everywhere] + [everywhere] * pieces,
        out_specs=anywhere,
        scratch_shapes=[pltpu.VMEM((2 * tiles, ROWS, LANES), jnp.bfloat16)]
        + [pltpu.VMEM(out_shape, jnp.bfloat16), pltpu.SemaphoreType.DMA((angles // (2 * BATCH),))]
        + [pltpu.VMEM((BATCH, len(blocks) * ROWS, span), jnp.bfloat16)] * 2,
        compiler_params=pltpu.CompilerParams(
            vmem_limit_bytes=14 * MEBI + 2 * radon_tiles.size + 2 * math.prod(out_shape)
        ),
        cost_estimate=guess(4 + len(blocks) // 4),
        name=name,
    )(idx, radon_tiles, *vol_pieces)


def back_project_kernel(blocks, has_start, outs, idx_ref, radon_hbm, grad_hbm, *refs):
    start_ref, refs = (refs[0], refs[1:]) if has_start else (None, refs)
    out_refs, refs = refs[:outs], refs[outs:]
    acc_refs, refs = refs[:CHAINS], refs[CHAINS:]
    radon_ref, grad_ref, radon_sems, grad_sems, w_ref, *refs = refs
    contrib_refs = refs[:2]
    angles, block, span = radon_ref.shape
    pairs = len(blocks) // 2
    feeds = span // block
    coef_blocks = acc_refs[0].shape[0]
    steps = angles // CHAINS

    def copies(step):
        here = pl.ds(step * CHAINS, CHAINS)
        return (
            pltpu.make_async_copy(radon_hbm.at[here], radon_ref.at[here], radon_sems.at[step]),
            pltpu.make_async_copy(grad_hbm.at[here], grad_ref.at[here], grad_sems.at[step]),
        )

    def arrived(step):
        for copy in copies(step):
            copy.wait()

    @pl.loop(0, steps)
    def _(step):
        for copy in copies(step):
            copy.start()

    if has_start:
        start_copy = pltpu.make_async_copy(start_ref, acc_refs[0], refs[2])
        start_copy.start()

    @pl.loop(0, coef_blocks, unroll=16)
    def _(t):
        for acc_ref in acc_refs[1:] if has_start else acc_refs:
            acc_ref[t] = jnp.zeros((GROUP, LANES), jnp.float32)

    low = lower_half((GROUP, LANES))
    low_rows = lower_half((block, LANES))

    def widen(slot, a):
        for jp in range(feeds // 2):
            tile = radon_ref[a, :, jp * LANES : (jp + 1) * LANES].astype(jnp.float32)
            turned = swap_halves(tile)
            for side, (first, second) in enumerate(((tile, turned), (turned, tile))):
                lanes = slice((2 * jp + side) * LANES, (2 * jp + side + 1) * LANES)
                w_ref[slot, :block, lanes] = jnp.where(low_rows, first, 0.0).astype(jnp.bfloat16)
                w_ref[slot, block:, lanes] = jnp.where(low_rows, 0.0, second).astype(jnp.bfloat16)

    def multiply(start, half, contrib_ref):
        for n in range(CHAINS):
            a = start + n
            widen(half * CHAINS + n, a)
            lhs = []
            for pair in range(pairs):
                tile = grad_ref[a, :, pair * LANES : (pair + 1) * LANES].astype(jnp.float32)
                real, imag = tile[:GROUP], tile[GROUP:]
                even = jnp.where(low, real, swap_halves(imag))
                odd = jnp.where(low, swap_halves(real), imag)
                lhs.append(jnp.concatenate([even, odd], axis=0).astype(jnp.bfloat16))
            contrib_ref[n] = jnp.dot(
                jnp.concatenate(lhs, axis=0),
                w_ref[half * CHAINS + n],
                preferred_element_type=jnp.float32,
            )

    def scatter(start, contrib_ref):
        for i, b in enumerate(blocks):
            row = i * GROUP
            for j in range(feeds):
                for n in range(CHAINS):
                    tile = contrib_ref[n, row : row + GROUP, j * LANES : (j + 1) * LANES]
                    acc_refs[n][idx_ref[start + n, b * feeds + j]] += tile

    arrived(0)
    multiply(0, 0, contrib_refs[0])
    if has_start:
        start_copy.wait()

    @pl.loop(0, steps // 2)
    def _(half):
        step = 2 * half
        start = step * CHAINS
        arrived(step + 1)
        multiply(start + CHAINS, 1, contrib_refs[1])
        scatter(start, contrib_refs[0])

        @pl.when(step + 2 < steps)
        def _():
            arrived(step + 2)

        multiply(jnp.minimum(start + 2 * CHAINS, angles - CHAINS), 0, contrib_refs[0])
        scatter(start + CHAINS, contrib_refs[1])

    def total(t):
        sums = [acc_ref[t] for acc_ref in acc_refs]
        while len(sums) > 1:
            sums = [sums[i] + sums[i + 1] for i in range(0, len(sums), 2)]
        return sums[0]

    if outs == 1:

        @pl.loop(0, coef_blocks, unroll=16)
        def _(t):
            out_refs[0][t] = total(t)

    else:
        per_piece = out_refs[0].shape[1] // LANES
        for k, out_ref in enumerate(out_refs):

            @pl.loop(0, per_piece, unroll=16)
            def _(t):
                lanes = pl.ds(pl.multiple_of(t * LANES, LANES), LANES)
                even = total(2 * (k * per_piece + t))
                odd = total(2 * (k * per_piece + t) + 1)
                real = jnp.where(low, even, swap_halves(odd))
                imag = jnp.where(low, swap_halves(even), odd)
                out_ref[:, lanes] = jnp.concatenate([real, imag], axis=0).astype(out_ref.dtype)


def back_project(idx, radon_tiles, grads, blocks, start, pieces, piece_width, name):
    angles, block, span = radon_tiles.shape
    coef_blocks = pieces * piece_width // block
    rows = len(blocks) * GROUP
    has_start = start is not None
    if has_start:
        out_shape = [jax.ShapeDtypeStruct((ROWS, piece_width), jnp.bfloat16)] * pieces
    else:
        out_shape = [jax.ShapeDtypeStruct((coef_blocks, GROUP, LANES), jnp.float32)]
    operands = [idx, radon_tiles, grads] + ([start] if has_start else [])
    return pl.pallas_call(
        functools.partial(back_project_kernel, blocks, has_start, len(out_shape)),
        out_shape=out_shape,
        in_specs=[scalars] + [anywhere] * (len(operands) - 1),
        out_specs=[everywhere] * len(out_shape),
        scratch_shapes=[pltpu.VMEM((coef_blocks, GROUP, LANES), jnp.float32)] * CHAINS
        + [pltpu.VMEM(radon_tiles.shape, jnp.bfloat16), pltpu.VMEM(grads.shape, jnp.bfloat16)]
        + [pltpu.SemaphoreType.DMA((angles // CHAINS,))] * 2
        + [pltpu.VMEM((2 * CHAINS, 2 * block, 2 * span), jnp.bfloat16)]
        + [pltpu.VMEM((CHAINS, rows, 2 * span), jnp.float32)] * 2
        + [pltpu.SemaphoreType.DMA] * has_start,
        compiler_params=pltpu.CompilerParams(vmem_limit_bytes=60 * MEBI),
        cost_estimate=guess(4 + len(blocks) // 4),
        name=name,
    )(*operands)


def add_slots(meta_ref, probe_ref, forward_ref, inverse_ref, ext_ref, acc_ref, amp_refs, scratch, first):
    wave_ref, half_ref, delta_ref, back_ref = scratch
    n_pos = lax.axis_size("pos")
    groups = ext_ref.shape[0]
    width = probe_ref.shape[1]
    slots = amp_refs[0].shape[0]
    tile_width = (acc_ref.shape[2] - width) // len(amp_refs)
    chunk = 4
    crows = chunk * GROUP
    chunks = groups // chunk
    wide = width // LANES
    lane_id = lax.broadcasted_iota(jnp.int32, (crows, LANES), 1)

    def product(left, right):
        return jnp.dot(left, right, preferred_element_type=jnp.float32)

    for tile, amp_ref in enumerate(amp_refs):
        order = first + tile
        tile_start = lax.rem(lax.axis_index("pos") + order, n_pos) * tile_width - tile * tile_width
        count = meta_ref[order, slots]

        @pl.loop(0, (count + 1) // 2)
        def _(step):
            shifts, starts, lives = [], [], []
            for n in range(2):
                offset = meta_ref[order, step * 2 + n] - tile_start
                shifts.append(offset % LANES)
                lane_tile = offset // LANES
                starts.append(
                    [pl.multiple_of((lane_tile + m) * LANES, LANES) for m in range(wide + 1)]
                )
                lives.append((step * 2 + n < count).astype(jnp.float32))
            for n in range(2):
                keep = lane_id < LANES - shifts[n]
                back_shift = (LANES - shifts[n]) % LANES
                for ch in range(chunks):
                    rows = slice(ch * crows, (ch + 1) * crows)
                    low_rows = slice(width + ch * crows, width + (ch + 1) * crows)
                    turned = []
                    for start in starts[n]:
                        both = ext_ref[ch * chunk : (ch + 1) * chunk, :, pl.ds(start, LANES)]
                        both = both.astype(jnp.float32)
                        turned.append(
                            [
                                pltpu.roll(
                                    both[:, c * GROUP : (c + 1) * GROUP].reshape(crows, LANES),
                                    back_shift,
                                    1,
                                )
                                for c in range(2)
                            ]
                        )
                    for m in range(wide):
                        lanes = slice(m * LANES, (m + 1) * LANES)
                        put = slice(n * width + m * LANES, n * width + (m + 1) * LANES)
                        patch_re = jnp.where(keep, turned[m][0], turned[m + 1][0])
                        patch_im = jnp.where(keep, turned[m][1], turned[m + 1][1])
                        probe_re = probe_ref[0, rows, lanes].astype(jnp.float32)
                        probe_im = probe_ref[1, rows, lanes].astype(jnp.float32)
                        wave_re = probe_re * patch_re - probe_im * patch_im
                        wave_im = probe_re * patch_im + probe_im * patch_re
                        wave_ref[rows, put] = wave_re.astype(jnp.bfloat16)
                        wave_ref[low_rows, put] = wave_im.astype(jnp.bfloat16)
                mine = slice(n * width, (n + 1) * width)
                half = product(forward_ref[...], wave_ref[:, mine]).astype(jnp.bfloat16)
                half_ref[mine, :width] = half[:width]
                half_ref[mine, width:] = half[width:]
            for n in range(2):
                mine = slice(n * width, (n + 1) * width)
                far = product(half_ref[mine, :], inverse_ref[...])
                for ch in range(chunks):
                    rows = slice(ch * crows, (ch + 1) * crows)
                    low_rows = slice(width + ch * crows, width + (ch + 1) * crows)
                    far_re, far_im = far[rows, :width], far[rows, width:]
                    power = far_re * far_re + far_im * far_im
                    amps = amp_ref[step * 2 + n, rows, :].astype(jnp.float32)
                    factor = amps * lax.rsqrt(jnp.maximum(power, 1.0)) - 1.0
                    delta_ref[rows, mine] = (far_re * factor).astype(jnp.bfloat16)
                    delta_ref[low_rows, mine] = (far_im * factor).astype(jnp.bfloat16)
                back = product(inverse_ref[...], delta_ref[:, mine]).astype(jnp.bfloat16)
                back_ref[mine, :width] = back[:width]
                back_ref[mine, width:] = back[width:]
            for n in range(2):
                mine = slice(n * width, (n + 1) * width)
                near = product(back_ref[mine, :], forward_ref[...])
                past = lane_id >= shifts[n]
                for ch in range(chunks):
                    rows = slice(ch * crows, (ch + 1) * crows)
                    turned = []
                    for m in range(wide):
                        lanes = slice(m * LANES, (m + 1) * LANES)
                        probe_re = probe_ref[0, rows, lanes].astype(jnp.float32) * lives[n]
                        probe_im = probe_ref[1, rows, lanes].astype(jnp.float32) * lives[n]
                        near_re = near[rows, m * LANES : (m + 1) * LANES]
                        near_im = near[rows, width + m * LANES : width + (m + 1) * LANES]
                        turned.append(
                            [
                                pltpu.roll(probe_re * near_re + probe_im * near_im, shifts[n], 1),
                                pltpu.roll(probe_re * near_im - probe_im * near_re, shifts[n], 1),
                            ]
                        )
                    for m in range(wide + 1):
                        for c in range(2):
                            behind = turned[m - 1][c] if m > 0 else 0.0
                            ahead = turned[m][c] if m < wide else 0.0
                            here = (c, rows, pl.ds(starts[n][m], LANES))
                            acc_ref[here] += jnp.where(past, ahead, behind)


def exit_first_kernel(tiles, meta_ref, probe_ref, forward_ref, inverse_ref, sino_ref, *refs):
    amp_refs, refs = refs[:tiles], refs[tiles:]
    partial_ref, grad_ref, spill_ref, acc_ref, *scratch = refs
    groups = sino_ref.shape[0]
    width = probe_ref.shape[1]
    done = sino_ref.shape[2] - width

    @pl.loop(0, groups)
    def _(g):
        rows = pl.ds(pl.multiple_of(g * GROUP, GROUP), GROUP)
        for c in range(2):
            acc_ref[c, rows, :] = jnp.zeros((GROUP, acc_ref.shape[2]), jnp.float32)

    add_slots(
        meta_ref, probe_ref, forward_ref, inverse_ref, sino_ref, acc_ref, amp_refs, scratch, 0
    )

    @pl.loop(0, groups)
    def _(g):
        rows = pl.ds(pl.multiple_of(g * GROUP, GROUP), GROUP)
        whole = [acc_ref[c, rows, width:done] for c in range(2)]
        grad_ref[g] = jnp.concatenate(whole, axis=0).astype(jnp.bfloat16)
        for c in range(2):
            partial_ref[c, rows, :] = acc_ref[c, rows, :width]
            spill_ref[c, rows, :] = acc_ref[c, rows, done:]


def exit_rest_kernel(
    tiles, meta_ref, probe_ref, forward_ref, inverse_ref, early_ref, late_ref, partial_ref, spill_ref, *refs
):
    amp_refs, refs = refs[:tiles], refs[tiles:]
    out_ref, ext_ref, acc_ref, *scratch = refs
    groups = early_ref.shape[0]
    width = probe_ref.shape[1]
    done = width + late_ref.shape[2]

    @pl.loop(0, groups)
    def _(g):
        ext_ref[g, :, :width] = early_ref[g, :, early_ref.shape[2] - width :]
        ext_ref[g, :, width:done] = late_ref[g]
        ext_ref[g, :, done:] = early_ref[g, :, :width]
        rows = pl.ds(pl.multiple_of(g * GROUP, GROUP), GROUP)
        for c in range(2):
            acc_ref[c, rows, :width] = spill_ref[c, rows, :]
            acc_ref[c, rows, width:] = jnp.zeros((GROUP, done), jnp.float32)

    add_slots(
        meta_ref, probe_ref, forward_ref, inverse_ref, ext_ref, acc_ref, amp_refs, scratch,
        lax.axis_size("pos") - tiles,
    )

    @pl.loop(0, groups)
    def _(g):
        rows = pl.ds(pl.multiple_of(g * GROUP, GROUP), GROUP)
        here = [acc_ref[c, rows, :done] for c in range(2)]
        wrapped = [acc_ref[c, rows, done:] + partial_ref[c, rows, :] for c in range(2)]
        out_ref[g, :, :done] = jnp.concatenate(here, axis=0).astype(jnp.bfloat16)
        out_ref[g, :, done:] = jnp.concatenate(wrapped, axis=0).astype(jnp.bfloat16)


def exit_scratch(groups, width, reach):
    return [pltpu.VMEM((2, groups * GROUP, reach), jnp.float32)] + [
        pltpu.VMEM((2 * width, 2 * width), jnp.bfloat16)
    ] * 4


def exit_first(meta, probe_field, tables, sino, amps):
    groups, rows, reach = sino.shape
    width = probe_field.shape[1]
    slices = groups * GROUP
    edge = jax.ShapeDtypeStruct((2, slices, width), jnp.float32)
    grad = jax.ShapeDtypeStruct((groups, rows, reach - 2 * width), jnp.bfloat16)
    return pl.pallas_call(
        functools.partial(exit_first_kernel, len(amps)),
        out_shape=[edge, grad, edge],
        in_specs=[scalars] + [everywhere] * (4 + len(amps)),
        out_specs=[everywhere] * 3,
        scratch_shapes=exit_scratch(groups, width, reach),
        compiler_params=pltpu.CompilerParams(vmem_limit_bytes=60 * MEBI),
        cost_estimate=guess(10),
        name="exit_first",
    )(meta, probe_field, *tables, sino, *amps)


def exit_rest(meta, probe_field, tables, early, late, partial, spill, amps):
    groups, rows = late.shape[:2]
    width = probe_field.shape[1]
    reach = late.shape[2] + 2 * width
    return pl.pallas_call(
        functools.partial(exit_rest_kernel, len(amps)),
        out_shape=jax.ShapeDtypeStruct((groups, rows, reach), jnp.bfloat16),
        in_specs=[scalars] + [everywhere] * (7 + len(amps)),
        out_specs=everywhere,
        scratch_shapes=[pltpu.VMEM((groups, rows, reach), jnp.bfloat16)]
        + exit_scratch(groups, width, reach),
        compiler_params=pltpu.CompilerParams(vmem_limit_bytes=60 * MEBI),
        cost_estimate=guess(10),
        name="exit_rest",
    )(meta, probe_field, *tables, early, late, partial, spill, *amps)


def to_groups(received, own_slices):
    if own_slices == GROUP:
        return received
    devices, rows, columns = received.shape
    merge = GROUP // own_slices
    split = received.reshape(devices // merge, merge, 2, own_slices, columns)
    return split.transpose(0, 2, 1, 3, 4).reshape(devices // merge, ROWS, columns)


def from_groups(grouped, own_slices):
    if own_slices == GROUP:
        return grouped
    groups, rows, columns = grouped.shape
    merge = GROUP // own_slices
    split = grouped.reshape(groups, 2, merge, own_slices, columns)
    return split.transpose(0, 2, 1, 3, 4).reshape(groups * merge, 2 * own_slices, columns)


def pad_rows(block, own_slices):
    if own_slices == GROUP:
        return block
    lead, columns = block.shape[:-2], block.shape[-1]
    split = block.reshape(lead + (2, own_slices, columns))
    more = [(0, 0)] * (split.ndim - 2) + [(0, GROUP - own_slices), (0, 0)]
    return jnp.pad(split, more).reshape(lead + (ROWS, columns))


def cut_rows(block, own_slices):
    if own_slices == GROUP:
        return block
    lead, columns = block.shape[:-2], block.shape[-1]
    split = block.reshape(lead + (2, GROUP, columns))[..., :own_slices, :]
    return split.reshape(lead + (2 * own_slices, columns))


def everyone(chunk):
    return lax.all_to_all(chunk, ("ang", "pos"), 0, 0, tiled=True)


def on_device(volume, radon_tiles, tile_blocks, probe_field, amplitudes, offsets, counts):
    n_pos = lax.axis_size("pos")
    pos = lax.axis_index("pos")
    angles, det_blocks, feeds = tile_blocks.shape
    block_size = radon_tiles.shape[1]
    columns = det_blocks * block_size
    tile_width = columns // n_pos
    slab = volume.shape[1]
    width = volume.shape[2]
    own = slab // n_pos
    rows = 2 * own
    blocks_each = width // block_size

    def slices_for(j):
        start = (pos + j) % n_pos * own
        return lax.dynamic_slice_in_dim(volume, start, own, 1).reshape(rows, width)

    vol_pieces = rotate_pos([slices_for(j) for j in range(n_pos)], 1)
    vol_pieces, amplitudes = lax.optimization_barrier((vol_pieces, amplitudes))
    amp_pieces = rotate_pos(
        [
            lax.dynamic_index_in_dim(amplitudes, (pos - j) % n_pos, 0, keepdims=False)
            for j in range(n_pos)
        ],
        -1,
    )

    owner = tile_blocks // blocks_each
    within = tile_blocks % blocks_each
    piece = (pos - owner) % n_pos
    crossed = (within + jnp.arange(feeds, dtype=jnp.int32)) % 2
    tiles_each = width // LANES

    def by_chunk(idx):
        idx = idx.reshape(angles // n_pos, n_pos, n_pos, det_blocks // n_pos * feeds)
        idx = jnp.stack([jnp.roll(idx[:, p], -p, axis=1) for p in range(n_pos)], axis=1)
        return idx.reshape(angles, det_blocks * feeds)

    tile_idx = by_chunk(crossed * (n_pos * tiles_each) + piece * tiles_each + within // 2)
    block_idx = by_chunk(piece * blocks_each + within)
    padded = [pad_rows(piece, own) for piece in vol_pieces]
    probe_width = probe_field.shape[1]
    tables = dft_tables(probe_width)
    half = n_pos // 2
    reach = (half * tile_width + probe_width) // block_size
    edge = probe_width // block_size
    early_blocks = list(range(reach))
    late_blocks = list(range(reach, det_blocks))
    first_blocks = list(range(edge, half * tile_width // block_size))
    rest_blocks = list(range(half * tile_width // block_size, det_blocks)) + list(range(edge))

    sino_early = project(tile_idx, radon_tiles, padded, early_blocks, "project_early")
    sino_early, padded, offsets, counts = lax.optimization_barrier(
        (sino_early, padded, offsets, counts)
    )
    meta = jnp.concatenate([offsets, counts], axis=1)
    meta = rotate_pos(
        [lax.dynamic_slice_in_dim(meta, (pos - j) % n_pos, 1, 0) for j in range(n_pos)], -1
    )
    meta = jnp.concatenate(meta, axis=0)
    padded, meta = lax.optimization_barrier((padded, meta))
    sino_late = project(tile_idx, radon_tiles, padded, late_blocks, "project_late")
    got_early = everyone(cut_rows(sino_early, own))
    got_early, sino_late = lax.optimization_barrier((got_early, sino_late))
    got_late = everyone(cut_rows(sino_late, own))
    got_early, got_late = to_groups(got_early, own), to_groups(got_late, own)
    got_early, amp_pieces = lax.optimization_barrier((got_early, amp_pieces))
    partial, first_grad, spill = exit_first(meta, probe_field, tables, got_early, amp_pieces[:half])
    first_sent, got_late = lax.optimization_barrier((first_grad, got_late))
    rest_grad = exit_rest(
        meta, probe_field, tables, got_early, got_late, partial, spill, amp_pieces[half:]
    )
    back_first = everyone(from_groups(first_sent, own))
    back_first, rest_sent = lax.optimization_barrier((back_first, rest_grad))
    back_rest = everyone(from_groups(rest_sent, own))
    first_sum = back_project(
        block_idx, radon_tiles, pad_rows(back_first, own), first_blocks, None, n_pos, width, "back_first"
    )[0]
    wrapped = rest_grad.shape[2] - probe_width
    tile_pieces = [jnp.concatenate([rest_grad[:, :, wrapped:], first_grad[:, :, : tile_width - probe_width]], axis=2)]
    for j in range(1, n_pos):
        source, begin = (first_grad, j * tile_width - probe_width) if j < half else (rest_grad, (j - half) * tile_width)
        tile_pieces.append(source[:, :, begin : begin + tile_width])
    tile_pieces = rotate_pos(tile_pieces, 1)
    obj_pieces = back_project(
        block_idx, radon_tiles, pad_rows(back_rest, own), rest_blocks, first_sum, n_pos, width, "back_rest"
    )
    groups = rest_grad.shape[0]
    tile_pieces = [tile_pieces[-j % n_pos] for j in range(n_pos)]
    tile_pieces = [
        piece.reshape(groups, 2, GROUP, tile_width).transpose(1, 0, 2, 3).reshape(2, groups * GROUP, tile_width)
        for piece in tile_pieces
    ]
    proj_grad = jnp.stack(in_order(tile_pieces, -pos % n_pos), axis=2).astype(jnp.float32)
    obj_pieces = rotate_pos([cut_rows(piece, own) for piece in obj_pieces], -1)
    obj_pieces = [piece.reshape(2, own, width) for piece in in_order(obj_pieces, -pos % n_pos)]
    object_grad = jnp.concatenate(obj_pieces, axis=1).astype(jnp.float32)
    new_volume = volume.astype(jnp.float32) + step_size * object_grad
    return (new_volume, proj_grad)


def solution(mesh):
    in_specs = (
        P(None, "ang", "pos"),
        P(),
        P(),
        P(),
        P("ang", "pos", None, None),
        P("ang", "pos"),
        P("ang", "pos"),
    )
    out_specs = (P(None, "ang", "pos"), P(None, None, "ang", "pos"))
    return jax.shard_map(
        on_device, mesh=mesh, in_specs=in_specs, out_specs=out_specs, check_vma=False
    )
```

```python
import functools
import math

import jax
import jax.numpy as jnp
import numpy as np
from jax import lax
from jax.experimental import pallas as pl
from jax.experimental.pallas import tpu as pltpu
from jax.sharding import PartitionSpec as P

step_size = 0.1
LANES = 128
ROWS = 16
GROUP = 8
MEBI = 1024 * 1024
everywhere = pl.BlockSpec(memory_space=pltpu.VMEM)
anywhere = pl.BlockSpec(memory_space=pl.ANY)
scalars = pl.BlockSpec(memory_space=pltpu.SMEM)
CHAINS = 4
BATCH = 4


def dft_tables(width):
    index = np.arange(width)
    turn = 2.0 * math.pi / width * (index[:, None] * index[None, :] % width)
    cosine = jnp.asarray(np.cos(turn) / math.sqrt(width), jnp.bfloat16)
    sine_neg = jnp.asarray(-np.sin(turn) / math.sqrt(width), jnp.bfloat16)
    forward = jnp.block([[cosine, -sine_neg], [sine_neg, cosine]])
    inverse = jnp.block([[cosine, sine_neg], [-sine_neg, cosine]])
    return (forward, inverse)


def rotate_pos(pieces, sign):
    count = len(pieces)
    return [pieces[0]] + [
        lax.ppermute(pieces[j], "pos", [(i, (i + sign * j) % count) for i in range(count)])
        for j in range(1, count)
    ]


def in_order(pieces, first):
    count = len(pieces)
    bit = 1
    while bit < count:
        flip = (first & bit) != 0
        pieces = [jnp.where(flip, pieces[(k + bit) % count], pieces[k]) for k in range(count)]
        bit *= 2
    return pieces


def lower_half(shape):
    return lax.broadcasted_iota(jnp.int32, shape, len(shape) - 1) < LANES // 2


def swap_halves(tile):
    return pltpu.roll(tile, LANES // 2, 1)


def arrange(vol_refs, vv_ref):
    per_piece = vol_refs[0].shape[1] // LANES
    tiles = per_piece * len(vol_refs)
    batch = 16
    source = lax.broadcasted_iota(jnp.int32, (LANES, LANES), 0)
    target = lax.broadcasted_iota(jnp.int32, (LANES, LANES), 1)
    swap = ((source + LANES // 2) % LANES == target).astype(jnp.bfloat16)
    for k, vol_ref in enumerate(vol_refs):

        @pl.loop(0, per_piece // batch, unroll=2)
        def _(step):
            stack = []
            for i in range(batch):
                t = step * batch + i
                tile = vol_ref[:, pl.ds(pl.multiple_of(t * LANES, LANES), LANES)]
                vv_ref[k * per_piece + t] = tile
                stack.append(tile)
            swapped = jnp.dot(
                jnp.concatenate(stack, axis=0), swap, preferred_element_type=jnp.float32
            ).astype(jnp.bfloat16)
            for i in range(batch):
                t = step * batch + i
                vv_ref[tiles + k * per_piece + t] = swapped[i * ROWS : (i + 1) * ROWS]


def project_blocks(blocks, idx_ref, radon_ref, vv_ref, out_hbm, out_ref, out_sems, lhs_refs):
    angles, block, span = radon_ref.shape
    feeds = span // block
    low = lower_half((ROWS, LANES))
    batch = lhs_refs[0].shape[0]

    def gather(start, lhs_ref):
        for n in range(batch):
            a = start + n
            for i, b in enumerate(blocks):
                row = i * ROWS
                for jp in range(feeds // 2):
                    at = b * feeds + 2 * jp
                    first = vv_ref[idx_ref[a, at]]
                    second = vv_ref[idx_ref[a, at + 1]]
                    lhs_ref[n, row : row + ROWS, jp * LANES : (jp + 1) * LANES] = jnp.where(
                        low, first, second
                    )

    def multiply(start, lhs_ref):
        for n in range(batch):
            a = start + n
            product = lax.dot_general(
                lhs_ref[n], radon_ref[a], (((1,), (1,)), ((), ())), preferred_element_type=jnp.float32
            )
            for pair in range(len(blocks) // 2):
                row = 2 * pair * ROWS
                tile = jnp.concatenate(
                    [product[row : row + ROWS], product[row + ROWS : row + 2 * ROWS]], axis=1
                )
                out_ref[a, :, pair * LANES : (pair + 1) * LANES] = tile.astype(jnp.bfloat16)

    def leave(step):
        here = pl.ds(step * 2 * batch, 2 * batch)
        return pltpu.make_async_copy(out_ref.at[here], out_hbm.at[here], out_sems.at[step])

    gather(0, lhs_refs[0])

    @pl.loop(0, angles // (2 * batch))
    def _(step):
        start = step * 2 * batch

        @pl.when(step > 0)
        def _():
            leave(step - 1).start()

        multiply(start, lhs_refs[0])
        gather(start + batch, lhs_refs[1])
        multiply(start + batch, lhs_refs[1])
        gather(jnp.minimum(start + 2 * batch, angles - batch), lhs_refs[0])

    leave(angles // (2 * batch) - 1).start()

    @pl.loop(0, angles // (2 * batch))
    def _(step):
        leave(step).wait()


def project_kernel(blocks, pieces, idx_ref, radon_ref, *refs):
    vol_refs = refs[:pieces]
    out_hbm, vv_ref, out_ref, out_sems, *lhs_refs = refs[pieces:]
    arrange(vol_refs, vv_ref)
    project_blocks(blocks, idx_ref, radon_ref, vv_ref, out_hbm, out_ref, out_sems, lhs_refs)


def guess(microseconds):
    return pl.CostEstimate(
        flops=int(microseconds * 1.15e9), bytes_accessed=int(microseconds * 1e5), transcendentals=0
    )


def project(idx, radon_tiles, vol_pieces, blocks, name):
    angles, block, span = radon_tiles.shape
    pieces = len(vol_pieces)
    tiles = pieces * vol_pieces[0].shape[1] // LANES
    out_shape = (angles, ROWS, len(blocks) * block)
    return pl.pallas_call(
        functools.partial(project_kernel, blocks, pieces),
        out_shape=jax.ShapeDtypeStruct(out_shape, jnp.bfloat16),
        in_specs=[scalars, everywhere] + [everywhere] * pieces,
        out_specs=anywhere,
        scratch_shapes=[pltpu.VMEM((2 * tiles, ROWS, LANES), jnp.bfloat16)]
        + [pltpu.VMEM(out_shape, jnp.bfloat16), pltpu.SemaphoreType.DMA((angles // (2 * BATCH),))]
        + [pltpu.VMEM((BATCH, len(blocks) * ROWS, span), jnp.bfloat16)] * 2,
        compiler_params=pltpu.CompilerParams(
            vmem_limit_bytes=14 * MEBI + 2 * radon_tiles.size + 2 * math.prod(out_shape)
        ),
        cost_estimate=guess(4 + len(blocks) // 4),
        name=name,
    )(idx, radon_tiles, *vol_pieces)


def back_project_kernel(blocks, has_start, outs, idx_ref, radon_hbm, grad_hbm, *refs):
    start_ref, refs = (refs[0], refs[1:]) if has_start else (None, refs)
    out_refs, refs = refs[:outs], refs[outs:]
    acc_refs, refs = refs[:CHAINS], refs[CHAINS:]
    radon_ref, grad_ref, radon_sem, grad_sem, w_ref, *refs = refs
    contrib_refs = refs[:2]
    angles, block, span = radon_ref.shape
    pairs = len(blocks) // 2
    feeds = span // block
    coef_blocks = acc_refs[0].shape[0]

    radon_copy = pltpu.make_async_copy(radon_hbm, radon_ref, radon_sem)
    grad_copy = pltpu.make_async_copy(grad_hbm, grad_ref, grad_sem)
    radon_copy.start()
    grad_copy.start()
    if has_start:
        start_copy = pltpu.make_async_copy(start_ref, acc_refs[0], refs[2])
        start_copy.start()

    @pl.loop(0, coef_blocks, unroll=16)
    def _(t):
        for acc_ref in acc_refs[1:] if has_start else acc_refs:
            acc_ref[t] = jnp.zeros((GROUP, LANES), jnp.float32)

    low = lower_half((GROUP, LANES))
    low_rows = lower_half((block, LANES))

    def widen(slot, a):
        for jp in range(feeds // 2):
            tile = radon_ref[a, :, jp * LANES : (jp + 1) * LANES].astype(jnp.float32)
            turned = swap_halves(tile)
            for side, (first, second) in enumerate(((tile, turned), (turned, tile))):
                lanes = slice((2 * jp + side) * LANES, (2 * jp + side + 1) * LANES)
                w_ref[slot, :block, lanes] = jnp.where(low_rows, first, 0.0).astype(jnp.bfloat16)
                w_ref[slot, block:, lanes] = jnp.where(low_rows, 0.0, second).astype(jnp.bfloat16)

    def multiply(start, half, contrib_ref):
        for n in range(CHAINS):
            a = start + n
            widen(half * CHAINS + n, a)
            lhs = [grad_ref[a, :, pair * LANES : (pair + 1) * LANES] for pair in range(pairs)]
            contrib_ref[n] = jnp.dot(
                jnp.concatenate(lhs, axis=0),
                w_ref[half * CHAINS + n],
                preferred_element_type=jnp.float32,
            )

    def scatter(start, contrib_ref):
        for i, b in enumerate(blocks):
            row = i * GROUP
            for j in range(feeds):
                for n in range(CHAINS):
                    tile = contrib_ref[n, row : row + GROUP, j * LANES : (j + 1) * LANES]
                    acc_refs[n][idx_ref[start + n, b * feeds + j]] += tile

    radon_copy.wait()
    grad_copy.wait()
    multiply(0, 0, contrib_refs[0])
    if has_start:
        start_copy.wait()

    @pl.loop(0, angles // (2 * CHAINS))
    def _(step):
        start = step * 2 * CHAINS
        multiply(start + CHAINS, 1, contrib_refs[1])
        scatter(start, contrib_refs[0])
        multiply(jnp.minimum(start + 2 * CHAINS, angles - CHAINS), 0, contrib_refs[0])
        scatter(start + CHAINS, contrib_refs[1])

    def total(t):
        sums = [acc_ref[t] for acc_ref in acc_refs]
        while len(sums) > 1:
            sums = [sums[i] + sums[i + 1] for i in range(0, len(sums), 2)]
        return sums[0]

    if outs == 1:

        @pl.loop(0, coef_blocks, unroll=16)
        def _(t):
            out_refs[0][t] = total(t)

    else:
        per_piece = out_refs[0].shape[1] // LANES
        for k, out_ref in enumerate(out_refs):

            @pl.loop(0, per_piece, unroll=16)
            def _(t):
                lanes = pl.ds(pl.multiple_of(t * LANES, LANES), LANES)
                even = total(2 * (k * per_piece + t))
                odd = total(2 * (k * per_piece + t) + 1)
                real = jnp.where(low, even, swap_halves(odd))
                imag = jnp.where(low, swap_halves(even), odd)
                out_ref[:, lanes] = jnp.concatenate([real, imag], axis=0).astype(out_ref.dtype)


def back_project(idx, radon_tiles, grads, blocks, start, pieces, piece_width, name):
    angles, block, span = radon_tiles.shape
    coef_blocks = pieces * piece_width // block
    rows = len(blocks) * GROUP
    has_start = start is not None
    if has_start:
        out_shape = [jax.ShapeDtypeStruct((ROWS, piece_width), jnp.bfloat16)] * pieces
    else:
        out_shape = [jax.ShapeDtypeStruct((coef_blocks, GROUP, LANES), jnp.float32)]
    operands = [idx, radon_tiles, grads] + ([start] if has_start else [])
    return pl.pallas_call(
        functools.partial(back_project_kernel, blocks, has_start, len(out_shape)),
        out_shape=out_shape,
        in_specs=[scalars] + [anywhere] * (len(operands) - 1),
        out_specs=[everywhere] * len(out_shape),
        scratch_shapes=[pltpu.VMEM((coef_blocks, GROUP, LANES), jnp.float32)] * CHAINS
        + [pltpu.VMEM(radon_tiles.shape, jnp.bfloat16), pltpu.VMEM(grads.shape, jnp.bfloat16)]
        + [pltpu.SemaphoreType.DMA] * 2
        + [pltpu.VMEM((2 * CHAINS, 2 * block, 2 * span), jnp.bfloat16)]
        + [pltpu.VMEM((CHAINS, rows, 2 * span), jnp.float32)] * 2
        + [pltpu.SemaphoreType.DMA] * has_start,
        compiler_params=pltpu.CompilerParams(vmem_limit_bytes=60 * MEBI),
        cost_estimate=guess(4 + len(blocks) // 4),
        name=name,
    )(*operands)


def add_slots(meta_ref, probe_ref, forward_ref, inverse_ref, ext_ref, acc_ref, amp_refs, scratch, first):
    wave_ref, half_ref, delta_ref, back_ref = scratch
    n_pos = lax.axis_size("pos")
    groups = ext_ref.shape[0]
    width = probe_ref.shape[1]
    slots = amp_refs[0].shape[0]
    tile_width = (acc_ref.shape[2] - width) // len(amp_refs)
    chunk = 4
    crows = chunk * GROUP
    chunks = groups // chunk
    wide = width // LANES
    lane_id = lax.broadcasted_iota(jnp.int32, (crows, LANES), 1)

    def product(left, right):
        return jnp.dot(left, right, preferred_element_type=jnp.float32)

    for tile, amp_ref in enumerate(amp_refs):
        order = first + tile
        tile_start = lax.rem(lax.axis_index("pos") + order, n_pos) * tile_width - tile * tile_width
        count = meta_ref[order, slots]

        @pl.loop(0, (count + 1) // 2)
        def _(step):
            shifts, starts, lives = [], [], []
            for n in range(2):
                offset = meta_ref[order, step * 2 + n] - tile_start
                shifts.append(offset % LANES)
                lane_tile = offset // LANES
                starts.append(
                    [pl.multiple_of((lane_tile + m) * LANES, LANES) for m in range(wide + 1)]
                )
                lives.append((step * 2 + n < count).astype(jnp.float32))
            for n in range(2):
                keep = lane_id < LANES - shifts[n]
                back_shift = (LANES - shifts[n]) % LANES
                for ch in range(chunks):
                    rows = slice(ch * crows, (ch + 1) * crows)
                    low_rows = slice(width + ch * crows, width + (ch + 1) * crows)
                    turned = []
                    for start in starts[n]:
                        both = ext_ref[ch * chunk : (ch + 1) * chunk, :, pl.ds(start, LANES)]
                        both = both.astype(jnp.float32)
                        turned.append(
                            [
                                pltpu.roll(
                                    both[:, c * GROUP : (c + 1) * GROUP].reshape(crows, LANES),
                                    back_shift,
                                    1,
                                )
                                for c in range(2)
                            ]
                        )
                    for m in range(wide):
                        lanes = slice(m * LANES, (m + 1) * LANES)
                        put = slice(n * width + m * LANES, n * width + (m + 1) * LANES)
                        patch_re = jnp.where(keep, turned[m][0], turned[m + 1][0])
                        patch_im = jnp.where(keep, turned[m][1], turned[m + 1][1])
                        probe_re = probe_ref[0, rows, lanes].astype(jnp.float32)
                        probe_im = probe_ref[1, rows, lanes].astype(jnp.float32)
                        wave_re = probe_re * patch_re - probe_im * patch_im
                        wave_im = probe_re * patch_im + probe_im * patch_re
                        wave_ref[rows, put] = wave_re.astype(jnp.bfloat16)
                        wave_ref[low_rows, put] = wave_im.astype(jnp.bfloat16)
                mine = slice(n * width, (n + 1) * width)
                half = product(forward_ref[...], wave_ref[:, mine]).astype(jnp.bfloat16)
                half_ref[mine, :width] = half[:width]
                half_ref[mine, width:] = half[width:]
            for n in range(2):
                mine = slice(n * width, (n + 1) * width)
                far = product(half_ref[mine, :], inverse_ref[...])
                for ch in range(chunks):
                    rows = slice(ch * crows, (ch + 1) * crows)
                    low_rows = slice(width + ch * crows, width + (ch + 1) * crows)
                    far_re, far_im = far[rows, :width], far[rows, width:]
                    power = far_re * far_re + far_im * far_im
                    amps = amp_ref[step * 2 + n, rows, :].astype(jnp.float32)
                    factor = amps * lax.rsqrt(jnp.maximum(power, 1.0)) - 1.0
                    delta_ref[rows, mine] = (far_re * factor).astype(jnp.bfloat16)
                    delta_ref[low_rows, mine] = (far_im * factor).astype(jnp.bfloat16)
                back = product(inverse_ref[...], delta_ref[:, mine]).astype(jnp.bfloat16)
                back_ref[mine, :width] = back[:width]
                back_ref[mine, width:] = back[width:]
            for n in range(2):
                mine = slice(n * width, (n + 1) * width)
                near = product(back_ref[mine, :], forward_ref[...])
                past = lane_id >= shifts[n]
                for ch in range(chunks):
                    rows = slice(ch * crows, (ch + 1) * crows)
                    turned = []
                    for m in range(wide):
                        lanes = slice(m * LANES, (m + 1) * LANES)
                        probe_re = probe_ref[0, rows, lanes].astype(jnp.float32) * lives[n]
                        probe_im = probe_ref[1, rows, lanes].astype(jnp.float32) * lives[n]
                        near_re = near[rows, m * LANES : (m + 1) * LANES]
                        near_im = near[rows, width + m * LANES : width + (m + 1) * LANES]
                        turned.append(
                            [
                                pltpu.roll(probe_re * near_re + probe_im * near_im, shifts[n], 1),
                                pltpu.roll(probe_re * near_im - probe_im * near_re, shifts[n], 1),
                            ]
                        )
                    for m in range(wide + 1):
                        for c in range(2):
                            behind = turned[m - 1][c] if m > 0 else 0.0
                            ahead = turned[m][c] if m < wide else 0.0
                            here = (c, rows, pl.ds(starts[n][m], LANES))
                            acc_ref[here] += jnp.where(past, ahead, behind)


def pack_blocks(packed_ref, g, real, imag, begin):
    low = lower_half((GROUP, LANES))
    for t in range(real.shape[1] // LANES):
        lanes = slice(t * LANES, (t + 1) * LANES)
        even = jnp.where(low, real[:, lanes], swap_halves(imag[:, lanes]))
        odd = jnp.where(low, swap_halves(real[:, lanes]), imag[:, lanes])
        put = slice(begin + t * LANES, begin + (t + 1) * LANES)
        packed_ref[g, :, put] = jnp.concatenate([even, odd], axis=0).astype(jnp.bfloat16)


def exit_first_kernel(tiles, meta_ref, probe_ref, forward_ref, inverse_ref, sino_ref, *refs):
    amp_refs, refs = refs[:tiles], refs[tiles:]
    partial_ref, grad_ref, packed_ref, spill_ref, acc_ref, *scratch = refs
    groups = sino_ref.shape[0]
    width = probe_ref.shape[1]
    done = sino_ref.shape[2] - width

    @pl.loop(0, groups)
    def _(g):
        rows = pl.ds(pl.multiple_of(g * GROUP, GROUP), GROUP)
        for c in range(2):
            acc_ref[c, rows, :] = jnp.zeros((GROUP, acc_ref.shape[2]), jnp.float32)

    add_slots(
        meta_ref, probe_ref, forward_ref, inverse_ref, sino_ref, acc_ref, amp_refs, scratch, 0
    )

    @pl.loop(0, groups)
    def _(g):
        rows = pl.ds(pl.multiple_of(g * GROUP, GROUP), GROUP)
        whole = [acc_ref[c, rows, width:done] for c in range(2)]
        grad_ref[g] = jnp.concatenate(whole, axis=0).astype(jnp.bfloat16)
        pack_blocks(packed_ref, g, *whole, 0)
        for c in range(2):
            partial_ref[c, rows, :] = acc_ref[c, rows, :width]
            spill_ref[c, rows, :] = acc_ref[c, rows, done:]


def exit_rest_kernel(
    tiles, meta_ref, probe_ref, forward_ref, inverse_ref, early_ref, late_ref, partial_ref, spill_ref, *refs
):
    amp_refs, refs = refs[:tiles], refs[tiles:]
    out_ref, packed_ref, ext_ref, acc_ref, *scratch = refs
    groups = early_ref.shape[0]
    width = probe_ref.shape[1]
    done = width + late_ref.shape[2]

    @pl.loop(0, groups)
    def _(g):
        ext_ref[g, :, :width] = early_ref[g, :, early_ref.shape[2] - width :]
        ext_ref[g, :, width:done] = late_ref[g]
        ext_ref[g, :, done:] = early_ref[g, :, :width]
        rows = pl.ds(pl.multiple_of(g * GROUP, GROUP), GROUP)
        for c in range(2):
            acc_ref[c, rows, :width] = spill_ref[c, rows, :]
            acc_ref[c, rows, width:] = jnp.zeros((GROUP, done), jnp.float32)

    add_slots(
        meta_ref, probe_ref, forward_ref, inverse_ref, ext_ref, acc_ref, amp_refs, scratch,
        lax.axis_size("pos") - tiles,
    )

    @pl.loop(0, groups)
    def _(g):
        rows = pl.ds(pl.multiple_of(g * GROUP, GROUP), GROUP)
        here = [acc_ref[c, rows, :done] for c in range(2)]
        wrapped = [acc_ref[c, rows, done:] + partial_ref[c, rows, :] for c in range(2)]
        out_ref[g, :, :done] = jnp.concatenate(here, axis=0).astype(jnp.bfloat16)
        out_ref[g, :, done:] = jnp.concatenate(wrapped, axis=0).astype(jnp.bfloat16)
        pack_blocks(packed_ref, g, *here, 0)
        pack_blocks(packed_ref, g, *wrapped, done)


def exit_scratch(groups, width, reach):
    return [pltpu.VMEM((2, groups * GROUP, reach), jnp.float32)] + [
        pltpu.VMEM((2 * width, 2 * width), jnp.bfloat16)
    ] * 4


def exit_first(meta, probe_field, tables, sino, amps):
    groups, rows, reach = sino.shape
    width = probe_field.shape[1]
    slices = groups * GROUP
    edge = jax.ShapeDtypeStruct((2, slices, width), jnp.float32)
    grad = jax.ShapeDtypeStruct((groups, rows, reach - 2 * width), jnp.bfloat16)
    return pl.pallas_call(
        functools.partial(exit_first_kernel, len(amps)),
        out_shape=[edge, grad, grad, edge],
        in_specs=[scalars] + [everywhere] * (4 + len(amps)),
        out_specs=[everywhere] * 4,
        scratch_shapes=exit_scratch(groups, width, reach),
        compiler_params=pltpu.CompilerParams(vmem_limit_bytes=60 * MEBI),
        cost_estimate=guess(10),
        name="exit_first",
    )(meta, probe_field, *tables, sino, *amps)


def exit_rest(meta, probe_field, tables, early, late, partial, spill, amps):
    groups, rows = late.shape[:2]
    width = probe_field.shape[1]
    reach = late.shape[2] + 2 * width
    return pl.pallas_call(
        functools.partial(exit_rest_kernel, len(amps)),
        out_shape=[jax.ShapeDtypeStruct((groups, rows, reach), jnp.bfloat16)] * 2,
        in_specs=[scalars] + [everywhere] * (7 + len(amps)),
        out_specs=[everywhere] * 2,
        scratch_shapes=[pltpu.VMEM((groups, rows, reach), jnp.bfloat16)]
        + exit_scratch(groups, width, reach),
        compiler_params=pltpu.CompilerParams(vmem_limit_bytes=60 * MEBI),
        cost_estimate=guess(10),
        name="exit_rest",
    )(meta, probe_field, *tables, early, late, partial, spill, *amps)


def to_groups(received, own_slices):
    if own_slices == GROUP:
        return received
    devices, rows, columns = received.shape
    merge = GROUP // own_slices
    split = received.reshape(devices // merge, merge, 2, own_slices, columns)
    return split.transpose(0, 2, 1, 3, 4).reshape(devices // merge, ROWS, columns)


def from_groups(grouped, own_slices):
    if own_slices == GROUP:
        return grouped
    groups, rows, columns = grouped.shape
    merge = GROUP // own_slices
    split = grouped.reshape(groups, 2, merge, own_slices, columns)
    return split.transpose(0, 2, 1, 3, 4).reshape(groups * merge, 2 * own_slices, columns)


def pad_rows(block, own_slices):
    if own_slices == GROUP:
        return block
    lead, columns = block.shape[:-2], block.shape[-1]
    split = block.reshape(lead + (2, own_slices, columns))
    more = [(0, 0)] * (split.ndim - 2) + [(0, GROUP - own_slices), (0, 0)]
    return jnp.pad(split, more).reshape(lead + (ROWS, columns))


def cut_rows(block, own_slices):
    if own_slices == GROUP:
        return block
    lead, columns = block.shape[:-2], block.shape[-1]
    split = block.reshape(lead + (2, GROUP, columns))[..., :own_slices, :]
    return split.reshape(lead + (2 * own_slices, columns))


def everyone(chunk):
    return lax.all_to_all(chunk, ("ang", "pos"), 0, 0, tiled=True)


def on_device(volume, radon_tiles, tile_blocks, probe_field, amplitudes, offsets, counts):
    n_pos = lax.axis_size("pos")
    pos = lax.axis_index("pos")
    angles, det_blocks, feeds = tile_blocks.shape
    block_size = radon_tiles.shape[1]
    columns = det_blocks * block_size
    tile_width = columns // n_pos
    slab = volume.shape[1]
    width = volume.shape[2]
    own = slab // n_pos
    rows = 2 * own
    blocks_each = width // block_size

    def slices_for(j):
        start = (pos + j) % n_pos * own
        return lax.dynamic_slice_in_dim(volume, start, own, 1).reshape(rows, width)

    vol_pieces = rotate_pos([slices_for(j) for j in range(n_pos)], 1)
    vol_pieces, amplitudes = lax.optimization_barrier((vol_pieces, amplitudes))
    amp_pieces = rotate_pos(
        [
            lax.dynamic_index_in_dim(amplitudes, (pos - j) % n_pos, 0, keepdims=False)
            for j in range(n_pos)
        ],
        -1,
    )

    owner = tile_blocks // blocks_each
    within = tile_blocks % blocks_each
    piece = (pos - owner) % n_pos
    crossed = (within + jnp.arange(feeds, dtype=jnp.int32)) % 2
    tiles_each = width // LANES

    def by_chunk(idx):
        idx = idx.reshape(angles // n_pos, n_pos, n_pos, det_blocks // n_pos * feeds)
        idx = jnp.stack([jnp.roll(idx[:, p], -p, axis=1) for p in range(n_pos)], axis=1)
        return idx.reshape(angles, det_blocks * feeds)

    tile_idx = by_chunk(crossed * (n_pos * tiles_each) + piece * tiles_each + within // 2)
    block_idx = by_chunk(piece * blocks_each + within)
    padded = [pad_rows(piece, own) for piece in vol_pieces]
    probe_width = probe_field.shape[1]
    tables = dft_tables(probe_width)
    half = n_pos // 2
    reach = (half * tile_width + probe_width) // block_size
    edge = probe_width // block_size
    early_blocks = list(range(reach))
    late_blocks = list(range(reach, det_blocks))
    first_blocks = list(range(edge, half * tile_width // block_size))
    rest_blocks = list(range(half * tile_width // block_size, det_blocks)) + list(range(edge))

    sino_early = project(tile_idx, radon_tiles, padded, early_blocks, "project_early")
    sino_early, padded, offsets, counts = lax.optimization_barrier(
        (sino_early, padded, offsets, counts)
    )
    meta = jnp.concatenate([offsets, counts], axis=1)
    meta = rotate_pos(
        [lax.dynamic_slice_in_dim(meta, (pos - j) % n_pos, 1, 0) for j in range(n_pos)], -1
    )
    meta = jnp.concatenate(meta, axis=0)
    padded, meta = lax.optimization_barrier((padded, meta))
    sino_late = project(tile_idx, radon_tiles, padded, late_blocks, "project_late")
    got_early = everyone(cut_rows(sino_early, own))
    got_early, sino_late = lax.optimization_barrier((got_early, sino_late))
    got_late = everyone(cut_rows(sino_late, own))
    got_early, got_late = to_groups(got_early, own), to_groups(got_late, own)
    got_early, amp_pieces = lax.optimization_barrier((got_early, amp_pieces))
    partial, first_grad, first_sent, spill = exit_first(meta, probe_field, tables, got_early, amp_pieces[:half])
    first_sent, got_late = lax.optimization_barrier((first_sent, got_late))
    rest_grad, rest_sent = exit_rest(
        meta, probe_field, tables, got_early, got_late, partial, spill, amp_pieces[half:]
    )
    back_first = everyone(from_groups(first_sent, own))
    back_first, rest_sent = lax.optimization_barrier((back_first, rest_sent))
    back_rest = everyone(from_groups(rest_sent, own))
    first_sum = back_project(
        block_idx, radon_tiles, pad_rows(back_first, own), first_blocks, None, n_pos, width, "back_first"
    )[0]
    wrapped = rest_grad.shape[2] - probe_width
    tile_pieces = [jnp.concatenate([rest_grad[:, :, wrapped:], first_grad[:, :, : tile_width - probe_width]], axis=2)]
    for j in range(1, n_pos):
        source, begin = (first_grad, j * tile_width - probe_width) if j < half else (rest_grad, (j - half) * tile_width)
        tile_pieces.append(source[:, :, begin : begin + tile_width])
    tile_pieces = rotate_pos(tile_pieces, 1)
    obj_pieces = back_project(
        block_idx, radon_tiles, pad_rows(back_rest, own), rest_blocks, first_sum, n_pos, width, "back_rest"
    )
    groups = rest_grad.shape[0]
    tile_pieces = [tile_pieces[-j % n_pos] for j in range(n_pos)]
    tile_pieces = [
        piece.reshape(groups, 2, GROUP, tile_width).transpose(1, 0, 2, 3).reshape(2, groups * GROUP, tile_width)
        for piece in tile_pieces
    ]
    proj_grad = jnp.stack(in_order(tile_pieces, -pos % n_pos), axis=2).astype(jnp.float32)
    obj_pieces = rotate_pos([cut_rows(piece, own) for piece in obj_pieces], -1)
    obj_pieces = [piece.reshape(2, own, width) for piece in in_order(obj_pieces, -pos % n_pos)]
    object_grad = jnp.concatenate(obj_pieces, axis=1).astype(jnp.float32)
    new_volume = volume.astype(jnp.float32) + step_size * object_grad
    return (new_volume, proj_grad)


def solution(mesh):
    in_specs = (
        P(None, "ang", "pos"),
        P(),
        P(),
        P(),
        P("ang", "pos", None, None),
        P("ang", "pos"),
        P("ang", "pos"),
    )
    out_specs = (P(None, "ang", "pos"), P(None, None, "ang", "pos"))
    return jax.shard_map(
        on_device, mesh=mesh, in_specs=in_specs, out_specs=out_specs, check_vma=False
    )
```

```python
import functools
import math

import jax
import jax.numpy as jnp
import numpy as np
from jax import lax
from jax.experimental import pallas as pl
from jax.experimental.pallas import tpu as pltpu
from jax.sharding import PartitionSpec as P

step_size = 0.1
LANES = 128
ROWS = 16
GROUP = 8
MEBI = 1024 * 1024
everywhere = pl.BlockSpec(memory_space=pltpu.VMEM)
anywhere = pl.BlockSpec(memory_space=pl.ANY)
scalars = pl.BlockSpec(memory_space=pltpu.SMEM)
CHAINS = 4
BATCH = 4


def dft_tables(width):
    index = np.arange(width)
    turn = 2.0 * math.pi / width * (index[:, None] * index[None, :] % width)
    cosine = jnp.asarray(np.cos(turn) / math.sqrt(width), jnp.bfloat16)
    sine_neg = jnp.asarray(-np.sin(turn) / math.sqrt(width), jnp.bfloat16)
    forward = jnp.block([[cosine, -sine_neg], [sine_neg, cosine]])
    inverse = jnp.block([[cosine, sine_neg], [-sine_neg, cosine]])
    return (forward, inverse)


def rotate_pos(pieces, sign):
    count = len(pieces)
    return [pieces[0]] + [
        lax.ppermute(pieces[j], "pos", [(i, (i + sign * j) % count) for i in range(count)])
        for j in range(1, count)
    ]


def in_order(pieces, first):
    count = len(pieces)
    bit = 1
    while bit < count:
        flip = (first & bit) != 0
        pieces = [jnp.where(flip, pieces[(k + bit) % count], pieces[k]) for k in range(count)]
        bit *= 2
    return pieces


def lower_half(shape):
    return lax.broadcasted_iota(jnp.int32, shape, len(shape) - 1) < LANES // 2


def swap_halves(tile):
    return pltpu.roll(tile, LANES // 2, 1)


def arrange(vol_refs, vv_ref):
    per_piece = vol_refs[0].shape[1] // LANES
    tiles = per_piece * len(vol_refs)
    batch = 16
    source = lax.broadcasted_iota(jnp.int32, (LANES, LANES), 0)
    target = lax.broadcasted_iota(jnp.int32, (LANES, LANES), 1)
    swap = ((source + LANES // 2) % LANES == target).astype(jnp.bfloat16)
    for k, vol_ref in enumerate(vol_refs):

        @pl.loop(0, per_piece // batch, unroll=2)
        def _(step):
            stack = []
            for i in range(batch):
                t = step * batch + i
                tile = vol_ref[:, pl.ds(pl.multiple_of(t * LANES, LANES), LANES)]
                vv_ref[k * per_piece + t] = tile
                stack.append(tile)
            swapped = jnp.dot(
                jnp.concatenate(stack, axis=0), swap, preferred_element_type=jnp.float32
            ).astype(jnp.bfloat16)
            for i in range(batch):
                t = step * batch + i
                vv_ref[tiles + k * per_piece + t] = swapped[i * ROWS : (i + 1) * ROWS]


def project_blocks(blocks, idx_ref, radon_ref, vv_ref, out_hbm, out_ref, out_sems, lhs_refs):
    angles, block, span = radon_ref.shape
    feeds = span // block
    low = lower_half((ROWS, LANES))
    batch = lhs_refs[0].shape[0]

    per_angle = idx_ref.shape[0] // angles

    def gather(start, lhs_ref):
        for n in range(batch):
            base = (start + n) * per_angle
            for i, b in enumerate(blocks):
                row = i * ROWS
                for jp in range(feeds // 2):
                    at = b * feeds + 2 * jp
                    first = vv_ref[idx_ref[base + at]]
                    second = vv_ref[idx_ref[base + at + 1]]
                    lhs_ref[n, row : row + ROWS, jp * LANES : (jp + 1) * LANES] = jnp.where(
                        low, first, second
                    )

    def multiply(start, lhs_ref):
        for n in range(batch):
            a = start + n
            product = lax.dot_general(
                lhs_ref[n], radon_ref[a], (((1,), (1,)), ((), ())), preferred_element_type=jnp.float32
            )
            for pair in range(len(blocks) // 2):
                row = 2 * pair * ROWS
                tile = jnp.concatenate(
                    [product[row : row + ROWS], product[row + ROWS : row + 2 * ROWS]], axis=1
                )
                out_ref[a, :, pair * LANES : (pair + 1) * LANES] = tile.astype(jnp.bfloat16)

    def leave(step):
        here = pl.ds(step * 2 * batch, 2 * batch)
        return pltpu.make_async_copy(out_ref.at[here], out_hbm.at[here], out_sems.at[step])

    gather(0, lhs_refs[0])

    @pl.loop(0, angles // (2 * batch))
    def _(step):
        start = step * 2 * batch

        @pl.when(step > 0)
        def _():
            leave(step - 1).start()

        multiply(start, lhs_refs[0])
        gather(start + batch, lhs_refs[1])
        multiply(start + batch, lhs_refs[1])
        gather(jnp.minimum(start + 2 * batch, angles - batch), lhs_refs[0])

    leave(angles // (2 * batch) - 1).start()

    @pl.loop(0, angles // (2 * batch))
    def _(step):
        leave(step).wait()


def project_kernel(blocks, pieces, idx_ref, radon_ref, *refs):
    vol_refs = refs[:pieces]
    out_hbm, vv_ref, out_ref, out_sems, *lhs_refs = refs[pieces:]
    arrange(vol_refs, vv_ref)
    project_blocks(blocks, idx_ref, radon_ref, vv_ref, out_hbm, out_ref, out_sems, lhs_refs)


def guess(microseconds):
    return pl.CostEstimate(
        flops=int(microseconds * 1.15e9), bytes_accessed=int(microseconds * 1e5), transcendentals=0
    )


def project(idx, radon_tiles, vol_pieces, blocks, name):
    angles, block, span = radon_tiles.shape
    pieces = len(vol_pieces)
    tiles = pieces * vol_pieces[0].shape[1] // LANES
    out_shape = (angles, ROWS, len(blocks) * block)
    return pl.pallas_call(
        functools.partial(project_kernel, blocks, pieces),
        out_shape=jax.ShapeDtypeStruct(out_shape, jnp.bfloat16),
        in_specs=[scalars, everywhere] + [everywhere] * pieces,
        out_specs=anywhere,
        scratch_shapes=[pltpu.VMEM((2 * tiles, ROWS, LANES), jnp.bfloat16)]
        + [pltpu.VMEM(out_shape, jnp.bfloat16), pltpu.SemaphoreType.DMA((angles // (2 * BATCH),))]
        + [pltpu.VMEM((BATCH, len(blocks) * ROWS, span), jnp.bfloat16)] * 2,
        compiler_params=pltpu.CompilerParams(
            vmem_limit_bytes=14 * MEBI + 2 * radon_tiles.size + 2 * math.prod(out_shape)
        ),
        cost_estimate=guess(4 + len(blocks) // 4),
        name=name,
    )(idx, radon_tiles, *vol_pieces)


def back_project_kernel(blocks, has_start, outs, idx_ref, radon_ref, grad_ref, *refs):
    start_ref, refs = (refs[0], refs[1:]) if has_start else (None, refs)
    out_refs, refs = refs[:outs], refs[outs:]
    acc_refs, (w_ref, *contrib_refs) = refs[:CHAINS], refs[CHAINS:]
    if has_start:
        contrib_refs, start_sem = contrib_refs[:-1], contrib_refs[-1]
        start_copy = pltpu.make_async_copy(start_ref, acc_refs[0], start_sem)
        start_copy.start()
    angles, block, span = radon_ref.shape
    pairs = len(blocks) // 2
    feeds = span // block
    coef_blocks = acc_refs[0].shape[0]

    @pl.loop(0, coef_blocks, unroll=16)
    def _(t):
        for acc_ref in acc_refs[1:] if has_start else acc_refs:
            acc_ref[t] = jnp.zeros((GROUP, LANES), jnp.float32)

    low = lower_half((GROUP, LANES))
    low_rows = lower_half((block, LANES))
    w_ref[...] = jnp.zeros_like(w_ref)

    def widen(slot, a):
        for jp in range(feeds // 2):
            tile = radon_ref[a, :, jp * LANES : (jp + 1) * LANES].astype(jnp.float32)
            turned = swap_halves(tile)
            for side, (first, second) in enumerate(((tile, turned), (turned, tile))):
                lanes = slice((2 * jp + side) * LANES, (2 * jp + side + 1) * LANES)
                w_ref[slot, :block, lanes] = jnp.where(low_rows, first, 0.0).astype(jnp.bfloat16)
                w_ref[slot, block:, lanes] = jnp.where(low_rows, 0.0, second).astype(jnp.bfloat16)

    def multiply(start, half, contrib_ref):
        for n in range(CHAINS):
            a = start + n
            widen(half * CHAINS + n, a)
            lhs = []
            for pair in range(pairs):
                tile = grad_ref[a, :, pair * LANES : (pair + 1) * LANES].astype(jnp.float32)
                real, imag = tile[:GROUP], tile[GROUP:]
                even = jnp.where(low, real, swap_halves(imag))
                odd = jnp.where(low, swap_halves(real), imag)
                lhs.append(jnp.concatenate([even, odd], axis=0).astype(jnp.bfloat16))
            contrib_ref[n] = jnp.dot(
                jnp.concatenate(lhs, axis=0),
                w_ref[half * CHAINS + n],
                preferred_element_type=jnp.float32,
            )

    per_angle = idx_ref.shape[0] // angles

    def scatter(start, contrib_ref):
        bases = [(start + n) * per_angle for n in range(CHAINS)]
        for i, b in enumerate(blocks):
            row = i * GROUP
            for j in range(feeds):
                for n in range(CHAINS):
                    tile = contrib_ref[n, row : row + GROUP, j * LANES : (j + 1) * LANES]
                    acc_refs[n][idx_ref[bases[n] + (b * feeds + j)]] += tile

    multiply(0, 0, contrib_refs[0])
    if has_start:
        start_copy.wait()

    @pl.loop(0, angles // (2 * CHAINS))
    def _(step):
        start = step * 2 * CHAINS
        multiply(start + CHAINS, 1, contrib_refs[1])
        scatter(start, contrib_refs[0])
        multiply(jnp.minimum(start + 2 * CHAINS, angles - CHAINS), 0, contrib_refs[0])
        scatter(start + CHAINS, contrib_refs[1])

    def total(t):
        sums = [acc_ref[t] for acc_ref in acc_refs]
        while len(sums) > 1:
            sums = [sums[i] + sums[i + 1] for i in range(0, len(sums), 2)]
        return sums[0]

    if outs == 1:

        @pl.loop(0, coef_blocks, unroll=16)
        def _(t):
            out_refs[0][t] = total(t)

    else:
        per_piece = out_refs[0].shape[1] // LANES
        for k, out_ref in enumerate(out_refs):

            @pl.loop(0, per_piece, unroll=16)
            def _(t):
                lanes = pl.ds(pl.multiple_of(t * LANES, LANES), LANES)
                even = total(2 * (k * per_piece + t))
                odd = total(2 * (k * per_piece + t) + 1)
                real = jnp.where(low, even, swap_halves(odd))
                imag = jnp.where(low, swap_halves(even), odd)
                out_ref[:, lanes] = jnp.concatenate([real, imag], axis=0).astype(out_ref.dtype)


def back_project(idx, radon_tiles, grads, blocks, start, pieces, piece_width, name):
    angles, block, span = radon_tiles.shape
    coef_blocks = pieces * piece_width // block
    rows = len(blocks) * GROUP
    has_start = start is not None
    if has_start:
        out_shape = [jax.ShapeDtypeStruct((ROWS, piece_width), jnp.bfloat16)] * pieces
    else:
        out_shape = [jax.ShapeDtypeStruct((coef_blocks, GROUP, LANES), jnp.float32)]
    operands = [idx, radon_tiles, grads] + ([start] if has_start else [])
    return pl.pallas_call(
        functools.partial(back_project_kernel, blocks, has_start, len(out_shape)),
        out_shape=out_shape,
        in_specs=[scalars] + [everywhere] * 2 + [pl.BlockSpec(memory_space=pl.ANY)] * has_start,
        out_specs=[everywhere] * len(out_shape),
        scratch_shapes=[pltpu.VMEM((coef_blocks, GROUP, LANES), jnp.float32)] * CHAINS
        + [pltpu.VMEM((2 * CHAINS, 2 * block, 2 * span), jnp.bfloat16)]
        + [pltpu.VMEM((CHAINS, rows, 2 * span), jnp.float32)] * 2
        + [pltpu.SemaphoreType.DMA] * has_start,
        compiler_params=pltpu.CompilerParams(vmem_limit_bytes=60 * MEBI),
        cost_estimate=guess(4 + len(blocks) // 4),
        name=name,
    )(*operands)


def add_slots(meta_ref, probe_ref, forward_ref, inverse_ref, ext_ref, acc_ref, amp_refs, scratch, first):
    wave_ref, half_ref, delta_ref, back_ref = scratch
    n_pos = lax.axis_size("pos")
    groups = ext_ref.shape[0]
    width = probe_ref.shape[1]
    slots = amp_refs[0].shape[0]
    tile_width = (acc_ref.shape[2] - width) // len(amp_refs)
    chunk = 4
    crows = chunk * GROUP
    chunks = groups // chunk
    wide = width // LANES
    lane_id = lax.broadcasted_iota(jnp.int32, (crows, LANES), 1)

    def product(left, right):
        return jnp.dot(left, right, preferred_element_type=jnp.float32)

    for tile, amp_ref in enumerate(amp_refs):
        order = first + tile
        tile_start = lax.rem(lax.axis_index("pos") + order, n_pos) * tile_width - tile * tile_width
        count = meta_ref[order, slots]

        @pl.loop(0, (count + 1) // 2)
        def _(step):
            shifts, starts, lives = [], [], []
            for n in range(2):
                offset = meta_ref[order, step * 2 + n] - tile_start
                shifts.append(offset % LANES)
                lane_tile = offset // LANES
                starts.append(
                    [pl.multiple_of((lane_tile + m) * LANES, LANES) for m in range(wide + 1)]
                )
                lives.append((step * 2 + n < count).astype(jnp.float32))
            for n in range(2):
                keep = lane_id < LANES - shifts[n]
                back_shift = (LANES - shifts[n]) % LANES
                for ch in range(chunks):
                    rows = slice(ch * crows, (ch + 1) * crows)
                    low_rows = slice(width + ch * crows, width + (ch + 1) * crows)
                    turned = []
                    for start in starts[n]:
                        both = ext_ref[ch * chunk : (ch + 1) * chunk, :, pl.ds(start, LANES)]
                        both = both.astype(jnp.float32)
                        turned.append(
                            [
                                pltpu.roll(
                                    both[:, c * GROUP : (c + 1) * GROUP].reshape(crows, LANES),
                                    back_shift,
                                    1,
                                )
                                for c in range(2)
                            ]
                        )
                    for m in range(wide):
                        lanes = slice(m * LANES, (m + 1) * LANES)
                        put = slice(n * width + m * LANES, n * width + (m + 1) * LANES)
                        patch_re = jnp.where(keep, turned[m][0], turned[m + 1][0])
                        patch_im = jnp.where(keep, turned[m][1], turned[m + 1][1])
                        probe_re = probe_ref[0, rows, lanes].astype(jnp.float32)
                        probe_im = probe_ref[1, rows, lanes].astype(jnp.float32)
                        wave_re = probe_re * patch_re - probe_im * patch_im
                        wave_im = probe_re * patch_im + probe_im * patch_re
                        wave_ref[rows, put] = wave_re.astype(jnp.bfloat16)
                        wave_ref[low_rows, put] = wave_im.astype(jnp.bfloat16)
                mine = slice(n * width, (n + 1) * width)
                half = product(forward_ref[...], wave_ref[:, mine]).astype(jnp.bfloat16)
                half_ref[mine, :width] = half[:width]
                half_ref[mine, width:] = half[width:]
            for n in range(2):
                mine = slice(n * width, (n + 1) * width)
                far = product(half_ref[mine, :], inverse_ref[...])
                for ch in range(chunks):
                    rows = slice(ch * crows, (ch + 1) * crows)
                    low_rows = slice(width + ch * crows, width + (ch + 1) * crows)
                    far_re, far_im = far[rows, :width], far[rows, width:]
                    power = far_re * far_re + far_im * far_im
                    amps = amp_ref[step * 2 + n, rows, :].astype(jnp.float32)
                    factor = amps * lax.rsqrt(jnp.maximum(power, 1.0)) - 1.0
                    delta_ref[rows, mine] = (far_re * factor).astype(jnp.bfloat16)
                    delta_ref[low_rows, mine] = (far_im * factor).astype(jnp.bfloat16)
                back = product(inverse_ref[...], delta_ref[:, mine]).astype(jnp.bfloat16)
                back_ref[mine, :width] = back[:width]
                back_ref[mine, width:] = back[width:]
            for n in range(2):
                mine = slice(n * width, (n + 1) * width)
                near = product(back_ref[mine, :], forward_ref[...])
                past = lane_id >= shifts[n]
                for ch in range(chunks):
                    rows = slice(ch * crows, (ch + 1) * crows)
                    turned = []
                    for m in range(wide):
                        lanes = slice(m * LANES, (m + 1) * LANES)
                        probe_re = probe_ref[0, rows, lanes].astype(jnp.float32) * lives[n]
                        probe_im = probe_ref[1, rows, lanes].astype(jnp.float32) * lives[n]
                        near_re = near[rows, m * LANES : (m + 1) * LANES]
                        near_im = near[rows, width + m * LANES : width + (m + 1) * LANES]
                        turned.append(
                            [
                                pltpu.roll(probe_re * near_re + probe_im * near_im, shifts[n], 1),
                                pltpu.roll(probe_re * near_im - probe_im * near_re, shifts[n], 1),
                            ]
                        )
                    for m in range(wide + 1):
                        for c in range(2):
                            behind = turned[m - 1][c] if m > 0 else 0.0
                            ahead = turned[m][c] if m < wide else 0.0
                            here = (c, rows, pl.ds(starts[n][m], LANES))
                            acc_ref[here] += jnp.where(past, ahead, behind)


def exit_first_kernel(tiles, meta_ref, probe_ref, forward_ref, inverse_ref, sino_ref, *refs):
    amp_refs, refs = refs[:tiles], refs[tiles:]
    partial_ref, grad_ref, spill_ref, acc_ref, *scratch = refs
    groups = sino_ref.shape[0]
    width = probe_ref.shape[1]
    done = sino_ref.shape[2] - width

    @pl.loop(0, groups)
    def _(g):
        rows = pl.ds(pl.multiple_of(g * GROUP, GROUP), GROUP)
        for c in range(2):
            acc_ref[c, rows, :] = jnp.zeros((GROUP, acc_ref.shape[2]), jnp.float32)

    add_slots(
        meta_ref, probe_ref, forward_ref, inverse_ref, sino_ref, acc_ref, amp_refs, scratch, 0
    )

    @pl.loop(0, groups)
    def _(g):
        rows = pl.ds(pl.multiple_of(g * GROUP, GROUP), GROUP)
        whole = [acc_ref[c, rows, width:done] for c in range(2)]
        grad_ref[g] = jnp.concatenate(whole, axis=0).astype(jnp.bfloat16)
        for c in range(2):
            partial_ref[c, rows, :] = acc_ref[c, rows, :width]
            spill_ref[c, rows, :] = acc_ref[c, rows, done:]


def exit_rest_kernel(
    tiles, meta_ref, probe_ref, forward_ref, inverse_ref, early_ref, late_ref, partial_ref, spill_ref, *refs
):
    amp_refs, refs = refs[:tiles], refs[tiles:]
    out_ref, ext_ref, acc_ref, *scratch = refs
    groups = early_ref.shape[0]
    width = probe_ref.shape[1]
    done = width + late_ref.shape[2]

    @pl.loop(0, groups)
    def _(g):
        ext_ref[g, :, :width] = early_ref[g, :, early_ref.shape[2] - width :]
        ext_ref[g, :, width:done] = late_ref[g]
        ext_ref[g, :, done:] = early_ref[g, :, :width]
        rows = pl.ds(pl.multiple_of(g * GROUP, GROUP), GROUP)
        for c in range(2):
            acc_ref[c, rows, :width] = spill_ref[c, rows, :]
            acc_ref[c, rows, width:] = jnp.zeros((GROUP, done), jnp.float32)

    add_slots(
        meta_ref, probe_ref, forward_ref, inverse_ref, ext_ref, acc_ref, amp_refs, scratch,
        lax.axis_size("pos") - tiles,
    )

    @pl.loop(0, groups)
    def _(g):
        rows = pl.ds(pl.multiple_of(g * GROUP, GROUP), GROUP)
        here = [acc_ref[c, rows, :done] for c in range(2)]
        wrapped = [acc_ref[c, rows, done:] + partial_ref[c, rows, :] for c in range(2)]
        out_ref[g, :, :done] = jnp.concatenate(here, axis=0).astype(jnp.bfloat16)
        out_ref[g, :, done:] = jnp.concatenate(wrapped, axis=0).astype(jnp.bfloat16)


def exit_scratch(groups, width, reach):
    return [pltpu.VMEM((2, groups * GROUP, reach), jnp.float32)] + [
        pltpu.VMEM((2 * width, 2 * width), jnp.bfloat16)
    ] * 4


def exit_first(meta, probe_field, tables, sino, amps):
    groups, rows, reach = sino.shape
    width = probe_field.shape[1]
    slices = groups * GROUP
    edge = jax.ShapeDtypeStruct((2, slices, width), jnp.float32)
    grad = jax.ShapeDtypeStruct((groups, rows, reach - 2 * width), jnp.bfloat16)
    return pl.pallas_call(
        functools.partial(exit_first_kernel, len(amps)),
        out_shape=[edge, grad, edge],
        in_specs=[scalars] + [everywhere] * (4 + len(amps)),
        out_specs=[everywhere] * 3,
        scratch_shapes=exit_scratch(groups, width, reach),
        compiler_params=pltpu.CompilerParams(vmem_limit_bytes=60 * MEBI),
        cost_estimate=guess(10),
        name="exit_first",
    )(meta, probe_field, *tables, sino, *amps)


def exit_rest(meta, probe_field, tables, early, late, partial, spill, amps):
    groups, rows = late.shape[:2]
    width = probe_field.shape[1]
    reach = late.shape[2] + 2 * width
    return pl.pallas_call(
        functools.partial(exit_rest_kernel, len(amps)),
        out_shape=jax.ShapeDtypeStruct((groups, rows, reach), jnp.bfloat16),
        in_specs=[scalars] + [everywhere] * (7 + len(amps)),
        out_specs=everywhere,
        scratch_shapes=[pltpu.VMEM((groups, rows, reach), jnp.bfloat16)]
        + exit_scratch(groups, width, reach),
        compiler_params=pltpu.CompilerParams(vmem_limit_bytes=60 * MEBI),
        cost_estimate=guess(10),
        name="exit_rest",
    )(meta, probe_field, *tables, early, late, partial, spill, *amps)


def to_groups(received, own_slices):
    if own_slices == GROUP:
        return received
    devices, rows, columns = received.shape
    merge = GROUP // own_slices
    split = received.reshape(devices // merge, merge, 2, own_slices, columns)
    return split.transpose(0, 2, 1, 3, 4).reshape(devices // merge, ROWS, columns)


def from_groups(grouped, own_slices):
    if own_slices == GROUP:
        return grouped
    groups, rows, columns = grouped.shape
    merge = GROUP // own_slices
    split = grouped.reshape(groups, 2, merge, own_slices, columns)
    return split.transpose(0, 2, 1, 3, 4).reshape(groups * merge, 2 * own_slices, columns)


def pad_rows(block, own_slices):
    if own_slices == GROUP:
        return block
    lead, columns = block.shape[:-2], block.shape[-1]
    split = block.reshape(lead + (2, own_slices, columns))
    more = [(0, 0)] * (split.ndim - 2) + [(0, GROUP - own_slices), (0, 0)]
    return jnp.pad(split, more).reshape(lead + (ROWS, columns))


def cut_rows(block, own_slices):
    if own_slices == GROUP:
        return block
    lead, columns = block.shape[:-2], block.shape[-1]
    split = block.reshape(lead + (2, GROUP, columns))[..., :own_slices, :]
    return split.reshape(lead + (2 * own_slices, columns))


def everyone(chunk):
    return lax.all_to_all(chunk, ("ang", "pos"), 0, 0, tiled=True)


def on_device(volume, radon_tiles, tile_blocks, probe_field, amplitudes, offsets, counts):
    n_pos = lax.axis_size("pos")
    pos = lax.axis_index("pos")
    angles, det_blocks, feeds = tile_blocks.shape
    block_size = radon_tiles.shape[1]
    columns = det_blocks * block_size
    tile_width = columns // n_pos
    slab = volume.shape[1]
    width = volume.shape[2]
    own = slab // n_pos
    rows = 2 * own
    blocks_each = width // block_size

    def slices_for(j):
        start = (pos + j) % n_pos * own
        return lax.dynamic_slice_in_dim(volume, start, own, 1).reshape(rows, width)

    vol_pieces = rotate_pos([slices_for(j) for j in range(n_pos)], 1)
    vol_pieces, amplitudes = lax.optimization_barrier((vol_pieces, amplitudes))
    amp_pieces = rotate_pos(
        [
            lax.dynamic_index_in_dim(amplitudes, (pos - j) % n_pos, 0, keepdims=False)
            for j in range(n_pos)
        ],
        -1,
    )

    owner = tile_blocks // blocks_each
    within = tile_blocks % blocks_each
    piece = (pos - owner) % n_pos
    crossed = (within + jnp.arange(feeds, dtype=jnp.int32)) % 2
    tiles_each = width // LANES

    def by_chunk(idx):
        idx = idx.reshape(angles // n_pos, n_pos, n_pos, det_blocks // n_pos * feeds)
        idx = jnp.stack([jnp.roll(idx[:, p], -p, axis=1) for p in range(n_pos)], axis=1)
        return idx.reshape(angles * det_blocks * feeds)

    tile_idx = by_chunk(crossed * (n_pos * tiles_each) + piece * tiles_each + within // 2)
    block_idx = by_chunk(piece * blocks_each + within)
    padded = [pad_rows(piece, own) for piece in vol_pieces]
    probe_width = probe_field.shape[1]
    tables = dft_tables(probe_width)
    half = n_pos // 2
    reach = (half * tile_width + probe_width) // block_size
    edge = probe_width // block_size
    early_blocks = list(range(reach))
    late_blocks = list(range(reach, det_blocks))
    first_blocks = list(range(edge, half * tile_width // block_size))
    rest_blocks = list(range(half * tile_width // block_size, det_blocks)) + list(range(edge))

    sino_early = project(tile_idx, radon_tiles, padded, early_blocks, "project_early")
    sino_early, padded, offsets, counts = lax.optimization_barrier(
        (sino_early, padded, offsets, counts)
    )
    meta = jnp.concatenate([offsets, counts], axis=1)
    meta = rotate_pos(
        [lax.dynamic_slice_in_dim(meta, (pos - j) % n_pos, 1, 0) for j in range(n_pos)], -1
    )
    meta = jnp.concatenate(meta, axis=0)
    padded, meta = lax.optimization_barrier((padded, meta))
    sino_late = project(tile_idx, radon_tiles, padded, late_blocks, "project_late")
    got_early = everyone(cut_rows(sino_early, own))
    got_early, sino_late = lax.optimization_barrier((got_early, sino_late))
    got_late = everyone(cut_rows(sino_late, own))
    got_early, got_late = to_groups(got_early, own), to_groups(got_late, own)
    got_early, amp_pieces = lax.optimization_barrier((got_early, amp_pieces))
    partial, first_grad, spill = exit_first(meta, probe_field, tables, got_early, amp_pieces[:half])
    first_sent, got_late = lax.optimization_barrier((first_grad, got_late))
    rest_grad = exit_rest(
        meta, probe_field, tables, got_early, got_late, partial, spill, amp_pieces[half:]
    )
    back_first = everyone(from_groups(first_sent, own))
    back_first, rest_sent = lax.optimization_barrier((back_first, rest_grad))
    back_rest = everyone(from_groups(rest_sent, own))
    first_sum = back_project(
        block_idx, radon_tiles, pad_rows(back_first, own), first_blocks, None, n_pos, width, "back_first"
    )[0]
    wrapped = rest_grad.shape[2] - probe_width
    tile_pieces = [jnp.concatenate([rest_grad[:, :, wrapped:], first_grad[:, :, : tile_width - probe_width]], axis=2)]
    for j in range(1, n_pos):
        source, begin = (first_grad, j * tile_width - probe_width) if j < half else (rest_grad, (j - half) * tile_width)
        tile_pieces.append(source[:, :, begin : begin + tile_width])
    tile_pieces = rotate_pos(tile_pieces, 1)
    obj_pieces = back_project(
        block_idx, radon_tiles, pad_rows(back_rest, own), rest_blocks, first_sum, n_pos, width, "back_rest"
    )
    groups = rest_grad.shape[0]
    tile_pieces = [tile_pieces[-j % n_pos] for j in range(n_pos)]
    tile_pieces = [
        piece.reshape(groups, 2, GROUP, tile_width).transpose(1, 0, 2, 3).reshape(2, groups * GROUP, tile_width)
        for piece in tile_pieces
    ]
    proj_grad = jnp.stack(in_order(tile_pieces, -pos % n_pos), axis=2).astype(jnp.float32)
    obj_pieces = rotate_pos([cut_rows(piece, own) for piece in obj_pieces], -1)
    obj_pieces = [piece.reshape(2, own, width) for piece in in_order(obj_pieces, -pos % n_pos)]
    object_grad = jnp.concatenate(obj_pieces, axis=1).astype(jnp.float32)
    new_volume = volume.astype(jnp.float32) + step_size * object_grad
    return (new_volume, proj_grad)


def solution(mesh):
    in_specs = (
        P(None, "ang", "pos"),
        P(),
        P(),
        P(),
        P("ang", "pos", None, None),
        P("ang", "pos"),
        P("ang", "pos"),
    )
    out_specs = (P(None, "ang", "pos"), P(None, None, "ang", "pos"))
    return jax.shard_map(
        on_device, mesh=mesh, in_specs=in_specs, out_specs=out_specs, check_vma=False
    )
```

```python
import functools
import math

import jax
import jax.numpy as jnp
import numpy as np
from jax import lax
from jax.experimental import pallas as pl
from jax.experimental.pallas import tpu as pltpu
from jax.sharding import PartitionSpec as P

step_size = 0.1
LANES = 128
ROWS = 16
GROUP = 8
MEBI = 1024 * 1024
everywhere = pl.BlockSpec(memory_space=pltpu.VMEM)
anywhere = pl.BlockSpec(memory_space=pl.ANY)
scalars = pl.BlockSpec(memory_space=pltpu.SMEM)
CHAINS = 4
BATCH = 4


def dft_tables(width):
    index = np.arange(width)
    turn = 2.0 * math.pi / width * (index[:, None] * index[None, :] % width)
    cosine = jnp.asarray(np.cos(turn) / math.sqrt(width), jnp.bfloat16)
    sine_neg = jnp.asarray(-np.sin(turn) / math.sqrt(width), jnp.bfloat16)
    forward = jnp.block([[cosine, -sine_neg], [sine_neg, cosine]])
    inverse = jnp.block([[cosine, sine_neg], [-sine_neg, cosine]])
    return (forward, inverse)


def rotate_pos(pieces, sign):
    count = len(pieces)
    return [pieces[0]] + [
        lax.ppermute(pieces[j], "pos", [(i, (i + sign * j) % count) for i in range(count)])
        for j in range(1, count)
    ]


def in_order(pieces, first):
    count = len(pieces)
    bit = 1
    while bit < count:
        flip = (first & bit) != 0
        pieces = [jnp.where(flip, pieces[(k + bit) % count], pieces[k]) for k in range(count)]
        bit *= 2
    return pieces


def lower_half(shape):
    return lax.broadcasted_iota(jnp.int32, shape, len(shape) - 1) < LANES // 2


def swap_halves(tile):
    return pltpu.roll(tile, LANES // 2, 1)


def arrange(vol_refs, vv_ref):
    per_piece = vol_refs[0].shape[1] // LANES
    tiles = per_piece * len(vol_refs)
    batch = 16
    source = lax.broadcasted_iota(jnp.int32, (LANES, LANES), 0)
    target = lax.broadcasted_iota(jnp.int32, (LANES, LANES), 1)
    swap = ((source + LANES // 2) % LANES == target).astype(jnp.bfloat16)
    for k, vol_ref in enumerate(vol_refs):

        @pl.loop(0, per_piece // batch, unroll=2)
        def _(step):
            stack = []
            for i in range(batch):
                t = step * batch + i
                tile = vol_ref[:, pl.ds(pl.multiple_of(t * LANES, LANES), LANES)]
                vv_ref[k * per_piece + t] = tile
                stack.append(tile)
            swapped = jnp.dot(
                jnp.concatenate(stack, axis=0), swap, preferred_element_type=jnp.float32
            ).astype(jnp.bfloat16)
            for i in range(batch):
                t = step * batch + i
                vv_ref[tiles + k * per_piece + t] = swapped[i * ROWS : (i + 1) * ROWS]


def project_blocks(blocks, idx_ref, radon_ref, vv_ref, out_hbm, out_ref, out_sems, lhs_refs):
    angles, block, span = radon_ref.shape
    feeds = span // block
    low = lower_half((ROWS, LANES))
    batch = lhs_refs[0].shape[0]

    per_angle = idx_ref.shape[0] // angles

    def gather(start, lhs_ref):
        for n in range(batch):
            base = (start + n) * per_angle
            for i, b in enumerate(blocks):
                row = i * ROWS
                for jp in range(feeds // 2):
                    at = b * feeds + 2 * jp
                    first = vv_ref[idx_ref[base + at]]
                    second = vv_ref[idx_ref[base + at + 1]]
                    lhs_ref[n, row : row + ROWS, jp * LANES : (jp + 1) * LANES] = jnp.where(
                        low, first, second
                    )

    def multiply(start, lhs_ref):
        per_half = len(blocks) // 4 * 2 * ROWS
        for n in range(batch):
            a = start + n
            for begin, end in ((0, per_half), (per_half, len(blocks) * ROWS)):
                product = lax.dot_general(
                    lhs_ref[n, begin:end, :],
                    radon_ref[a],
                    (((1,), (1,)), ((), ())),
                    preferred_element_type=jnp.float32,
                )
                for row in range(0, end - begin, 2 * ROWS):
                    tile = jnp.concatenate(
                        [product[row : row + ROWS], product[row + ROWS : row + 2 * ROWS]], axis=1
                    )
                    lane = (begin + row) // (2 * ROWS) * LANES
                    out_ref[a, :, lane : lane + LANES] = tile.astype(jnp.bfloat16)

    def leave(step):
        here = pl.ds(step * 2 * batch, 2 * batch)
        return pltpu.make_async_copy(out_ref.at[here], out_hbm.at[here], out_sems.at[step])

    gather(0, lhs_refs[0])

    @pl.loop(0, angles // (2 * batch))
    def _(step):
        start = step * 2 * batch

        @pl.when(step > 0)
        def _():
            leave(step - 1).start()

        multiply(start, lhs_refs[0])
        gather(start + batch, lhs_refs[1])
        multiply(start + batch, lhs_refs[1])
        gather(jnp.minimum(start + 2 * batch, angles - batch), lhs_refs[0])

    leave(angles // (2 * batch) - 1).start()

    @pl.loop(0, angles // (2 * batch))
    def _(step):
        leave(step).wait()


def project_kernel(blocks, pieces, idx_ref, radon_ref, *refs):
    vol_refs = refs[:pieces]
    out_hbm, vv_ref, out_ref, out_sems, *lhs_refs = refs[pieces:]
    arrange(vol_refs, vv_ref)
    project_blocks(blocks, idx_ref, radon_ref, vv_ref, out_hbm, out_ref, out_sems, lhs_refs)


def guess(microseconds):
    return pl.CostEstimate(
        flops=int(microseconds * 1.15e9), bytes_accessed=int(microseconds * 1e5), transcendentals=0
    )


def project(idx, radon_tiles, vol_pieces, blocks, name):
    angles, block, span = radon_tiles.shape
    pieces = len(vol_pieces)
    tiles = pieces * vol_pieces[0].shape[1] // LANES
    out_shape = (angles, ROWS, len(blocks) * block)
    return pl.pallas_call(
        functools.partial(project_kernel, blocks, pieces),
        out_shape=jax.ShapeDtypeStruct(out_shape, jnp.bfloat16),
        in_specs=[scalars, everywhere] + [everywhere] * pieces,
        out_specs=anywhere,
        scratch_shapes=[pltpu.VMEM((2 * tiles, ROWS, LANES), jnp.bfloat16)]
        + [pltpu.VMEM(out_shape, jnp.bfloat16), pltpu.SemaphoreType.DMA((angles // (2 * BATCH),))]
        + [pltpu.VMEM((BATCH, len(blocks) * ROWS, span), jnp.bfloat16)] * 2,
        compiler_params=pltpu.CompilerParams(
            vmem_limit_bytes=14 * MEBI + 2 * radon_tiles.size + 2 * math.prod(out_shape)
        ),
        cost_estimate=guess(4 + len(blocks) // 4),
        name=name,
    )(idx, radon_tiles, *vol_pieces)


def back_project_kernel(blocks, has_start, outs, idx_ref, radon_ref, grad_ref, *refs):
    start_ref, refs = (refs[0], refs[1:]) if has_start else (None, refs)
    out_refs, refs = refs[:outs], refs[outs:]
    acc_refs, (w_ref, *contrib_refs) = refs[:CHAINS], refs[CHAINS:]
    if has_start:
        contrib_refs, start_sem = contrib_refs[:-1], contrib_refs[-1]
        start_copy = pltpu.make_async_copy(start_ref, acc_refs[0], start_sem)
        start_copy.start()
    angles, block, span = radon_ref.shape
    pairs = len(blocks) // 2
    feeds = span // block
    coef_blocks = acc_refs[0].shape[0]

    @pl.loop(0, coef_blocks, unroll=16)
    def _(t):
        for acc_ref in acc_refs[1:] if has_start else acc_refs:
            acc_ref[t] = jnp.zeros((GROUP, LANES), jnp.float32)

    low = lower_half((GROUP, LANES))
    low_rows = lower_half((block, LANES))
    w_ref[...] = jnp.zeros_like(w_ref)

    def widen(slot, a):
        for jp in range(feeds // 2):
            tile = radon_ref[a, :, jp * LANES : (jp + 1) * LANES].astype(jnp.float32)
            turned = swap_halves(tile)
            for side, (first, second) in enumerate(((tile, turned), (turned, tile))):
                lanes = slice((2 * jp + side) * LANES, (2 * jp + side + 1) * LANES)
                w_ref[slot, :block, lanes] = jnp.where(low_rows, first, 0.0).astype(jnp.bfloat16)
                w_ref[slot, block:, lanes] = jnp.where(low_rows, 0.0, second).astype(jnp.bfloat16)

    def multiply(start, half, contrib_ref):
        for n in range(CHAINS):
            a = start + n
            widen(half * CHAINS + n, a)
            lhs = []
            for pair in range(pairs):
                tile = grad_ref[a, :, pair * LANES : (pair + 1) * LANES].astype(jnp.float32)
                real, imag = tile[:GROUP], tile[GROUP:]
                even = jnp.where(low, real, swap_halves(imag))
                odd = jnp.where(low, swap_halves(real), imag)
                lhs.append(jnp.concatenate([even, odd], axis=0).astype(jnp.bfloat16))
            lhs = jnp.concatenate(lhs, axis=0)
            for lanes in (slice(0, span), slice(span, 2 * span)):
                contrib_ref[n, :, lanes] = jnp.dot(
                    lhs, w_ref[half * CHAINS + n, :, lanes], preferred_element_type=jnp.float32
                )

    per_angle = idx_ref.shape[0] // angles

    def scatter(start, contrib_ref):
        bases = [(start + n) * per_angle for n in range(CHAINS)]
        for i, b in enumerate(blocks):
            row = i * GROUP
            for j in range(feeds):
                for n in range(CHAINS):
                    tile = contrib_ref[n, row : row + GROUP, j * LANES : (j + 1) * LANES]
                    acc_refs[n][idx_ref[bases[n] + (b * feeds + j)]] += tile

    multiply(0, 0, contrib_refs[0])
    if has_start:
        start_copy.wait()

    @pl.loop(0, angles // (2 * CHAINS))
    def _(step):
        start = step * 2 * CHAINS
        multiply(start + CHAINS, 1, contrib_refs[1])
        scatter(start, contrib_refs[0])
        multiply(jnp.minimum(start + 2 * CHAINS, angles - CHAINS), 0, contrib_refs[0])
        scatter(start + CHAINS, contrib_refs[1])

    def total(t):
        sums = [acc_ref[t] for acc_ref in acc_refs]
        while len(sums) > 1:
            sums = [sums[i] + sums[i + 1] for i in range(0, len(sums), 2)]
        return sums[0]

    if outs == 1:

        @pl.loop(0, coef_blocks, unroll=16)
        def _(t):
            out_refs[0][t] = total(t)

    else:
        per_piece = out_refs[0].shape[1] // LANES
        for k, out_ref in enumerate(out_refs):

            @pl.loop(0, per_piece, unroll=16)
            def _(t):
                lanes = pl.ds(pl.multiple_of(t * LANES, LANES), LANES)
                even = total(2 * (k * per_piece + t))
                odd = total(2 * (k * per_piece + t) + 1)
                real = jnp.where(low, even, swap_halves(odd))
                imag = jnp.where(low, swap_halves(even), odd)
                out_ref[:, lanes] = jnp.concatenate([real, imag], axis=0).astype(out_ref.dtype)


def back_project(idx, radon_tiles, grads, blocks, start, pieces, piece_width, name):
    angles, block, span = radon_tiles.shape
    coef_blocks = pieces * piece_width // block
    rows = len(blocks) * GROUP
    has_start = start is not None
    if has_start:
        out_shape = [jax.ShapeDtypeStruct((ROWS, piece_width), jnp.bfloat16)] * pieces
    else:
        out_shape = [jax.ShapeDtypeStruct((coef_blocks, GROUP, LANES), jnp.float32)]
    operands = [idx, radon_tiles, grads] + ([start] if has_start else [])
    return pl.pallas_call(
        functools.partial(back_project_kernel, blocks, has_start, len(out_shape)),
        out_shape=out_shape,
        in_specs=[scalars] + [everywhere] * 2 + [pl.BlockSpec(memory_space=pl.ANY)] * has_start,
        out_specs=[everywhere] * len(out_shape),
        scratch_shapes=[pltpu.VMEM((coef_blocks, GROUP, LANES), jnp.float32)] * CHAINS
        + [pltpu.VMEM((2 * CHAINS, 2 * block, 2 * span), jnp.bfloat16)]
        + [pltpu.VMEM((CHAINS, rows, 2 * span), jnp.float32)] * 2
        + [pltpu.SemaphoreType.DMA] * has_start,
        compiler_params=pltpu.CompilerParams(vmem_limit_bytes=60 * MEBI),
        cost_estimate=guess(4 + len(blocks) // 4),
        name=name,
    )(*operands)


def add_slots(meta_ref, probe_ref, forward_ref, inverse_ref, ext_ref, acc_ref, amp_refs, scratch, first):
    wave_ref, half_ref, delta_ref, back_ref = scratch
    n_pos = lax.axis_size("pos")
    groups = ext_ref.shape[0]
    width = probe_ref.shape[1]
    slots = amp_refs[0].shape[0]
    tile_width = (acc_ref.shape[2] - width) // len(amp_refs)
    chunk = 4
    crows = chunk * GROUP
    chunks = groups // chunk
    wide = width // LANES
    lane_id = lax.broadcasted_iota(jnp.int32, (crows, LANES), 1)

    def product(left, right):
        return jnp.dot(left, right, preferred_element_type=jnp.float32)

    for tile, amp_ref in enumerate(amp_refs):
        order = first + tile
        tile_start = lax.rem(lax.axis_index("pos") + order, n_pos) * tile_width - tile * tile_width
        count = meta_ref[order, slots]

        @pl.loop(0, (count + 1) // 2)
        def _(step):
            shifts, starts, lives = [], [], []
            for n in range(2):
                offset = meta_ref[order, step * 2 + n] - tile_start
                shifts.append(offset % LANES)
                lane_tile = offset // LANES
                starts.append(
                    [pl.multiple_of((lane_tile + m) * LANES, LANES) for m in range(wide + 1)]
                )
                lives.append((step * 2 + n < count).astype(jnp.float32))
            for n in range(2):
                keep = lane_id < LANES - shifts[n]
                back_shift = (LANES - shifts[n]) % LANES
                for ch in range(chunks):
                    rows = slice(ch * crows, (ch + 1) * crows)
                    low_rows = slice(width + ch * crows, width + (ch + 1) * crows)
                    turned = []
                    for start in starts[n]:
                        both = ext_ref[ch * chunk : (ch + 1) * chunk, :, pl.ds(start, LANES)]
                        both = both.astype(jnp.float32)
                        turned.append(
                            [
                                pltpu.roll(
                                    both[:, c * GROUP : (c + 1) * GROUP].reshape(crows, LANES),
                                    back_shift,
                                    1,
                                )
                                for c in range(2)
                            ]
                        )
                    for m in range(wide):
                        lanes = slice(m * LANES, (m + 1) * LANES)
                        put = slice(n * width + m * LANES, n * width + (m + 1) * LANES)
                        patch_re = jnp.where(keep, turned[m][0], turned[m + 1][0])
                        patch_im = jnp.where(keep, turned[m][1], turned[m + 1][1])
                        probe_re = probe_ref[0, rows, lanes].astype(jnp.float32)
                        probe_im = probe_ref[1, rows, lanes].astype(jnp.float32)
                        wave_re = probe_re * patch_re - probe_im * patch_im
                        wave_im = probe_re * patch_im + probe_im * patch_re
                        wave_ref[rows, put] = wave_re.astype(jnp.bfloat16)
                        wave_ref[low_rows, put] = wave_im.astype(jnp.bfloat16)
                mine = slice(n * width, (n + 1) * width)
                half = product(forward_ref[...], wave_ref[:, mine]).astype(jnp.bfloat16)
                half_ref[mine, :width] = half[:width]
                half_ref[mine, width:] = half[width:]
            for n in range(2):
                mine = slice(n * width, (n + 1) * width)
                far = product(half_ref[mine, :], inverse_ref[...])
                for ch in range(chunks):
                    rows = slice(ch * crows, (ch + 1) * crows)
                    low_rows = slice(width + ch * crows, width + (ch + 1) * crows)
                    far_re, far_im = far[rows, :width], far[rows, width:]
                    power = far_re * far_re + far_im * far_im
                    amps = amp_ref[step * 2 + n, rows, :].astype(jnp.float32)
                    factor = amps * lax.rsqrt(jnp.maximum(power, 1.0)) - 1.0
                    delta_ref[rows, mine] = (far_re * factor).astype(jnp.bfloat16)
                    delta_ref[low_rows, mine] = (far_im * factor).astype(jnp.bfloat16)
                back = product(inverse_ref[...], delta_ref[:, mine]).astype(jnp.bfloat16)
                back_ref[mine, :width] = back[:width]
                back_ref[mine, width:] = back[width:]
            for n in range(2):
                mine = slice(n * width, (n + 1) * width)
                near = product(back_ref[mine, :], forward_ref[...])
                past = lane_id >= shifts[n]
                for ch in range(chunks):
                    rows = slice(ch * crows, (ch + 1) * crows)
                    turned = []
                    for m in range(wide):
                        lanes = slice(m * LANES, (m + 1) * LANES)
                        probe_re = probe_ref[0, rows, lanes].astype(jnp.float32) * lives[n]
                        probe_im = probe_ref[1, rows, lanes].astype(jnp.float32) * lives[n]
                        near_re = near[rows, m * LANES : (m + 1) * LANES]
                        near_im = near[rows, width + m * LANES : width + (m + 1) * LANES]
                        turned.append(
                            [
                                pltpu.roll(probe_re * near_re + probe_im * near_im, shifts[n], 1),
                                pltpu.roll(probe_re * near_im - probe_im * near_re, shifts[n], 1),
                            ]
                        )
                    for m in range(wide + 1):
                        for c in range(2):
                            behind = turned[m - 1][c] if m > 0 else 0.0
                            ahead = turned[m][c] if m < wide else 0.0
                            here = (c, rows, pl.ds(starts[n][m], LANES))
                            acc_ref[here] += jnp.where(past, ahead, behind)


def exit_first_kernel(tiles, meta_ref, probe_ref, forward_ref, inverse_ref, sino_ref, *refs):
    amp_refs, refs = refs[:tiles], refs[tiles:]
    partial_ref, grad_ref, spill_ref, acc_ref, *scratch = refs
    groups = sino_ref.shape[0]
    width = probe_ref.shape[1]
    done = sino_ref.shape[2] - width

    @pl.loop(0, groups)
    def _(g):
        rows = pl.ds(pl.multiple_of(g * GROUP, GROUP), GROUP)
        for c in range(2):
            acc_ref[c, rows, :] = jnp.zeros((GROUP, acc_ref.shape[2]), jnp.float32)

    add_slots(
        meta_ref, probe_ref, forward_ref, inverse_ref, sino_ref, acc_ref, amp_refs, scratch, 0
    )

    @pl.loop(0, groups)
    def _(g):
        rows = pl.ds(pl.multiple_of(g * GROUP, GROUP), GROUP)
        whole = [acc_ref[c, rows, width:done] for c in range(2)]
        grad_ref[g] = jnp.concatenate(whole, axis=0).astype(jnp.bfloat16)
        for c in range(2):
            partial_ref[c, rows, :] = acc_ref[c, rows, :width]
            spill_ref[c, rows, :] = acc_ref[c, rows, done:]


def exit_rest_kernel(
    tiles, meta_ref, probe_ref, forward_ref, inverse_ref, early_ref, late_ref, partial_ref, spill_ref, *refs
):
    amp_refs, refs = refs[:tiles], refs[tiles:]
    out_ref, ext_ref, acc_ref, *scratch = refs
    groups = early_ref.shape[0]
    width = probe_ref.shape[1]
    done = width + late_ref.shape[2]

    @pl.loop(0, groups)
    def _(g):
        ext_ref[g, :, :width] = early_ref[g, :, early_ref.shape[2] - width :]
        ext_ref[g, :, width:done] = late_ref[g]
        ext_ref[g, :, done:] = early_ref[g, :, :width]
        rows = pl.ds(pl.multiple_of(g * GROUP, GROUP), GROUP)
        for c in range(2):
            acc_ref[c, rows, :width] = spill_ref[c, rows, :]
            acc_ref[c, rows, width:] = jnp.zeros((GROUP, done), jnp.float32)

    add_slots(
        meta_ref, probe_ref, forward_ref, inverse_ref, ext_ref, acc_ref, amp_refs, scratch,
        lax.axis_size("pos") - tiles,
    )

    @pl.loop(0, groups)
    def _(g):
        rows = pl.ds(pl.multiple_of(g * GROUP, GROUP), GROUP)
        here = [acc_ref[c, rows, :done] for c in range(2)]
        wrapped = [acc_ref[c, rows, done:] + partial_ref[c, rows, :] for c in range(2)]
        out_ref[g, :, :done] = jnp.concatenate(here, axis=0).astype(jnp.bfloat16)
        out_ref[g, :, done:] = jnp.concatenate(wrapped, axis=0).astype(jnp.bfloat16)


def exit_scratch(groups, width, reach):
    return [pltpu.VMEM((2, groups * GROUP, reach), jnp.float32)] + [
        pltpu.VMEM((2 * width, 2 * width), jnp.bfloat16)
    ] * 4


def exit_first(meta, probe_field, tables, sino, amps):
    groups, rows, reach = sino.shape
    width = probe_field.shape[1]
    slices = groups * GROUP
    edge = jax.ShapeDtypeStruct((2, slices, width), jnp.float32)
    grad = jax.ShapeDtypeStruct((groups, rows, reach - 2 * width), jnp.bfloat16)
    return pl.pallas_call(
        functools.partial(exit_first_kernel, len(amps)),
        out_shape=[edge, grad, edge],
        in_specs=[scalars] + [everywhere] * (4 + len(amps)),
        out_specs=[everywhere] * 3,
        scratch_shapes=exit_scratch(groups, width, reach),
        compiler_params=pltpu.CompilerParams(vmem_limit_bytes=60 * MEBI),
        cost_estimate=guess(10),
        name="exit_first",
    )(meta, probe_field, *tables, sino, *amps)


def exit_rest(meta, probe_field, tables, early, late, partial, spill, amps):
    groups, rows = late.shape[:2]
    width = probe_field.shape[1]
    reach = late.shape[2] + 2 * width
    return pl.pallas_call(
        functools.partial(exit_rest_kernel, len(amps)),
        out_shape=jax.ShapeDtypeStruct((groups, rows, reach), jnp.bfloat16),
        in_specs=[scalars] + [everywhere] * (7 + len(amps)),
        out_specs=everywhere,
        scratch_shapes=[pltpu.VMEM((groups, rows, reach), jnp.bfloat16)]
        + exit_scratch(groups, width, reach),
        compiler_params=pltpu.CompilerParams(vmem_limit_bytes=60 * MEBI),
        cost_estimate=guess(10),
        name="exit_rest",
    )(meta, probe_field, *tables, early, late, partial, spill, *amps)


def to_groups(received, own_slices):
    if own_slices == GROUP:
        return received
    devices, rows, columns = received.shape
    merge = GROUP // own_slices
    split = received.reshape(devices // merge, merge, 2, own_slices, columns)
    return split.transpose(0, 2, 1, 3, 4).reshape(devices // merge, ROWS, columns)


def from_groups(grouped, own_slices):
    if own_slices == GROUP:
        return grouped
    groups, rows, columns = grouped.shape
    merge = GROUP // own_slices
    split = grouped.reshape(groups, 2, merge, own_slices, columns)
    return split.transpose(0, 2, 1, 3, 4).reshape(groups * merge, 2 * own_slices, columns)


def pad_rows(block, own_slices):
    if own_slices == GROUP:
        return block
    lead, columns = block.shape[:-2], block.shape[-1]
    split = block.reshape(lead + (2, own_slices, columns))
    more = [(0, 0)] * (split.ndim - 2) + [(0, GROUP - own_slices), (0, 0)]
    return jnp.pad(split, more).reshape(lead + (ROWS, columns))


def cut_rows(block, own_slices):
    if own_slices == GROUP:
        return block
    lead, columns = block.shape[:-2], block.shape[-1]
    split = block.reshape(lead + (2, GROUP, columns))[..., :own_slices, :]
    return split.reshape(lead + (2 * own_slices, columns))


def everyone(chunk):
    return lax.all_to_all(chunk, ("ang", "pos"), 0, 0, tiled=True)


def on_device(volume, radon_tiles, tile_blocks, probe_field, amplitudes, offsets, counts):
    n_pos = lax.axis_size("pos")
    pos = lax.axis_index("pos")
    angles, det_blocks, feeds = tile_blocks.shape
    block_size = radon_tiles.shape[1]
    columns = det_blocks * block_size
    tile_width = columns // n_pos
    slab = volume.shape[1]
    width = volume.shape[2]
    own = slab // n_pos
    rows = 2 * own
    blocks_each = width // block_size

    def slices_for(j):
        start = (pos + j) % n_pos * own
        return lax.dynamic_slice_in_dim(volume, start, own, 1).reshape(rows, width)

    vol_pieces = rotate_pos([slices_for(j) for j in range(n_pos)], 1)
    vol_pieces, amplitudes = lax.optimization_barrier((vol_pieces, amplitudes))
    amp_pieces = rotate_pos(
        [
            lax.dynamic_index_in_dim(amplitudes, (pos - j) % n_pos, 0, keepdims=False)
            for j in range(n_pos)
        ],
        -1,
    )

    owner = tile_blocks // blocks_each
    within = tile_blocks % blocks_each
    piece = (pos - owner) % n_pos
    crossed = (within + jnp.arange(feeds, dtype=jnp.int32)) % 2
    tiles_each = width // LANES

    def by_chunk(idx):
        idx = idx.reshape(angles // n_pos, n_pos, n_pos, det_blocks // n_pos * feeds)
        idx = jnp.stack([jnp.roll(idx[:, p], -p, axis=1) for p in range(n_pos)], axis=1)
        return idx.reshape(angles * det_blocks * feeds)

    tile_idx = by_chunk(crossed * (n_pos * tiles_each) + piece * tiles_each + within // 2)
    block_idx = by_chunk(piece * blocks_each + within)
    padded = [pad_rows(piece, own) for piece in vol_pieces]
    probe_width = probe_field.shape[1]
    tables = dft_tables(probe_width)
    half = n_pos // 2
    reach = (half * tile_width + probe_width) // block_size
    edge = probe_width // block_size
    early_blocks = list(range(reach))
    late_blocks = list(range(reach, det_blocks))
    first_blocks = list(range(edge, half * tile_width // block_size))
    rest_blocks = list(range(half * tile_width // block_size, det_blocks)) + list(range(edge))

    sino_early = project(tile_idx, radon_tiles, padded, early_blocks, "project_early")
    sino_early, padded, offsets, counts = lax.optimization_barrier(
        (sino_early, padded, offsets, counts)
    )
    meta = jnp.concatenate([offsets, counts], axis=1)
    meta = rotate_pos(
        [lax.dynamic_slice_in_dim(meta, (pos - j) % n_pos, 1, 0) for j in range(n_pos)], -1
    )
    meta = jnp.concatenate(meta, axis=0)
    padded, meta = lax.optimization_barrier((padded, meta))
    sino_late = project(tile_idx, radon_tiles, padded, late_blocks, "project_late")
    got_early = everyone(cut_rows(sino_early, own))
    got_early, sino_late = lax.optimization_barrier((got_early, sino_late))
    got_late = everyone(cut_rows(sino_late, own))
    got_early, got_late = to_groups(got_early, own), to_groups(got_late, own)
    got_early, amp_pieces = lax.optimization_barrier((got_early, amp_pieces))
    partial, first_grad, spill = exit_first(meta, probe_field, tables, got_early, amp_pieces[:half])
    first_sent, got_late = lax.optimization_barrier((first_grad, got_late))
    rest_grad = exit_rest(
        meta, probe_field, tables, got_early, got_late, partial, spill, amp_pieces[half:]
    )
    back_first = everyone(from_groups(first_sent, own))
    back_first, rest_sent = lax.optimization_barrier((back_first, rest_grad))
    back_rest = everyone(from_groups(rest_sent, own))
    first_sum = back_project(
        block_idx, radon_tiles, pad_rows(back_first, own), first_blocks, None, n_pos, width, "back_first"
    )[0]
    wrapped = rest_grad.shape[2] - probe_width
    tile_pieces = [jnp.concatenate([rest_grad[:, :, wrapped:], first_grad[:, :, : tile_width - probe_width]], axis=2)]
    for j in range(1, n_pos):
        source, begin = (first_grad, j * tile_width - probe_width) if j < half else (rest_grad, (j - half) * tile_width)
        tile_pieces.append(source[:, :, begin : begin + tile_width])
    tile_pieces = rotate_pos(tile_pieces, 1)
    obj_pieces = back_project(
        block_idx, radon_tiles, pad_rows(back_rest, own), rest_blocks, first_sum, n_pos, width, "back_rest"
    )
    groups = rest_grad.shape[0]
    tile_pieces = [tile_pieces[-j % n_pos] for j in range(n_pos)]
    tile_pieces = [
        piece.reshape(groups, 2, GROUP, tile_width).transpose(1, 0, 2, 3).reshape(2, groups * GROUP, tile_width)
        for piece in tile_pieces
    ]
    proj_grad = jnp.stack(in_order(tile_pieces, -pos % n_pos), axis=2).astype(jnp.float32)
    obj_pieces = rotate_pos([cut_rows(piece, own) for piece in obj_pieces], -1)
    obj_pieces = [piece.reshape(2, own, width) for piece in in_order(obj_pieces, -pos % n_pos)]
    object_grad = jnp.concatenate(obj_pieces, axis=1).astype(jnp.float32)
    new_volume = volume.astype(jnp.float32) + step_size * object_grad
    return (new_volume, proj_grad)


def solution(mesh):
    in_specs = (
        P(None, "ang", "pos"),
        P(),
        P(),
        P(),
        P("ang", "pos", None, None),
        P("ang", "pos"),
        P("ang", "pos"),
    )
    out_specs = (P(None, "ang", "pos"), P(None, None, "ang", "pos"))
    return jax.shard_map(
        on_device, mesh=mesh, in_specs=in_specs, out_specs=out_specs, check_vma=False
    )
```

```python
import functools
import math

import jax
import jax.numpy as jnp
import numpy as np
from jax import lax
from jax.experimental import pallas as pl
from jax.experimental.pallas import tpu as pltpu
from jax.sharding import PartitionSpec as P

step_size = 0.1
LANES = 128
ROWS = 16
GROUP = 8
MEBI = 1024 * 1024
everywhere = pl.BlockSpec(memory_space=pltpu.VMEM)
anywhere = pl.BlockSpec(memory_space=pl.ANY)
scalars = pl.BlockSpec(memory_space=pltpu.SMEM)
CHAINS = 4
BATCH = 8


def dft_tables(width):
    index = np.arange(width)
    turn = 2.0 * math.pi / width * (index[:, None] * index[None, :] % width)
    cosine = jnp.asarray(np.cos(turn) / math.sqrt(width), jnp.bfloat16)
    sine_neg = jnp.asarray(-np.sin(turn) / math.sqrt(width), jnp.bfloat16)
    forward = jnp.block([[cosine, -sine_neg], [sine_neg, cosine]])
    inverse = jnp.block([[cosine, sine_neg], [-sine_neg, cosine]])
    return (forward, inverse)


def rotate_pos(pieces, sign):
    count = len(pieces)
    return [pieces[0]] + [
        lax.ppermute(pieces[j], "pos", [(i, (i + sign * j) % count) for i in range(count)])
        for j in range(1, count)
    ]


def in_order(pieces, first):
    count = len(pieces)
    bit = 1
    while bit < count:
        flip = (first & bit) != 0
        pieces = [jnp.where(flip, pieces[(k + bit) % count], pieces[k]) for k in range(count)]
        bit *= 2
    return pieces


def lower_half(shape):
    return lax.broadcasted_iota(jnp.int32, shape, len(shape) - 1) < LANES // 2


def swap_halves(tile):
    return pltpu.roll(tile, LANES // 2, 1)


def arrange(vol_refs, vv_ref):
    per_piece = vol_refs[0].shape[1] // LANES
    tiles = per_piece * len(vol_refs)
    batch = 16
    source = lax.broadcasted_iota(jnp.int32, (LANES, LANES), 0)
    target = lax.broadcasted_iota(jnp.int32, (LANES, LANES), 1)
    swap = ((source + LANES // 2) % LANES == target).astype(jnp.bfloat16)
    for k, vol_ref in enumerate(vol_refs):

        @pl.loop(0, per_piece // batch, unroll=2)
        def _(step):
            stack = []
            for i in range(batch):
                t = step * batch + i
                tile = vol_ref[:, pl.ds(pl.multiple_of(t * LANES, LANES), LANES)]
                vv_ref[k * per_piece + t] = tile
                stack.append(tile)
            swapped = jnp.dot(
                jnp.concatenate(stack, axis=0), swap, preferred_element_type=jnp.float32
            ).astype(jnp.bfloat16)
            for i in range(batch):
                t = step * batch + i
                vv_ref[tiles + k * per_piece + t] = swapped[i * ROWS : (i + 1) * ROWS]


def project_blocks(blocks, idx_ref, radon_ref, vv_ref, out_hbm, out_ref, out_sems, lhs_refs):
    angles, block, span = radon_ref.shape
    feeds = span // block
    low = lower_half((ROWS, LANES))
    batch = lhs_refs[0].shape[0]

    per_angle = idx_ref.shape[0] // angles

    def gather(start, lhs_ref):
        for n in range(batch):
            base = (start + n) * per_angle
            for i, b in enumerate(blocks):
                row = i * ROWS
                for jp in range(feeds // 2):
                    at = b * feeds + 2 * jp
                    first = vv_ref[idx_ref[base + at]]
                    second = vv_ref[idx_ref[base + at + 1]]
                    lhs_ref[n, row : row + ROWS, jp * LANES : (jp + 1) * LANES] = jnp.where(
                        low, first, second
                    )

    def multiply(start, lhs_ref):
        for n in range(batch):
            a = start + n
            product = lax.dot_general(
                lhs_ref[n], radon_ref[a], (((1,), (1,)), ((), ())), preferred_element_type=jnp.float32
            )
            for pair in range(len(blocks) // 2):
                row = 2 * pair * ROWS
                tile = jnp.concatenate(
                    [product[row : row + ROWS], product[row + ROWS : row + 2 * ROWS]], axis=1
                )
                out_ref[a, :, pair * LANES : (pair + 1) * LANES] = tile.astype(jnp.bfloat16)

    def leave(step):
        here = pl.ds(step * 2 * batch, 2 * batch)
        return pltpu.make_async_copy(out_ref.at[here], out_hbm.at[here], out_sems.at[step])

    gather(0, lhs_refs[0])

    @pl.loop(0, angles // (2 * batch))
    def _(step):
        start = step * 2 * batch

        @pl.when(step > 0)
        def _():
            leave(step - 1).start()

        multiply(start, lhs_refs[0])
        gather(start + batch, lhs_refs[1])
        multiply(start + batch, lhs_refs[1])
        gather(jnp.minimum(start + 2 * batch, angles - batch), lhs_refs[0])

    leave(angles // (2 * batch) - 1).start()

    @pl.loop(0, angles // (2 * batch))
    def _(step):
        leave(step).wait()


def project_kernel(blocks, pieces, idx_ref, radon_ref, *refs):
    vol_refs = refs[:pieces]
    out_hbm, vv_ref, out_ref, out_sems, *lhs_refs = refs[pieces:]
    arrange(vol_refs, vv_ref)
    project_blocks(blocks, idx_ref, radon_ref, vv_ref, out_hbm, out_ref, out_sems, lhs_refs)


def guess(microseconds):
    return pl.CostEstimate(
        flops=int(microseconds * 1.15e9), bytes_accessed=int(microseconds * 1e5), transcendentals=0
    )


def project(idx, radon_tiles, vol_pieces, blocks, name):
    angles, block, span = radon_tiles.shape
    pieces = len(vol_pieces)
    tiles = pieces * vol_pieces[0].shape[1] // LANES
    out_shape = (angles, ROWS, len(blocks) * block)
    return pl.pallas_call(
        functools.partial(project_kernel, blocks, pieces),
        out_shape=jax.ShapeDtypeStruct(out_shape, jnp.bfloat16),
        in_specs=[scalars, everywhere] + [everywhere] * pieces,
        out_specs=anywhere,
        scratch_shapes=[pltpu.VMEM((2 * tiles, ROWS, LANES), jnp.bfloat16)]
        + [pltpu.VMEM(out_shape, jnp.bfloat16), pltpu.SemaphoreType.DMA((angles // (2 * BATCH),))]
        + [pltpu.VMEM((BATCH, len(blocks) * ROWS, span), jnp.bfloat16)] * 2,
        compiler_params=pltpu.CompilerParams(
            vmem_limit_bytes=14 * MEBI + 2 * radon_tiles.size + 2 * math.prod(out_shape)
        ),
        cost_estimate=guess(4 + len(blocks) // 4),
        name=name,
    )(idx, radon_tiles, *vol_pieces)


def back_project_kernel(blocks, has_start, outs, idx_ref, radon_ref, grad_ref, *refs):
    start_ref, refs = (refs[0], refs[1:]) if has_start else (None, refs)
    out_refs, refs = refs[:outs], refs[outs:]
    acc_refs, (w_ref, *contrib_refs) = refs[:CHAINS], refs[CHAINS:]
    if has_start:
        contrib_refs, start_sem = contrib_refs[:-1], contrib_refs[-1]
        start_copy = pltpu.make_async_copy(start_ref, acc_refs[0], start_sem)
        start_copy.start()
    angles, block, span = radon_ref.shape
    pairs = len(blocks) // 2
    feeds = span // block
    coef_blocks = acc_refs[0].shape[0]

    @pl.loop(0, coef_blocks, unroll=16)
    def _(t):
        for acc_ref in acc_refs[1:] if has_start else acc_refs:
            acc_ref[t] = jnp.zeros((GROUP, LANES), jnp.float32)

    low = lower_half((GROUP, LANES))
    low_rows = lower_half((block, LANES))
    w_ref[...] = jnp.zeros_like(w_ref)

    def widen(slot, a):
        for jp in range(feeds // 2):
            tile = radon_ref[a, :, jp * LANES : (jp + 1) * LANES].astype(jnp.float32)
            turned = swap_halves(tile)
            for side, (first, second) in enumerate(((tile, turned), (turned, tile))):
                lanes = slice((2 * jp + side) * LANES, (2 * jp + side + 1) * LANES)
                w_ref[slot, :block, lanes] = jnp.where(low_rows, first, 0.0).astype(jnp.bfloat16)
                w_ref[slot, block:, lanes] = jnp.where(low_rows, 0.0, second).astype(jnp.bfloat16)

    def multiply(start, half, contrib_ref):
        for n in range(CHAINS):
            a = start + n
            widen(half * CHAINS + n, a)
            lhs = []
            for pair in range(pairs):
                tile = grad_ref[a, :, pair * LANES : (pair + 1) * LANES].astype(jnp.float32)
                real, imag = tile[:GROUP], tile[GROUP:]
                even = jnp.where(low, real, swap_halves(imag))
                odd = jnp.where(low, swap_halves(real), imag)
                lhs.append(jnp.concatenate([even, odd], axis=0).astype(jnp.bfloat16))
            contrib_ref[n] = jnp.dot(
                jnp.concatenate(lhs, axis=0),
                w_ref[half * CHAINS + n],
                preferred_element_type=jnp.float32,
            )

    per_angle = idx_ref.shape[0] // angles

    def scatter(start, contrib_ref):
        bases = [(start + n) * per_angle for n in range(CHAINS)]
        for i, b in enumerate(blocks):
            row = i * GROUP
            for j in range(feeds):
                for n in range(CHAINS):
                    tile = contrib_ref[n, row : row + GROUP, j * LANES : (j + 1) * LANES]
                    acc_refs[n][idx_ref[bases[n] + (b * feeds + j)]] += tile

    multiply(0, 0, contrib_refs[0])
    if has_start:
        start_copy.wait()

    @pl.loop(0, angles // (2 * CHAINS))
    def _(step):
        start = step * 2 * CHAINS
        multiply(start + CHAINS, 1, contrib_refs[1])
        scatter(start, contrib_refs[0])
        multiply(jnp.minimum(start + 2 * CHAINS, angles - CHAINS), 0, contrib_refs[0])
        scatter(start + CHAINS, contrib_refs[1])

    def total(t):
        sums = [acc_ref[t] for acc_ref in acc_refs]
        while len(sums) > 1:
            sums = [sums[i] + sums[i + 1] for i in range(0, len(sums), 2)]
        return sums[0]

    if outs == 1:

        @pl.loop(0, coef_blocks, unroll=16)
        def _(t):
            out_refs[0][t] = total(t)

    else:
        per_piece = out_refs[0].shape[1] // LANES
        for k, out_ref in enumerate(out_refs):

            @pl.loop(0, per_piece, unroll=16)
            def _(t):
                lanes = pl.ds(pl.multiple_of(t * LANES, LANES), LANES)
                even = total(2 * (k * per_piece + t))
                odd = total(2 * (k * per_piece + t) + 1)
                real = jnp.where(low, even, swap_halves(odd))
                imag = jnp.where(low, swap_halves(even), odd)
                out_ref[:, lanes] = jnp.concatenate([real, imag], axis=0).astype(out_ref.dtype)


def back_project(idx, radon_tiles, grads, blocks, start, pieces, piece_width, name):
    angles, block, span = radon_tiles.shape
    coef_blocks = pieces * piece_width // block
    rows = len(blocks) * GROUP
    has_start = start is not None
    if has_start:
        out_shape = [jax.ShapeDtypeStruct((ROWS, piece_width), jnp.bfloat16)] * pieces
    else:
        out_shape = [jax.ShapeDtypeStruct((coef_blocks, GROUP, LANES), jnp.float32)]
    operands = [idx, radon_tiles, grads] + ([start] if has_start else [])
    return pl.pallas_call(
        functools.partial(back_project_kernel, blocks, has_start, len(out_shape)),
        out_shape=out_shape,
        in_specs=[scalars] + [everywhere] * 2 + [pl.BlockSpec(memory_space=pl.ANY)] * has_start,
        out_specs=[everywhere] * len(out_shape),
        scratch_shapes=[pltpu.VMEM((coef_blocks, GROUP, LANES), jnp.float32)] * CHAINS
        + [pltpu.VMEM((2 * CHAINS, 2 * block, 2 * span), jnp.bfloat16)]
        + [pltpu.VMEM((CHAINS, rows, 2 * span), jnp.float32)] * 2
        + [pltpu.SemaphoreType.DMA] * has_start,
        compiler_params=pltpu.CompilerParams(vmem_limit_bytes=60 * MEBI),
        cost_estimate=guess(4 + len(blocks) // 4),
        name=name,
    )(*operands)


def add_slots(meta_ref, probe_ref, forward_ref, inverse_ref, ext_ref, acc_ref, amp_refs, scratch, first):
    wave_ref, half_ref, delta_ref, back_ref = scratch
    n_pos = lax.axis_size("pos")
    groups = ext_ref.shape[0]
    width = probe_ref.shape[1]
    slots = amp_refs[0].shape[0]
    tile_width = (acc_ref.shape[2] - width) // len(amp_refs)
    chunk = 4
    crows = chunk * GROUP
    chunks = groups // chunk
    wide = width // LANES
    lane_id = lax.broadcasted_iota(jnp.int32, (crows, LANES), 1)

    def product(left, right):
        return jnp.dot(left, right, preferred_element_type=jnp.float32)

    for tile, amp_ref in enumerate(amp_refs):
        order = first + tile
        tile_start = lax.rem(lax.axis_index("pos") + order, n_pos) * tile_width - tile * tile_width
        count = meta_ref[order, slots]

        @pl.loop(0, (count + 1) // 2)
        def _(step):
            shifts, starts, lives = [], [], []
            for n in range(2):
                offset = meta_ref[order, step * 2 + n] - tile_start
                shifts.append(offset % LANES)
                lane_tile = offset // LANES
                starts.append(
                    [pl.multiple_of((lane_tile + m) * LANES, LANES) for m in range(wide + 1)]
                )
                lives.append((step * 2 + n < count).astype(jnp.float32))
            for n in range(2):
                keep = lane_id < LANES - shifts[n]
                back_shift = (LANES - shifts[n]) % LANES
                for ch in range(chunks):
                    rows = slice(ch * crows, (ch + 1) * crows)
                    low_rows = slice(width + ch * crows, width + (ch + 1) * crows)
                    turned = []
                    for start in starts[n]:
                        both = ext_ref[ch * chunk : (ch + 1) * chunk, :, pl.ds(start, LANES)]
                        both = both.astype(jnp.float32)
                        turned.append(
                            [
                                pltpu.roll(
                                    both[:, c * GROUP : (c + 1) * GROUP].reshape(crows, LANES),
                                    back_shift,
                                    1,
                                )
                                for c in range(2)
                            ]
                        )
                    for m in range(wide):
                        lanes = slice(m * LANES, (m + 1) * LANES)
                        put = slice(n * width + m * LANES, n * width + (m + 1) * LANES)
                        patch_re = jnp.where(keep, turned[m][0], turned[m + 1][0])
                        patch_im = jnp.where(keep, turned[m][1], turned[m + 1][1])
                        probe_re = probe_ref[0, rows, lanes].astype(jnp.float32)
                        probe_im = probe_ref[1, rows, lanes].astype(jnp.float32)
                        wave_re = probe_re * patch_re - probe_im * patch_im
                        wave_im = probe_re * patch_im + probe_im * patch_re
                        wave_ref[rows, put] = wave_re.astype(jnp.bfloat16)
                        wave_ref[low_rows, put] = wave_im.astype(jnp.bfloat16)
                mine = slice(n * width, (n + 1) * width)
                half = product(forward_ref[...], wave_ref[:, mine]).astype(jnp.bfloat16)
                half_ref[mine, :width] = half[:width]
                half_ref[mine, width:] = half[width:]
            for n in range(2):
                mine = slice(n * width, (n + 1) * width)
                far = product(half_ref[mine, :], inverse_ref[...])
                for ch in range(chunks):
                    rows = slice(ch * crows, (ch + 1) * crows)
                    low_rows = slice(width + ch * crows, width + (ch + 1) * crows)
                    far_re, far_im = far[rows, :width], far[rows, width:]
                    power = far_re * far_re + far_im * far_im
                    amps = amp_ref[step * 2 + n, rows, :].astype(jnp.float32)
                    factor = amps * lax.rsqrt(jnp.maximum(power, 1.0)) - 1.0
                    delta_ref[rows, mine] = (far_re * factor).astype(jnp.bfloat16)
                    delta_ref[low_rows, mine] = (far_im * factor).astype(jnp.bfloat16)
                back = product(inverse_ref[...], delta_ref[:, mine]).astype(jnp.bfloat16)
                back_ref[mine, :width] = back[:width]
                back_ref[mine, width:] = back[width:]
            for n in range(2):
                mine = slice(n * width, (n + 1) * width)
                near = product(back_ref[mine, :], forward_ref[...])
                past = lane_id >= shifts[n]
                for ch in range(chunks):
                    rows = slice(ch * crows, (ch + 1) * crows)
                    turned = []
                    for m in range(wide):
                        lanes = slice(m * LANES, (m + 1) * LANES)
                        probe_re = probe_ref[0, rows, lanes].astype(jnp.float32) * lives[n]
                        probe_im = probe_ref[1, rows, lanes].astype(jnp.float32) * lives[n]
                        near_re = near[rows, m * LANES : (m + 1) * LANES]
                        near_im = near[rows, width + m * LANES : width + (m + 1) * LANES]
                        turned.append(
                            [
                                pltpu.roll(probe_re * near_re + probe_im * near_im, shifts[n], 1),
                                pltpu.roll(probe_re * near_im - probe_im * near_re, shifts[n], 1),
                            ]
                        )
                    for m in range(wide + 1):
                        for c in range(2):
                            behind = turned[m - 1][c] if m > 0 else 0.0
                            ahead = turned[m][c] if m < wide else 0.0
                            here = (c, rows, pl.ds(starts[n][m], LANES))
                            acc_ref[here] += jnp.where(past, ahead, behind)


def exit_first_kernel(tiles, meta_ref, probe_ref, forward_ref, inverse_ref, sino_ref, *refs):
    amp_refs, refs = refs[:tiles], refs[tiles:]
    partial_ref, grad_ref, spill_ref, acc_ref, *scratch = refs
    groups = sino_ref.shape[0]
    width = probe_ref.shape[1]
    done = sino_ref.shape[2] - width

    @pl.loop(0, groups)
    def _(g):
        rows = pl.ds(pl.multiple_of(g * GROUP, GROUP), GROUP)
        for c in range(2):
            acc_ref[c, rows, :] = jnp.zeros((GROUP, acc_ref.shape[2]), jnp.float32)

    add_slots(
        meta_ref, probe_ref, forward_ref, inverse_ref, sino_ref, acc_ref, amp_refs, scratch, 0
    )

    @pl.loop(0, groups)
    def _(g):
        rows = pl.ds(pl.multiple_of(g * GROUP, GROUP), GROUP)
        whole = [acc_ref[c, rows, width:done] for c in range(2)]
        grad_ref[g] = jnp.concatenate(whole, axis=0).astype(jnp.bfloat16)
        for c in range(2):
            partial_ref[c, rows, :] = acc_ref[c, rows, :width]
            spill_ref[c, rows, :] = acc_ref[c, rows, done:]


def exit_rest_kernel(
    tiles, meta_ref, probe_ref, forward_ref, inverse_ref, early_ref, late_ref, partial_ref, spill_ref, *refs
):
    amp_refs, refs = refs[:tiles], refs[tiles:]
    out_ref, ext_ref, acc_ref, *scratch = refs
    groups = early_ref.shape[0]
    width = probe_ref.shape[1]
    done = width + late_ref.shape[2]

    @pl.loop(0, groups)
    def _(g):
        ext_ref[g, :, :width] = early_ref[g, :, early_ref.shape[2] - width :]
        ext_ref[g, :, width:done] = late_ref[g]
        ext_ref[g, :, done:] = early_ref[g, :, :width]
        rows = pl.ds(pl.multiple_of(g * GROUP, GROUP), GROUP)
        for c in range(2):
            acc_ref[c, rows, :width] = spill_ref[c, rows, :]
            acc_ref[c, rows, width:] = jnp.zeros((GROUP, done), jnp.float32)

    add_slots(
        meta_ref, probe_ref, forward_ref, inverse_ref, ext_ref, acc_ref, amp_refs, scratch,
        lax.axis_size("pos") - tiles,
    )

    @pl.loop(0, groups)
    def _(g):
        rows = pl.ds(pl.multiple_of(g * GROUP, GROUP), GROUP)
        here = [acc_ref[c, rows, :done] for c in range(2)]
        wrapped = [acc_ref[c, rows, done:] + partial_ref[c, rows, :] for c in range(2)]
        out_ref[g, :, :done] = jnp.concatenate(here, axis=0).astype(jnp.bfloat16)
        out_ref[g, :, done:] = jnp.concatenate(wrapped, axis=0).astype(jnp.bfloat16)


def exit_scratch(groups, width, reach):
    return [pltpu.VMEM((2, groups * GROUP, reach), jnp.float32)] + [
        pltpu.VMEM((2 * width, 2 * width), jnp.bfloat16)
    ] * 4


def exit_first(meta, probe_field, tables, sino, amps):
    groups, rows, reach = sino.shape
    width = probe_field.shape[1]
    slices = groups * GROUP
    edge = jax.ShapeDtypeStruct((2, slices, width), jnp.float32)
    grad = jax.ShapeDtypeStruct((groups, rows, reach - 2 * width), jnp.bfloat16)
    return pl.pallas_call(
        functools.partial(exit_first_kernel, len(amps)),
        out_shape=[edge, grad, edge],
        in_specs=[scalars] + [everywhere] * (4 + len(amps)),
        out_specs=[everywhere] * 3,
        scratch_shapes=exit_scratch(groups, width, reach),
        compiler_params=pltpu.CompilerParams(vmem_limit_bytes=60 * MEBI),
        cost_estimate=guess(10),
        name="exit_first",
    )(meta, probe_field, *tables, sino, *amps)


def exit_rest(meta, probe_field, tables, early, late, partial, spill, amps):
    groups, rows = late.shape[:2]
    width = probe_field.shape[1]
    reach = late.shape[2] + 2 * width
    return pl.pallas_call(
        functools.partial(exit_rest_kernel, len(amps)),
        out_shape=jax.ShapeDtypeStruct((groups, rows, reach), jnp.bfloat16),
        in_specs=[scalars] + [everywhere] * (7 + len(amps)),
        out_specs=everywhere,
        scratch_shapes=[pltpu.VMEM((groups, rows, reach), jnp.bfloat16)]
        + exit_scratch(groups, width, reach),
        compiler_params=pltpu.CompilerParams(vmem_limit_bytes=60 * MEBI),
        cost_estimate=guess(10),
        name="exit_rest",
    )(meta, probe_field, *tables, early, late, partial, spill, *amps)


def to_groups(received, own_slices):
    if own_slices == GROUP:
        return received
    devices, rows, columns = received.shape
    merge = GROUP // own_slices
    split = received.reshape(devices // merge, merge, 2, own_slices, columns)
    return split.transpose(0, 2, 1, 3, 4).reshape(devices // merge, ROWS, columns)


def from_groups(grouped, own_slices):
    if own_slices == GROUP:
        return grouped
    groups, rows, columns = grouped.shape
    merge = GROUP // own_slices
    split = grouped.reshape(groups, 2, merge, own_slices, columns)
    return split.transpose(0, 2, 1, 3, 4).reshape(groups * merge, 2 * own_slices, columns)


def pad_rows(block, own_slices):
    if own_slices == GROUP:
        return block
    lead, columns = block.shape[:-2], block.shape[-1]
    split = block.reshape(lead + (2, own_slices, columns))
    more = [(0, 0)] * (split.ndim - 2) + [(0, GROUP - own_slices), (0, 0)]
    return jnp.pad(split, more).reshape(lead + (ROWS, columns))


def cut_rows(block, own_slices):
    if own_slices == GROUP:
        return block
    lead, columns = block.shape[:-2], block.shape[-1]
    split = block.reshape(lead + (2, GROUP, columns))[..., :own_slices, :]
    return split.reshape(lead + (2 * own_slices, columns))


def everyone(chunk):
    return lax.all_to_all(chunk, ("ang", "pos"), 0, 0, tiled=True)


def on_device(volume, radon_tiles, tile_blocks, probe_field, amplitudes, offsets, counts):
    n_pos = lax.axis_size("pos")
    pos = lax.axis_index("pos")
    angles, det_blocks, feeds = tile_blocks.shape
    block_size = radon_tiles.shape[1]
    columns = det_blocks * block_size
    tile_width = columns // n_pos
    slab = volume.shape[1]
    width = volume.shape[2]
    own = slab // n_pos
    rows = 2 * own
    blocks_each = width // block_size

    source, cuts = volume, {}
    for j in list(range(1, n_pos)) + [0]:
        start = (pos + j) % n_pos * own
        cuts[j] = lax.dynamic_slice_in_dim(source, start, own, 1).reshape(rows, width)
        source, cuts[j] = lax.optimization_barrier((source, cuts[j]))
    vol_pieces = rotate_pos([cuts[j] for j in range(n_pos)], 1)
    vol_pieces, amplitudes = lax.optimization_barrier((vol_pieces, amplitudes))
    amp_pieces = rotate_pos(
        [
            lax.dynamic_index_in_dim(amplitudes, (pos - j) % n_pos, 0, keepdims=False)
            for j in range(n_pos)
        ],
        -1,
    )

    owner = tile_blocks // blocks_each
    within = tile_blocks % blocks_each
    piece = (pos - owner) % n_pos
    crossed = (within + jnp.arange(feeds, dtype=jnp.int32)) % 2
    tiles_each = width // LANES

    def by_chunk(idx):
        idx = idx.reshape(angles // n_pos, n_pos, n_pos, det_blocks // n_pos * feeds)
        idx = jnp.stack([jnp.roll(idx[:, p], -p, axis=1) for p in range(n_pos)], axis=1)
        return idx.reshape(angles * det_blocks * feeds)

    tile_idx = by_chunk(crossed * (n_pos * tiles_each) + piece * tiles_each + within // 2)
    block_idx = by_chunk(piece * blocks_each + within)
    padded = [pad_rows(piece, own) for piece in vol_pieces]
    probe_width = probe_field.shape[1]
    tables = dft_tables(probe_width)
    half = n_pos // 2
    reach = (half * tile_width + probe_width) // block_size
    edge = probe_width // block_size
    early_blocks = list(range(reach))
    late_blocks = list(range(reach, det_blocks))
    first_blocks = list(range(edge, half * tile_width // block_size))
    rest_blocks = list(range(half * tile_width // block_size, det_blocks)) + list(range(edge))

    sino_early = project(tile_idx, radon_tiles, padded, early_blocks, "project_early")
    sino_early, padded, offsets, counts = lax.optimization_barrier(
        (sino_early, padded, offsets, counts)
    )
    meta = jnp.concatenate([offsets, counts], axis=1)
    meta = rotate_pos(
        [lax.dynamic_slice_in_dim(meta, (pos - j) % n_pos, 1, 0) for j in range(n_pos)], -1
    )
    meta = jnp.concatenate(meta, axis=0)
    padded, meta = lax.optimization_barrier((padded, meta))
    sino_late = project(tile_idx, radon_tiles, padded, late_blocks, "project_late")
    got_early = everyone(cut_rows(sino_early, own))
    got_early, sino_late = lax.optimization_barrier((got_early, sino_late))
    got_late = everyone(cut_rows(sino_late, own))
    got_early, got_late = to_groups(got_early, own), to_groups(got_late, own)
    got_early, amp_pieces = lax.optimization_barrier((got_early, amp_pieces))
    partial, first_grad, spill = exit_first(meta, probe_field, tables, got_early, amp_pieces[:half])
    first_sent, got_late = lax.optimization_barrier((first_grad, got_late))
    rest_grad = exit_rest(
        meta, probe_field, tables, got_early, got_late, partial, spill, amp_pieces[half:]
    )
    back_first = everyone(from_groups(first_sent, own))
    back_first, rest_sent = lax.optimization_barrier((back_first, rest_grad))
    back_rest = everyone(from_groups(rest_sent, own))
    first_sum = back_project(
        block_idx, radon_tiles, pad_rows(back_first, own), first_blocks, None, n_pos, width, "back_first"
    )[0]
    wrapped = rest_grad.shape[2] - probe_width
    tile_pieces = [jnp.concatenate([rest_grad[:, :, wrapped:], first_grad[:, :, : tile_width - probe_width]], axis=2)]
    for j in range(1, n_pos):
        source, begin = (first_grad, j * tile_width - probe_width) if j < half else (rest_grad, (j - half) * tile_width)
        tile_pieces.append(source[:, :, begin : begin + tile_width])
    tile_pieces = rotate_pos(tile_pieces, 1)
    obj_pieces = back_project(
        block_idx, radon_tiles, pad_rows(back_rest, own), rest_blocks, first_sum, n_pos, width, "back_rest"
    )
    groups = rest_grad.shape[0]
    tile_pieces = [tile_pieces[-j % n_pos] for j in range(n_pos)]
    tile_pieces = [
        piece.reshape(groups, 2, GROUP, tile_width).transpose(1, 0, 2, 3).reshape(2, groups * GROUP, tile_width)
        for piece in tile_pieces
    ]
    proj_grad = jnp.stack(in_order(tile_pieces, -pos % n_pos), axis=2).astype(jnp.float32)
    obj_pieces = rotate_pos([cut_rows(piece, own) for piece in obj_pieces], -1)
    obj_pieces = [piece.reshape(2, own, width) for piece in in_order(obj_pieces, -pos % n_pos)]
    object_grad = jnp.concatenate(obj_pieces, axis=1).astype(jnp.float32)
    new_volume = volume.astype(jnp.float32) + step_size * object_grad
    return (new_volume, proj_grad)


def solution(mesh):
    in_specs = (
        P(None, "ang", "pos"),
        P(),
        P(),
        P(),
        P("ang", "pos", None, None),
        P("ang", "pos"),
        P("ang", "pos"),
    )
    out_specs = (P(None, "ang", "pos"), P(None, None, "ang", "pos"))
    return jax.shard_map(
        on_device, mesh=mesh, in_specs=in_specs, out_specs=out_specs, check_vma=False
    )
```

```python
import functools
import math

import jax
import jax.numpy as jnp
import numpy as np
from jax import lax
from jax.experimental import pallas as pl
from jax.experimental.pallas import tpu as pltpu
from jax.sharding import PartitionSpec as P

step_size = 0.1
LANES = 128
ROWS = 16
GROUP = 8
MEBI = 1024 * 1024
everywhere = pl.BlockSpec(memory_space=pltpu.VMEM)
anywhere = pl.BlockSpec(memory_space=pl.ANY)
scalars = pl.BlockSpec(memory_space=pltpu.SMEM)
CHAINS = 4
BATCH = 4


def dft_tables(width):
    index = np.arange(width)
    turn = 2.0 * math.pi / width * (index[:, None] * index[None, :] % width)
    cosine = jnp.asarray(np.cos(turn) / math.sqrt(width), jnp.bfloat16)
    sine_neg = jnp.asarray(-np.sin(turn) / math.sqrt(width), jnp.bfloat16)
    forward = jnp.block([[cosine, -sine_neg], [sine_neg, cosine]])
    inverse = jnp.block([[cosine, sine_neg], [-sine_neg, cosine]])
    return (forward, inverse)


def send_pos(piece, step):
    count = lax.axis_size("pos")
    return lax.ppermute(piece, "pos", [(i, (i + step) % count) for i in range(count)])


def rotate_pos(pieces, sign):
    count = len(pieces)
    return [pieces[0]] + [
        lax.ppermute(pieces[j], "pos", [(i, (i + sign * j) % count) for i in range(count)])
        for j in range(1, count)
    ]


def in_order(pieces, first):
    count = len(pieces)
    bit = 1
    while bit < count:
        flip = (first & bit) != 0
        pieces = [jnp.where(flip, pieces[(k + bit) % count], pieces[k]) for k in range(count)]
        bit *= 2
    return pieces


def lower_half(shape):
    return lax.broadcasted_iota(jnp.int32, shape, len(shape) - 1) < LANES // 2


def swap_halves(tile):
    return pltpu.roll(tile, LANES // 2, 1)


def arrange(vol_refs, vv_ref):
    per_piece = vol_refs[0].shape[1] // LANES
    tiles = per_piece * len(vol_refs)
    batch = 16
    source = lax.broadcasted_iota(jnp.int32, (LANES, LANES), 0)
    target = lax.broadcasted_iota(jnp.int32, (LANES, LANES), 1)
    swap = ((source + LANES // 2) % LANES == target).astype(jnp.bfloat16)
    for k, vol_ref in enumerate(vol_refs):

        @pl.loop(0, per_piece // batch, unroll=2)
        def _(step):
            stack = []
            for i in range(batch):
                t = step * batch + i
                tile = vol_ref[:, pl.ds(pl.multiple_of(t * LANES, LANES), LANES)]
                vv_ref[k * per_piece + t] = tile
                stack.append(tile)
            swapped = jnp.dot(
                jnp.concatenate(stack, axis=0), swap, preferred_element_type=jnp.float32
            ).astype(jnp.bfloat16)
            for i in range(batch):
                t = step * batch + i
                vv_ref[tiles + k * per_piece + t] = swapped[i * ROWS : (i + 1) * ROWS]


def project_blocks(blocks, idx_ref, radon_ref, vv_ref, out_hbm, out_ref, out_sems, lhs_refs):
    angles, block, span = radon_ref.shape
    feeds = span // block
    low = lower_half((ROWS, LANES))
    batch = lhs_refs[0].shape[0]

    per_angle = idx_ref.shape[0] // angles

    def gather(start, lhs_ref):
        for n in range(batch):
            base = (start + n) * per_angle
            for i, b in enumerate(blocks):
                row = i * ROWS
                for jp in range(feeds // 2):
                    at = b * feeds + 2 * jp
                    first = vv_ref[idx_ref[base + at]]
                    second = vv_ref[idx_ref[base + at + 1]]
                    lhs_ref[n, row : row + ROWS, jp * LANES : (jp + 1) * LANES] = jnp.where(
                        low, first, second
                    )

    def multiply(start, lhs_ref):
        for n in range(batch):
            a = start + n
            product = lax.dot_general(
                lhs_ref[n], radon_ref[a], (((1,), (1,)), ((), ())), preferred_element_type=jnp.float32
            )
            for pair in range(len(blocks) // 2):
                row = 2 * pair * ROWS
                tile = jnp.concatenate(
                    [product[row : row + ROWS], product[row + ROWS : row + 2 * ROWS]], axis=1
                )
                out_ref[a, :, pair * LANES : (pair + 1) * LANES] = tile.astype(jnp.bfloat16)

    def leave(step):
        here = pl.ds(step * 2 * batch, 2 * batch)
        return pltpu.make_async_copy(out_ref.at[here], out_hbm.at[here], out_sems.at[step])

    gather(0, lhs_refs[0])

    @pl.loop(0, angles // (2 * batch))
    def _(step):
        start = step * 2 * batch

        @pl.when(step > 0)
        def _():
            leave(step - 1).start()

        multiply(start, lhs_refs[0])
        gather(start + batch, lhs_refs[1])
        multiply(start + batch, lhs_refs[1])
        gather(jnp.minimum(start + 2 * batch, angles - batch), lhs_refs[0])

    leave(angles // (2 * batch) - 1).start()

    @pl.loop(0, angles // (2 * batch))
    def _(step):
        leave(step).wait()


def project_kernel(blocks, pieces, idx_ref, radon_ref, *refs):
    vol_refs = refs[:pieces]
    out_hbm, vv_ref, out_ref, out_sems, *lhs_refs = refs[pieces:]
    arrange(vol_refs, vv_ref)
    project_blocks(blocks, idx_ref, radon_ref, vv_ref, out_hbm, out_ref, out_sems, lhs_refs)


def guess(microseconds):
    return pl.CostEstimate(
        flops=int(microseconds * 1.15e9), bytes_accessed=int(microseconds * 1e5), transcendentals=0
    )


def project(idx, radon_tiles, vol_pieces, blocks, name):
    angles, block, span = radon_tiles.shape
    pieces = len(vol_pieces)
    tiles = pieces * vol_pieces[0].shape[1] // LANES
    out_shape = (angles, ROWS, len(blocks) * block)
    return pl.pallas_call(
        functools.partial(project_kernel, blocks, pieces),
        out_shape=jax.ShapeDtypeStruct(out_shape, jnp.bfloat16),
        in_specs=[scalars, everywhere] + [everywhere] * pieces,
        out_specs=anywhere,
        scratch_shapes=[pltpu.VMEM((2 * tiles, ROWS, LANES), jnp.bfloat16)]
        + [pltpu.VMEM(out_shape, jnp.bfloat16), pltpu.SemaphoreType.DMA((angles // (2 * BATCH),))]
        + [pltpu.VMEM((BATCH, len(blocks) * ROWS, span), jnp.bfloat16)] * 2,
        compiler_params=pltpu.CompilerParams(
            vmem_limit_bytes=14 * MEBI + 2 * radon_tiles.size + 2 * math.prod(out_shape)
        ),
        cost_estimate=guess(4 + len(blocks) // 4),
        name=name,
    )(idx, radon_tiles, *vol_pieces)


def back_project_kernel(blocks, has_start, outs, idx_ref, radon_ref, grad_ref, *refs):
    start_ref, refs = (refs[0], refs[1:]) if has_start else (None, refs)
    out_refs, refs = refs[:outs], refs[outs:]
    if has_start:
        *refs, out_sems = refs
        *refs, sums_ref = refs
    acc_refs, (w_ref, *contrib_refs) = refs[:CHAINS], refs[CHAINS:]
    if has_start:
        contrib_refs, start_sem = contrib_refs[:-1], contrib_refs[-1]
        start_copy = pltpu.make_async_copy(start_ref, acc_refs[0], start_sem)
        start_copy.start()
    angles, block, span = radon_ref.shape
    pairs = len(blocks) // 2
    feeds = span // block
    coef_blocks = acc_refs[0].shape[0]

    @pl.loop(0, coef_blocks, unroll=16)
    def _(t):
        for acc_ref in acc_refs[1:] if has_start else acc_refs:
            acc_ref[t] = jnp.zeros((GROUP, LANES), jnp.float32)

    low = lower_half((GROUP, LANES))
    low_rows = lower_half((block, LANES))
    w_ref[...] = jnp.zeros_like(w_ref)

    def widen(slot, a):
        for jp in range(feeds // 2):
            tile = radon_ref[a, :, jp * LANES : (jp + 1) * LANES].astype(jnp.float32)
            turned = swap_halves(tile)
            for side, (first, second) in enumerate(((tile, turned), (turned, tile))):
                lanes = slice((2 * jp + side) * LANES, (2 * jp + side + 1) * LANES)
                w_ref[slot, :block, lanes] = jnp.where(low_rows, first, 0.0).astype(jnp.bfloat16)
                w_ref[slot, block:, lanes] = jnp.where(low_rows, 0.0, second).astype(jnp.bfloat16)

    def multiply(start, half, contrib_ref):
        for n in range(CHAINS):
            a = start + n
            widen(half * CHAINS + n, a)
            lhs = []
            for pair in range(pairs):
                tile = grad_ref[a, :, pair * LANES : (pair + 1) * LANES].astype(jnp.float32)
                real, imag = tile[:GROUP], tile[GROUP:]
                even = jnp.where(low, real, swap_halves(imag))
                odd = jnp.where(low, swap_halves(real), imag)
                lhs.append(jnp.concatenate([even, odd], axis=0).astype(jnp.bfloat16))
            contrib_ref[n] = jnp.dot(
                jnp.concatenate(lhs, axis=0),
                w_ref[half * CHAINS + n],
                preferred_element_type=jnp.float32,
            )

    per_angle = idx_ref.shape[0] // angles

    def scatter(start, contrib_ref):
        bases = [(start + n) * per_angle for n in range(CHAINS)]
        for i, b in enumerate(blocks):
            row = i * GROUP
            for j in range(feeds):
                for n in range(CHAINS):
                    tile = contrib_ref[n, row : row + GROUP, j * LANES : (j + 1) * LANES]
                    acc_refs[n][idx_ref[bases[n] + (b * feeds + j)]] += tile

    multiply(0, 0, contrib_refs[0])
    if has_start:
        start_copy.wait()

    @pl.loop(0, angles // (2 * CHAINS))
    def _(step):
        start = step * 2 * CHAINS
        multiply(start + CHAINS, 1, contrib_refs[1])
        scatter(start, contrib_refs[0])
        multiply(jnp.minimum(start + 2 * CHAINS, angles - CHAINS), 0, contrib_refs[0])
        scatter(start + CHAINS, contrib_refs[1])

    def total(t):
        sums = [acc_ref[t] for acc_ref in acc_refs]
        while len(sums) > 1:
            sums = [sums[i] + sums[i + 1] for i in range(0, len(sums), 2)]
        return sums[0]

    if outs == 1:

        @pl.loop(0, coef_blocks, unroll=16)
        def _(t):
            out_refs[0][t] = total(t)

    else:
        per_piece = out_refs[0].shape[1] // LANES
        leaving = []
        for k, out_ref in enumerate(out_refs):

            @pl.loop(0, per_piece, unroll=16)
            def _(t):
                lanes = pl.ds(pl.multiple_of(t * LANES, LANES), LANES)
                even = total(2 * (k * per_piece + t))
                odd = total(2 * (k * per_piece + t) + 1)
                real = jnp.where(low, even, swap_halves(odd))
                imag = jnp.where(low, swap_halves(even), odd)
                sums_ref[k, :, lanes] = jnp.concatenate([real, imag], axis=0).astype(out_ref.dtype)

            leaving.append(pltpu.make_async_copy(sums_ref.at[k], out_ref, out_sems.at[k]))
            leaving[k].start()
        for copy in leaving:
            copy.wait()


def back_project(idx, radon_tiles, grads, blocks, start, pieces, piece_width, name):
    angles, block, span = radon_tiles.shape
    coef_blocks = pieces * piece_width // block
    rows = len(blocks) * GROUP
    has_start = start is not None
    if has_start:
        out_shape = [jax.ShapeDtypeStruct((ROWS, piece_width), jnp.bfloat16)] * pieces
    else:
        out_shape = [jax.ShapeDtypeStruct((coef_blocks, GROUP, LANES), jnp.float32)]
    operands = [idx, radon_tiles, grads] + ([start] if has_start else [])
    return pl.pallas_call(
        functools.partial(back_project_kernel, blocks, has_start, len(out_shape)),
        out_shape=out_shape,
        in_specs=[scalars] + [everywhere] * 2 + [pl.BlockSpec(memory_space=pl.ANY)] * has_start,
        out_specs=[anywhere if has_start else everywhere] * len(out_shape),
        scratch_shapes=[pltpu.VMEM((coef_blocks, GROUP, LANES), jnp.float32)] * CHAINS
        + [pltpu.VMEM((2 * CHAINS, 2 * block, 2 * span), jnp.bfloat16)]
        + [pltpu.VMEM((CHAINS, rows, 2 * span), jnp.float32)] * 2
        + [pltpu.SemaphoreType.DMA] * has_start
        + [pltpu.VMEM((pieces, ROWS, piece_width), jnp.bfloat16)] * has_start
        + [pltpu.SemaphoreType.DMA((pieces,))] * has_start,
        compiler_params=pltpu.CompilerParams(vmem_limit_bytes=60 * MEBI),
        cost_estimate=guess(4 + len(blocks) // 4),
        name=name,
    )(*operands)


def add_slots(meta_ref, probe_ref, forward_ref, inverse_ref, ext_ref, acc_ref, amp_refs, scratch, first):
    wave_ref, half_ref, delta_ref, back_ref = scratch
    n_pos = lax.axis_size("pos")
    groups = ext_ref.shape[0]
    width = probe_ref.shape[1]
    slots = amp_refs[0].shape[0]
    tile_width = (acc_ref.shape[2] - width) // len(amp_refs)
    chunk = 4
    crows = chunk * GROUP
    chunks = groups // chunk
    wide = width // LANES
    lane_id = lax.broadcasted_iota(jnp.int32, (crows, LANES), 1)

    def product(left, right):
        return jnp.dot(left, right, preferred_element_type=jnp.float32)

    for tile, amp_ref in enumerate(amp_refs):
        order = first + tile
        tile_start = lax.rem(lax.axis_index("pos") + order, n_pos) * tile_width - tile * tile_width
        count = meta_ref[order, slots]

        @pl.loop(0, (count + 1) // 2)
        def _(step):
            shifts, starts, lives = [], [], []
            for n in range(2):
                offset = meta_ref[order, step * 2 + n] - tile_start
                shifts.append(offset % LANES)
                lane_tile = offset // LANES
                starts.append(
                    [pl.multiple_of((lane_tile + m) * LANES, LANES) for m in range(wide + 1)]
                )
                lives.append((step * 2 + n < count).astype(jnp.float32))
            for n in range(2):
                keep = lane_id < LANES - shifts[n]
                back_shift = (LANES - shifts[n]) % LANES
                for ch in range(chunks):
                    rows = slice(ch * crows, (ch + 1) * crows)
                    low_rows = slice(width + ch * crows, width + (ch + 1) * crows)
                    turned = []
                    for start in starts[n]:
                        both = ext_ref[ch * chunk : (ch + 1) * chunk, :, pl.ds(start, LANES)]
                        both = both.astype(jnp.float32)
                        turned.append(
                            [
                                pltpu.roll(
                                    both[:, c * GROUP : (c + 1) * GROUP].reshape(crows, LANES),
                                    back_shift,
                                    1,
                                )
                                for c in range(2)
                            ]
                        )
                    for m in range(wide):
                        lanes = slice(m * LANES, (m + 1) * LANES)
                        put = slice(n * width + m * LANES, n * width + (m + 1) * LANES)
                        patch_re = jnp.where(keep, turned[m][0], turned[m + 1][0])
                        patch_im = jnp.where(keep, turned[m][1], turned[m + 1][1])
                        probe_re = probe_ref[0, rows, lanes].astype(jnp.float32)
                        probe_im = probe_ref[1, rows, lanes].astype(jnp.float32)
                        wave_re = probe_re * patch_re - probe_im * patch_im
                        wave_im = probe_re * patch_im + probe_im * patch_re
                        wave_ref[rows, put] = wave_re.astype(jnp.bfloat16)
                        wave_ref[low_rows, put] = wave_im.astype(jnp.bfloat16)
                mine = slice(n * width, (n + 1) * width)
                half = product(forward_ref[...], wave_ref[:, mine]).astype(jnp.bfloat16)
                half_ref[mine, :width] = half[:width]
                half_ref[mine, width:] = half[width:]
            for n in range(2):
                mine = slice(n * width, (n + 1) * width)
                far = product(half_ref[mine, :], inverse_ref[...])
                for ch in range(chunks):
                    rows = slice(ch * crows, (ch + 1) * crows)
                    low_rows = slice(width + ch * crows, width + (ch + 1) * crows)
                    far_re, far_im = far[rows, :width], far[rows, width:]
                    power = far_re * far_re + far_im * far_im
                    amps = amp_ref[step * 2 + n, rows, :].astype(jnp.float32)
                    factor = amps * lax.rsqrt(jnp.maximum(power, 1.0)) - 1.0
                    delta_ref[rows, mine] = (far_re * factor).astype(jnp.bfloat16)
                    delta_ref[low_rows, mine] = (far_im * factor).astype(jnp.bfloat16)
                back = product(inverse_ref[...], delta_ref[:, mine]).astype(jnp.bfloat16)
                back_ref[mine, :width] = back[:width]
                back_ref[mine, width:] = back[width:]
            for n in range(2):
                mine = slice(n * width, (n + 1) * width)
                near = product(back_ref[mine, :], forward_ref[...])
                past = lane_id >= shifts[n]
                for ch in range(chunks):
                    rows = slice(ch * crows, (ch + 1) * crows)
                    turned = []
                    for m in range(wide):
                        lanes = slice(m * LANES, (m + 1) * LANES)
                        probe_re = probe_ref[0, rows, lanes].astype(jnp.float32) * lives[n]
                        probe_im = probe_ref[1, rows, lanes].astype(jnp.float32) * lives[n]
                        near_re = near[rows, m * LANES : (m + 1) * LANES]
                        near_im = near[rows, width + m * LANES : width + (m + 1) * LANES]
                        turned.append(
                            [
                                pltpu.roll(probe_re * near_re + probe_im * near_im, shifts[n], 1),
                                pltpu.roll(probe_re * near_im - probe_im * near_re, shifts[n], 1),
                            ]
                        )
                    for m in range(wide + 1):
                        for c in range(2):
                            behind = turned[m - 1][c] if m > 0 else 0.0
                            ahead = turned[m][c] if m < wide else 0.0
                            here = (c, rows, pl.ds(starts[n][m], LANES))
                            acc_ref[here] += jnp.where(past, ahead, behind)


def exit_first_kernel(tiles, meta_ref, probe_ref, forward_ref, inverse_ref, sino_ref, *refs):
    amp_refs, refs = refs[:tiles], refs[tiles:]
    partial_ref, grad_ref, spill_ref, acc_ref, *scratch = refs
    groups = sino_ref.shape[0]
    width = probe_ref.shape[1]
    done = sino_ref.shape[2] - width

    @pl.loop(0, groups)
    def _(g):
        rows = pl.ds(pl.multiple_of(g * GROUP, GROUP), GROUP)
        for c in range(2):
            acc_ref[c, rows, :] = jnp.zeros((GROUP, acc_ref.shape[2]), jnp.float32)

    add_slots(
        meta_ref, probe_ref, forward_ref, inverse_ref, sino_ref, acc_ref, amp_refs, scratch, 0
    )

    @pl.loop(0, groups)
    def _(g):
        rows = pl.ds(pl.multiple_of(g * GROUP, GROUP), GROUP)
        whole = [acc_ref[c, rows, width:done] for c in range(2)]
        grad_ref[g] = jnp.concatenate(whole, axis=0).astype(jnp.bfloat16)
        for c in range(2):
            partial_ref[c, rows, :] = acc_ref[c, rows, :width]
            spill_ref[c, rows, :] = acc_ref[c, rows, done:]


def exit_rest_kernel(
    tiles, meta_ref, probe_ref, forward_ref, inverse_ref, early_ref, late_ref, partial_ref, spill_ref, *refs
):
    amp_refs, refs = refs[:tiles], refs[tiles:]
    out_ref, ext_ref, acc_ref, *scratch = refs
    groups = early_ref.shape[0]
    width = probe_ref.shape[1]
    done = width + late_ref.shape[2]

    @pl.loop(0, groups)
    def _(g):
        ext_ref[g, :, :width] = early_ref[g, :, early_ref.shape[2] - width :]
        ext_ref[g, :, width:done] = late_ref[g]
        ext_ref[g, :, done:] = early_ref[g, :, :width]
        rows = pl.ds(pl.multiple_of(g * GROUP, GROUP), GROUP)
        for c in range(2):
            acc_ref[c, rows, :width] = spill_ref[c, rows, :]
            acc_ref[c, rows, width:] = jnp.zeros((GROUP, done), jnp.float32)

    add_slots(
        meta_ref, probe_ref, forward_ref, inverse_ref, ext_ref, acc_ref, amp_refs, scratch,
        lax.axis_size("pos") - tiles,
    )

    @pl.loop(0, groups)
    def _(g):
        rows = pl.ds(pl.multiple_of(g * GROUP, GROUP), GROUP)
        here = [acc_ref[c, rows, :done] for c in range(2)]
        wrapped = [acc_ref[c, rows, done:] + partial_ref[c, rows, :] for c in range(2)]
        out_ref[g, :, :done] = jnp.concatenate(here, axis=0).astype(jnp.bfloat16)
        out_ref[g, :, done:] = jnp.concatenate(wrapped, axis=0).astype(jnp.bfloat16)


def exit_scratch(groups, width, reach):
    return [pltpu.VMEM((2, groups * GROUP, reach), jnp.float32)] + [
        pltpu.VMEM((2 * width, 2 * width), jnp.bfloat16)
    ] * 4


def exit_first(meta, probe_field, tables, sino, amps):
    groups, rows, reach = sino.shape
    width = probe_field.shape[1]
    slices = groups * GROUP
    edge = jax.ShapeDtypeStruct((2, slices, width), jnp.float32)
    grad = jax.ShapeDtypeStruct((groups, rows, reach - 2 * width), jnp.bfloat16)
    return pl.pallas_call(
        functools.partial(exit_first_kernel, len(amps)),
        out_shape=[edge, grad, edge],
        in_specs=[scalars] + [everywhere] * (4 + len(amps)),
        out_specs=[everywhere] * 3,
        scratch_shapes=exit_scratch(groups, width, reach),
        compiler_params=pltpu.CompilerParams(vmem_limit_bytes=60 * MEBI),
        cost_estimate=guess(10),
        name="exit_first",
    )(meta, probe_field, *tables, sino, *amps)


def exit_rest(meta, probe_field, tables, early, late, partial, spill, amps):
    groups, rows = late.shape[:2]
    width = probe_field.shape[1]
    reach = late.shape[2] + 2 * width
    return pl.pallas_call(
        functools.partial(exit_rest_kernel, len(amps)),
        out_shape=jax.ShapeDtypeStruct((groups, rows, reach), jnp.bfloat16),
        in_specs=[scalars] + [everywhere] * (7 + len(amps)),
        out_specs=everywhere,
        scratch_shapes=[pltpu.VMEM((groups, rows, reach), jnp.bfloat16)]
        + exit_scratch(groups, width, reach),
        compiler_params=pltpu.CompilerParams(vmem_limit_bytes=60 * MEBI),
        cost_estimate=guess(10),
        name="exit_rest",
    )(meta, probe_field, *tables, early, late, partial, spill, *amps)


def to_groups(received, own_slices):
    if own_slices == GROUP:
        return received
    devices, rows, columns = received.shape
    merge = GROUP // own_slices
    split = received.reshape(devices // merge, merge, 2, own_slices, columns)
    return split.transpose(0, 2, 1, 3, 4).reshape(devices // merge, ROWS, columns)


def from_groups(grouped, own_slices):
    if own_slices == GROUP:
        return grouped
    groups, rows, columns = grouped.shape
    merge = GROUP // own_slices
    split = grouped.reshape(groups, 2, merge, own_slices, columns)
    return split.transpose(0, 2, 1, 3, 4).reshape(groups * merge, 2 * own_slices, columns)


def pad_rows(block, own_slices):
    if own_slices == GROUP:
        return block
    lead, columns = block.shape[:-2], block.shape[-1]
    split = block.reshape(lead + (2, own_slices, columns))
    more = [(0, 0)] * (split.ndim - 2) + [(0, GROUP - own_slices), (0, 0)]
    return jnp.pad(split, more).reshape(lead + (ROWS, columns))


def cut_rows(block, own_slices):
    if own_slices == GROUP:
        return block
    lead, columns = block.shape[:-2], block.shape[-1]
    split = block.reshape(lead + (2, GROUP, columns))[..., :own_slices, :]
    return split.reshape(lead + (2 * own_slices, columns))


def everyone(chunk):
    return lax.all_to_all(chunk, ("ang", "pos"), 0, 0, tiled=True)


def on_device(volume, radon_tiles, tile_blocks, probe_field, amplitudes, offsets, counts):
    n_pos = lax.axis_size("pos")
    pos = lax.axis_index("pos")
    angles, det_blocks, feeds = tile_blocks.shape
    block_size = radon_tiles.shape[1]
    columns = det_blocks * block_size
    tile_width = columns // n_pos
    slab = volume.shape[1]
    width = volume.shape[2]
    own = slab // n_pos
    rows = 2 * own
    blocks_each = width // block_size

    def slices_for(j):
        start = (pos + j) % n_pos * own
        return lax.dynamic_slice_in_dim(volume, start, own, 1).reshape(rows, width)

    vol_pieces = rotate_pos([slices_for(j) for j in range(n_pos)], 1)
    vol_pieces, amplitudes = lax.optimization_barrier((vol_pieces, amplitudes))
    amp_pieces = rotate_pos(
        [
            lax.dynamic_index_in_dim(amplitudes, (pos - j) % n_pos, 0, keepdims=False)
            for j in range(n_pos)
        ],
        -1,
    )

    owner = tile_blocks // blocks_each
    within = tile_blocks % blocks_each
    piece = (pos - owner) % n_pos
    crossed = (within + jnp.arange(feeds, dtype=jnp.int32)) % 2
    tiles_each = width // LANES

    def by_chunk(idx):
        idx = idx.reshape(angles // n_pos, n_pos, n_pos, det_blocks // n_pos * feeds)
        idx = jnp.stack([jnp.roll(idx[:, p], -p, axis=1) for p in range(n_pos)], axis=1)
        return idx.reshape(angles * det_blocks * feeds)

    tile_idx = by_chunk(crossed * (n_pos * tiles_each) + piece * tiles_each + within // 2)
    block_idx = by_chunk(piece * blocks_each + within)
    padded = [pad_rows(piece, own) for piece in vol_pieces]
    probe_width = probe_field.shape[1]
    tables = dft_tables(probe_width)
    half = n_pos // 2
    reach = (half * tile_width + probe_width) // block_size
    edge = probe_width // block_size
    early_blocks = list(range(reach))
    late_blocks = list(range(reach, det_blocks))
    first_blocks = list(range(edge, half * tile_width // block_size))
    rest_blocks = list(range(half * tile_width // block_size, det_blocks)) + list(range(edge))

    sino_early = project(tile_idx, radon_tiles, padded, early_blocks, "project_early")
    sino_early, padded, offsets, counts = lax.optimization_barrier(
        (sino_early, padded, offsets, counts)
    )
    meta = jnp.concatenate([offsets, counts], axis=1)
    meta = rotate_pos(
        [lax.dynamic_slice_in_dim(meta, (pos - j) % n_pos, 1, 0) for j in range(n_pos)], -1
    )
    meta = jnp.concatenate(meta, axis=0)
    padded, meta = lax.optimization_barrier((padded, meta))
    sino_late = project(tile_idx, radon_tiles, padded, late_blocks, "project_late")
    got_early = everyone(cut_rows(sino_early, own))
    got_early, sino_late = lax.optimization_barrier((got_early, sino_late))
    got_late = everyone(cut_rows(sino_late, own))
    got_early, got_late = to_groups(got_early, own), to_groups(got_late, own)
    got_early, amp_pieces = lax.optimization_barrier((got_early, amp_pieces))
    partial, first_grad, spill = exit_first(meta, probe_field, tables, got_early, amp_pieces[:half])
    first_sent, got_late = lax.optimization_barrier((first_grad, got_late))
    rest_grad = exit_rest(
        meta, probe_field, tables, got_early, got_late, partial, spill, amp_pieces[half:]
    )
    back_first = everyone(from_groups(first_sent, own))
    wrapped = rest_grad.shape[2] - probe_width
    tile_pieces = [jnp.concatenate([rest_grad[:, :, wrapped:], first_grad[:, :, : tile_width - probe_width]], axis=2)]
    for j in range(1, n_pos):
        source, begin = (first_grad, j * tile_width - probe_width) if j < half else (rest_grad, (j - half) * tile_width)
        tile_pieces.append(source[:, :, begin : begin + tile_width])
    tile_pieces = [tile_pieces[0]] + [send_pos(tile_pieces[j], j) for j in range(1, half)] + tile_pieces[half:]
    back_first, rest_sent, tile_pieces[1:half] = lax.optimization_barrier(
        (back_first, rest_grad, tile_pieces[1:half])
    )
    back_rest = everyone(from_groups(rest_sent, own))
    first_sum = back_project(
        block_idx, radon_tiles, pad_rows(back_first, own), first_blocks, None, n_pos, width, "back_first"
    )[0]
    tile_pieces = tile_pieces[:half] + [send_pos(tile_pieces[j], j) for j in range(half, n_pos)]
    obj_pieces = back_project(
        block_idx, radon_tiles, pad_rows(back_rest, own), rest_blocks, first_sum, n_pos, width, "back_rest"
    )
    groups = rest_grad.shape[0]
    tile_pieces = [tile_pieces[-j % n_pos] for j in range(n_pos)]
    tile_pieces = [
        piece.reshape(groups, 2, GROUP, tile_width).transpose(1, 0, 2, 3).reshape(2, groups * GROUP, tile_width)
        for piece in tile_pieces
    ]
    proj_grad = jnp.stack(in_order(tile_pieces, -pos % n_pos), axis=2).astype(jnp.float32)
    obj_pieces = rotate_pos([cut_rows(piece, own) for piece in obj_pieces], -1)
    obj_pieces = [piece.reshape(2, own, width) for piece in in_order(obj_pieces, -pos % n_pos)]
    object_grad = jnp.concatenate(obj_pieces, axis=1).astype(jnp.float32)
    new_volume = volume.astype(jnp.float32) + step_size * object_grad
    return (new_volume, proj_grad)


def solution(mesh):
    in_specs = (
        P(None, "ang", "pos"),
        P(),
        P(),
        P(),
        P("ang", "pos", None, None),
        P("ang", "pos"),
        P("ang", "pos"),
    )
    out_specs = (P(None, "ang", "pos"), P(None, None, "ang", "pos"))
    return jax.shard_map(
        on_device, mesh=mesh, in_specs=in_specs, out_specs=out_specs, check_vma=False
    )
```
